32 devices in a mesh: group: 2 (over x), tm: 8 (over z, y), space: 2 (over core).
Axes of the slice: x: 2, y: 2, z: 4, core: 2. Of those that a mesh axis runs over, the one named last changes fastest.
Arguments:
- iterate: float32 [1024, 128, 512], P(('group', 'space'), 'tm'), parts along dimension 0, may hold values from -3 to 3
- initial: float32 [1024, 512], P(('group', 'space')), parts along dimension 0, may hold values from -4 to 4
Outputs:
- new_iterate: float32 [1024, 128, 512], P(('group', 'space'), 'tm'), parts along dimension 0
The draws below stay inside these ranges and needn't reach their ends.
There are 2 independent parts, one for each index of `group`. The reference program is written for one: setup_inputs(seed, part) draws one part's arguments, and reference() takes and returns one part's arrays. A program takes and returns all parts, laid end to end along the dimension named above; each array names one. Nothing has to cross between parts.
All inputs are finite; a program needn't handle non-finite values.
Results may differ from the reference program's by a relative error of at most 0.0003.
Values sent between devices are 32-bit elements; how exact they have to be, the bound alone decides.
No kernel may reach another device: no remote copies, remote signals or barrier semaphores. Data moves between devices by JAX's collectives and lax.ppermute only.
A program may use at most 192 MiB of HBM per device.

```python
import math
import jax
import jax.numpy as jnp
from jax import lax

NX = 512
NY = 512
STEPS = 128


def shard_levels(key, dims, shards, smallest, largest):
    def one(axis_at, parts):
        steps = jax.random.uniform(jax.random.fold_in(jax.random.fold_in(key, 6), axis_at), (parts,), jnp.float32, smallest / len(shards), largest / len(shards))
        return jnp.repeat(jnp.exp(steps), dims[axis_at] // parts).reshape((-1,) + (1,) * (len(dims) - axis_at - 1))

    loudness = one(*shards[0])
    for cut in shards[1:]:
        loudness = loudness * one(*cut)
    return loudness


def noise(own_key, shape, width, reach, shards=(), kind=jnp.bfloat16):
    array = width * jax.random.normal(own_key, shape, jnp.float32)
    if shards:
        array = array * shard_levels(own_key, shape, shards, -0.22, 0.18)
    return jnp.clip(array, -reach, reach).astype(kind)


def setup_inputs(seed: int = 0, part: int = 0) -> dict:
    arg_keys = jax.random.split(jax.random.key(seed), 3)
    part_keys = jax.random.split(jax.random.fold_in(arg_keys[2], part), 3)
    return {
        "iterate": noise(part_keys[0], (NX, STEPS, NY), 0.6, 3.0, ((0, 2), (1, 8)), jnp.float32),
        "initial": noise(part_keys[1], (NX, NY), 1.0, 4.0, ((0, 2),), jnp.float32),
    }


circulant_alpha = 0.01
DIFFUSION = 2.0
REACTION_STEP = 0.5
HIGHEST = lax.Precision.HIGHEST

def sine_table(row_index, column_index, length):
    product = (row_index + 1)[:, None] * (column_index + 1)[None, :] % (2 * (length + 1))
    return math.sqrt(2.0 / (length + 1)) * jnp.sin(product.astype(jnp.float32) * (math.pi / (length + 1)))

def wave_tables(length):
    index_k = jnp.arange(length, dtype=jnp.int32)
    product = index_k[:, None] * index_k[None, :] % length
    angles = product.astype(jnp.float32) * (2.0 * math.pi / length)
    return (jnp.cos(angles), jnp.sin(angles))

def decay_power(step_index, length, factor):
    return jnp.exp(factor * math.log(circulant_alpha) / length * step_index.astype(jnp.float32))

def stencil_eigen(mode_index, length):
    sines = jnp.sin(mode_index.astype(jnp.float32) * (math.pi / (2.0 * (length + 1))) + math.pi / (2.0 * (length + 1)))
    return 4.0 * sines * sines

def forward_time(values):
    cos_table, sin_table = wave_tables(values.shape[1])
    real_part = jnp.einsum('kt,rty->rky', cos_table, values, precision=HIGHEST)
    imag_part = -jnp.einsum('kt,rty->rky', sin_table, values, precision=HIGHEST)
    return jnp.concatenate([real_part, imag_part], axis=2)

def inverse_time(values):
    length = values.shape[1]
    half_width = values.shape[2] // 2
    cos_table, sin_table = wave_tables(length)
    real_part = values[:, :, :half_width]
    imag_part = values[:, :, half_width:]
    summed = jnp.einsum('tk,rky->rty', cos_table, real_part, precision=HIGHEST)
    summed = summed - jnp.einsum('tk,rky->rty', sin_table, imag_part, precision=HIGHEST)
    return summed / length

def divide_spectrum(values, freq_index, mode_x, mode_y, length, size_x, size_y):
    half_width = values.shape[2] // 2
    real_part = values[:, :, :half_width]
    imag_part = values[:, :, half_width:]
    factor = math.exp(math.log(circulant_alpha) / length)
    angles = freq_index.astype(jnp.float32) * (2.0 * math.pi / length)
    spatial = DIFFUSION * (stencil_eigen(mode_x, size_x)[:, None, None] + stencil_eigen(mode_y, size_y)[None, None, :])
    eigen_real = 1.0 - factor * jnp.cos(angles)[None, :, None] + spatial
    eigen_imag = factor * jnp.sin(angles)[None, :, None]
    denominator = eigen_real * eigen_real + eigen_imag * eigen_imag
    new_real = (real_part * eigen_real + imag_part * eigen_imag) / denominator
    new_imag = (imag_part * eigen_real - real_part * eigen_imag) / denominator
    return jnp.concatenate([new_real, new_imag], axis=2)

def reference(iterate, initial):
    padded = jnp.pad(iterate, ((1, 1), (0, 0), (1, 1)))
    laplace = padded[2:, :, 1:-1] + padded[:-2, :, 1:-1] + padded[1:-1, :, 2:] + padded[1:-1, :, :-2] - 4.0 * iterate
    previous = jnp.concatenate([initial[:, None, :], iterate[:, :-1, :]], axis=1)
    residual = previous - iterate + DIFFUSION * laplace + REACTION_STEP * (iterate - iterate * iterate * iterate)
    step_index = jnp.arange(STEPS, dtype=jnp.int32)
    scaled = residual * decay_power(step_index, STEPS, 1.0)[None, :, None]
    index_x = jnp.arange(NX, dtype=jnp.int32)
    index_y = jnp.arange(NY, dtype=jnp.int32)
    table_x = sine_table(index_x, index_x, NX)
    table_y = sine_table(index_y, index_y, NY)
    modes = jnp.einsum('px,xty->pty', table_x, scaled, precision=HIGHEST)
    modes = jnp.einsum('pty,yz->ptz', modes, table_y, precision=HIGHEST)
    spectrum = forward_time(modes)
    solved = divide_spectrum(spectrum, step_index, index_x, index_y, STEPS, NX, NY)
    back = inverse_time(solved)
    back = jnp.einsum('px,xty->pty', table_x, back, precision=HIGHEST)
    back = jnp.einsum('pty,yz->ptz', back, table_y, precision=HIGHEST)
    return iterate + back * decay_power(step_index, STEPS, -1.0)[None, :, None]
```

```python
import math

import jax
import jax.numpy as jnp
from jax import lax
from jax.sharding import PartitionSpec as P

circulant_alpha = 0.01
DIFFUSION = 2.0
REACTION_STEP = 0.5
PRECISION = lax.Precision.HIGH


def sine_table(row_index, column_index, length):
    product = (row_index + 1)[:, None] * (column_index + 1)[None, :] % (2 * (length + 1))
    return math.sqrt(2.0 / (length + 1)) * jnp.sin(
        product.astype(jnp.float32) * (math.pi / (length + 1))
    )


def stencil_eigen(mode_index, length):
    sines = jnp.sin((mode_index + 1).astype(jnp.float32) * (math.pi / (2.0 * (length + 1))))
    return 4.0 * sines * sines


def swapped(block):
    return lax.ppermute(block, "space", [(0, 1), (1, 0)])


def carried_in(last, slab_decay):
    slabs = lax.axis_size("tm")
    rows = last.shape[0] // slabs
    lasts = lax.all_to_all(last.reshape(slabs, rows, -1), "tm", 0, 0, tiled=True)
    decay = lax.dynamic_slice_in_dim(slab_decay, lax.axis_index("tm") * rows, rows, 0)
    state = lasts[0]
    whole = decay
    for slab in range(1, slabs):
        state = lasts[slab] + decay * state
        whole = whole * decay
    state = circulant_alpha * state / (1.0 - circulant_alpha * whole)
    befores = []
    for slab in range(slabs):
        befores.append(state)
        state = lasts[slab] + decay * state
    befores = lax.all_to_all(jnp.stack(befores), "tm", 0, 0, tiled=True)
    return befores.reshape(last.shape)


def shards(iterate, initial):
    rows, steps, width = iterate.shape
    slab = lax.axis_index("tm")
    slabs = lax.axis_size("tm")
    strip = lax.axis_index("space")
    strips = lax.axis_size("space")
    total = rows * strips
    half = width // strips
    wrap = lax.ppermute(iterate[:, steps - 1, :], "tm", [(slabs - 1, 0)])
    extra = jnp.where(slab == 0, initial - circulant_alpha * wrap, 0.0)
    force = REACTION_STEP * (iterate - iterate * iterate * iterate)
    force = force.at[:, 0, :].add(extra)
    own_x = strip * rows + jnp.arange(rows, dtype=jnp.int32)
    other_x = (1 - strip) * rows + jnp.arange(rows, dtype=jnp.int32)
    own_y = strip * half + jnp.arange(half, dtype=jnp.int32)
    other_y = (1 - strip) * half + jnp.arange(half, dtype=jnp.int32)
    all_x = jnp.arange(total, dtype=jnp.int32)
    all_y = jnp.arange(width, dtype=jnp.int32)
    table_own_y = sine_table(all_y, own_y, width)
    table_other_y = sine_table(all_y, other_y, width)
    table_own_x = sine_table(all_x, own_x, total)
    table_other_x = sine_table(all_x, other_x, total)

    def dot(spec, first, second):
        return jnp.einsum(spec, first, second, precision=PRECISION)

    keep = dot("xty,yq->txq", force, table_own_y)
    send = dot("xty,yq->txq", force, table_other_y)
    got = swapped(send)
    modes = dot("px,txq->tpq", table_own_x, keep) + dot("px,txq->tpq", table_other_x, got)
    decay = 1.0 / (
        1.0 + DIFFUSION * (stencil_eigen(all_x, total)[:, None] + stencil_eigen(own_y, width)[None, :])
    )
    state = decay * modes[0]
    slab_decay = decay
    for step in range(1, steps):
        state = decay * (state + modes[step])
        slab_decay = slab_decay * decay
    state = carried_in(state, slab_decay)
    solved = []
    for step in range(steps):
        state = decay * (state + modes[step])
        solved.append(state)
    solved = jnp.stack(solved)
    keep = dot("px,tpq->txq", table_own_x, solved)
    send = dot("px,tpq->txq", table_other_x, solved)
    got = swapped(send)
    return dot("txq,yq->xty", keep, table_own_y) + dot("txq,yq->xty", got, table_other_y)


def solution(mesh):
    return jax.shard_map(
        shards,
        mesh=mesh,
        in_specs=(P(("group", "space"), "tm", None), P(("group", "space"), None)),
        out_specs=P(("group", "space"), "tm", None),
        check_vma=False,
    )
```

```python
import functools
import math

import jax
import jax.numpy as jnp
import numpy as np
from jax import lax
from jax.experimental import pallas as pl
from jax.experimental.pallas import tpu as pltpu
from jax.sharding import PartitionSpec as P

circulant_alpha = 0.01
DIFFUSION = 2.0
REACTION_STEP = 0.5
VMEM_BYTES = 56 * 1024 * 1024
LANES = 128
SUBLANES = 8


def sine_table(row_index, column_index, length):
    product = np.outer(row_index + 1, column_index + 1) % (2 * (length + 1))
    return math.sqrt(2.0 / (length + 1)) * np.sin(product * (math.pi / (length + 1)))


def stencil_eigen(mode_index, length):
    return 4.0 * np.sin((mode_index + 1) * (math.pi / (2.0 * (length + 1)))) ** 2


def constant(table):
    return jnp.asarray(np.asarray(table, np.float32))


def second_tables(width):
    half = width // 2
    return np.stack([sine_table(np.arange(half), np.arange(s, width, 2), width) for s in (0, 1)])


def first_tables(total):
    rows = total // 2
    return np.stack(
        [
            np.stack(
                [sine_table(np.arange(c, total, 2), s * rows + np.arange(rows), total) for c in (0, 1)]
            )
            for s in (0, 1)
        ]
    )


def decay_tables(total, width):
    first, second = stencil_eigen(np.arange(total), total), stencil_eigen(np.arange(width), width)
    decay = 1.0 / (1.0 + DIFFUSION * (first[:, None] + second[None, :]))
    return np.stack(
        [np.stack([decay[c::2, s::2] for c in (0, 1)]) for s in (0, 1)]
    )


def dot(first, second):
    return lax.dot_general(
        first,
        second,
        (((1,), (0,)), ((), ())),
        precision=lax.Precision.HIGH,
        preferred_element_type=jnp.float32,
    )


def lanes_reversed(block):
    index = LANES - 1 - lax.broadcasted_iota(jnp.int32, (block.shape[0], LANES), 1)
    parts = [
        jnp.take_along_axis(block[:, at : at + LANES], index, axis=1, mode="promise_in_bounds")
        for at in range(0, block.shape[1], LANES)
    ]
    return jnp.concatenate(parts[::-1], axis=1)


def store_rows_reversed(ref, at, block):
    rows, width = block.shape
    index = SUBLANES - 1 - lax.broadcasted_iota(jnp.int32, (SUBLANES, width), 0)
    for row in range(0, rows, SUBLANES):
        ref[at, pl.ds(rows - SUBLANES - row, SUBLANES), :] = jnp.take_along_axis(
            block[row : row + SUBLANES], index, axis=0, mode="promise_in_bounds"
        )


def forward_second_kernel(place, field, initial, own_table, other_table, keep, send):
    rows, steps, width = field.shape
    half = width // 2
    cells = field[...]
    force = jnp.swapaxes(REACTION_STEP * (cells - cells * cells * cells), 0, 1)
    is_first = (place[0] == 0).astype(jnp.float32)
    head = force[0] + is_first * initial[...]
    stacked = jnp.concatenate(
        [head, force[1:].reshape((steps - 1) * rows, width), field[:, steps - 1, :]], axis=0
    )
    sign = 1.0 - 2.0 * place[1].astype(jnp.float32)
    lower = stacked[:, :half]
    upper = sign * lanes_reversed(stacked[:, half:])
    keep[...] = dot(lower + upper, own_table[0]).reshape(keep.shape)
    other = dot(lower - upper, other_table[0])
    for step in range(steps + 1):
        store_rows_reversed(send, step, other[step * rows : (step + 1) * rows])


def forward_second(place, field, initial, tables):
    rows, steps, width = field.shape
    half = width // 2
    block = min(32, rows)
    count = rows // block
    out = jax.ShapeDtypeStruct((steps + 1, rows, half), jnp.float32)
    table = (1, half, half)
    return pl.pallas_call(
        forward_second_kernel,
        grid_spec=pltpu.PrefetchScalarGridSpec(
            num_scalar_prefetch=1,
            grid=(count,),
            in_specs=[
                pl.BlockSpec((block, steps, width), lambda i, place: (i, 0, 0)),
                pl.BlockSpec((block, width), lambda i, place: (i, 0)),
                pl.BlockSpec(table, lambda i, place: (place[1], 0, 0)),
                pl.BlockSpec(table, lambda i, place: (1 - place[1], 0, 0)),
            ],
            out_specs=[
                pl.BlockSpec((steps + 1, block, half), lambda i, place: (0, i, 0)),
                pl.BlockSpec((steps + 1, block, half), lambda i, place: (0, count - 1 - i, 0)),
            ],
        ),
        out_shape=[out, out],
        compiler_params=pltpu.CompilerParams(vmem_limit_bytes=VMEM_BYTES),
        name="forward_second",
    )(place, field, initial, tables, tables)


def forward_first_kernel(steps, slabs, place, keep, got, table, decay, modes, last, state):
    step = pl.program_id(0)
    near, far = keep[0], got[0]

    @pl.when(step == 0)
    def _():
        state[...] = jnp.zeros_like(state)

    parts = [dot(table[0, 0], near + far), dot(table[0, 1], near - far)]

    @pl.when(step < steps)
    def _():
        for c in (0, 1):
            modes[0, c] = parts[c]
            state[c] = decay[0, c] * (state[c] + parts[c])

    @pl.when(step == steps)
    def _():
        is_last = (place[0] == slabs - 1).astype(jnp.float32)
        for c in (0, 1):
            last[c] = state[c] - is_last * parts[c]


def forward_first(place, keep, got, tables, decays, slabs):
    steps, rows, half = keep.shape
    steps = steps - 1
    return pl.pallas_call(
        functools.partial(forward_first_kernel, steps, slabs),
        grid_spec=pltpu.PrefetchScalarGridSpec(
            num_scalar_prefetch=1,
            grid=(steps + 1,),
            in_specs=[
                pl.BlockSpec((1, rows, half), lambda i, place: (i, 0, 0)),
                pl.BlockSpec((1, rows, half), lambda i, place: (i, 0, 0)),
                pl.BlockSpec((1, 2, rows, rows), lambda i, place: (place[1], 0, 0, 0)),
                pl.BlockSpec((1, 2, rows, half), lambda i, place: (place[1], 0, 0, 0)),
            ],
            out_specs=[
                pl.BlockSpec((1, 2, rows, half), lambda i, place: (jnp.minimum(i, steps - 1), 0, 0, 0)),
                pl.BlockSpec((2, rows, half), lambda i, place: (0, 0, 0)),
            ],
            scratch_shapes=[pltpu.VMEM((2, rows, half), jnp.float32)],
        ),
        out_shape=[
            jax.ShapeDtypeStruct((steps, 2, rows, half), jnp.float32),
            jax.ShapeDtypeStruct((2, rows, half), jnp.float32),
        ],
        compiler_params=pltpu.CompilerParams(vmem_limit_bytes=VMEM_BYTES),
        name="forward_first",
    )(place, keep, got, tables, decays)


def close_kernel(place, lasts, decay, gain, befores):
    slabs = lasts.shape[0]
    state = lasts[0]
    for slab in range(1, slabs):
        state = lasts[slab] + decay[0] * state
    state = gain[0] * state
    for slab in range(slabs):
        befores[slab] = state
        if slab < slabs - 1:
            state = lasts[slab] + decay[0] * state


def close(place, lasts, slab_decays, gains):
    slabs, rows, half = lasts.shape
    table = pl.BlockSpec((1, rows, half), lambda i, place: (place[1], place[0], 0))
    whole = pl.BlockSpec((slabs, rows, half), lambda i, place: (0, 0, 0))
    return pl.pallas_call(
        close_kernel,
        grid_spec=pltpu.PrefetchScalarGridSpec(
            num_scalar_prefetch=1, grid=(1,), in_specs=[whole, table, table], out_specs=whole
        ),
        out_shape=jax.ShapeDtypeStruct(lasts.shape, jnp.float32),
        compiler_params=pltpu.CompilerParams(vmem_limit_bytes=VMEM_BYTES),
        name="close",
    )(place, lasts, slab_decays, gains)


def inverse_first_kernel(place, modes, before, table, decay, keep, send, state):
    @pl.when(pl.program_id(0) == 0)
    def _():
        state[...] = before[...]

    parts = []
    for c in (0, 1):
        solved = decay[0, c] * (state[c] + modes[0, c])
        state[c] = solved
        parts.append(dot(table[0, c], solved))
    keep[0] = parts[0] + parts[1]
    store_rows_reversed(send, 0, parts[0] - parts[1])


def inverse_first(place, modes, before, tables, decays):
    steps, _, rows, half = modes.shape
    out = jax.ShapeDtypeStruct((steps, rows, half), jnp.float32)
    return pl.pallas_call(
        inverse_first_kernel,
        grid_spec=pltpu.PrefetchScalarGridSpec(
            num_scalar_prefetch=1,
            grid=(steps,),
            in_specs=[
                pl.BlockSpec((1, 2, rows, half), lambda i, place: (i, 0, 0, 0)),
                pl.BlockSpec((2, rows, half), lambda i, place: (0, 0, 0)),
                pl.BlockSpec((1, 2, rows, rows), lambda i, place: (place[1], 0, 0, 0)),
                pl.BlockSpec((1, 2, rows, half), lambda i, place: (place[1], 0, 0, 0)),
            ],
            out_specs=[
                pl.BlockSpec((1, rows, half), lambda i, place: (i, 0, 0)),
                pl.BlockSpec((1, rows, half), lambda i, place: (i, 0, 0)),
            ],
            scratch_shapes=[pltpu.VMEM((2, rows, half), jnp.float32)],
        ),
        out_shape=[out, out],
        compiler_params=pltpu.CompilerParams(vmem_limit_bytes=VMEM_BYTES),
        name="inverse_first",
    )(place, modes, before, tables, decays)


def inverse_second_kernel(place, keep, got, own_table, other_table, out):
    steps, rows, half = keep.shape
    own = dot(keep[...].reshape(steps * rows, half), own_table[0])
    other = dot(got[...].reshape(steps * rows, half), other_table[0])
    sign = 1.0 - 2.0 * place[1].astype(jnp.float32)
    lower = own + other
    upper = lanes_reversed(sign * (own - other))
    for part, at in ((lower, 0), (upper, half)):
        out[:, :, at : at + half] = jnp.swapaxes(part.reshape(steps, rows, half), 0, 1)


def inverse_second(place, keep, got, tables):
    steps, rows, half = keep.shape
    block = min(32, rows)
    table = (1, half, half)
    slab = pl.BlockSpec((steps, block, half), lambda i, place: (0, i, 0))
    return pl.pallas_call(
        inverse_second_kernel,
        grid_spec=pltpu.PrefetchScalarGridSpec(
            num_scalar_prefetch=1,
            grid=(rows // block,),
            in_specs=[
                slab,
                slab,
                pl.BlockSpec(table, lambda i, place: (place[1], 0, 0)),
                pl.BlockSpec(table, lambda i, place: (1 - place[1], 0, 0)),
            ],
            out_specs=pl.BlockSpec((block, steps, 2 * half), lambda i, place: (i, 0, 0)),
        ),
        out_shape=jax.ShapeDtypeStruct((rows, steps, 2 * half), jnp.float32),
        compiler_params=pltpu.CompilerParams(vmem_limit_bytes=VMEM_BYTES),
        name="inverse_second",
    )(place, keep, got, tables, tables)


def swapped(block):
    return lax.ppermute(block, "space", [(0, 1), (1, 0)])


def shards(iterate, initial):
    rows, steps, width = iterate.shape
    slabs = lax.axis_size("tm")
    total = rows * lax.axis_size("space")
    half = width // 2
    place = jnp.stack([lax.axis_index("tm"), lax.axis_index("space")]).astype(jnp.int32)
    second = second_tables(width)
    first = first_tables(total)
    decay = decay_tables(total, width)
    slab_decay = decay**steps
    gain = circulant_alpha / (1.0 - circulant_alpha * slab_decay**slabs)
    flat = (2, total, half)
    keep, send = forward_second(place, iterate, initial, constant(second))
    modes, last = forward_first(place, keep, swapped(send), constant(first), constant(decay), slabs)
    lasts = lax.all_to_all(last.reshape(slabs, total // slabs, half), "tm", 0, 0, tiled=True)
    befores = close(place, lasts, constant(slab_decay.reshape(flat)), constant(gain.reshape(flat)))
    before = lax.all_to_all(befores, "tm", 0, 0, tiled=True).reshape(last.shape)
    keep, send = inverse_first(
        place, modes, before, constant(np.swapaxes(first, 2, 3)), constant(decay)
    )
    return inverse_second(place, keep, swapped(send), constant(np.swapaxes(second, 1, 2)))


def solution(mesh):
    return jax.shard_map(
        shards,
        mesh=mesh,
        in_specs=(P(("group", "space"), "tm", None), P(("group", "space"), None)),
        out_specs=P(("group", "space"), "tm", None),
        check_vma=False,
    )
```

```python
import functools
import math

import jax
import jax.numpy as jnp
import numpy as np
from jax import lax
from jax.experimental import pallas as pl
from jax.experimental.pallas import tpu as pltpu
from jax.sharding import PartitionSpec as P

circulant_alpha = 0.01
DIFFUSION = 2.0
REACTION_STEP = 0.5
VMEM_BYTES = 28 * 1024 * 1024
LANES = 128
SUBLANES = 8
TILE = 16


def sine_table(row_index, column_index, length):
    product = np.outer(row_index + 1, column_index + 1) % (2 * (length + 1))
    return math.sqrt(2.0 / (length + 1)) * np.sin(product * (math.pi / (length + 1)))


def stencil_eigen(mode_index, length):
    return 4.0 * np.sin((mode_index + 1) * (math.pi / (2.0 * (length + 1)))) ** 2


def second_tables(width):
    half = width // 2
    return np.stack([sine_table(np.arange(half), np.arange(s, width, 2), width) for s in (0, 1)])


def first_tables(total):
    rows = total // 2
    return np.stack(
        [
            np.stack(
                [sine_table(s * rows + np.arange(rows), np.arange(c, total, 2), total) for c in (0, 1)]
            )
            for s in (0, 1)
        ]
    )


def decay_tables(total, width):
    first, second = stencil_eigen(np.arange(total), total), stencil_eigen(np.arange(width), width)
    decay = 1.0 / (1.0 + DIFFUSION * (second[:, None] + first[None, :]))
    return np.stack([np.stack([decay[s::2, c::2] for c in (0, 1)]) for s in (0, 1)])


def constant(table):
    return jnp.asarray(np.asarray(table, np.float32))


def split_constant(table):
    table = np.asarray(table, np.float32)
    high = table.astype(jnp.bfloat16)
    low = (table - high.astype(np.float32)).astype(jnp.bfloat16)
    return jnp.asarray(np.concatenate([high, high, low], axis=-2))


def store_split(ref, at, lane, block):
    depth = ref.shape[-1] // 3
    width = block.shape[-1]
    high = block.astype(jnp.bfloat16)
    low = (block - high.astype(jnp.float32)).astype(jnp.bfloat16)
    for part, value in enumerate((high, low, high)):
        ref[(*at, pl.ds(part * depth + lane, width))] = value


def dot(first, second):
    return jnp.dot(first, second, preferred_element_type=jnp.float32)


def lanes_reversed(block):
    index = LANES - 1 - lax.broadcasted_iota(jnp.int32, (block.shape[0], LANES), 1)
    return jnp.take_along_axis(block, index, axis=1, mode="promise_in_bounds")


def store_rows_reversed(ref, at, block):
    rows, width = block.shape
    index = SUBLANES - 1 - lax.broadcasted_iota(jnp.int32, (SUBLANES, width), 0)
    for row in range(0, rows, SUBLANES):
        ref[at, pl.ds(rows - SUBLANES - row, SUBLANES), :] = jnp.take_along_axis(
            block[row : row + SUBLANES], index, axis=0, mode="promise_in_bounds"
        )


def forward_second_kernel(place, field, initial, own_table, other_table, keep, send, own, other):
    rows, steps, width = field.shape
    half = width // 2
    group = min(SUBLANES, steps)
    is_first = (place[0] == 0).astype(jnp.float32)
    sign = 1.0 - 2.0 * place[1].astype(jnp.float32)

    def put(at, lane, lower, upper):
        shape = lower.shape
        upper = sign * lanes_reversed(upper.reshape(-1, LANES)).reshape(shape)
        store_split(own, at, lane, lower + upper)
        store_split(other, at, lane, lower - upper)

    for row in range(0, rows, TILE):
        cells_at = pl.ds(row, TILE)
        for lane in range(0, half, LANES):
            lanes = (lane, width - LANES - lane)
            for step in range(0, steps, group):
                forces = []
                for at in lanes:
                    cells = field[cells_at, pl.ds(step, group), pl.ds(at, LANES)]
                    force = REACTION_STEP * (cells - cells * cells * cells)
                    force = jnp.swapaxes(force, 0, 1)
                    if step == 0:
                        head = force[:1] + is_first * initial[cells_at, pl.ds(at, LANES)][None]
                        force = jnp.concatenate([head, force[1:]], axis=0)
                    forces.append(force)
                put((pl.ds(step, group), cells_at), lane, *forces)
            ends = [field[cells_at, steps - 1, pl.ds(at, LANES)][None] for at in lanes]
            put((pl.ds(steps, 1), cells_at), lane, *ends)
    keep[...] = dot(own[...].reshape(-1, 3 * half), own_table[0]).reshape(keep.shape)
    result = dot(other[...].reshape(-1, 3 * half), other_table[0])
    for step in range(steps + 1):
        store_rows_reversed(send, step, result[step * rows : (step + 1) * rows])


def forward_second(place, field, initial, tables):
    rows, steps, width = field.shape
    half = width // 2
    block = min(64, rows)
    count = rows // block
    out = jax.ShapeDtypeStruct((steps + 1, rows, half), jnp.float32)
    table = (1, 3 * half, half)
    return pl.pallas_call(
        forward_second_kernel,
        grid_spec=pltpu.PrefetchScalarGridSpec(
            num_scalar_prefetch=1,
            grid=(count,),
            in_specs=[
                pl.BlockSpec((block, steps, width), lambda i, place: (i, 0, 0)),
                pl.BlockSpec((block, width), lambda i, place: (i, 0)),
                pl.BlockSpec(table, lambda i, place: (place[1], 0, 0)),
                pl.BlockSpec(table, lambda i, place: (1 - place[1], 0, 0)),
            ],
            out_specs=[
                pl.BlockSpec((steps + 1, block, half), lambda i, place: (0, i, 0)),
                pl.BlockSpec((steps + 1, block, half), lambda i, place: (0, count - 1 - i, 0)),
            ],
            scratch_shapes=[pltpu.VMEM((steps + 1, block, 3 * half), jnp.bfloat16)] * 2,
        ),
        out_shape=[out, out],
        compiler_params=pltpu.CompilerParams(vmem_limit_bytes=VMEM_BYTES),
        name="forward_second",
    )(place, field, initial, tables, tables)


def forward_first_kernel(
    slabs, place, keep, keep_end, got, got_end, table, decay, modes, last, state, split, split_end
):
    step = pl.program_id(0)
    block, rows, half = keep.shape

    @pl.when(step == 0)
    def _():
        state[...] = jnp.zeros_like(state)

    for at in range(block):
        near, far = keep[at], got[at]
        for c, cells in enumerate((near + far, near - far)):
            store_split(split, (c, pl.ds(at * half, half)), 0, cells.T)
    for c in (0, 1):
        modes[:, c] = dot(split[c], table[0, c]).reshape(block, half, rows)
    for c in (0, 1):
        for row in range(0, half, TILE):
            tile = pl.ds(row, TILE)
            value, rate = state[c, tile], decay[0, c, tile]
            for at in range(block):
                value = rate * (value + modes[at, c, tile])
            state[c, tile] = value

    @pl.when(step == pl.num_programs(0) - 1)
    def _():
        is_last = (place[0] == slabs - 1).astype(jnp.float32)
        near, far = keep_end[0], got_end[0]
        for c, cells in enumerate((near + far, near - far)):
            store_split(split_end, (c, slice(None)), 0, cells.T)
            last[c] = state[c] - is_last * dot(split_end[c], table[0, c])


def forward_first(place, keep, got, tables, decays, slabs):
    steps, rows, half = keep.shape
    steps = steps - 1
    block = min(4, steps)
    step_block = pl.BlockSpec((block, rows, half), lambda i, place: (i, 0, 0))
    end_block = pl.BlockSpec((1, rows, half), lambda i, place: (steps, 0, 0))
    return pl.pallas_call(
        functools.partial(forward_first_kernel, slabs),
        grid_spec=pltpu.PrefetchScalarGridSpec(
            num_scalar_prefetch=1,
            grid=(steps // block,),
            in_specs=[
                step_block,
                end_block,
                step_block,
                end_block,
                pl.BlockSpec((1, 2, 3 * rows, rows), lambda i, place: (place[1], 0, 0, 0)),
                pl.BlockSpec((1, 2, half, rows), lambda i, place: (place[1], 0, 0, 0)),
            ],
            out_specs=[
                pl.BlockSpec((block, 2, half, rows), lambda i, place: (i, 0, 0, 0)),
                pl.BlockSpec((2, half, rows), lambda i, place: (0, 0, 0)),
            ],
            scratch_shapes=[
                pltpu.VMEM((2, half, rows), jnp.float32),
                pltpu.VMEM((2, block * half, 3 * rows), jnp.bfloat16),
                pltpu.VMEM((2, half, 3 * rows), jnp.bfloat16),
            ],
        ),
        out_shape=[
            jax.ShapeDtypeStruct((steps, 2, half, rows), jnp.float32),
            jax.ShapeDtypeStruct((2, half, rows), jnp.float32),
        ],
        compiler_params=pltpu.CompilerParams(vmem_limit_bytes=VMEM_BYTES),
        name="forward_first",
    )(place, keep, keep, got, got, tables, decays)


def close_kernel(place, lasts, decay, gain, before):
    slabs = lasts.shape[0]
    slab = place[0]
    rate = decay[0]
    state = lasts[slab]
    for step in range(1, slabs):
        at = lax.rem(slab + step, slabs)
        state = state * jnp.where(at == 0, circulant_alpha, 1.0)
        state = lasts[at] + rate * state
    state = state * jnp.where(slab == 0, circulant_alpha, 1.0)
    before[...] = gain[0] * state


def close(place, lasts, slab_decays, gains):
    slabs, rows, width = lasts.shape
    block = min(64, rows)
    table = pl.BlockSpec((1, block, width), lambda i, place: (place[1], i, 0))
    return pl.pallas_call(
        close_kernel,
        grid_spec=pltpu.PrefetchScalarGridSpec(
            num_scalar_prefetch=1,
            grid=(rows // block,),
            in_specs=[
                pl.BlockSpec((slabs, block, width), lambda i, place: (0, i, 0)),
                table,
                table,
            ],
            out_specs=pl.BlockSpec((block, width), lambda i, place: (i, 0)),
        ),
        out_shape=jax.ShapeDtypeStruct((rows, width), jnp.float32),
        compiler_params=pltpu.CompilerParams(vmem_limit_bytes=VMEM_BYTES),
        name="close",
    )(place, lasts, slab_decays, gains)


def inverse_first_kernel(place, modes, before, table, decay, keep, send, state, split):
    block, _, half, rows = modes.shape

    @pl.when(pl.program_id(0) == 0)
    def _():
        state[...] = before[...]

    for c in (0, 1):
        for row in range(0, half, TILE):
            tile = pl.ds(row, TILE)
            value, rate = state[c, tile], decay[0, c, tile]
            for at in range(block):
                value = rate * (value + modes[at, c, tile])
                store_split(split, (c, pl.ds(at * half + row, TILE)), 0, value)
            state[c, tile] = value
    even = dot(split[0], table[0, 0])
    odd = dot(split[1], table[0, 1])
    for at in range(block):
        part = slice(at * half, (at + 1) * half)
        keep[at] = (even[part] + odd[part]).T
        store_rows_reversed(send, at, (even[part] - odd[part]).T)


def inverse_first(place, modes, before, tables, decays):
    steps, _, half, rows = modes.shape
    block = min(4, steps)
    out = jax.ShapeDtypeStruct((steps, rows, half), jnp.float32)
    return pl.pallas_call(
        inverse_first_kernel,
        grid_spec=pltpu.PrefetchScalarGridSpec(
            num_scalar_prefetch=1,
            grid=(steps // block,),
            in_specs=[
                pl.BlockSpec((block, 2, half, rows), lambda i, place: (i, 0, 0, 0)),
                pl.BlockSpec((2, half, rows), lambda i, place: (0, 0, 0)),
                pl.BlockSpec((1, 2, 3 * rows, rows), lambda i, place: (place[1], 0, 0, 0)),
                pl.BlockSpec((1, 2, half, rows), lambda i, place: (place[1], 0, 0, 0)),
            ],
            out_specs=[
                pl.BlockSpec((block, rows, half), lambda i, place: (i, 0, 0)),
                pl.BlockSpec((block, rows, half), lambda i, place: (i, 0, 0)),
            ],
            scratch_shapes=[
                pltpu.VMEM((2, half, rows), jnp.float32),
                pltpu.VMEM((2, block * half, 3 * rows), jnp.bfloat16),
            ],
        ),
        out_shape=[out, out],
        compiler_params=pltpu.CompilerParams(vmem_limit_bytes=VMEM_BYTES),
        name="inverse_first",
    )(place, modes, before, tables, decays)


def inverse_second_kernel(
    place, keep, got, own_table, other_table, out, own, other, own_result, other_result
):
    steps, rows, half = keep.shape
    width = 2 * half
    group = min(SUBLANES, steps)
    sign = 1.0 - 2.0 * place[1].astype(jnp.float32)
    for step in range(steps):
        for row in range(0, rows, TILE):
            tile = pl.ds(row, TILE)
            store_split(own, (step, tile), 0, keep[step, tile])
            store_split(other, (step, tile), 0, got[step, tile])
    shape = own_result.shape
    own_result[...] = dot(own[...].reshape(-1, 3 * half), own_table[0]).reshape(shape)
    other_result[...] = dot(other[...].reshape(-1, 3 * half), other_table[0]).reshape(shape)
    for row in range(0, rows, SUBLANES):
        for step in range(0, steps, group):
            for lane in range(0, half, LANES):
                at = (pl.ds(step, group), pl.ds(row, SUBLANES), pl.ds(lane, LANES))
                first, second = own_result[at], other_result[at]
                upper = sign * (first - second)
                upper = lanes_reversed(upper.reshape(-1, LANES)).reshape(upper.shape)
                place_at = (pl.ds(row, SUBLANES), pl.ds(step, group))
                out[(*place_at, pl.ds(lane, LANES))] = jnp.swapaxes(first + second, 0, 1)
                out[(*place_at, pl.ds(width - LANES - lane, LANES))] = jnp.swapaxes(upper, 0, 1)


def inverse_second(place, keep, got, tables):
    steps, rows, half = keep.shape
    block = min(64, rows)
    table = (1, 3 * half, half)
    slab = pl.BlockSpec((steps, block, half), lambda i, place: (0, i, 0))
    return pl.pallas_call(
        inverse_second_kernel,
        grid_spec=pltpu.PrefetchScalarGridSpec(
            num_scalar_prefetch=1,
            grid=(rows // block,),
            in_specs=[
                slab,
                slab,
                pl.BlockSpec(table, lambda i, place: (place[1], 0, 0)),
                pl.BlockSpec(table, lambda i, place: (1 - place[1], 0, 0)),
            ],
            out_specs=pl.BlockSpec((block, steps, 2 * half), lambda i, place: (i, 0, 0)),
            scratch_shapes=[pltpu.VMEM((steps, block, 3 * half), jnp.bfloat16)] * 2
            + [pltpu.VMEM((steps, block, half), jnp.float32)] * 2,
        ),
        out_shape=jax.ShapeDtypeStruct((rows, steps, 2 * half), jnp.float32),
        compiler_params=pltpu.CompilerParams(vmem_limit_bytes=VMEM_BYTES),
        name="inverse_second",
    )(place, keep, got, tables, tables)


def swapped(block):
    return lax.ppermute(block, "space", [(0, 1), (1, 0)])


def shards(iterate, initial):
    rows, steps, width = iterate.shape
    slabs = lax.axis_size("tm")
    total = rows * lax.axis_size("space")
    half = width // 2
    place = jnp.stack([lax.axis_index("tm"), lax.axis_index("space")]).astype(jnp.int32)
    second = second_tables(width)
    first = first_tables(total)
    decay = decay_tables(total, width)
    slab_decay = (decay**steps).reshape(2, width, rows)
    gain = 1.0 / (1.0 - circulant_alpha * slab_decay**slabs)
    keep, send = forward_second(place, iterate, initial, split_constant(second))
    modes, last = forward_first(
        place, keep, swapped(send), split_constant(first), constant(decay), slabs
    )
    lasts = lax.all_gather(last.reshape(width, rows), "tm")
    before = close(place, lasts, constant(slab_decay), constant(gain)).reshape(last.shape)
    keep, send = inverse_first(
        place, modes, before, split_constant(np.swapaxes(first, 2, 3)), constant(decay)
    )
    return inverse_second(place, keep, swapped(send), split_constant(np.swapaxes(second, 1, 2)))


def solution(mesh):
    return jax.shard_map(
        shards,
        mesh=mesh,
        in_specs=(P(("group", "space"), "tm", None), P(("group", "space"), None)),
        out_specs=P(("group", "space"), "tm", None),
        check_vma=False,
    )
```

```python
import functools
import math

import jax
import jax.numpy as jnp
import numpy as np
from jax import lax
from jax.experimental import pallas as pl
from jax.experimental.pallas import tpu as pltpu
from jax.sharding import PartitionSpec as P

circulant_alpha = 0.01
DIFFUSION = 2.0
REACTION_STEP = 0.5
VMEM_BYTES = 28 * 1024 * 1024
LANES = 128
SUBLANES = 8
TILE = 16
CHUNKS = 2


def sine_table(row_index, column_index, length):
    product = np.outer(row_index + 1, column_index + 1) % (2 * (length + 1))
    return math.sqrt(2.0 / (length + 1)) * np.sin(product * (math.pi / (length + 1)))


def stencil_eigen(mode_index, length):
    return 4.0 * np.sin((mode_index + 1) * (math.pi / (2.0 * (length + 1)))) ** 2


def second_tables(width):
    half = width // 2
    return np.stack([sine_table(np.arange(half), np.arange(s, width, 2), width) for s in (0, 1)])


def first_tables(total):
    rows = total // 2
    return np.stack(
        [
            np.stack(
                [sine_table(s * rows + np.arange(rows), np.arange(c, total, 2), total) for c in (0, 1)]
            )
            for s in (0, 1)
        ]
    )


def decay_tables(total, width):
    first, second = stencil_eigen(np.arange(total), total), stencil_eigen(np.arange(width), width)
    decay = 1.0 / (1.0 + DIFFUSION * (second[:, None] + first[None, :]))
    return np.stack([np.stack([decay[s::2, c::2] for c in (0, 1)]) for s in (0, 1)])


def constant(table):
    return jnp.asarray(np.asarray(table, np.float32))


def split_constant(table):
    table = np.asarray(table, np.float32)
    high = table.astype(jnp.bfloat16)
    low = (table - high.astype(np.float32)).astype(jnp.bfloat16)
    return jnp.asarray(np.concatenate([high, high, low], axis=-2))


def store_split(ref, at, lane, block):
    depth = ref.shape[-1] // 3
    width = block.shape[-1]
    high = block.astype(jnp.bfloat16)
    low = (block - high.astype(jnp.float32)).astype(jnp.bfloat16)
    for part, value in enumerate((high, low, high)):
        ref[(*at, pl.ds(part * depth + lane, width))] = value


def dot(first, second):
    return jnp.dot(first, second, preferred_element_type=jnp.float32)


def lanes_reversed(block):
    index = LANES - 1 - lax.broadcasted_iota(jnp.int32, (block.shape[0], LANES), 1)
    return jnp.take_along_axis(block, index, axis=1, mode="promise_in_bounds")


def store_rows_reversed(ref, at, block):
    rows, width = block.shape
    index = SUBLANES - 1 - lax.broadcasted_iota(jnp.int32, (SUBLANES, width), 0)
    for row in range(0, rows, SUBLANES):
        ref[at, pl.ds(rows - SUBLANES - row, SUBLANES), :] = jnp.take_along_axis(
            block[row : row + SUBLANES], index, axis=0, mode="promise_in_bounds"
        )


def in_hbm(array):
    return pltpu.with_memory_space_constraint(array, pltpu.HBM)


def call(kernel, name, grid, in_specs, out_specs, out_shape, scratch, flops):
    return pl.pallas_call(
        kernel,
        grid_spec=pltpu.PrefetchScalarGridSpec(
            num_scalar_prefetch=1,
            grid=(grid,),
            in_specs=in_specs,
            out_specs=out_specs,
            scratch_shapes=scratch,
        ),
        out_shape=out_shape,
        compiler_params=pltpu.CompilerParams(vmem_limit_bytes=VMEM_BYTES),
        cost_estimate=pl.CostEstimate(flops=flops, bytes_accessed=1 << 23, transcendentals=0),
        name=name,
    )


def floats(*shape):
    return jax.ShapeDtypeStruct(shape, jnp.float32)


def forward_second_kernel(place, field, initial, own_table, other_table, *refs):
    keeps, sends, (own, other) = refs[:CHUNKS], refs[CHUNKS : 2 * CHUNKS], refs[2 * CHUNKS :]
    rows, steps, width = field.shape
    half = width // 2
    part = half // CHUNKS
    group = min(SUBLANES, steps)
    is_first = (place[0] == 0).astype(jnp.float32)
    sign = 1.0 - 2.0 * place[1].astype(jnp.float32)

    def put(at, lane, lower, upper):
        shape = lower.shape
        upper = sign * lanes_reversed(upper.reshape(-1, LANES)).reshape(shape)
        store_split(own, at, lane, lower + upper)
        store_split(other, at, lane, lower - upper)

    for row in range(0, rows, TILE):
        cells_at = pl.ds(row, TILE)
        for lane in range(0, half, LANES):
            lanes = (lane, width - LANES - lane)
            for step in range(0, steps, group):
                forces = []
                for at in lanes:
                    cells = field[cells_at, pl.ds(step, group), pl.ds(at, LANES)]
                    force = REACTION_STEP * (cells - cells * cells * cells)
                    force = jnp.swapaxes(force, 0, 1)
                    if step == 0:
                        head = force[:1] + is_first * initial[cells_at, pl.ds(at, LANES)][None]
                        force = jnp.concatenate([head, force[1:]], axis=0)
                    forces.append(force)
                put((pl.ds(step, group), cells_at), lane, *forces)
            ends = [field[cells_at, steps - 1, pl.ds(at, LANES)][None] for at in lanes]
            put((pl.ds(steps, 1), cells_at), lane, *ends)
    kept = dot(own[...].reshape(-1, 3 * half), own_table[0])
    sent = dot(other[...].reshape(-1, 3 * half), other_table[0])
    for chunk in range(CHUNKS):
        lanes = slice(chunk * part, (chunk + 1) * part)
        keeps[chunk][...] = kept[:, lanes].reshape(steps + 1, rows, part)
        for step in range(steps + 1):
            store_rows_reversed(sends[chunk], step, sent[step * rows : (step + 1) * rows, lanes])


def forward_second(place, field, initial, tables):
    rows, steps, width = field.shape
    half = width // 2
    part = half // CHUNKS
    block = min(64, rows)
    count = rows // block
    table = (1, 3 * half, half)
    shape = (steps + 1, block, part)
    outs = call(
        forward_second_kernel,
        "forward_second",
        count,
        [
            pl.BlockSpec((block, steps, width), lambda i, place: (i, 0, 0)),
            pl.BlockSpec((block, width), lambda i, place: (i, 0)),
            pl.BlockSpec(table, lambda i, place: (place[1], 0, 0)),
            pl.BlockSpec(table, lambda i, place: (1 - place[1], 0, 0)),
        ],
        [pl.BlockSpec(shape, lambda i, place: (0, i, 0))] * CHUNKS
        + [pl.BlockSpec(shape, lambda i, place: (0, count - 1 - i, 0))] * CHUNKS,
        [floats(steps + 1, rows, part)] * (2 * CHUNKS),
        [pltpu.VMEM((steps + 1, block, 3 * half), jnp.bfloat16)] * 2,
        1 << 32,
    )(place, in_hbm(field), in_hbm(initial), in_hbm(tables), in_hbm(tables))
    return outs[:CHUNKS], outs[CHUNKS:]


def ranks(slabs):
    return slabs // 2


def forward_first_kernel(slabs, place, keep, keep_end, got, got_end, table, decay, modes, *refs):
    size = ranks(slabs)
    lasts, (state, split, split_end) = refs[:size], refs[size:]
    step = pl.program_id(0)
    block, rows, part = keep.shape

    @pl.when(step == 0)
    def _():
        state[...] = jnp.zeros_like(state)

    for at in range(block):
        near, far = keep[at], got[at]
        for c, cells in enumerate((near + far, near - far)):
            store_split(split, (c, pl.ds(at * part, part)), 0, cells.T)
    for c in (0, 1):
        modes[:, c] = dot(split[c], table[0, c]).reshape(block, part, rows)
    for c in (0, 1):
        for row in range(0, part, TILE):
            tile, at_state = pl.ds(row, TILE), pl.ds(c * part + row, TILE)
            value, rate = state[at_state], decay[0, c, tile]
            for at in range(block):
                value = rate * (value + modes[at, c, tile])
            state[at_state] = value

    @pl.when(step == pl.num_programs(0) - 1)
    def _():
        is_last = (place[0] == slabs - 1).astype(jnp.float32)
        near, far = keep_end[0], got_end[0]
        for c, cells in enumerate((near + far, near - far)):
            store_split(split_end, (c, slice(None)), 0, cells.T)
            at_state = pl.ds(c * part, part)
            state[at_state] = state[at_state] - is_last * dot(split_end[c], table[0, c])
        rank = lax.rem(place[0], size)
        share = 2 * part // size
        for partner in range(size):
            at = pl.multiple_of((rank ^ partner) * share, share)
            lasts[partner][...] = state[pl.ds(at, share)]


def forward_first(place, chunk, keep, got, tables, decays, slabs):
    steps, rows, part = keep.shape
    steps = steps - 1
    block = min(4, steps)
    size = ranks(slabs)
    share = 2 * part // size
    step_block = pl.BlockSpec((block, rows, part), lambda i, place: (i, 0, 0))
    end_block = pl.BlockSpec((1, rows, part), lambda i, place: (steps, 0, 0))
    outs = call(
        functools.partial(forward_first_kernel, slabs),
        "forward_first",
        steps // block,
        [
            step_block,
            end_block,
            step_block,
            end_block,
            pl.BlockSpec((1, 2, 3 * rows, rows), lambda i, place: (place[1], 0, 0, 0)),
            pl.BlockSpec((1, 2, part, rows), lambda i, place: (place[1], 0, chunk, 0)),
        ],
        [pl.BlockSpec((block, 2, part, rows), lambda i, place: (i, 0, 0, 0))]
        + [pl.BlockSpec((share, rows), lambda i, place: (0, 0))] * size,
        [floats(steps, 2, part, rows)] + [floats(share, rows)] * size,
        [
            pltpu.VMEM((2 * part, rows), jnp.float32),
            pltpu.VMEM((2, block * part, 3 * rows), jnp.bfloat16),
            pltpu.VMEM((2, part, 3 * rows), jnp.bfloat16),
        ],
        1 << 31,
    )(place, keep, keep, got, got, in_hbm(tables), in_hbm(decays))
    return outs[0], outs[1:]


def half_sum_kernel(slabs, place, decay, *refs):
    size = ranks(slabs)
    lasts, ordered, total = refs[:size], refs[size], refs[size + 1]
    rank = lax.rem(place[0], size)
    for partner in range(size):
        ordered[rank ^ partner] = lasts[partner][...]
    state = ordered[0]
    for at in range(1, size):
        state = ordered[at] + decay[0] * state
    total[...] = state


def half_sum(place, lasts, slab_decays, slabs):
    size = ranks(slabs)
    share, rows = lasts[0].shape
    whole = pl.BlockSpec((share, rows), lambda i, place: (0, 0))
    return call(
        functools.partial(half_sum_kernel, slabs),
        "half_sum",
        1,
        [pl.BlockSpec((1, share, rows), lambda i, place: (place[1], lax.rem(place[0], size), 0))]
        + [whole] * size,
        [pl.BlockSpec((size, share, rows), lambda i, place: (0, 0, 0)), whole],
        [floats(size, share, rows), floats(share, rows)],
        [],
        1 << 20,
    )(place, in_hbm(slab_decays), *lasts)


def close_kernel(slabs, place, decay, half_decay, gain, ordered, near, far, *refs):
    size = ranks(slabs)
    befores, states = refs[:size], refs[size]
    rank = lax.rem(place[0], size)
    entering = jnp.where(place[0] < size, circulant_alpha, 1.0)
    state = gain[0] * (entering * far[...] + circulant_alpha * half_decay[0] * near[...])
    for at in range(size):
        states[at] = state
        if at < size - 1:
            state = ordered[at] + decay[0] * state
    for partner in range(size):
        befores[partner][...] = states[rank ^ partner]


def close(place, ordered, near, far, slab_decays, half_decays, gains, slabs):
    size, share, rows = ordered.shape
    table = pl.BlockSpec((1, share, rows), lambda i, place: (place[1], lax.rem(place[0], size), 0))
    whole = pl.BlockSpec((share, rows), lambda i, place: (0, 0))
    return call(
        functools.partial(close_kernel, slabs),
        "close",
        1,
        [table] * 3 + [pl.BlockSpec((size, share, rows), lambda i, place: (0, 0, 0)), whole, whole],
        [whole] * size,
        [floats(share, rows)] * size,
        [pltpu.VMEM((size, share, rows), jnp.float32)],
        1 << 20,
    )(place, in_hbm(slab_decays), in_hbm(half_decays), in_hbm(gains), ordered, near, far)


def inverse_first_kernel(slabs, place, modes, table, decay, *refs):
    size = ranks(slabs)
    befores, (keep, send, state, split) = refs[:size], refs[size:]
    block, _, part, rows = modes.shape

    @pl.when(pl.program_id(0) == 0)
    def _():
        rank = lax.rem(place[0], size)
        share = 2 * part // size
        for partner in range(size):
            at = pl.multiple_of((rank ^ partner) * share, share)
            state[pl.ds(at, share)] = befores[partner][...]

    for c in (0, 1):
        for row in range(0, part, TILE):
            tile, at_state = pl.ds(row, TILE), pl.ds(c * part + row, TILE)
            value, rate = state[at_state], decay[0, c, tile]
            for at in range(block):
                value = rate * (value + modes[at, c, tile])
                store_split(split, (c, pl.ds(at * part + row, TILE)), 0, value)
            state[at_state] = value
    even = dot(split[0], table[0, 0])
    odd = dot(split[1], table[0, 1])
    for at in range(block):
        piece = slice(at * part, (at + 1) * part)
        keep[at] = (even[piece] + odd[piece]).T
        store_rows_reversed(send, at, (even[piece] - odd[piece]).T)


def inverse_first(place, chunk, modes, befores, tables, decays, slabs):
    steps, _, part, rows = modes.shape
    block = min(4, steps)
    whole = pl.BlockSpec(befores[0].shape, lambda i, place: (0, 0))
    return call(
        functools.partial(inverse_first_kernel, slabs),
        "inverse_first",
        steps // block,
        [
            pl.BlockSpec((block, 2, part, rows), lambda i, place: (i, 0, 0, 0)),
            pl.BlockSpec((1, 2, 3 * rows, rows), lambda i, place: (place[1], 0, 0, 0)),
            pl.BlockSpec((1, 2, part, rows), lambda i, place: (place[1], 0, chunk, 0)),
        ]
        + [whole] * len(befores),
        [pl.BlockSpec((block, rows, part), lambda i, place: (i, 0, 0))] * 2,
        [floats(steps, rows, part)] * 2,
        [
            pltpu.VMEM((2 * part, rows), jnp.float32),
            pltpu.VMEM((2, block * part, 3 * rows), jnp.bfloat16),
        ],
        1 << 31,
    )(place, modes, in_hbm(tables), in_hbm(decays), *befores)


def inverse_second_kernel(place, own_table, other_table, *refs):
    keeps, gots, refs = refs[:CHUNKS], refs[CHUNKS : 2 * CHUNKS], refs[2 * CHUNKS :]
    out, own, other, own_result, other_result = refs
    steps, rows, part = keeps[0].shape
    half = part * CHUNKS
    width = 2 * half
    group = min(SUBLANES, steps)
    sign = 1.0 - 2.0 * place[1].astype(jnp.float32)
    for step in range(steps):
        for row in range(0, rows, TILE):
            tile = pl.ds(row, TILE)
            for chunk in range(CHUNKS):
                store_split(own, (step, tile), chunk * part, keeps[chunk][step, tile])
                store_split(other, (step, tile), chunk * part, gots[chunk][step, tile])
    shape = own_result.shape
    own_result[...] = dot(own[...].reshape(-1, 3 * half), own_table[0]).reshape(shape)
    other_result[...] = dot(other[...].reshape(-1, 3 * half), other_table[0]).reshape(shape)
    for row in range(0, rows, SUBLANES):
        for step in range(0, steps, group):
            for lane in range(0, half, LANES):
                at = (pl.ds(step, group), pl.ds(row, SUBLANES), pl.ds(lane, LANES))
                first, second = own_result[at], other_result[at]
                upper = sign * (first - second)
                upper = lanes_reversed(upper.reshape(-1, LANES)).reshape(upper.shape)
                place_at = (pl.ds(row, SUBLANES), pl.ds(step, group))
                out[(*place_at, pl.ds(lane, LANES))] = jnp.swapaxes(first + second, 0, 1)
                out[(*place_at, pl.ds(width - LANES - lane, LANES))] = jnp.swapaxes(upper, 0, 1)


def inverse_second(place, keeps, gots, tables):
    steps, rows, part = keeps[0].shape
    half = part * CHUNKS
    block = min(64, rows)
    table = (1, 3 * half, half)
    return call(
        inverse_second_kernel,
        "inverse_second",
        rows // block,
        [
            pl.BlockSpec(table, lambda i, place: (place[1], 0, 0)),
            pl.BlockSpec(table, lambda i, place: (1 - place[1], 0, 0)),
        ]
        + [pl.BlockSpec((steps, block, part), lambda i, place: (0, i, 0))] * (2 * CHUNKS),
        pl.BlockSpec((block, steps, 2 * half), lambda i, place: (i, 0, 0)),
        floats(rows, steps, 2 * half),
        [pltpu.VMEM((steps, block, 3 * half), jnp.bfloat16)] * 2
        + [pltpu.VMEM((steps, block, half), jnp.float32)] * 2,
        1 << 32,
    )(place, in_hbm(tables), in_hbm(tables), *keeps, *gots)


def swapped(block):
    return lax.ppermute(block, "space", [(0, 1), (1, 0)])


def with_partner(block, distance):
    slabs = lax.axis_size("tm")
    return lax.ppermute(block, "tm", [(slab, slab ^ distance) for slab in range(slabs)])


def among_ranks(blocks):
    return [blocks[0]] + [with_partner(block, at) for at, block in enumerate(blocks) if at]


def by_chunk(table, parts):
    strips, _, half, rows = table.shape
    size = half // parts
    return [
        table[:, :, at * size : (at + 1) * size].reshape(strips, 2 * size, rows) for at in range(parts)
    ]


def shards(iterate, initial):
    rows, steps, width = iterate.shape
    slabs = lax.axis_size("tm")
    total = rows * lax.axis_size("space")
    place = jnp.stack([lax.axis_index("tm"), lax.axis_index("space")]).astype(jnp.int32)
    second = second_tables(width)
    first = first_tables(total)
    decay = decay_tables(total, width)
    slab_decay = decay**steps
    half_decay = slab_decay ** ranks(slabs)
    gain = 1.0 / (1.0 - circulant_alpha * half_decay * half_decay)
    closing = [
        [constant(part) for part in parts]
        for parts in zip(*(by_chunk(table, CHUNKS) for table in (slab_decay, half_decay, gain)))
    ]
    first_table, decays = split_constant(first), constant(decay)
    keeps, sends = forward_second(place, iterate, initial, split_constant(second))
    gots = [swapped(send) for send in sends]
    modes, befores = [], []
    for chunk in range(CHUNKS):
        own_modes, lasts = forward_first(
            place, chunk, keeps[chunk], gots[chunk], first_table, decays, slabs
        )
        modes.append(own_modes)
        slab_part, half_part, gain_part = closing[chunk]
        ordered, near = half_sum(place, among_ranks(lasts), slab_part, slabs)
        far = with_partner(near, ranks(slabs))
        befores.append(
            among_ranks(close(place, ordered, near, far, slab_part, half_part, gain_part, slabs))
        )
    inverse_table = split_constant(np.swapaxes(first, 2, 3))
    keeps, sends = zip(
        *(
            inverse_first(place, chunk, modes[chunk], befores[chunk], inverse_table, decays, slabs)
            for chunk in range(CHUNKS)
        )
    )
    gots = [swapped(send) for send in sends]
    return inverse_second(place, keeps, gots, split_constant(np.swapaxes(second, 1, 2)))


def solution(mesh):
    return jax.shard_map(
        shards,
        mesh=mesh,
        in_specs=(P(("group", "space"), "tm", None), P(("group", "space"), None)),
        out_specs=P(("group", "space"), "tm", None),
        check_vma=False,
    )
```

```python
import functools
import math

import jax
import jax.numpy as jnp
import numpy as np
from jax import lax
from jax.experimental import pallas as pl
from jax.experimental.pallas import tpu as pltpu
from jax.sharding import PartitionSpec as P

circulant_alpha = 0.01
DIFFUSION = 2.0
REACTION_STEP = 0.5
VMEM_BYTES = 20 * 1024 * 1024
LANES = 128
SUBLANES = 8
TILE = 16
CHUNKS = 2


def sine_table(row_index, column_index, length):
    product = np.outer(row_index + 1, column_index + 1) % (2 * (length + 1))
    return math.sqrt(2.0 / (length + 1)) * np.sin(product * (math.pi / (length + 1)))


def stencil_eigen(mode_index, length):
    return 4.0 * np.sin((mode_index + 1) * (math.pi / (2.0 * (length + 1)))) ** 2


def second_tables(width):
    half = width // 2
    return np.stack([sine_table(np.arange(half), np.arange(s, width, 2), width) for s in (0, 1)])


def first_tables(total):
    rows = total // 2
    return np.stack(
        [
            np.stack(
                [sine_table(s * rows + np.arange(rows), np.arange(c, total, 2), total) for c in (0, 1)]
            )
            for s in (0, 1)
        ]
    )


def decay_tables(total, width):
    first, second = stencil_eigen(np.arange(total), total), stencil_eigen(np.arange(width), width)
    decay = 1.0 / (1.0 + DIFFUSION * (second[:, None] + first[None, :]))
    return np.stack([np.stack([decay[s::2, c::2] for c in (0, 1)]) for s in (0, 1)])


def constant(table):
    return jnp.asarray(np.asarray(table, np.float32))


def split_constant(table):
    table = np.asarray(table, np.float32)
    high = table.astype(jnp.bfloat16)
    low = (table - high.astype(np.float32)).astype(jnp.bfloat16)
    return jnp.asarray(np.concatenate([high, high, low], axis=-2))


def store_split(ref, at, lane, block):
    depth = ref.shape[-1] // 3
    width = block.shape[-1]
    high = block.astype(jnp.bfloat16)
    low = (block - high.astype(jnp.float32)).astype(jnp.bfloat16)
    for part, value in enumerate((high, low, high)):
        ref[(*at, pl.ds(part * depth + lane, width))] = value


def dot(first, second):
    return jnp.dot(first, second, preferred_element_type=jnp.float32)


def lanes_reversed(block):
    index = LANES - 1 - lax.broadcasted_iota(jnp.int32, (block.shape[0], LANES), 1)
    return jnp.take_along_axis(block, index, axis=1, mode="promise_in_bounds")


def store_rows_reversed(ref, at, start, block):
    rows, width = block.shape
    index = SUBLANES - 1 - lax.broadcasted_iota(jnp.int32, (SUBLANES, width), 0)
    for row in range(0, rows, SUBLANES):
        to = pl.multiple_of(start + rows - SUBLANES - row, SUBLANES)
        ref[at, pl.ds(to, SUBLANES), :] = jnp.take_along_axis(
            block[row : row + SUBLANES], index, axis=0, mode="promise_in_bounds"
        )


IN_VMEM = pl.BlockSpec(memory_space=pltpu.VMEM)
IN_SMEM = pl.BlockSpec(memory_space=pltpu.SMEM)


def in_hbm(array):
    return pltpu.with_memory_space_constraint(array, pltpu.HBM)


def floats(*shape):
    return jax.ShapeDtypeStruct(shape, jnp.float32)


def call(kernel, name, in_specs, out_specs, out_shape, scratch, flops, grid=None):
    if grid is None:
        spec = pl.GridSpec(
            in_specs=[IN_SMEM, *in_specs], out_specs=out_specs, scratch_shapes=scratch
        )
    else:
        spec = pltpu.PrefetchScalarGridSpec(
            num_scalar_prefetch=1,
            grid=(grid,),
            in_specs=in_specs,
            out_specs=out_specs,
            scratch_shapes=scratch,
        )
    return pl.pallas_call(
        kernel,
        grid_spec=spec,
        out_shape=out_shape,
        compiler_params=pltpu.CompilerParams(vmem_limit_bytes=VMEM_BYTES),
        cost_estimate=pl.CostEstimate(flops=flops, bytes_accessed=1 << 23, transcendentals=0),
        name=name,
    )


def forward_second_kernel(place, field, initial, own_table, other_table, *refs):
    keeps, sends, (own, other) = refs[:CHUNKS], refs[CHUNKS : 2 * CHUNKS], refs[2 * CHUNKS :]
    rows, steps, width = field.shape
    half = width // 2
    part = half // CHUNKS
    group = min(SUBLANES, steps)
    is_first = (place[0] == 0).astype(jnp.float32)
    sign = 1.0 - 2.0 * place[1].astype(jnp.float32)
    block = pl.program_id(0)
    kept_at = pl.ds(pl.multiple_of(block * rows, rows), rows)
    sent_at = (pl.num_programs(0) - 1 - block) * rows

    def put(at, lane, lower, upper):
        shape = lower.shape
        upper = sign * lanes_reversed(upper.reshape(-1, LANES)).reshape(shape)
        store_split(own, at, lane, lower + upper)
        store_split(other, at, lane, lower - upper)

    for row in range(0, rows, TILE):
        cells_at = pl.ds(row, TILE)
        for lane in range(0, half, LANES):
            lanes = (lane, width - LANES - lane)
            for step in range(0, steps, group):
                forces = []
                for at in lanes:
                    cells = field[cells_at, pl.ds(step, group), pl.ds(at, LANES)]
                    force = REACTION_STEP * (cells - cells * cells * cells)
                    force = jnp.swapaxes(force, 0, 1)
                    if step == 0:
                        head = force[:1] + is_first * initial[cells_at, pl.ds(at, LANES)][None]
                        force = jnp.concatenate([head, force[1:]], axis=0)
                    forces.append(force)
                put((pl.ds(step, group), cells_at), lane, *forces)
            ends = [field[cells_at, steps - 1, pl.ds(at, LANES)][None] for at in lanes]
            put((pl.ds(steps, 1), cells_at), lane, *ends)
    kept = dot(own[...].reshape(-1, 3 * half), own_table[0])
    sent = dot(other[...].reshape(-1, 3 * half), other_table[0])
    for chunk in range(CHUNKS):
        lanes = slice(chunk * part, (chunk + 1) * part)
        keeps[chunk][:, kept_at, :] = kept[:, lanes].reshape(steps + 1, rows, part)
        for step in range(steps + 1):
            store_rows_reversed(
                sends[chunk], step, sent_at, sent[step * rows : (step + 1) * rows, lanes]
            )


def forward_second(place, field, initial, tables):
    rows, steps, width = field.shape
    half = width // 2
    part = half // CHUNKS
    block = min(32, rows)
    table = (1, 3 * half, half)
    outs = call(
        forward_second_kernel,
        "forward_second",
        [
            pl.BlockSpec((block, steps, width), lambda i, place: (i, 0, 0)),
            pl.BlockSpec((block, width), lambda i, place: (i, 0)),
            pl.BlockSpec(table, lambda i, place: (place[1], 0, 0)),
            pl.BlockSpec(table, lambda i, place: (1 - place[1], 0, 0)),
        ],
        [IN_VMEM] * (2 * CHUNKS),
        [floats(steps + 1, rows, part)] * (2 * CHUNKS),
        [pltpu.VMEM((steps + 1, block, 3 * half), jnp.bfloat16)] * 2,
        1 << 32,
        rows // block,
    )(place, in_hbm(field), in_hbm(initial), in_hbm(tables), in_hbm(tables))
    return outs[:CHUNKS], outs[CHUNKS:]


def ranks(slabs):
    return slabs // 2


def forward_first_kernel(slabs, chunk, place, keep, got, table, decay, modes, *refs):
    size = ranks(slabs)
    lasts, (state, split, split_end) = refs[:size], refs[size:]
    steps, _, part, rows = modes.shape
    block = split.shape[1] // part
    strip = place[1]
    state[...] = jnp.zeros_like(state)
    for step in range(0, steps, block):
        for c in (0, 1):
            for at in range(block):
                near, far = keep[step + at], got[step + at]
                cells = near - far if c else near + far
                store_split(split, (c, pl.ds(at * part, part)), 0, cells.T)
            result = dot(split[c], table[strip, c])
            modes[pl.ds(step, block), c] = result.reshape(block, part, rows)
        for c in (0, 1):
            for row in range(0, part, TILE):
                tile, at_state = pl.ds(row, TILE), pl.ds(c * part + row, TILE)
                value = state[at_state]
                rate = decay[strip, c, pl.ds(chunk * part + row, TILE)]
                for at in range(block):
                    value = rate * (value + modes[step + at, c, tile])
                state[at_state] = value
    is_last = (place[0] == slabs - 1).astype(jnp.float32)
    near, far = keep[steps], got[steps]
    for c, cells in enumerate((near + far, near - far)):
        store_split(split_end, (c, slice(None)), 0, cells.T)
        at_state = pl.ds(c * part, part)
        state[at_state] = state[at_state] - is_last * dot(split_end[c], table[strip, c])
    rank = lax.rem(place[0], size)
    share = 2 * part // size
    for partner in range(size):
        at = pl.multiple_of((rank ^ partner) * share, share)
        lasts[partner][...] = state[pl.ds(at, share)]


def forward_first(place, chunk, keep, got, tables, decays, slabs):
    steps, rows, part = keep.shape
    steps = steps - 1
    block = min(8, steps)
    size = ranks(slabs)
    share = 2 * part // size
    outs = call(
        functools.partial(forward_first_kernel, slabs, chunk),
        "forward_first",
        [IN_VMEM] * 4,
        [IN_VMEM] * (1 + size),
        [floats(steps, 2, part, rows)] + [floats(share, rows)] * size,
        [
            pltpu.VMEM((2 * part, rows), jnp.float32),
            pltpu.VMEM((2, block * part, 3 * rows), jnp.bfloat16),
            pltpu.VMEM((2, part, 3 * rows), jnp.bfloat16),
        ],
        1 << 31,
    )(place, keep, got, tables, decays)
    return outs[0], outs[1:]


def half_sum_kernel(slabs, chunk, place, closing, *refs):
    size = ranks(slabs)
    lasts, ordered, total = refs[:size], refs[size], refs[size + 1]
    share = total.shape[0]
    rank = lax.rem(place[0], size)
    decay = closing[place[1], chunk, 0, pl.ds(pl.multiple_of(rank * share, share), share)]
    for partner in range(size):
        ordered[rank ^ partner] = lasts[partner][...]
    state = ordered[0]
    for at in range(1, size):
        state = ordered[at] + decay * state
    total[...] = state


def half_sum(place, chunk, lasts, closing, slabs):
    size = ranks(slabs)
    share, rows = lasts[0].shape
    return call(
        functools.partial(half_sum_kernel, slabs, chunk),
        "half_sum",
        [IN_VMEM] * (1 + size),
        [IN_VMEM] * 2,
        [floats(size, share, rows), floats(share, rows)],
        [],
        1 << 20,
    )(place, closing, *lasts)


def close_kernel(slabs, chunk, place, closing, ordered, near, far, *refs):
    size = ranks(slabs)
    befores, states = refs[:size], refs[size]
    share = near.shape[0]
    rank = lax.rem(place[0], size)
    at_share = pl.ds(pl.multiple_of(rank * share, share), share)
    decay, half_decay, gain = (closing[place[1], chunk, at, at_share] for at in range(3))
    entering = jnp.where(place[0] < size, circulant_alpha, 1.0)
    state = gain * (entering * far[...] + circulant_alpha * half_decay * near[...])
    for at in range(size):
        states[at] = state
        if at < size - 1:
            state = ordered[at] + decay * state
    for partner in range(size):
        befores[partner][...] = states[rank ^ partner]


def close(place, chunk, ordered, near, far, closing, slabs):
    size, share, rows = ordered.shape
    return call(
        functools.partial(close_kernel, slabs, chunk),
        "close",
        [IN_VMEM] * 4,
        [IN_VMEM] * size,
        [floats(share, rows)] * size,
        [pltpu.VMEM((size, share, rows), jnp.float32)],
        1 << 20,
    )(place, closing, ordered, near, far)


def inverse_first_kernel(slabs, chunk, place, modes, table, decay, *refs):
    size = ranks(slabs)
    befores, (keep, send, state, split) = refs[:size], refs[size:]
    steps, _, part, rows = modes.shape
    block = split.shape[1] // part
    strip = place[1]
    rank = lax.rem(place[0], size)
    share = 2 * part // size
    for partner in range(size):
        at = pl.multiple_of((rank ^ partner) * share, share)
        state[pl.ds(at, share)] = befores[partner][...]
    for step in range(0, steps, block):
        results = []
        for c in (0, 1):
            for row in range(0, part, TILE):
                tile, at_state = pl.ds(row, TILE), pl.ds(c * part + row, TILE)
                value = state[at_state]
                rate = decay[strip, c, pl.ds(chunk * part + row, TILE)]
                for at in range(block):
                    value = rate * (value + modes[step + at, c, tile])
                    store_split(split, (c, pl.ds(at * part + row, TILE)), 0, value)
                state[at_state] = value
            results.append(dot(split[c], table[strip, c]))
        even, odd = results
        for at in range(block):
            piece = slice(at * part, (at + 1) * part)
            keep[step + at] = (even[piece] + odd[piece]).T
            store_rows_reversed(send, step + at, 0, (even[piece] - odd[piece]).T)


def inverse_first(place, chunk, modes, befores, tables, decays, slabs):
    steps, _, part, rows = modes.shape
    block = min(8, steps)
    return call(
        functools.partial(inverse_first_kernel, slabs, chunk),
        "inverse_first",
        [IN_VMEM] * (3 + len(befores)),
        [IN_VMEM] * 2,
        [floats(steps, rows, part)] * 2,
        [
            pltpu.VMEM((2 * part, rows), jnp.float32),
            pltpu.VMEM((2, block * part, 3 * rows), jnp.bfloat16),
        ],
        1 << 31,
    )(place, modes, tables, decays, *befores)


def inverse_second_kernel(place, tables, *refs):
    keeps, gots, refs = refs[:CHUNKS], refs[CHUNKS : 2 * CHUNKS], refs[2 * CHUNKS :]
    out, own, other, own_result, other_result = refs
    rows, steps, width = out.shape
    part = keeps[0].shape[2]
    half = part * CHUNKS
    group = min(SUBLANES, steps)
    strip = place[1]
    sign = 1.0 - 2.0 * strip.astype(jnp.float32)
    start = pl.program_id(0) * rows
    for step in range(steps):
        for row in range(0, rows, TILE):
            tile = pl.ds(row, TILE)
            source = pl.ds(pl.multiple_of(start + row, TILE), TILE)
            for chunk in range(CHUNKS):
                store_split(own, (step, tile), chunk * part, keeps[chunk][step, source])
                store_split(other, (step, tile), chunk * part, gots[chunk][step, source])
    shape = own_result.shape
    own_result[...] = dot(own[...].reshape(-1, 3 * half), tables[strip]).reshape(shape)
    other_result[...] = dot(other[...].reshape(-1, 3 * half), tables[1 - strip]).reshape(shape)
    for row in range(0, rows, SUBLANES):
        for step in range(0, steps, group):
            for lane in range(0, half, LANES):
                at = (pl.ds(step, group), pl.ds(row, SUBLANES), pl.ds(lane, LANES))
                first, second = own_result[at], other_result[at]
                upper = sign * (first - second)
                upper = lanes_reversed(upper.reshape(-1, LANES)).reshape(upper.shape)
                place_at = (pl.ds(row, SUBLANES), pl.ds(step, group))
                out[(*place_at, pl.ds(lane, LANES))] = jnp.swapaxes(first + second, 0, 1)
                out[(*place_at, pl.ds(width - LANES - lane, LANES))] = jnp.swapaxes(upper, 0, 1)


def inverse_second(place, keeps, gots, tables):
    steps, rows, part = keeps[0].shape
    half = part * CHUNKS
    block = min(32, rows)
    return call(
        inverse_second_kernel,
        "inverse_second",
        [IN_VMEM] * (1 + 2 * CHUNKS),
        pl.BlockSpec((block, steps, 2 * half), lambda i, place: (i, 0, 0)),
        floats(rows, steps, 2 * half),
        [pltpu.VMEM((steps, block, 3 * half), jnp.bfloat16)] * 2
        + [pltpu.VMEM((steps, block, half), jnp.float32)] * 2,
        1 << 32,
        rows // block,
    )(place, tables, *keeps, *gots)


def swapped(block):
    return lax.ppermute(block, "space", [(0, 1), (1, 0)])


def with_partner(block, distance):
    slabs = lax.axis_size("tm")
    return lax.ppermute(block, "tm", [(slab, slab ^ distance) for slab in range(slabs)])


def among_ranks(blocks):
    return [blocks[0]] + [with_partner(block, at) for at, block in enumerate(blocks) if at]


def by_chunk(table):
    strips, _, half, rows = table.shape
    parts = table.reshape(strips, 2, CHUNKS, half // CHUNKS, rows)
    return np.swapaxes(parts, 1, 2).reshape(strips, CHUNKS, 2 * half // CHUNKS, rows)


def shards(iterate, initial):
    rows, steps, width = iterate.shape
    slabs = lax.axis_size("tm")
    total = rows * lax.axis_size("space")
    place = jnp.stack([lax.axis_index("tm"), lax.axis_index("space")]).astype(jnp.int32)
    second = second_tables(width)
    first = first_tables(total)
    decay = decay_tables(total, width)
    slab_decay = decay**steps
    half_decay = slab_decay ** ranks(slabs)
    gain = 1.0 / (1.0 - circulant_alpha * half_decay * half_decay)
    closing = constant(
        np.stack([by_chunk(table) for table in (slab_decay, half_decay, gain)], axis=2)
    )
    first_table, decays = split_constant(first), constant(decay)
    keeps, sends = forward_second(place, iterate, initial, split_constant(second))
    gots = [swapped(send) for send in sends]
    modes, befores = [], []
    for chunk in range(CHUNKS):
        own_modes, lasts = forward_first(
            place, chunk, keeps[chunk], gots[chunk], first_table, decays, slabs
        )
        modes.append(own_modes)
        ordered, near = half_sum(place, chunk, among_ranks(lasts), closing, slabs)
        far = with_partner(near, ranks(slabs))
        befores.append(among_ranks(close(place, chunk, ordered, near, far, closing, slabs)))
    inverse_table = split_constant(np.swapaxes(first, 2, 3))
    keeps, sends = zip(
        *(
            inverse_first(place, chunk, modes[chunk], befores[chunk], inverse_table, decays, slabs)
            for chunk in range(CHUNKS)
        )
    )
    gots = [swapped(send) for send in sends]
    return inverse_second(place, keeps, gots, split_constant(np.swapaxes(second, 1, 2)))


def solution(mesh):
    return jax.shard_map(
        shards,
        mesh=mesh,
        in_specs=(P(("group", "space"), "tm", None), P(("group", "space"), None)),
        out_specs=P(("group", "space"), "tm", None),
        check_vma=False,
    )
```

```python
import functools
import math

import jax
import jax.numpy as jnp
import numpy as np
from jax import lax
from jax.experimental import pallas as pl
from jax.experimental.pallas import tpu as pltpu
from jax.sharding import PartitionSpec as P

circulant_alpha = 0.01
DIFFUSION = 2.0
REACTION_STEP = 0.5
VMEM_BYTES = 24 * 1024 * 1024
LANES = 128
SUBLANES = 8
TILE = 16
CHUNKS = 2


def sine_table(row_index, column_index, length):
    product = np.outer(row_index + 1, column_index + 1) % (2 * (length + 1))
    return math.sqrt(2.0 / (length + 1)) * np.sin(product * (math.pi / (length + 1)))


def stencil_eigen(mode_index, length):
    return 4.0 * np.sin((mode_index + 1) * (math.pi / (2.0 * (length + 1)))) ** 2


def second_tables(width):
    half = width // 2
    return np.stack([sine_table(np.arange(half), np.arange(s, width, 2), width) for s in (0, 1)])


def first_tables(total):
    rows = total // 2
    return np.stack(
        [
            np.stack(
                [sine_table(s * rows + np.arange(rows), np.arange(c, total, 2), total) for c in (0, 1)]
            )
            for s in (0, 1)
        ]
    )


def decay_tables(total, width):
    first, second = stencil_eigen(np.arange(total), total), stencil_eigen(np.arange(width), width)
    decay = 1.0 / (1.0 + DIFFUSION * (second[:, None] + first[None, :]))
    return np.stack([np.stack([decay[s::2, c::2] for c in (0, 1)]) for s in (0, 1)])


def constant(table):
    return jnp.asarray(np.asarray(table, np.float32))


def split_constant(table):
    table = np.asarray(table, np.float32)
    high = table.astype(jnp.bfloat16)
    low = (table - high.astype(np.float32)).astype(jnp.bfloat16)
    return jnp.asarray(np.concatenate([high, high, low], axis=-2))


def store_split(ref, at, lane, block):
    depth = ref.shape[-1] // 3
    width = block.shape[-1]
    high = block.astype(jnp.bfloat16)
    low = (block - high.astype(jnp.float32)).astype(jnp.bfloat16)
    for part, value in enumerate((high, low, high)):
        ref[(*at, pl.ds(part * depth + lane, width))] = value


def dot(first, second):
    return jnp.dot(first, second, preferred_element_type=jnp.float32)


def lanes_reversed(block):
    index = LANES - 1 - lax.broadcasted_iota(jnp.int32, (block.shape[0], LANES), 1)
    return jnp.take_along_axis(block, index, axis=1, mode="promise_in_bounds")


def store_rows_reversed(ref, start, block):
    rows, width = block.shape
    index = SUBLANES - 1 - lax.broadcasted_iota(jnp.int32, (SUBLANES, width), 0)
    for row in range(0, rows, SUBLANES):
        to = pl.multiple_of(start + rows - SUBLANES - row, SUBLANES)
        ref[pl.ds(to, SUBLANES), :] = jnp.take_along_axis(
            block[row : row + SUBLANES], index, axis=0, mode="promise_in_bounds"
        )


IN_VMEM = pl.BlockSpec(memory_space=pltpu.VMEM)
IN_SMEM = pl.BlockSpec(memory_space=pltpu.SMEM)


def in_hbm(array):
    return pltpu.with_memory_space_constraint(array, pltpu.HBM)


def floats(*shape):
    return jax.ShapeDtypeStruct(shape, jnp.float32)


def call(kernel, name, in_specs, out_specs, out_shape, scratch, flops, grid=None):
    if grid is None:
        spec = pl.GridSpec(
            in_specs=[IN_SMEM, *in_specs], out_specs=out_specs, scratch_shapes=scratch
        )
    else:
        spec = pltpu.PrefetchScalarGridSpec(
            num_scalar_prefetch=1,
            grid=(grid,),
            in_specs=in_specs,
            out_specs=out_specs,
            scratch_shapes=scratch,
        )
    return pl.pallas_call(
        kernel,
        grid_spec=spec,
        out_shape=out_shape,
        compiler_params=pltpu.CompilerParams(vmem_limit_bytes=VMEM_BYTES),
        cost_estimate=pl.CostEstimate(flops=flops, bytes_accessed=1 << 23, transcendentals=0),
        name=name,
    )


def forward_second_kernel(place, field, initial, own_table, other_table, *refs):
    keeps, sends, scratch = refs[:CHUNKS], refs[CHUNKS : 2 * CHUNKS], refs[2 * CHUNKS :]
    rows, steps, width = field.shape
    half = width // 2
    part = half // CHUNKS
    count = len(scratch) // 2
    piece = rows // count
    group = max(TILE // steps, 1)
    total = rows * pl.num_programs(0)
    start = pl.program_id(0) * rows
    mirror = total - rows - start
    is_first = (place[0] == 0).astype(jnp.float32)
    sign = 1.0 - 2.0 * place[1].astype(jnp.float32)
    ones = lax.broadcasted_iota(jnp.int32, (group, steps, width), 1) == 0
    ones = jnp.where(ones, is_first, 0.0)

    def put(own, other, at, cells):
        lower = cells[:, :half]
        upper = jnp.concatenate(
            [lanes_reversed(cells[:, lane : lane + LANES]) for lane in range(half, width, LANES)][::-1],
            axis=1,
        )
        store_split(own, (pl.ds(at, TILE),), 0, lower + sign * upper)
        store_split(other, (pl.ds(at, TILE),), 0, lower - sign * upper)

    for sub in range(count):
        own, other = scratch[2 * sub : 2 * sub + 2]
        for row in range(0, piece, group):
            at = pl.ds(sub * piece + row, group)
            cells = field[at]
            force = REACTION_STEP * (cells - cells * cells * cells) + ones * initial[at][:, None, :]
            put(own, other, row * steps, force.reshape(TILE, width))
        for row in range(0, piece, TILE):
            ends = field[pl.ds(sub * piece + row, TILE), steps - 1, :]
            put(own, other, piece * steps + row, ends)
        kept = dot(own[...], own_table[0])
        sent = dot(other[...], other_table[0])
        body = piece * steps
        kept_at = pl.multiple_of(start + sub * piece, piece)
        sent_at = pl.multiple_of(mirror + (count - 1 - sub) * piece, piece)
        for chunk in range(CHUNKS):
            keep, send = keeps[chunk], sends[chunk]
            lanes = slice(chunk * part, (chunk + 1) * part)
            keep[pl.ds(pl.multiple_of(kept_at * steps, body), body), :] = kept[:body, lanes]
            keep[pl.ds(total * steps + kept_at, piece), :] = kept[body:, lanes]
            base = pl.multiple_of(sent_at * steps, body)
            for row in range(piece):
                line = sent[row * steps : (row + 1) * steps, lanes]
                send[pl.ds(base + (piece - 1 - row) * steps, steps), :] = line
            store_rows_reversed(send, total * steps + sent_at, sent[body:, lanes])


def forward_second(place, field, initial, tables):
    rows, steps, width = field.shape
    half = width // 2
    block, pieces = min(64, rows), 2
    table = (1, 3 * half, half)
    depth = (steps + 1) * block // pieces
    outs = call(
        forward_second_kernel,
        "forward_second",
        [
            pl.BlockSpec((block, steps, width), lambda i, place: (i, 0, 0)),
            pl.BlockSpec((block, width), lambda i, place: (i, 0)),
            pl.BlockSpec(table, lambda i, place: (place[1], 0, 0)),
            pl.BlockSpec(table, lambda i, place: (1 - place[1], 0, 0)),
        ],
        [IN_VMEM] * (2 * CHUNKS),
        [floats((steps + 1) * rows, half // CHUNKS)] * (2 * CHUNKS),
        [pltpu.VMEM((depth, 3 * half), jnp.bfloat16)] * (2 * pieces),
        1 << 32,
        rows // block,
    )(place, in_hbm(field), in_hbm(initial), in_hbm(tables), in_hbm(tables))
    return outs[:CHUNKS], outs[CHUNKS:]


def ranks(slabs):
    return slabs // 2


def forward_first_kernel(slabs, chunk, place, keep, got, table, decay, modes, *refs):
    size = ranks(slabs)
    lasts, (state, split, split_end) = refs[:size], refs[size:]
    steps, _, part, rows = modes.shape
    block = split.shape[1] // part
    strip = place[1]
    state[...] = jnp.zeros_like(state)
    for step in range(0, steps, block):
        for c in (0, 1):
            for at in range(block):
                cells_at = pl.ds(step + at, rows, stride=steps)
                near, far = keep[cells_at, :], got[cells_at, :]
                cells = near - far if c else near + far
                store_split(split, (c, pl.ds(at * part, part)), 0, cells.T)
            result = dot(split[c], table[strip, c])
            modes[pl.ds(step, block), c] = result.reshape(block, part, rows)
        for c in (0, 1):
            for row in range(0, part, TILE):
                tile, at_state = pl.ds(row, TILE), pl.ds(c * part + row, TILE)
                value = state[at_state]
                rate = decay[strip, c, pl.ds(chunk * part + row, TILE)]
                for at in range(block):
                    value = rate * (value + modes[step + at, c, tile])
                state[at_state] = value
    is_last = (place[0] == slabs - 1).astype(jnp.float32)
    near, far = keep[pl.ds(rows * steps, rows)], got[pl.ds(rows * steps, rows)]
    for c, cells in enumerate((near + far, near - far)):
        store_split(split_end, (c, slice(None)), 0, cells.T)
        at_state = pl.ds(c * part, part)
        state[at_state] = state[at_state] - is_last * dot(split_end[c], table[strip, c])
    rank = lax.rem(place[0], size)
    share = 2 * part // size
    for partner in range(size):
        at = pl.multiple_of((rank ^ partner) * share, share)
        lasts[partner][...] = state[pl.ds(at, share)]


def forward_first(place, chunk, keep, got, tables, decays, slabs):
    rows, part = tables.shape[-1], keep.shape[1]
    steps = keep.shape[0] // rows - 1
    block = min(8, steps)
    size = ranks(slabs)
    share = 2 * part // size
    outs = call(
        functools.partial(forward_first_kernel, slabs, chunk),
        "forward_first",
        [IN_VMEM] * 4,
        [IN_VMEM] * (1 + size),
        [floats(steps, 2, part, rows)] + [floats(share, rows)] * size,
        [
            pltpu.VMEM((2 * part, rows), jnp.float32),
            pltpu.VMEM((2, block * part, 3 * rows), jnp.bfloat16),
            pltpu.VMEM((2, part, 3 * rows), jnp.bfloat16),
        ],
        1 << 31,
    )(place, keep, got, tables, decays)
    return outs[0], outs[1:]


def half_sum_kernel(slabs, chunk, place, closing, *refs):
    size = ranks(slabs)
    lasts, ordered, total = refs[:size], refs[size], refs[size + 1]
    share = total.shape[0]
    rank = lax.rem(place[0], size)
    decay = closing[place[1], chunk, 0, pl.ds(pl.multiple_of(rank * share, share), share)]
    for partner in range(size):
        ordered[rank ^ partner] = lasts[partner][...]
    state = ordered[0]
    for at in range(1, size):
        state = ordered[at] + decay * state
    total[...] = state


def half_sum(place, chunk, lasts, closing, slabs):
    size = ranks(slabs)
    share, rows = lasts[0].shape
    return call(
        functools.partial(half_sum_kernel, slabs, chunk),
        "half_sum",
        [IN_VMEM] * (1 + size),
        [IN_VMEM] * 2,
        [floats(size, share, rows), floats(share, rows)],
        [],
        1 << 20,
    )(place, closing, *lasts)


def close_kernel(slabs, chunk, place, closing, ordered, near, far, *refs):
    size = ranks(slabs)
    befores, states = refs[:size], refs[size]
    share = near.shape[0]
    rank = lax.rem(place[0], size)
    at_share = pl.ds(pl.multiple_of(rank * share, share), share)
    decay, half_decay, gain = (closing[place[1], chunk, at, at_share] for at in range(3))
    entering = jnp.where(place[0] < size, circulant_alpha, 1.0)
    state = gain * (entering * far[...] + circulant_alpha * half_decay * near[...])
    for at in range(size):
        states[at] = state
        if at < size - 1:
            state = ordered[at] + decay * state
    for partner in range(size):
        befores[partner][...] = states[rank ^ partner]


def close(place, chunk, ordered, near, far, closing, slabs):
    size, share, rows = ordered.shape
    return call(
        functools.partial(close_kernel, slabs, chunk),
        "close",
        [IN_VMEM] * 4,
        [IN_VMEM] * size,
        [floats(share, rows)] * size,
        [pltpu.VMEM((size, share, rows), jnp.float32)],
        1 << 20,
    )(place, closing, ordered, near, far)


def inverse_first_kernel(slabs, chunk, place, modes, table, decay, *refs):
    size = ranks(slabs)
    befores, (keep, send, state, split) = refs[:size], refs[size:]
    steps, _, part, rows = modes.shape
    block = split.shape[1] // part
    strip = place[1]
    rank = lax.rem(place[0], size)
    share = 2 * part // size
    for partner in range(size):
        at = pl.multiple_of((rank ^ partner) * share, share)
        state[pl.ds(at, share)] = befores[partner][...]
    for step in range(0, steps, block):
        results = []
        for c in (0, 1):
            for row in range(0, part, TILE):
                tile, at_state = pl.ds(row, TILE), pl.ds(c * part + row, TILE)
                value = state[at_state]
                rate = decay[strip, c, pl.ds(chunk * part + row, TILE)]
                for at in range(block):
                    value = rate * (value + modes[step + at, c, tile])
                    store_split(split, (c, pl.ds(at * part + row, TILE)), 0, value)
                state[at_state] = value
            results.append(dot(split[c], table[strip, c]))
        even, odd = results
        for at in range(block):
            piece = slice(at * part, (at + 1) * part)
            cells_at = pl.ds(step + at, rows, stride=steps)
            keep[cells_at, :] = (even[piece] + odd[piece]).T
            send[cells_at, :] = (even[piece] - odd[piece]).T


def inverse_first(place, chunk, modes, befores, tables, decays, slabs):
    steps, _, part, rows = modes.shape
    block = min(8, steps)
    return call(
        functools.partial(inverse_first_kernel, slabs, chunk),
        "inverse_first",
        [IN_VMEM] * (3 + len(befores)),
        [IN_VMEM] * 2,
        [floats(steps * rows, part)] * 2,
        [
            pltpu.VMEM((2 * part, rows), jnp.float32),
            pltpu.VMEM((2, block * part, 3 * rows), jnp.bfloat16),
        ],
        1 << 31,
    )(place, modes, tables, decays, *befores)


def inverse_second_kernel(place, tables, *refs):
    keeps, gots, refs = refs[:CHUNKS], refs[CHUNKS : 2 * CHUNKS], refs[2 * CHUNKS :]
    out, scratch = refs[0], refs[1:]
    rows, steps, width = out.shape
    part = keeps[0].shape[1]
    half = part * CHUNKS
    count = len(scratch) // 4
    piece = rows // count
    group = max(TILE // steps, 1)
    strip = place[1]
    sign = 1.0 - 2.0 * strip.astype(jnp.float32)
    total = rows * pl.num_programs(0)
    start = pl.program_id(0) * rows
    mirror = total - rows - start
    for sub in range(count):
        own, other, own_result, other_result = scratch[4 * sub : 4 * sub + 4]
        kept_at = pl.multiple_of((start + sub * piece) * steps, piece * steps)
        sent_at = pl.multiple_of((mirror + (count - 1 - sub) * piece) * steps, piece * steps)
        for row in range(0, piece, group):
            to = (pl.ds(row * steps, TILE),)
            for chunk in range(CHUNKS):
                store_split(own, to, chunk * part, keeps[chunk][pl.ds(kept_at + row * steps, TILE)])
                lines = [
                    gots[chunk][pl.ds(sent_at + (piece - 1 - row - at) * steps, steps)]
                    for at in range(group)
                ]
                store_split(other, to, chunk * part, jnp.concatenate(lines, axis=0))
        own_result[...] = dot(own[...], tables[strip])
        other_result[...] = dot(other[...], tables[1 - strip])
        for row in range(0, piece, group):
            at = pl.ds(row * steps, TILE)
            first, second = own_result[at], other_result[at]
            upper = sign * (first - second)
            parts = [
                lanes_reversed(upper[:, lane : lane + LANES]) for lane in range(0, half, LANES)
            ][::-1]
            whole = jnp.concatenate([first + second, *parts], axis=1)
            out[pl.ds(sub * piece + row, group)] = whole.reshape(group, TILE // group, width)


def inverse_second(place, keeps, gots, tables, steps):
    part = keeps[0].shape[1]
    rows = keeps[0].shape[0] // steps
    half = part * CHUNKS
    block, pieces = min(64, rows), 2
    depth = steps * block // pieces
    return call(
        inverse_second_kernel,
        "inverse_second",
        [IN_VMEM] * (1 + 2 * CHUNKS),
        pl.BlockSpec((block, steps, 2 * half), lambda i, place: (i, 0, 0)),
        floats(rows, steps, 2 * half),
        (
            [pltpu.VMEM((depth, 3 * half), jnp.bfloat16)] * 2
            + [pltpu.VMEM((depth, half), jnp.float32)] * 2
        )
        * pieces,
        1 << 32,
        rows // block,
    )(place, tables, *keeps, *gots)


def swapped(block):
    return lax.ppermute(block, "space", [(0, 1), (1, 0)])


def with_partner(block, distance):
    slabs = lax.axis_size("tm")
    return lax.ppermute(block, "tm", [(slab, slab ^ distance) for slab in range(slabs)])


def among_ranks(blocks):
    return [blocks[0]] + [with_partner(block, at) for at, block in enumerate(blocks) if at]


def by_chunk(table):
    strips, _, half, rows = table.shape
    parts = table.reshape(strips, 2, CHUNKS, half // CHUNKS, rows)
    return np.swapaxes(parts, 1, 2).reshape(strips, CHUNKS, 2 * half // CHUNKS, rows)


def shards(iterate, initial):
    rows, steps, width = iterate.shape
    slabs = lax.axis_size("tm")
    total = rows * lax.axis_size("space")
    place = jnp.stack([lax.axis_index("tm"), lax.axis_index("space")]).astype(jnp.int32)
    second = second_tables(width)
    first = first_tables(total)
    decay = decay_tables(total, width)
    slab_decay = decay**steps
    half_decay = slab_decay ** ranks(slabs)
    gain = 1.0 / (1.0 - circulant_alpha * half_decay * half_decay)
    closing = constant(
        np.stack([by_chunk(table) for table in (slab_decay, half_decay, gain)], axis=2)
    )
    first_table, decays = split_constant(first), constant(decay)
    keeps, sends = forward_second(place, iterate, initial, split_constant(second))
    gots = [swapped(send) for send in sends]
    modes, befores = [], []
    for chunk in range(CHUNKS):
        own_modes, lasts = forward_first(
            place, chunk, keeps[chunk], gots[chunk], first_table, decays, slabs
        )
        modes.append(own_modes)
        ordered, near = half_sum(place, chunk, among_ranks(lasts), closing, slabs)
        far = with_partner(near, ranks(slabs))
        befores.append(among_ranks(close(place, chunk, ordered, near, far, closing, slabs)))
    inverse_table = split_constant(np.swapaxes(first, 2, 3))
    keeps, sends = zip(
        *(
            inverse_first(place, chunk, modes[chunk], befores[chunk], inverse_table, decays, slabs)
            for chunk in range(CHUNKS)
        )
    )
    gots = [swapped(send) for send in sends]
    return inverse_second(place, keeps, gots, split_constant(np.swapaxes(second, 1, 2)), steps)


def solution(mesh):
    return jax.shard_map(
        shards,
        mesh=mesh,
        in_specs=(P(("group", "space"), "tm", None), P(("group", "space"), None)),
        out_specs=P(("group", "space"), "tm", None),
        check_vma=False,
    )
```

```python
import functools
import math

import jax
import jax.numpy as jnp
import numpy as np
from jax import lax
from jax.experimental import pallas as pl
from jax.experimental.pallas import tpu as pltpu
from jax.sharding import PartitionSpec as P

circulant_alpha = 0.01
DIFFUSION = 2.0
REACTION_STEP = 0.5
VMEM_BYTES = 24 * 1024 * 1024
LANES = 128
SUBLANES = 8
TILE = 16
CHUNKS = 2


def sine_table(row_index, column_index, length):
    product = np.outer(row_index + 1, column_index + 1) % (2 * (length + 1))
    return math.sqrt(2.0 / (length + 1)) * np.sin(product * (math.pi / (length + 1)))


def stencil_eigen(mode_index, length):
    return 4.0 * np.sin((mode_index + 1) * (math.pi / (2.0 * (length + 1)))) ** 2


def second_tables(width):
    half = width // 2
    return np.stack([sine_table(np.arange(half), np.arange(s, width, 2), width) for s in (0, 1)])


def first_tables(total):
    rows = total // 2
    return np.stack(
        [
            np.stack(
                [sine_table(s * rows + np.arange(rows), np.arange(c, total, 2), total) for c in (0, 1)]
            )
            for s in (0, 1)
        ]
    )


def decay_tables(total, width):
    first, second = stencil_eigen(np.arange(total), total), stencil_eigen(np.arange(width), width)
    decay = 1.0 / (1.0 + DIFFUSION * (second[:, None] + first[None, :]))
    return np.stack([np.stack([decay[s::2, c::2] for c in (0, 1)]) for s in (0, 1)])


def constant(table):
    return jnp.asarray(np.asarray(table, np.float32))


def split_constant(table):
    table = np.asarray(table, np.float32)
    high = table.astype(jnp.bfloat16)
    low = (table - high.astype(np.float32)).astype(jnp.bfloat16)
    return jnp.asarray(np.concatenate([high, high, low], axis=-2))


def store_split(ref, at, lane, block):
    depth = ref.shape[-1] // 3
    width = block.shape[-1]
    high = block.astype(jnp.bfloat16)
    low = (block - high.astype(jnp.float32)).astype(jnp.bfloat16)
    for part, value in enumerate((high, low, high)):
        ref[(*at, pl.ds(part * depth + lane, width))] = value


def dot(first, second):
    return jnp.dot(first, second, preferred_element_type=jnp.float32)


def lanes_reversed(block):
    index = LANES - 1 - lax.broadcasted_iota(jnp.int32, (block.shape[0], LANES), 1)
    return jnp.take_along_axis(block, index, axis=1, mode="promise_in_bounds")


def store_rows_reversed(ref, start, block):
    rows, width = block.shape
    index = SUBLANES - 1 - lax.broadcasted_iota(jnp.int32, (SUBLANES, width), 0)
    for row in range(0, rows, SUBLANES):
        to = pl.multiple_of(start + rows - SUBLANES - row, SUBLANES)
        ref[pl.ds(to, SUBLANES), :] = jnp.take_along_axis(
            block[row : row + SUBLANES], index, axis=0, mode="promise_in_bounds"
        )


IN_VMEM = pl.BlockSpec(memory_space=pltpu.VMEM)
IN_SMEM = pl.BlockSpec(memory_space=pltpu.SMEM)


def in_hbm(array):
    return pltpu.with_memory_space_constraint(array, pltpu.HBM)


def floats(*shape):
    return jax.ShapeDtypeStruct(shape, jnp.float32)


def call(kernel, name, in_specs, out_specs, out_shape, scratch, flops, grid=None):
    if grid is None:
        spec = pl.GridSpec(
            in_specs=[IN_SMEM, *in_specs], out_specs=out_specs, scratch_shapes=scratch
        )
    else:
        spec = pltpu.PrefetchScalarGridSpec(
            num_scalar_prefetch=1,
            grid=(grid,),
            in_specs=in_specs,
            out_specs=out_specs,
            scratch_shapes=scratch,
        )
    return pl.pallas_call(
        kernel,
        grid_spec=spec,
        out_shape=out_shape,
        compiler_params=pltpu.CompilerParams(vmem_limit_bytes=VMEM_BYTES),
        cost_estimate=pl.CostEstimate(flops=flops, bytes_accessed=1 << 23, transcendentals=0),
        name=name,
    )


def forward_second_kernel(place, field, initial, table, sums, *refs):
    sends, scratch = refs[:CHUNKS], refs[CHUNKS:]
    rows, steps, width = field.shape
    half = width // 2
    part = half // CHUNKS
    piece = rows // len(scratch)
    group = max(TILE // steps, 1)
    head = min(steps, SUBLANES)
    total = rows * pl.num_programs(0)
    start = pl.program_id(0) * rows
    mirror = total - rows - start
    is_first = (place[0] == 0).astype(jnp.float32)
    sign = 1.0 - 2.0 * place[1].astype(jnp.float32)
    firsts = lax.broadcasted_iota(jnp.int32, (group, head, width), 1) == 0
    firsts = jnp.where(firsts, is_first, 0.0)

    def put(other, at, sums_at, cells):
        lower = cells[:, :half]
        upper = sign * jnp.concatenate(
            [lanes_reversed(cells[:, lane : lane + LANES]) for lane in range(half, width, LANES)][::-1],
            axis=1,
        )
        sums[pl.ds(sums_at, TILE), :] = lower + upper
        store_split(other, (pl.ds(at, TILE),), 0, lower - upper)

    for sub, other in enumerate(scratch):
        kept_at = pl.multiple_of(start + sub * piece, piece)
        sent_at = pl.multiple_of(mirror + (len(scratch) - 1 - sub) * piece, piece)
        body = piece * steps
        kept_base = pl.multiple_of(kept_at * steps, body)
        for row in range(0, piece, group):
            at = pl.ds(sub * piece + row, group)
            cells = field[at]
            force = REACTION_STEP * (cells - cells * cells * cells)
            starts = force[:, :head] + firsts * initial[at][:, None, :]
            force = jnp.concatenate([starts, force[:, head:]], axis=1) if head < steps else starts
            put(other, row * steps, kept_base + row * steps, force.reshape(TILE, width))
        for row in range(0, piece, TILE):
            ends = field[pl.ds(sub * piece + row, TILE), steps - 1, :]
            put(other, body + row, total * steps + kept_at + row, ends)
        sent = dot(other[...], table[0])
        base = pl.multiple_of(sent_at * steps, body)
        for chunk, send in enumerate(sends):
            lanes = slice(chunk * part, (chunk + 1) * part)
            for row in range(piece):
                line = sent[row * steps : (row + 1) * steps, lanes]
                send[pl.ds(base + (piece - 1 - row) * steps, steps), :] = line
            store_rows_reversed(send, total * steps + sent_at, sent[body:, lanes])


def forward_second(place, field, initial, tables):
    rows, steps, width = field.shape
    half = width // 2
    block, pieces = min(64, rows), 2
    depth = (steps + 1) * block // pieces
    outs = call(
        forward_second_kernel,
        "forward_second",
        [
            pl.BlockSpec((block, steps, width), lambda i, place: (i, 0, 0)),
            pl.BlockSpec((block, width), lambda i, place: (i, 0)),
            pl.BlockSpec((1, 3 * half, half), lambda i, place: (1 - place[1], 0, 0)),
        ],
        [IN_VMEM] * (1 + CHUNKS),
        [floats((steps + 1) * rows, half)]
        + [floats((steps + 1) * rows, half // CHUNKS)] * CHUNKS,
        [pltpu.VMEM((depth, 3 * half), jnp.bfloat16)] * pieces,
        1 << 32,
        rows // block,
    )(place, in_hbm(field), in_hbm(initial), in_hbm(tables))
    return outs[0], outs[1:]


def times_table_kernel(inputs, place, tables, *refs):
    sources, refs = refs[:inputs], refs[inputs:]
    outs, scratch = refs[:-2], refs[-2:]
    piece = scratch[0].shape[0]
    for at in range(0, sources[0].shape[0], piece):
        split = scratch[at // piece % 2]
        for row in range(0, piece, TILE):
            lane = 0
            for source in sources:
                store_split(split, (pl.ds(row, TILE),), lane, source[pl.ds(at + row, TILE)])
                lane += source.shape[1]
        result = dot(split[...], tables[place[1]])
        lane = 0
        for out in outs:
            out[pl.ds(at, piece)] = result[:, lane : lane + out.shape[1]]
            lane += out.shape[1]


def times_table(place, sources, tables, widths, name):
    rows = sources[0].shape[0]
    depth = tables.shape[1]
    return call(
        functools.partial(times_table_kernel, len(sources)),
        name,
        [IN_VMEM] * (1 + len(sources)),
        [IN_VMEM] * len(widths),
        [floats(rows, width) for width in widths],
        [pltpu.VMEM((rows // 8, depth), jnp.bfloat16)] * 2,
        1 << 31,
    )(place, tables, *sources)


def ranks(slabs):
    return slabs // 2


def forward_first_kernel(slabs, chunk, place, keep, got, table, decay, modes, *refs):
    size = ranks(slabs)
    lasts, (state, split, split_end) = refs[:size], refs[size:]
    steps, _, part, rows = modes.shape
    block = split.shape[1] // part
    strip = place[1]
    state[...] = jnp.zeros_like(state)
    for step in range(0, steps, block):
        for c in (0, 1):
            for at in range(block):
                cells_at = pl.ds(step + at, rows, stride=steps)
                near, far = keep[cells_at, :], got[cells_at, :]
                cells = near - far if c else near + far
                store_split(split, (c, pl.ds(at * part, part)), 0, cells.T)
            result = dot(split[c], table[strip, c])
            modes[pl.ds(step, block), c] = result.reshape(block, part, rows)
        for c in (0, 1):
            for row in range(0, part, TILE):
                tile, at_state = pl.ds(row, TILE), pl.ds(c * part + row, TILE)
                value = state[at_state]
                rate = decay[strip, c, pl.ds(chunk * part + row, TILE)]
                for at in range(block):
                    value = rate * (value + modes[step + at, c, tile])
                state[at_state] = value
    is_last = (place[0] == slabs - 1).astype(jnp.float32)
    near, far = keep[pl.ds(rows * steps, rows)], got[pl.ds(rows * steps, rows)]
    for c, cells in enumerate((near + far, near - far)):
        store_split(split_end, (c, slice(None)), 0, cells.T)
        at_state = pl.ds(c * part, part)
        state[at_state] = state[at_state] - is_last * dot(split_end[c], table[strip, c])
    rank = lax.rem(place[0], size)
    share = 2 * part // size
    for partner in range(size):
        at = pl.multiple_of((rank ^ partner) * share, share)
        lasts[partner][...] = state[pl.ds(at, share)]


def forward_first(place, chunk, keep, got, tables, decays, slabs):
    rows, part = tables.shape[-1], keep.shape[1]
    steps = keep.shape[0] // rows - 1
    block = min(8, steps)
    size = ranks(slabs)
    share = 2 * part // size
    outs = call(
        functools.partial(forward_first_kernel, slabs, chunk),
        "forward_first",
        [IN_VMEM] * 4,
        [IN_VMEM] * (1 + size),
        [floats(steps, 2, part, rows)] + [floats(share, rows)] * size,
        [
            pltpu.VMEM((2 * part, rows), jnp.float32),
            pltpu.VMEM((2, block * part, 3 * rows), jnp.bfloat16),
            pltpu.VMEM((2, part, 3 * rows), jnp.bfloat16),
        ],
        1 << 31,
    )(place, keep, got, tables, decays)
    return outs[0], outs[1:]


def half_sum_kernel(slabs, chunk, place, closing, *refs):
    size = ranks(slabs)
    lasts, ordered, total = refs[:size], refs[size], refs[size + 1]
    share = total.shape[0]
    rank = lax.rem(place[0], size)
    decay = closing[place[1], chunk, 0, pl.ds(pl.multiple_of(rank * share, share), share)]
    for partner in range(size):
        ordered[rank ^ partner] = lasts[partner][...]
    state = ordered[0]
    for at in range(1, size):
        state = ordered[at] + decay * state
    total[...] = state


def half_sum(place, chunk, lasts, closing, slabs):
    size = ranks(slabs)
    share, rows = lasts[0].shape
    return call(
        functools.partial(half_sum_kernel, slabs, chunk),
        "half_sum",
        [IN_VMEM] * (1 + size),
        [IN_VMEM] * 2,
        [floats(size, share, rows), floats(share, rows)],
        [],
        1 << 20,
    )(place, closing, *lasts)


def close_kernel(slabs, chunk, place, closing, ordered, near, far, *refs):
    size = ranks(slabs)
    befores, states = refs[:size], refs[size]
    share = near.shape[0]
    rank = lax.rem(place[0], size)
    at_share = pl.ds(pl.multiple_of(rank * share, share), share)
    decay, half_decay, gain = (closing[place[1], chunk, at, at_share] for at in range(3))
    entering = jnp.where(place[0] < size, circulant_alpha, 1.0)
    state = gain * (entering * far[...] + circulant_alpha * half_decay * near[...])
    for at in range(size):
        states[at] = state
        if at < size - 1:
            state = ordered[at] + decay * state
    for partner in range(size):
        befores[partner][...] = states[rank ^ partner]


def close(place, chunk, ordered, near, far, closing, slabs):
    size, share, rows = ordered.shape
    return call(
        functools.partial(close_kernel, slabs, chunk),
        "close",
        [IN_VMEM] * 4,
        [IN_VMEM] * size,
        [floats(share, rows)] * size,
        [pltpu.VMEM((size, share, rows), jnp.float32)],
        1 << 20,
    )(place, closing, ordered, near, far)


def inverse_first_kernel(slabs, chunk, place, modes, table, decay, *refs):
    size = ranks(slabs)
    befores, (keep, send, state, split) = refs[:size], refs[size:]
    steps, _, part, rows = modes.shape
    block = split.shape[1] // part
    strip = place[1]
    rank = lax.rem(place[0], size)
    share = 2 * part // size
    for partner in range(size):
        at = pl.multiple_of((rank ^ partner) * share, share)
        state[pl.ds(at, share)] = befores[partner][...]
    for step in range(0, steps, block):
        results = []
        for c in (0, 1):
            for row in range(0, part, TILE):
                tile, at_state = pl.ds(row, TILE), pl.ds(c * part + row, TILE)
                value = state[at_state]
                rate = decay[strip, c, pl.ds(chunk * part + row, TILE)]
                for at in range(block):
                    value = rate * (value + modes[step + at, c, tile])
                    store_split(split, (c, pl.ds(at * part + row, TILE)), 0, value)
                state[at_state] = value
            results.append(dot(split[c], table[strip, c]))
        even, odd = results
        for at in range(block):
            piece = slice(at * part, (at + 1) * part)
            start = (step + at) * rows
            keep[pl.ds(start, rows), :] = (even[piece] + odd[piece]).T
            store_rows_reversed(send, start, (even[piece] - odd[piece]).T)


def inverse_first(place, chunk, modes, befores, tables, decays, slabs):
    steps, _, part, rows = modes.shape
    block = min(8, steps)
    return call(
        functools.partial(inverse_first_kernel, slabs, chunk),
        "inverse_first",
        [IN_VMEM] * (3 + len(befores)),
        [IN_VMEM] * 2,
        [floats(steps * rows, part)] * 2,
        [
            pltpu.VMEM((2 * part, rows), jnp.float32),
            pltpu.VMEM((2, block * part, 3 * rows), jnp.bfloat16),
        ],
        1 << 31,
    )(place, modes, tables, decays, *befores)


def inverse_second_kernel(place, tables, kept, *refs):
    gots, out, scratch = refs[:CHUNKS], refs[CHUNKS], refs[CHUNKS + 1 :]
    rows, steps, width = out.shape
    half = width // 2
    part = half // CHUNKS
    count = len(scratch) // 2
    piece = rows // count
    group = min(SUBLANES, steps)
    strip = place[1]
    sign = 1.0 - 2.0 * strip.astype(jnp.float32)
    start = pl.program_id(0) * rows
    for sub in range(count):
        split, result = scratch[2 * sub : 2 * sub + 2]
        base = pl.multiple_of(start + sub * piece, piece)
        for step in range(steps):
            for row in range(0, piece, TILE):
                for chunk, got in enumerate(gots):
                    cells = got[step, pl.ds(base + row, TILE)]
                    store_split(split, (step, pl.ds(row, TILE)), chunk * part, cells)
        product = dot(split[...].reshape(steps * piece, 3 * half), tables[1 - strip])
        result[...] = product.reshape(result.shape)
        for row in range(0, piece, SUBLANES):
            for step in range(0, steps, group):
                for lane in range(0, half, LANES):
                    at_steps, at_lanes = pl.ds(step, group), pl.ds(lane, LANES)
                    first = kept[at_steps, pl.ds(base + row, SUBLANES), at_lanes]
                    second = result[at_steps, pl.ds(row, SUBLANES), at_lanes]
                    upper = sign * (first - second)
                    upper = lanes_reversed(upper.reshape(-1, LANES)).reshape(upper.shape)
                    to = (pl.ds(sub * piece + row, SUBLANES), at_steps)
                    out[(*to, at_lanes)] = jnp.swapaxes(first + second, 0, 1)
                    to_lanes = pl.ds(width - LANES - lane, LANES)
                    out[(*to, to_lanes)] = jnp.swapaxes(upper, 0, 1)


def inverse_second(place, kept, gots, tables):
    steps, rows, part = gots[0].shape
    half = part * CHUNKS
    block, pieces = min(64, rows), 2
    piece = block // pieces
    return call(
        inverse_second_kernel,
        "inverse_second",
        [IN_VMEM] * (2 + CHUNKS),
        pl.BlockSpec((block, steps, 2 * half), lambda i, place: (i, 0, 0)),
        floats(rows, steps, 2 * half),
        [
            pltpu.VMEM((steps, piece, 3 * half), jnp.bfloat16),
            pltpu.VMEM((steps, piece, half), jnp.float32),
        ]
        * pieces,
        1 << 32,
        rows // block,
    )(place, tables, kept, *gots)


def swapped(block):
    return lax.ppermute(block, "space", [(0, 1), (1, 0)])


def with_partner(block, distance):
    slabs = lax.axis_size("tm")
    return lax.ppermute(block, "tm", [(slab, slab ^ distance) for slab in range(slabs)])


def among_ranks(blocks):
    return [blocks[0]] + [with_partner(block, at) for at, block in enumerate(blocks) if at]


def by_chunk(table):
    strips, _, half, rows = table.shape
    parts = table.reshape(strips, 2, CHUNKS, half // CHUNKS, rows)
    return np.swapaxes(parts, 1, 2).reshape(strips, CHUNKS, 2 * half // CHUNKS, rows)


def shards(iterate, initial):
    rows, steps, width = iterate.shape
    slabs = lax.axis_size("tm")
    total = rows * lax.axis_size("space")
    place = jnp.stack([lax.axis_index("tm"), lax.axis_index("space")]).astype(jnp.int32)
    second = second_tables(width)
    first = first_tables(total)
    decay = decay_tables(total, width)
    slab_decay = decay**steps
    half_decay = slab_decay ** ranks(slabs)
    gain = 1.0 / (1.0 - circulant_alpha * half_decay * half_decay)
    closing = constant(
        np.stack([by_chunk(table) for table in (slab_decay, half_decay, gain)], axis=2)
    )
    first_table, decays = split_constant(first), constant(decay)
    half = width // 2
    second_table = split_constant(second)
    sums, sends = forward_second(place, iterate, initial, second_table)
    gots = [swapped(send) for send in sends]
    keeps = times_table(place, [sums], second_table, [half // CHUNKS] * CHUNKS, "keep_second")
    modes, befores = [], []
    for chunk in range(CHUNKS):
        own_modes, lasts = forward_first(
            place, chunk, keeps[chunk], gots[chunk], first_table, decays, slabs
        )
        modes.append(own_modes)
        ordered, near = half_sum(place, chunk, among_ranks(lasts), closing, slabs)
        far = with_partner(near, ranks(slabs))
        befores.append(among_ranks(close(place, chunk, ordered, near, far, closing, slabs)))
    inverse_table = split_constant(np.swapaxes(first, 2, 3))
    keeps, sends = zip(
        *(
            inverse_first(place, chunk, modes[chunk], befores[chunk], inverse_table, decays, slabs)
            for chunk in range(CHUNKS)
        )
    )
    gots = [swapped(send).reshape(steps, rows, -1) for send in sends]
    inverse_table = split_constant(np.swapaxes(second, 1, 2))
    kept = times_table(place, keeps, inverse_table, [half], "keep_inverse")[0]
    return inverse_second(place, kept.reshape(steps, rows, half), gots, inverse_table)


def solution(mesh):
    return jax.shard_map(
        shards,
        mesh=mesh,
        in_specs=(P(("group", "space"), "tm", None), P(("group", "space"), None)),
        out_specs=P(("group", "space"), "tm", None),
        check_vma=False,
    )
```

```python
import functools
import math

import jax
import jax.numpy as jnp
import numpy as np
from jax import lax
from jax.experimental import pallas as pl
from jax.experimental.pallas import tpu as pltpu
from jax.sharding import PartitionSpec as P

circulant_alpha = 0.01
DIFFUSION = 2.0
REACTION_STEP = 0.5
VMEM_BYTES = 24 * 1024 * 1024
LANES = 128
SUBLANES = 8
TILE = 16
CHUNKS = 2


def sine_table(row_index, column_index, length):
    product = np.outer(row_index + 1, column_index + 1) % (2 * (length + 1))
    return math.sqrt(2.0 / (length + 1)) * np.sin(product * (math.pi / (length + 1)))


def stencil_eigen(mode_index, length):
    return 4.0 * np.sin((mode_index + 1) * (math.pi / (2.0 * (length + 1)))) ** 2


def second_tables(width):
    half = width // 2
    return np.stack([sine_table(np.arange(half), np.arange(s, width, 2), width) for s in (0, 1)])


def first_tables(total):
    rows = total // 2
    return np.stack(
        [
            np.stack(
                [sine_table(s * rows + np.arange(rows), np.arange(c, total, 2), total) for c in (0, 1)]
            )
            for s in (0, 1)
        ]
    )


def decay_tables(total, width):
    first, second = stencil_eigen(np.arange(total), total), stencil_eigen(np.arange(width), width)
    decay = 1.0 / (1.0 + DIFFUSION * (second[:, None] + first[None, :]))
    return np.stack([np.stack([decay[s::2, c::2] for c in (0, 1)]) for s in (0, 1)])


def constant(table):
    return jnp.asarray(np.asarray(table, np.float32))


def split_constant(table):
    table = np.asarray(table, np.float32)
    high = table.astype(jnp.bfloat16)
    low = (table - high.astype(np.float32)).astype(jnp.bfloat16)
    return jnp.asarray(np.concatenate([high, high, low], axis=-2))


def store_split(ref, at, lane, block):
    depth = ref.shape[-1] // 3
    width = block.shape[-1]
    high = block.astype(jnp.bfloat16)
    low = (block - high.astype(jnp.float32)).astype(jnp.bfloat16)
    for part, value in enumerate((high, low, high)):
        ref[(*at, pl.ds(part * depth + lane, width))] = value


def dot(first, second):
    return jnp.dot(first, second, preferred_element_type=jnp.float32)


def lanes_reversed(block):
    index = LANES - 1 - lax.broadcasted_iota(jnp.int32, (block.shape[0], LANES), 1)
    return jnp.take_along_axis(block, index, axis=1, mode="promise_in_bounds")


def store_rows_reversed(ref, start, block):
    rows, width = block.shape
    index = SUBLANES - 1 - lax.broadcasted_iota(jnp.int32, (SUBLANES, width), 0)
    for row in range(0, rows, SUBLANES):
        to = pl.multiple_of(start + rows - SUBLANES - row, SUBLANES)
        ref[pl.ds(to, SUBLANES), :] = jnp.take_along_axis(
            block[row : row + SUBLANES], index, axis=0, mode="promise_in_bounds"
        )


IN_VMEM = pl.BlockSpec(memory_space=pltpu.VMEM)
IN_SMEM = pl.BlockSpec(memory_space=pltpu.SMEM)


def in_hbm(array):
    return pltpu.with_memory_space_constraint(array, pltpu.HBM)


def floats(*shape):
    return jax.ShapeDtypeStruct(shape, jnp.float32)


def call(kernel, name, in_specs, out_specs, out_shape, scratch, flops, grid=None):
    if grid is None:
        spec = pl.GridSpec(
            in_specs=[IN_SMEM, *in_specs], out_specs=out_specs, scratch_shapes=scratch
        )
    else:
        spec = pltpu.PrefetchScalarGridSpec(
            num_scalar_prefetch=1,
            grid=(grid,),
            in_specs=in_specs,
            out_specs=out_specs,
            scratch_shapes=scratch,
        )
    return pl.pallas_call(
        kernel,
        grid_spec=spec,
        out_shape=out_shape,
        compiler_params=pltpu.CompilerParams(vmem_limit_bytes=VMEM_BYTES),
        cost_estimate=pl.CostEstimate(flops=flops, bytes_accessed=1 << 23, transcendentals=0),
        name=name,
    )


def forward_second_kernel(place, field, initial, table, sums, *refs):
    sends, scratch = refs[:CHUNKS], refs[CHUNKS:]
    rows, steps, width = field.shape
    half = width // 2
    part = half // CHUNKS
    piece = rows // len(scratch)
    group = max(TILE // steps, 1)
    head = min(steps, SUBLANES)
    total = rows * pl.num_programs(0)
    start = pl.program_id(0) * rows
    mirror = total - rows - start
    is_first = (place[0] == 0).astype(jnp.float32)
    sign = 1.0 - 2.0 * place[1].astype(jnp.float32)
    firsts = lax.broadcasted_iota(jnp.int32, (group, head, width), 1) == 0
    firsts = jnp.where(firsts, is_first, 0.0)

    def put(other, at, sums_at, cells):
        lower = cells[:, :half]
        upper = sign * jnp.concatenate(
            [lanes_reversed(cells[:, lane : lane + LANES]) for lane in range(half, width, LANES)][::-1],
            axis=1,
        )
        sums[pl.ds(sums_at, TILE), :] = lower + upper
        store_split(other, (pl.ds(at, TILE),), 0, lower - upper)

    for sub, other in enumerate(scratch):
        kept_at = pl.multiple_of(start + sub * piece, piece)
        sent_at = pl.multiple_of(mirror + (len(scratch) - 1 - sub) * piece, piece)
        body = piece * steps
        kept_base = pl.multiple_of(kept_at * steps, body)
        for row in range(0, piece, group):
            at = pl.ds(sub * piece + row, group)
            cells = field[at]
            force = REACTION_STEP * (cells - cells * cells * cells)
            starts = force[:, :head] + firsts * initial[at][:, None, :]
            force = jnp.concatenate([starts, force[:, head:]], axis=1) if head < steps else starts
            put(other, row * steps, kept_base + row * steps, force.reshape(TILE, width))
        for row in range(0, piece, TILE):
            ends = field[pl.ds(sub * piece + row, TILE), steps - 1, :]
            put(other, body + row, total * steps + kept_at + row, ends)
        sent = dot(other[...], table[0])
        base = pl.multiple_of(sent_at * steps, body)
        for chunk, send in enumerate(sends):
            lanes = slice(chunk * part, (chunk + 1) * part)
            for row in range(piece):
                line = sent[row * steps : (row + 1) * steps, lanes]
                send[pl.ds(base + (piece - 1 - row) * steps, steps), :] = line
            store_rows_reversed(send, total * steps + sent_at, sent[body:, lanes])


def forward_second(place, field, initial, tables):
    rows, steps, width = field.shape
    half = width // 2
    block, pieces = min(32, rows), 2
    depth = (steps + 1) * block // pieces
    outs = call(
        forward_second_kernel,
        "forward_second",
        [
            pl.BlockSpec((block, steps, width), lambda i, place: (i, 0, 0)),
            pl.BlockSpec((block, width), lambda i, place: (i, 0)),
            pl.BlockSpec((1, 3 * half, half), lambda i, place: (1 - place[1], 0, 0)),
        ],
        [IN_VMEM] * (1 + CHUNKS),
        [floats((steps + 1) * rows, half)]
        + [floats((steps + 1) * rows, half // CHUNKS)] * CHUNKS,
        [pltpu.VMEM((depth, 3 * half), jnp.bfloat16)] * pieces,
        1 << 32,
        rows // block,
    )(place, in_hbm(field), in_hbm(initial), in_hbm(tables))
    return outs[0], outs[1:]


def keep_second_kernel(place, tables, sums, *refs):
    keeps, scratch = refs[:CHUNKS], refs[CHUNKS:]
    depth = scratch[0].shape[0]
    for at in range(0, sums.shape[0], depth):
        split = scratch[at // depth % 2]
        for row in range(0, depth, TILE):
            store_split(split, (pl.ds(row, TILE),), 0, sums[pl.ds(at + row, TILE)])
        result = dot(split[...], tables[place[1]])
        for chunk, keep in enumerate(keeps):
            part = keep.shape[1]
            keep[pl.ds(at, depth)] = result[:, chunk * part : (chunk + 1) * part]


def keep_second(place, sums, tables):
    rows, half = sums.shape
    return call(
        keep_second_kernel,
        "keep_second",
        [IN_VMEM] * 2,
        [IN_VMEM] * CHUNKS,
        [floats(rows, half // CHUNKS)] * CHUNKS,
        [pltpu.VMEM((rows // 8, 3 * half), jnp.bfloat16)] * 2,
        1 << 31,
    )(place, tables, sums)


def ranks(slabs):
    return slabs // 2


def parcels(size):
    return [(0,), (1,), (2, 3)] if size == 4 else [(partner,) for partner in range(size)]


def forward_first_kernel(slabs, chunk, place, keep, got, table, decay, modes, *refs):
    size = ranks(slabs)
    lasts, (state, split, split_end) = refs[:-3], refs[-3:]
    steps, _, part, rows = modes.shape
    block = split.shape[1] // part
    strip = place[1]
    state[...] = jnp.zeros_like(state)
    for step in range(0, steps, block):
        for c in (0, 1):
            for at in range(block):
                cells_at = pl.ds(step + at, rows, stride=steps)
                near, far = keep[cells_at, :], got[cells_at, :]
                cells = near - far if c else near + far
                store_split(split, (c, pl.ds(at * part, part)), 0, cells.T)
            result = dot(split[c], table[strip, c])
            modes[pl.ds(step, block), c] = result.reshape(block, part, rows)
        for c in (0, 1):
            for row in range(0, part, TILE):
                tile, at_state = pl.ds(row, TILE), pl.ds(c * part + row, TILE)
                value = state[at_state]
                rate = decay[strip, c, pl.ds(chunk * part + row, TILE)]
                for at in range(block):
                    value = rate * (value + modes[step + at, c, tile])
                state[at_state] = value
    is_last = (place[0] == slabs - 1).astype(jnp.float32)
    near, far = keep[pl.ds(rows * steps, rows)], got[pl.ds(rows * steps, rows)]
    for c, cells in enumerate((near + far, near - far)):
        store_split(split_end, (c, slice(None)), 0, cells.T)
        at_state = pl.ds(c * part, part)
        state[at_state] = state[at_state] - is_last * dot(split_end[c], table[strip, c])
    rank = lax.rem(place[0], size)
    share = 2 * part // size
    for parcel, last in zip(parcels(size), lasts):
        for place_in, partner in enumerate(parcel):
            at = pl.multiple_of((rank ^ partner) * share, share)
            last[pl.ds(place_in * share, share)] = state[pl.ds(at, share)]


def forward_first(place, chunk, keep, got, tables, decays, slabs):
    rows, part = tables.shape[-1], keep.shape[1]
    steps = keep.shape[0] // rows - 1
    block = min(8, steps)
    size = ranks(slabs)
    share = 2 * part // size
    outs = call(
        functools.partial(forward_first_kernel, slabs, chunk),
        "forward_first",
        [IN_VMEM] * 4,
        [IN_VMEM] * (1 + len(parcels(size))),
        [floats(steps, 2, part, rows)]
        + [floats(len(parcel) * share, rows) for parcel in parcels(size)],
        [
            pltpu.VMEM((2 * part, rows), jnp.float32),
            pltpu.VMEM((2, block * part, 3 * rows), jnp.bfloat16),
            pltpu.VMEM((2, part, 3 * rows), jnp.bfloat16),
        ],
        1 << 31,
    )(place, keep, got, tables, decays)
    return outs[0], outs[1:]


def half_sum_kernel(slabs, chunk, place, closing, *refs):
    size = ranks(slabs)
    lasts, ordered, total = refs[:size], refs[size], refs[size + 1]
    share = total.shape[0]
    rank = lax.rem(place[0], size)
    decay = closing[place[1], chunk, 0, pl.ds(pl.multiple_of(rank * share, share), share)]
    for partner in range(size):
        ordered[rank ^ partner] = lasts[partner][pl.ds(0, share)]
    state = ordered[0]
    for at in range(1, size):
        state = ordered[at] + decay * state
    total[...] = state


def half_sum(place, chunk, lasts, closing, slabs):
    size = ranks(slabs)
    share, rows = lasts[0].shape
    return call(
        functools.partial(half_sum_kernel, slabs, chunk),
        "half_sum",
        [IN_VMEM] * (1 + size),
        [IN_VMEM] * 2,
        [floats(size, share, rows), floats(share, rows)],
        [],
        1 << 20,
    )(place, closing, *lasts)


def close_kernel(slabs, chunk, place, closing, ordered, near, far, *refs):
    size = ranks(slabs)
    befores, states = refs[:-1], refs[-1]
    share = near.shape[0]
    rank = lax.rem(place[0], size)
    at_share = pl.ds(pl.multiple_of(rank * share, share), share)
    decay, half_decay, gain = (closing[place[1], chunk, at, at_share] for at in range(3))
    entering = jnp.where(place[0] < size, circulant_alpha, 1.0)
    state = gain * (entering * far[...] + circulant_alpha * half_decay * near[...])
    for at in range(size):
        states[at] = state
        if at < size - 1:
            state = ordered[at] + decay * state
    for parcel, before in zip(parcels(size), befores):
        for place_in, partner in enumerate(parcel):
            before[pl.ds(place_in * share, share)] = states[rank ^ partner]


def close(place, chunk, ordered, near, far, closing, slabs):
    size, share, rows = ordered.shape
    return call(
        functools.partial(close_kernel, slabs, chunk),
        "close",
        [IN_VMEM] * 4,
        [IN_VMEM] * len(parcels(size)),
        [floats(len(parcel) * share, rows) for parcel in parcels(size)],
        [pltpu.VMEM((size, share, rows), jnp.float32)],
        1 << 20,
    )(place, closing, ordered, near, far)


def inverse_first_kernel(slabs, chunk, place, modes, table, decay, *refs):
    size = ranks(slabs)
    befores, (keep, send, state, split) = refs[:size], refs[size:]
    steps, _, part, rows = modes.shape
    block = split.shape[1] // part
    strip = place[1]
    rank = lax.rem(place[0], size)
    share = 2 * part // size
    for partner in range(size):
        at = pl.multiple_of((rank ^ partner) * share, share)
        state[pl.ds(at, share)] = befores[partner][pl.ds(0, share)]
    for step in range(0, steps, block):
        results = []
        for c in (0, 1):
            for row in range(0, part, TILE):
                tile, at_state = pl.ds(row, TILE), pl.ds(c * part + row, TILE)
                value = state[at_state]
                rate = decay[strip, c, pl.ds(chunk * part + row, TILE)]
                for at in range(block):
                    value = rate * (value + modes[step + at, c, tile])
                    store_split(split, (c, pl.ds(at * part + row, TILE)), 0, value)
                state[at_state] = value
            results.append(dot(split[c], table[strip, c]))
        even, odd = results
        for at in range(block):
            piece = slice(at * part, (at + 1) * part)
            start = (step + at) * rows
            keep[pl.ds(start, rows), :] = (even[piece] + odd[piece]).T
            send[pl.ds(start, rows), :] = (even[piece] - odd[piece]).T


def inverse_first(place, chunk, modes, befores, tables, decays, slabs):
    steps, _, part, rows = modes.shape
    block = min(8, steps)
    return call(
        functools.partial(inverse_first_kernel, slabs, chunk),
        "inverse_first",
        [IN_VMEM] * (3 + len(befores)),
        [IN_VMEM] * 2,
        [floats(steps * rows, part)] * 2,
        [
            pltpu.VMEM((2 * part, rows), jnp.float32),
            pltpu.VMEM((2, block * part, 3 * rows), jnp.bfloat16),
        ],
        1 << 31,
    )(place, modes, tables, decays, *befores)


def steps_of(ref, cells, steps):
    pitch = ref.shape[0] // steps
    lines = [ref[pl.ds(cell, steps, stride=pitch), :] for cell in cells]
    return lines[0] if len(lines) == 1 else jnp.concatenate(lines, axis=0)


def keep_inverse_kernel(steps, place, tables, *refs):
    keeps, out, scratch = refs[:CHUNKS], refs[CHUNKS], refs[CHUNKS + 1 :]
    part = keeps[0].shape[1]
    depth = scratch[0].shape[0]
    group = max(TILE // steps, 1)
    for at in range(0, out.shape[0], depth):
        split = scratch[at // depth % 2]
        for row in range(0, depth, TILE):
            cell = (at + row) // steps
            for chunk, keep in enumerate(keeps):
                cells = steps_of(keep, range(cell, cell + group), steps)
                store_split(split, (pl.ds(row, TILE),), chunk * part, cells)
        out[pl.ds(at, depth)] = dot(split[...], tables[place[1]])


def keep_inverse(place, keeps, tables, steps):
    rows, part = keeps[0].shape
    half = part * CHUNKS
    return call(
        functools.partial(keep_inverse_kernel, steps),
        "keep_inverse",
        [IN_VMEM] * (1 + CHUNKS),
        IN_VMEM,
        floats(rows, half),
        [pltpu.VMEM((rows // 8, 3 * half), jnp.bfloat16)] * 2,
        1 << 31,
    )(place, tables, *keeps)


def inverse_second_kernel(place, tables, kept, *refs):
    gots, out, scratch = refs[:CHUNKS], refs[CHUNKS], refs[CHUNKS + 1 :]
    rows, steps, width = out.shape
    half = width // 2
    part = half // CHUNKS
    count = len(scratch) // 2
    piece = rows // count
    group = max(TILE // steps, 1)
    strip = place[1]
    sign = 1.0 - 2.0 * strip.astype(jnp.float32)
    total = rows * pl.num_programs(0)
    start = pl.program_id(0) * rows
    for sub in range(count):
        split, result = scratch[2 * sub : 2 * sub + 2]
        base = start + sub * piece
        for row in range(0, piece, group):
            mirrors = [total - 1 - base - row - at for at in range(group)]
            for chunk, got in enumerate(gots):
                cells = steps_of(got, mirrors, steps)
                store_split(split, (pl.ds(row * steps, TILE),), chunk * part, cells)
        result[...] = dot(split[...], tables[1 - strip])
        kept_base = pl.multiple_of(base * steps, piece * steps)
        for row in range(0, piece, group):
            first = kept[pl.ds(kept_base + row * steps, TILE)]
            second = result[pl.ds(row * steps, TILE)]
            upper = sign * (first - second)
            parts = [
                lanes_reversed(upper[:, lane : lane + LANES]) for lane in range(0, half, LANES)
            ][::-1]
            whole = jnp.concatenate([first + second, *parts], axis=1)
            out[pl.ds(sub * piece + row, group)] = whole.reshape(group, TILE // group, width)


def inverse_second(place, kept, gots, tables, steps):
    rows, half = kept.shape[0] // steps, kept.shape[1]
    block, pieces = min(32, rows), 2
    depth = steps * block // pieces
    return call(
        inverse_second_kernel,
        "inverse_second",
        [IN_VMEM] * (2 + CHUNKS),
        pl.BlockSpec((block, steps, 2 * half), lambda i, place: (i, 0, 0)),
        floats(rows, steps, 2 * half),
        [pltpu.VMEM((depth, 3 * half), jnp.bfloat16), pltpu.VMEM((depth, half), jnp.float32)]
        * pieces,
        1 << 32,
        rows // block,
    )(place, tables, kept, *gots)


def swapped(block):
    return lax.ppermute(block, "space", [(0, 1), (1, 0)])


def with_partner(block, distance):
    slabs = lax.axis_size("tm")
    return lax.ppermute(block, "tm", [(slab, slab ^ distance) for slab in range(slabs)])


def among_ranks(blocks):
    if len(blocks) != 3:
        return [blocks[0]] + [with_partner(block, at) for at, block in enumerate(blocks) if at]
    own, near, pair = blocks
    pair = with_partner(pair, 2)
    near = with_partner(near, 1)
    return [own, near, pair, with_partner(pair[own.shape[0] :], 1)]


def by_chunk(table):
    strips, _, half, rows = table.shape
    parts = table.reshape(strips, 2, CHUNKS, half // CHUNKS, rows)
    return np.swapaxes(parts, 1, 2).reshape(strips, CHUNKS, 2 * half // CHUNKS, rows)


def shards(iterate, initial):
    rows, steps, width = iterate.shape
    slabs = lax.axis_size("tm")
    total = rows * lax.axis_size("space")
    place = jnp.stack([lax.axis_index("tm"), lax.axis_index("space")]).astype(jnp.int32)
    second = second_tables(width)
    first = first_tables(total)
    decay = decay_tables(total, width)
    slab_decay = decay**steps
    half_decay = slab_decay ** ranks(slabs)
    gain = 1.0 / (1.0 - circulant_alpha * half_decay * half_decay)
    closing = constant(
        np.stack([by_chunk(table) for table in (slab_decay, half_decay, gain)], axis=2)
    )
    first_table, decays = split_constant(first), constant(decay)
    second_table = split_constant(second)
    sums, sends = forward_second(place, iterate, initial, second_table)
    gots = [swapped(send) for send in sends]
    keeps = keep_second(place, sums, second_table)
    modes, befores = [], []
    for chunk in range(CHUNKS):
        own_modes, lasts = forward_first(
            place, chunk, keeps[chunk], gots[chunk], first_table, decays, slabs
        )
        modes.append(own_modes)
        ordered, near = half_sum(place, chunk, among_ranks(lasts), closing, slabs)
        far = with_partner(near, ranks(slabs))
        befores.append(among_ranks(close(place, chunk, ordered, near, far, closing, slabs)))
    inverse_table = split_constant(np.swapaxes(first, 2, 3))
    keeps, sends = zip(
        *(
            inverse_first(place, chunk, modes[chunk], befores[chunk], inverse_table, decays, slabs)
            for chunk in range(CHUNKS)
        )
    )
    gots = [swapped(send) for send in sends]
    inverse_table = split_constant(np.swapaxes(second, 1, 2))
    kept = keep_inverse(place, keeps, inverse_table, steps)
    return inverse_second(place, kept, gots, inverse_table, steps)


def solution(mesh):
    return jax.shard_map(
        shards,
        mesh=mesh,
        in_specs=(P(("group", "space"), "tm", None), P(("group", "space"), None)),
        out_specs=P(("group", "space"), "tm", None),
        check_vma=False,
    )
```

```python
import functools
import math

import jax
import jax.numpy as jnp
import numpy as np
from jax import lax
from jax.experimental import pallas as pl
from jax.experimental.pallas import tpu as pltpu
from jax.sharding import PartitionSpec as P

circulant_alpha = 0.01
DIFFUSION = 2.0
REACTION_STEP = 0.5
VMEM_BYTES = 24 * 1024 * 1024
LANES = 128
SUBLANES = 8
TILE = 16
CHUNKS = 2


def sine_table(row_index, column_index, length):
    product = np.outer(row_index + 1, column_index + 1) % (2 * (length + 1))
    return math.sqrt(2.0 / (length + 1)) * np.sin(product * (math.pi / (length + 1)))


def stencil_eigen(mode_index, length):
    return 4.0 * np.sin((mode_index + 1) * (math.pi / (2.0 * (length + 1)))) ** 2


def second_tables(width):
    half = width // 2
    return np.stack([sine_table(np.arange(half), np.arange(s, width, 2), width) for s in (0, 1)])


def first_tables(total):
    rows = total // 2
    return np.stack(
        [
            np.stack(
                [sine_table(s * rows + np.arange(rows), np.arange(c, total, 2), total) for c in (0, 1)]
            )
            for s in (0, 1)
        ]
    )


def decay_tables(total, width):
    first, second = stencil_eigen(np.arange(total), total), stencil_eigen(np.arange(width), width)
    decay = 1.0 / (1.0 + DIFFUSION * (second[:, None] + first[None, :]))
    return np.stack([np.stack([decay[s::2, c::2] for c in (0, 1)]) for s in (0, 1)])


def constant(table):
    return jnp.asarray(np.asarray(table, np.float32))


def split_constant(table):
    table = np.asarray(table, np.float32)
    high = table.astype(jnp.bfloat16)
    low = (table - high.astype(np.float32)).astype(jnp.bfloat16)
    return jnp.asarray(np.concatenate([high, high, low], axis=-2))


def store_split(ref, at, lane, block):
    depth = ref.shape[-1] // 3
    width = block.shape[-1]
    high = block.astype(jnp.bfloat16)
    low = (block - high.astype(jnp.float32)).astype(jnp.bfloat16)
    for part, value in enumerate((high, low, high)):
        ref[(*at, pl.ds(part * depth + lane, width))] = value


def dot(first, second):
    return jnp.dot(first, second, preferred_element_type=jnp.float32)


def lanes_reversed(block):
    index = LANES - 1 - lax.broadcasted_iota(jnp.int32, (block.shape[0], LANES), 1)
    return jnp.take_along_axis(block, index, axis=1, mode="promise_in_bounds")


def store_rows_reversed(ref, start, block):
    rows, width = block.shape
    index = SUBLANES - 1 - lax.broadcasted_iota(jnp.int32, (SUBLANES, width), 0)
    for row in range(0, rows, SUBLANES):
        to = pl.multiple_of(start + rows - SUBLANES - row, SUBLANES)
        ref[pl.ds(to, SUBLANES), :] = jnp.take_along_axis(
            block[row : row + SUBLANES], index, axis=0, mode="promise_in_bounds"
        )


IN_VMEM = pl.BlockSpec(memory_space=pltpu.VMEM)
IN_SMEM = pl.BlockSpec(memory_space=pltpu.SMEM)


def in_hbm(array):
    return pltpu.with_memory_space_constraint(array, pltpu.HBM)


def floats(*shape):
    return jax.ShapeDtypeStruct(shape, jnp.float32)


def call(kernel, name, in_specs, out_specs, out_shape, scratch, flops, grid=None):
    if grid is None:
        spec = pl.GridSpec(
            in_specs=[IN_SMEM, *in_specs], out_specs=out_specs, scratch_shapes=scratch
        )
    else:
        spec = pltpu.PrefetchScalarGridSpec(
            num_scalar_prefetch=1,
            grid=(grid,),
            in_specs=in_specs,
            out_specs=out_specs,
            scratch_shapes=scratch,
        )
    return pl.pallas_call(
        kernel,
        grid_spec=spec,
        out_shape=out_shape,
        compiler_params=pltpu.CompilerParams(vmem_limit_bytes=VMEM_BYTES),
        cost_estimate=pl.CostEstimate(flops=flops, bytes_accessed=1 << 23, transcendentals=0),
        name=name,
    )


def forward_second_kernel(place, field, initial, table, sums, *refs):
    sends, scratch = refs[:CHUNKS], refs[CHUNKS:]
    rows, steps, width = field.shape
    half = width // 2
    part = half // CHUNKS
    piece = rows // len(scratch)
    group = max(TILE // steps, 1)
    head = min(steps, SUBLANES)
    total = rows * pl.num_programs(0)
    start = pl.program_id(0) * rows
    mirror = total - rows - start
    is_first = (place[0] == 0).astype(jnp.float32)
    sign = 1.0 - 2.0 * place[1].astype(jnp.float32)
    firsts = lax.broadcasted_iota(jnp.int32, (group, head, width), 1) == 0
    firsts = jnp.where(firsts, is_first, 0.0)

    def put(other, at, sums_at, cells):
        lower = cells[:, :half]
        upper = sign * jnp.concatenate(
            [lanes_reversed(cells[:, lane : lane + LANES]) for lane in range(half, width, LANES)][::-1],
            axis=1,
        )
        sums[pl.ds(sums_at, TILE), :] = lower + upper
        store_split(other, (pl.ds(at, TILE),), 0, lower - upper)

    for sub, other in enumerate(scratch):
        kept_at = pl.multiple_of(start + sub * piece, piece)
        sent_at = pl.multiple_of(mirror + (len(scratch) - 1 - sub) * piece, piece)
        body = piece * steps
        kept_base = pl.multiple_of(kept_at * steps, body)
        for row in range(0, piece, group):
            at = pl.ds(sub * piece + row, group)
            cells = field[at]
            force = REACTION_STEP * (cells - cells * cells * cells)
            starts = force[:, :head] + firsts * initial[at][:, None, :]
            force = jnp.concatenate([starts, force[:, head:]], axis=1) if head < steps else starts
            put(other, row * steps, kept_base + row * steps, force.reshape(TILE, width))
        for row in range(0, piece, TILE):
            ends = field[pl.ds(sub * piece + row, TILE), steps - 1, :]
            put(other, body + row, total * steps + kept_at + row, ends)
        sent = dot(other[...], table[0])
        base = pl.multiple_of(sent_at * steps, body)
        for chunk, send in enumerate(sends):
            lanes = slice(chunk * part, (chunk + 1) * part)
            for row in range(piece):
                line = sent[row * steps : (row + 1) * steps, lanes]
                send[pl.ds(base + (piece - 1 - row) * steps, steps), :] = line
            store_rows_reversed(send, total * steps + sent_at, sent[body:, lanes])


def forward_second(place, field, initial, tables):
    rows, steps, width = field.shape
    half = width // 2
    block, pieces = min(64, rows), 2
    depth = (steps + 1) * block // pieces
    outs = call(
        forward_second_kernel,
        "forward_second",
        [
            pl.BlockSpec((block, steps, width), lambda i, place: (i, 0, 0)),
            pl.BlockSpec((block, width), lambda i, place: (i, 0)),
            pl.BlockSpec((1, 3 * half, half), lambda i, place: (1 - place[1], 0, 0)),
        ],
        [IN_VMEM] * (1 + CHUNKS),
        [floats((steps + 1) * rows, half)]
        + [floats((steps + 1) * rows, half // CHUNKS)] * CHUNKS,
        [pltpu.VMEM((depth, 3 * half), jnp.bfloat16)] * pieces,
        1 << 32,
        rows // block,
    )(place, in_hbm(field), in_hbm(initial), in_hbm(tables))
    return outs[0], outs[1:]


def times_table_kernel(inputs, place, tables, *refs):
    sources, refs = refs[:inputs], refs[inputs:]
    outs, scratch = refs[:-2], refs[-2:]
    piece = scratch[0].shape[0]
    for at in range(0, sources[0].shape[0], piece):
        split = scratch[at // piece % 2]
        for row in range(0, piece, TILE):
            lane = 0
            for source in sources:
                store_split(split, (pl.ds(row, TILE),), lane, source[pl.ds(at + row, TILE)])
                lane += source.shape[1]
        result = dot(split[...], tables[place[1]])
        lane = 0
        for out in outs:
            out[pl.ds(at, piece)] = result[:, lane : lane + out.shape[1]]
            lane += out.shape[1]


def times_table(place, sources, tables, widths, name):
    rows = sources[0].shape[0]
    depth = tables.shape[1]
    return call(
        functools.partial(times_table_kernel, len(sources)),
        name,
        [IN_VMEM] * (1 + len(sources)),
        [IN_VMEM] * len(widths),
        [floats(rows, width) for width in widths],
        [pltpu.VMEM((rows // 8, depth), jnp.bfloat16)] * 2,
        1 << 31,
    )(place, tables, *sources)


def ranks(slabs):
    return slabs // 2


def forward_first_kernel(slabs, chunk, place, keep, got, table, decay, modes, *refs):
    lasts, state, split, split_end = refs
    steps, _, part, rows = modes.shape
    block = split.shape[1] // part
    strip = place[1]
    state[...] = jnp.zeros_like(state)
    for step in range(0, steps, block):
        for c in (0, 1):
            for at in range(block):
                cells_at = pl.ds(step + at, rows, stride=steps)
                near, far = keep[cells_at, :], got[cells_at, :]
                cells = near - far if c else near + far
                store_split(split, (c, pl.ds(at * part, part)), 0, cells.T)
            result = dot(split[c], table[strip, c])
            modes[pl.ds(step, block), c] = result.reshape(block, part, rows)
        for c in (0, 1):
            for row in range(0, part, TILE):
                tile, at_state = pl.ds(row, TILE), pl.ds(c * part + row, TILE)
                value = state[at_state]
                rate = decay[strip, c, pl.ds(chunk * part + row, TILE)]
                for at in range(block):
                    value = rate * (value + modes[step + at, c, tile])
                state[at_state] = value
    is_last = (place[0] == slabs - 1).astype(jnp.float32)
    near, far = keep[pl.ds(rows * steps, rows)], got[pl.ds(rows * steps, rows)]
    for c, cells in enumerate((near + far, near - far)):
        store_split(split_end, (c, slice(None)), 0, cells.T)
        at_state = pl.ds(c * part, part)
        state[at_state] = state[at_state] - is_last * dot(split_end[c], table[strip, c])
    lasts[...] = state[...].reshape(lasts.shape)


def forward_first(place, chunk, keep, got, tables, decays, slabs):
    rows, part = tables.shape[-1], keep.shape[1]
    steps = keep.shape[0] // rows - 1
    block = min(8, steps)
    size = ranks(slabs)
    share = 2 * part // size
    return call(
        functools.partial(forward_first_kernel, slabs, chunk),
        "forward_first",
        [IN_VMEM] * 4,
        [IN_VMEM] * 2,
        [floats(steps, 2, part, rows), floats(size, share, rows)],
        [
            pltpu.VMEM((2 * part, rows), jnp.float32),
            pltpu.VMEM((2, block * part, 3 * rows), jnp.bfloat16),
            pltpu.VMEM((2, part, 3 * rows), jnp.bfloat16),
        ],
        1 << 31,
    )(place, keep, got, tables, decays)


def half_sum_kernel(chunk, place, closing, lasts, total):
    size, share, _ = lasts.shape
    rank = lax.rem(place[0], size)
    decay = closing[place[1], chunk, 0, pl.ds(pl.multiple_of(rank * share, share), share)]
    state = lasts[0]
    for at in range(1, size):
        state = lasts[at] + decay * state
    total[...] = state


def half_sum(place, chunk, lasts, closing):
    _, share, rows = lasts.shape
    return call(
        functools.partial(half_sum_kernel, chunk),
        "half_sum",
        [IN_VMEM] * 2,
        IN_VMEM,
        floats(share, rows),
        [],
        1 << 20,
    )(place, closing, lasts)


def close_kernel(chunk, place, closing, lasts, near, far, befores):
    size, share, _ = lasts.shape
    rank = lax.rem(place[0], size)
    at_share = pl.ds(pl.multiple_of(rank * share, share), share)
    decay, half_decay, gain = (closing[place[1], chunk, at, at_share] for at in range(3))
    entering = jnp.where(place[0] < size, circulant_alpha, 1.0)
    state = gain * (entering * far[...] + circulant_alpha * half_decay * near[...])
    for at in range(size):
        befores[at] = state
        if at < size - 1:
            state = lasts[at] + decay * state


def close(place, chunk, lasts, near, far, closing):
    return call(
        functools.partial(close_kernel, chunk),
        "close",
        [IN_VMEM] * 4,
        IN_VMEM,
        floats(*lasts.shape),
        [],
        1 << 20,
    )(place, closing, lasts, near, far)


def inverse_first_kernel(chunk, place, modes, table, decay, befores, keep, send, state, split):
    steps, _, part, rows = modes.shape
    block = split.shape[1] // part
    strip = place[1]
    state[...] = befores[...].reshape(state.shape)
    for step in range(0, steps, block):
        results = []
        for c in (0, 1):
            for row in range(0, part, TILE):
                tile, at_state = pl.ds(row, TILE), pl.ds(c * part + row, TILE)
                value = state[at_state]
                rate = decay[strip, c, pl.ds(chunk * part + row, TILE)]
                for at in range(block):
                    value = rate * (value + modes[step + at, c, tile])
                    store_split(split, (c, pl.ds(at * part + row, TILE)), 0, value)
                state[at_state] = value
            results.append(dot(split[c], table[strip, c]))
        even, odd = results
        for at in range(block):
            piece = slice(at * part, (at + 1) * part)
            start = (step + at) * rows
            keep[pl.ds(start, rows), :] = (even[piece] + odd[piece]).T
            store_rows_reversed(send, start, (even[piece] - odd[piece]).T)


def inverse_first(place, chunk, modes, befores, tables, decays):
    steps, _, part, rows = modes.shape
    block = min(8, steps)
    return call(
        functools.partial(inverse_first_kernel, chunk),
        "inverse_first",
        [IN_VMEM] * 4,
        [IN_VMEM] * 2,
        [floats(steps * rows, part)] * 2,
        [
            pltpu.VMEM((2 * part, rows), jnp.float32),
            pltpu.VMEM((2, block * part, 3 * rows), jnp.bfloat16),
        ],
        1 << 31,
    )(place, modes, tables, decays, befores)


def inverse_second_kernel(place, tables, kept, *refs):
    gots, out, scratch = refs[:CHUNKS], refs[CHUNKS], refs[CHUNKS + 1 :]
    rows, steps, width = out.shape
    half = width // 2
    part = half // CHUNKS
    count = len(scratch) // 2
    piece = rows // count
    group = min(SUBLANES, steps)
    strip = place[1]
    sign = 1.0 - 2.0 * strip.astype(jnp.float32)
    start = pl.program_id(0) * rows
    for sub in range(count):
        split, result = scratch[2 * sub : 2 * sub + 2]
        base = pl.multiple_of(start + sub * piece, piece)
        for step in range(steps):
            for row in range(0, piece, TILE):
                for chunk, got in enumerate(gots):
                    cells = got[step, pl.ds(base + row, TILE)]
                    store_split(split, (step, pl.ds(row, TILE)), chunk * part, cells)
        product = dot(split[...].reshape(steps * piece, 3 * half), tables[1 - strip])
        result[...] = product.reshape(result.shape)
        for row in range(0, piece, SUBLANES):
            for step in range(0, steps, group):
                for lane in range(0, half, LANES):
                    at_steps, at_lanes = pl.ds(step, group), pl.ds(lane, LANES)
                    first = kept[at_steps, pl.ds(base + row, SUBLANES), at_lanes]
                    second = result[at_steps, pl.ds(row, SUBLANES), at_lanes]
                    upper = sign * (first - second)
                    upper = lanes_reversed(upper.reshape(-1, LANES)).reshape(upper.shape)
                    to = (pl.ds(sub * piece + row, SUBLANES), at_steps)
                    out[(*to, at_lanes)] = jnp.swapaxes(first + second, 0, 1)
                    to_lanes = pl.ds(width - LANES - lane, LANES)
                    out[(*to, to_lanes)] = jnp.swapaxes(upper, 0, 1)


def inverse_second(place, kept, gots, tables):
    steps, rows, part = gots[0].shape
    half = part * CHUNKS
    block, pieces = min(64, rows), 2
    piece = block // pieces
    return call(
        inverse_second_kernel,
        "inverse_second",
        [IN_VMEM] * (2 + CHUNKS),
        pl.BlockSpec((block, steps, 2 * half), lambda i, place: (i, 0, 0)),
        floats(rows, steps, 2 * half),
        [
            pltpu.VMEM((steps, piece, 3 * half), jnp.bfloat16),
            pltpu.VMEM((steps, piece, half), jnp.float32),
        ]
        * pieces,
        1 << 32,
        rows // block,
    )(place, tables, kept, *gots)


def swapped(block):
    return lax.ppermute(block, "space", [(0, 1), (1, 0)])


def with_other_half(block):
    slabs = lax.axis_size("tm")
    size = ranks(slabs)
    return lax.ppermute(block, "tm", [(slab, (slab + size) % slabs) for slab in range(slabs)])


def among_ranks(blocks):
    slabs = lax.axis_size("tm")
    size = ranks(slabs)
    halves = [list(range(start, start + size)) for start in range(0, slabs, size)]
    return lax.all_to_all(blocks, "tm", 0, 0, axis_index_groups=halves, tiled=True)


def by_chunk(table):
    strips, _, half, rows = table.shape
    parts = table.reshape(strips, 2, CHUNKS, half // CHUNKS, rows)
    return np.swapaxes(parts, 1, 2).reshape(strips, CHUNKS, 2 * half // CHUNKS, rows)


def shards(iterate, initial):
    rows, steps, width = iterate.shape
    slabs = lax.axis_size("tm")
    total = rows * lax.axis_size("space")
    place = jnp.stack([lax.axis_index("tm"), lax.axis_index("space")]).astype(jnp.int32)
    second = second_tables(width)
    first = first_tables(total)
    decay = decay_tables(total, width)
    slab_decay = decay**steps
    half_decay = slab_decay ** ranks(slabs)
    gain = 1.0 / (1.0 - circulant_alpha * half_decay * half_decay)
    closing = constant(
        np.stack([by_chunk(table) for table in (slab_decay, half_decay, gain)], axis=2)
    )
    first_table, decays = split_constant(first), constant(decay)
    half = width // 2
    second_table = split_constant(second)
    sums, sends = forward_second(place, iterate, initial, second_table)
    gots = [swapped(send) for send in sends]
    keeps = times_table(place, [sums], second_table, [half // CHUNKS] * CHUNKS, "keep_second")
    modes, befores = [], []
    for chunk in range(CHUNKS):
        own_modes, lasts = forward_first(
            place, chunk, keeps[chunk], gots[chunk], first_table, decays, slabs
        )
        modes.append(own_modes)
        lasts = among_ranks(lasts)
        near = half_sum(place, chunk, lasts, closing)
        far = with_other_half(near)
        befores.append(among_ranks(close(place, chunk, lasts, near, far, closing)))
    inverse_table = split_constant(np.swapaxes(first, 2, 3))
    keeps, sends = zip(
        *(
            inverse_first(place, chunk, modes[chunk], befores[chunk], inverse_table, decays)
            for chunk in range(CHUNKS)
        )
    )
    gots = [swapped(send).reshape(steps, rows, -1) for send in sends]
    inverse_table = split_constant(np.swapaxes(second, 1, 2))
    kept = times_table(place, keeps, inverse_table, [half], "keep_inverse")[0]
    return inverse_second(place, kept.reshape(steps, rows, half), gots, inverse_table)


def solution(mesh):
    return jax.shard_map(
        shards,
        mesh=mesh,
        in_specs=(P(("group", "space"), "tm", None), P(("group", "space"), None)),
        out_specs=P(("group", "space"), "tm", None),
        check_vma=False,
    )
```

```python
import functools
import math

import jax
import jax.numpy as jnp
import numpy as np
from jax import lax
from jax.experimental import pallas as pl
from jax.experimental.pallas import tpu as pltpu
from jax.sharding import PartitionSpec as P

circulant_alpha = 0.01
DIFFUSION = 2.0
REACTION_STEP = 0.5
VMEM_BYTES = 24 * 1024 * 1024
LANES = 128
SUBLANES = 8
TILE = 16
CHUNKS = 2


def sine_table(row_index, column_index, length):
    product = np.outer(row_index + 1, column_index + 1) % (2 * (length + 1))
    return math.sqrt(2.0 / (length + 1)) * np.sin(product * (math.pi / (length + 1)))


def stencil_eigen(mode_index, length):
    return 4.0 * np.sin((mode_index + 1) * (math.pi / (2.0 * (length + 1)))) ** 2


def second_tables(width):
    half = width // 2
    return np.stack([sine_table(np.arange(half), np.arange(s, width, 2), width) for s in (0, 1)])


def first_tables(total):
    rows = total // 2
    return np.stack(
        [
            np.stack(
                [sine_table(s * rows + np.arange(rows), np.arange(c, total, 2), total) for c in (0, 1)]
            )
            for s in (0, 1)
        ]
    )


def decay_tables(total, width):
    first, second = stencil_eigen(np.arange(total), total), stencil_eigen(np.arange(width), width)
    decay = 1.0 / (1.0 + DIFFUSION * (second[:, None] + first[None, :]))
    return np.stack([np.stack([decay[s::2, c::2] for c in (0, 1)]) for s in (0, 1)])


def constant(table):
    return jnp.asarray(np.asarray(table, np.float32))


def split_constant(table):
    table = np.asarray(table, np.float32)
    high = table.astype(jnp.bfloat16)
    low = (table - high.astype(np.float32)).astype(jnp.bfloat16)
    return jnp.asarray(np.concatenate([high, high, low], axis=-2))


def store_split(ref, at, lane, block):
    depth = ref.shape[-1] // 3
    width = block.shape[-1]
    high = block.astype(jnp.bfloat16)
    low = (block - high.astype(jnp.float32)).astype(jnp.bfloat16)
    for part, value in enumerate((high, low, high)):
        ref[(*at, pl.ds(part * depth + lane, width))] = value


def dot(first, second):
    return jnp.dot(first, second, preferred_element_type=jnp.float32)


def lanes_reversed(block):
    index = LANES - 1 - lax.broadcasted_iota(jnp.int32, (block.shape[0], LANES), 1)
    return jnp.take_along_axis(block, index, axis=1, mode="promise_in_bounds")


def store_rows_reversed(ref, start, block):
    rows, width = block.shape
    index = SUBLANES - 1 - lax.broadcasted_iota(jnp.int32, (SUBLANES, width), 0)
    for row in range(0, rows, SUBLANES):
        to = pl.multiple_of(start + rows - SUBLANES - row, SUBLANES)
        ref[pl.ds(to, SUBLANES), :] = jnp.take_along_axis(
            block[row : row + SUBLANES], index, axis=0, mode="promise_in_bounds"
        )


def pitch_of(cells):
    return cells + SUBLANES * (1 - cells // SUBLANES % 2)


def steps_of(ref, cells, steps, pitch):
    lines = [ref[pl.ds(cell, steps, stride=pitch), :] for cell in cells]
    return lines[0] if len(lines) == 1 else jnp.concatenate(lines, axis=0)


IN_VMEM = pl.BlockSpec(memory_space=pltpu.VMEM)
IN_SMEM = pl.BlockSpec(memory_space=pltpu.SMEM)


def in_hbm(array):
    return pltpu.with_memory_space_constraint(array, pltpu.HBM)


def floats(*shape):
    return jax.ShapeDtypeStruct(shape, jnp.float32)


def call(kernel, name, in_specs, out_specs, out_shape, scratch, flops, grid=None):
    if grid is None:
        spec = pl.GridSpec(
            in_specs=[IN_SMEM, *in_specs], out_specs=out_specs, scratch_shapes=scratch
        )
    else:
        spec = pltpu.PrefetchScalarGridSpec(
            num_scalar_prefetch=1,
            grid=(grid,),
            in_specs=in_specs,
            out_specs=out_specs,
            scratch_shapes=scratch,
        )
    return pl.pallas_call(
        kernel,
        grid_spec=spec,
        out_shape=out_shape,
        compiler_params=pltpu.CompilerParams(vmem_limit_bytes=VMEM_BYTES),
        cost_estimate=pl.CostEstimate(flops=flops, bytes_accessed=1 << 23, transcendentals=0),
        name=name,
    )


def forward_second_kernel(place, field, initial, table, sums, *refs):
    sends, scratch = refs[:CHUNKS], refs[CHUNKS:]
    rows, steps, width = field.shape
    half = width // 2
    part = half // CHUNKS
    piece = rows // len(scratch)
    group = max(TILE // steps, 1)
    head = min(steps, SUBLANES)
    total = rows * pl.num_programs(0)
    pitch = sends[0].shape[0] // (steps + 1)
    start = pl.program_id(0) * rows
    mirror = total - rows - start
    is_first = (place[0] == 0).astype(jnp.float32)
    sign = 1.0 - 2.0 * place[1].astype(jnp.float32)
    firsts = lax.broadcasted_iota(jnp.int32, (group, head, width), 1) == 0
    firsts = jnp.where(firsts, is_first, 0.0)

    def put(other, at, sums_at, cells):
        lower = cells[:, :half]
        upper = sign * jnp.concatenate(
            [lanes_reversed(cells[:, lane : lane + LANES]) for lane in range(half, width, LANES)][::-1],
            axis=1,
        )
        sums[pl.ds(sums_at, TILE), :] = lower + upper
        store_split(other, (pl.ds(at, TILE),), 0, lower - upper)

    for sub, other in enumerate(scratch):
        kept_at = pl.multiple_of(start + sub * piece, piece)
        sent_at = pl.multiple_of(mirror + (len(scratch) - 1 - sub) * piece, piece)
        body = piece * steps
        kept_base = pl.multiple_of(kept_at * steps, body)
        for row in range(0, piece, group):
            at = pl.ds(sub * piece + row, group)
            cells = field[at]
            force = REACTION_STEP * (cells - cells * cells * cells)
            starts = force[:, :head] + firsts * initial[at][:, None, :]
            force = jnp.concatenate([starts, force[:, head:]], axis=1) if head < steps else starts
            put(other, row * steps, kept_base + row * steps, force.reshape(TILE, width))
        for row in range(0, piece, TILE):
            ends = field[pl.ds(sub * piece + row, TILE), steps - 1, :]
            put(other, body + row, total * steps + kept_at + row, ends)
        sent = dot(other[...], table[0])
        for chunk, send in enumerate(sends):
            lanes = slice(chunk * part, (chunk + 1) * part)
            for row in range(piece):
                line = sent[row * steps : (row + 1) * steps, lanes]
                send[pl.ds(sent_at + piece - 1 - row, steps, stride=pitch), :] = line
            store_rows_reversed(send, pitch * steps + sent_at, sent[body:, lanes])


def forward_second(place, field, initial, tables):
    rows, steps, width = field.shape
    half = width // 2
    block, pieces = min(64, rows), 2
    depth = (steps + 1) * block // pieces
    outs = call(
        forward_second_kernel,
        "forward_second",
        [
            pl.BlockSpec((block, steps, width), lambda i, place: (i, 0, 0)),
            pl.BlockSpec((block, width), lambda i, place: (i, 0)),
            pl.BlockSpec((1, 3 * half, half), lambda i, place: (1 - place[1], 0, 0)),
        ],
        [IN_VMEM] * (1 + CHUNKS),
        [floats((steps + 1) * rows, half)]
        + [floats((steps + 1) * pitch_of(rows), half // CHUNKS)] * CHUNKS,
        [pltpu.VMEM((depth, 3 * half), jnp.bfloat16)] * pieces,
        1 << 32,
        rows // block,
    )(place, in_hbm(field), in_hbm(initial), in_hbm(tables))
    return outs[0], outs[1:]


def keep_second_kernel(steps, place, tables, sums, *refs):
    keeps, scratch = refs[:CHUNKS], refs[CHUNKS:]
    depth = scratch[0].shape[0]
    cells = sums.shape[0] // (steps + 1)
    pitch = keeps[0].shape[0] // (steps + 1)
    for at in range(0, sums.shape[0], depth):
        split = scratch[at // depth % 2]
        for row in range(0, depth, TILE):
            store_split(split, (pl.ds(row, TILE),), 0, sums[pl.ds(at + row, TILE)])
        result = dot(split[...], tables[place[1]])
        for chunk, keep in enumerate(keeps):
            part = keep.shape[1]
            lanes = slice(chunk * part, (chunk + 1) * part)
            body = max(0, min(depth, cells * steps - at))
            for row in range(0, body, steps):
                line = result[row : row + steps, lanes]
                keep[pl.ds((at + row) // steps, steps, stride=pitch), :] = line
            if body < depth:
                ends = pl.ds(pitch * steps + at + body - cells * steps, depth - body)
                keep[ends, :] = result[body:, lanes]


def keep_second(place, sums, tables, steps):
    rows, half = sums.shape
    shape = ((steps + 1) * pitch_of(rows // (steps + 1)), half // CHUNKS)
    return call(
        functools.partial(keep_second_kernel, steps),
        "keep_second",
        [IN_VMEM] * 2,
        [IN_VMEM] * CHUNKS,
        [floats(*shape)] * CHUNKS,
        [pltpu.VMEM((rows // 8, 3 * half), jnp.bfloat16)] * 2,
        1 << 31,
    )(place, tables, sums)


def ranks(slabs):
    return slabs // 2


def forward_first_kernel(slabs, chunk, place, keep, got, table, decay, modes, *refs):
    size = ranks(slabs)
    lasts, (state, split, split_end) = refs[:size], refs[size:]
    steps, _, part, rows = modes.shape
    pitch = keep.shape[0] // (steps + 1)
    block = split.shape[1] // part
    strip = place[1]
    state[...] = jnp.zeros_like(state)
    for step in range(0, steps, block):
        for c in (0, 1):
            for at in range(block):
                cells_at = pl.ds((step + at) * pitch, rows)
                near, far = keep[cells_at], got[cells_at]
                cells = near - far if c else near + far
                store_split(split, (c, pl.ds(at * part, part)), 0, cells.T)
            result = dot(split[c], table[strip, c])
            modes[pl.ds(step, block), c] = result.reshape(block, part, rows)
        for c in (0, 1):
            for row in range(0, part, TILE):
                tile, at_state = pl.ds(row, TILE), pl.ds(c * part + row, TILE)
                value = state[at_state]
                rate = decay[strip, c, pl.ds(chunk * part + row, TILE)]
                for at in range(block):
                    value = rate * (value + modes[step + at, c, tile])
                state[at_state] = value
    is_last = (place[0] == slabs - 1).astype(jnp.float32)
    near, far = keep[pl.ds(pitch * steps, rows)], got[pl.ds(pitch * steps, rows)]
    for c, cells in enumerate((near + far, near - far)):
        store_split(split_end, (c, slice(None)), 0, cells.T)
        at_state = pl.ds(c * part, part)
        state[at_state] = state[at_state] - is_last * dot(split_end[c], table[strip, c])
    rank = lax.rem(place[0], size)
    share = 2 * part // size
    for partner in range(size):
        at = pl.multiple_of((rank ^ partner) * share, share)
        lasts[partner][...] = state[pl.ds(at, share)]


def forward_first(place, chunk, keep, got, tables, decays, slabs):
    rows, part = tables.shape[-1], keep.shape[1]
    steps = keep.shape[0] // pitch_of(rows) - 1
    block = min(8, steps)
    size = ranks(slabs)
    share = 2 * part // size
    outs = call(
        functools.partial(forward_first_kernel, slabs, chunk),
        "forward_first",
        [IN_VMEM] * 4,
        [IN_VMEM] * (1 + size),
        [floats(steps, 2, part, rows)] + [floats(share, rows)] * size,
        [
            pltpu.VMEM((2 * part, rows), jnp.float32),
            pltpu.VMEM((2, block * part, 3 * rows), jnp.bfloat16),
            pltpu.VMEM((2, part, 3 * rows), jnp.bfloat16),
        ],
        1 << 31,
    )(place, keep, got, tables, decays)
    return outs[0], outs[1:]


def half_sum_kernel(slabs, chunk, place, closing, *refs):
    size = ranks(slabs)
    lasts, ordered, total = refs[:size], refs[size], refs[size + 1]
    share = total.shape[0]
    rank = lax.rem(place[0], size)
    decay = closing[place[1], chunk, 0, pl.ds(pl.multiple_of(rank * share, share), share)]
    for partner in range(size):
        ordered[rank ^ partner] = lasts[partner][...]
    state = ordered[0]
    for at in range(1, size):
        state = ordered[at] + decay * state
    total[...] = state


def half_sum(place, chunk, lasts, closing, slabs):
    size = ranks(slabs)
    share, rows = lasts[0].shape
    return call(
        functools.partial(half_sum_kernel, slabs, chunk),
        "half_sum",
        [IN_VMEM] * (1 + size),
        [IN_VMEM] * 2,
        [floats(size, share, rows), floats(share, rows)],
        [],
        1 << 20,
    )(place, closing, *lasts)


def close_kernel(slabs, chunk, place, closing, ordered, near, far, *refs):
    size = ranks(slabs)
    befores, states = refs[:size], refs[size]
    share = near.shape[0]
    rank = lax.rem(place[0], size)
    at_share = pl.ds(pl.multiple_of(rank * share, share), share)
    decay, half_decay, gain = (closing[place[1], chunk, at, at_share] for at in range(3))
    entering = jnp.where(place[0] < size, circulant_alpha, 1.0)
    state = gain * (entering * far[...] + circulant_alpha * half_decay * near[...])
    for at in range(size):
        states[at] = state
        if at < size - 1:
            state = ordered[at] + decay * state
    for partner in range(size):
        befores[partner][...] = states[rank ^ partner]


def close(place, chunk, ordered, near, far, closing, slabs):
    size, share, rows = ordered.shape
    return call(
        functools.partial(close_kernel, slabs, chunk),
        "close",
        [IN_VMEM] * 4,
        [IN_VMEM] * size,
        [floats(share, rows)] * size,
        [pltpu.VMEM((size, share, rows), jnp.float32)],
        1 << 20,
    )(place, closing, ordered, near, far)


def inverse_first_kernel(slabs, chunk, place, modes, table, decay, *refs):
    size = ranks(slabs)
    befores, (keep, send, state, split) = refs[:size], refs[size:]
    steps, _, part, rows = modes.shape
    pitch = keep.shape[0] // steps
    block = split.shape[1] // part
    strip = place[1]
    rank = lax.rem(place[0], size)
    share = 2 * part // size
    for partner in range(size):
        at = pl.multiple_of((rank ^ partner) * share, share)
        state[pl.ds(at, share)] = befores[partner][...]
    for step in range(0, steps, block):
        results = []
        for c in (0, 1):
            for row in range(0, part, TILE):
                tile, at_state = pl.ds(row, TILE), pl.ds(c * part + row, TILE)
                value = state[at_state]
                rate = decay[strip, c, pl.ds(chunk * part + row, TILE)]
                for at in range(block):
                    value = rate * (value + modes[step + at, c, tile])
                    store_split(split, (c, pl.ds(at * part + row, TILE)), 0, value)
                state[at_state] = value
            results.append(dot(split[c], table[strip, c]))
        even, odd = results
        for at in range(block):
            piece = slice(at * part, (at + 1) * part)
            cells_at = pl.ds((step + at) * pitch, rows)
            keep[cells_at, :] = (even[piece] + odd[piece]).T
            send[cells_at, :] = (even[piece] - odd[piece]).T


def inverse_first(place, chunk, modes, befores, tables, decays, slabs):
    steps, _, part, rows = modes.shape
    block = min(8, steps)
    return call(
        functools.partial(inverse_first_kernel, slabs, chunk),
        "inverse_first",
        [IN_VMEM] * (3 + len(befores)),
        [IN_VMEM] * 2,
        [floats(steps * pitch_of(rows), part)] * 2,
        [
            pltpu.VMEM((2 * part, rows), jnp.float32),
            pltpu.VMEM((2, block * part, 3 * rows), jnp.bfloat16),
        ],
        1 << 31,
    )(place, modes, tables, decays, *befores)


def keep_inverse_kernel(steps, place, tables, *refs):
    keeps, out, scratch = refs[:CHUNKS], refs[CHUNKS], refs[CHUNKS + 1 :]
    part = keeps[0].shape[1]
    pitch = keeps[0].shape[0] // steps
    depth = scratch[0].shape[0]
    group = max(TILE // steps, 1)
    for at in range(0, out.shape[0], depth):
        split = scratch[at // depth % 2]
        for row in range(0, depth, TILE):
            cell = (at + row) // steps
            for chunk, keep in enumerate(keeps):
                cells = steps_of(keep, range(cell, cell + group), steps, pitch)
                store_split(split, (pl.ds(row, TILE),), chunk * part, cells)
        out[pl.ds(at, depth)] = dot(split[...], tables[place[1]])


def keep_inverse(place, keeps, tables, rows, steps):
    half = keeps[0].shape[1] * CHUNKS
    return call(
        functools.partial(keep_inverse_kernel, steps),
        "keep_inverse",
        [IN_VMEM] * (1 + CHUNKS),
        IN_VMEM,
        floats(rows * steps, half),
        [pltpu.VMEM((rows * steps // 8, 3 * half), jnp.bfloat16)] * 2,
        1 << 31,
    )(place, tables, *keeps)


def inverse_second_kernel(place, tables, kept, *refs):
    gots, out, scratch = refs[:CHUNKS], refs[CHUNKS], refs[CHUNKS + 1 :]
    rows, steps, width = out.shape
    half = width // 2
    part = half // CHUNKS
    pitch = gots[0].shape[0] // steps
    count = len(scratch) // 2
    piece = rows // count
    group = max(TILE // steps, 1)
    strip = place[1]
    sign = 1.0 - 2.0 * strip.astype(jnp.float32)
    total = rows * pl.num_programs(0)
    start = pl.program_id(0) * rows
    for sub in range(count):
        split, result = scratch[2 * sub : 2 * sub + 2]
        base = start + sub * piece
        for row in range(0, piece, group):
            mirrors = [total - 1 - base - row - at for at in range(group)]
            for chunk, got in enumerate(gots):
                cells = steps_of(got, mirrors, steps, pitch)
                store_split(split, (pl.ds(row * steps, TILE),), chunk * part, cells)
        result[...] = dot(split[...], tables[1 - strip])
        kept_base = pl.multiple_of(base * steps, piece * steps)
        for row in range(0, piece, group):
            first = kept[pl.ds(kept_base + row * steps, TILE)]
            second = result[pl.ds(row * steps, TILE)]
            upper = sign * (first - second)
            parts = [
                lanes_reversed(upper[:, lane : lane + LANES]) for lane in range(0, half, LANES)
            ][::-1]
            whole = jnp.concatenate([first + second, *parts], axis=1)
            out[pl.ds(sub * piece + row, group)] = whole.reshape(group, TILE // group, width)


def inverse_second(place, kept, gots, tables, steps):
    rows, half = kept.shape[0] // steps, kept.shape[1]
    block, pieces = min(64, rows), 2
    depth = steps * block // pieces
    return call(
        inverse_second_kernel,
        "inverse_second",
        [IN_VMEM] * (2 + CHUNKS),
        pl.BlockSpec((block, steps, 2 * half), lambda i, place: (i, 0, 0)),
        floats(rows, steps, 2 * half),
        [pltpu.VMEM((depth, 3 * half), jnp.bfloat16), pltpu.VMEM((depth, half), jnp.float32)]
        * pieces,
        1 << 32,
        rows // block,
    )(place, tables, kept, *gots)


def swapped(block):
    return lax.ppermute(block, "space", [(0, 1), (1, 0)])


def with_partner(block, distance):
    slabs = lax.axis_size("tm")
    return lax.ppermute(block, "tm", [(slab, slab ^ distance) for slab in range(slabs)])


def among_ranks(blocks):
    return [blocks[0]] + [with_partner(block, at) for at, block in enumerate(blocks) if at]


def by_chunk(table):
    strips, _, half, rows = table.shape
    parts = table.reshape(strips, 2, CHUNKS, half // CHUNKS, rows)
    return np.swapaxes(parts, 1, 2).reshape(strips, CHUNKS, 2 * half // CHUNKS, rows)


def shards(iterate, initial):
    rows, steps, width = iterate.shape
    slabs = lax.axis_size("tm")
    total = rows * lax.axis_size("space")
    place = jnp.stack([lax.axis_index("tm"), lax.axis_index("space")]).astype(jnp.int32)
    second = second_tables(width)
    first = first_tables(total)
    decay = decay_tables(total, width)
    slab_decay = decay**steps
    half_decay = slab_decay ** ranks(slabs)
    gain = 1.0 / (1.0 - circulant_alpha * half_decay * half_decay)
    closing = constant(
        np.stack([by_chunk(table) for table in (slab_decay, half_decay, gain)], axis=2)
    )
    first_table, decays = split_constant(first), constant(decay)
    second_table = split_constant(second)
    sums, sends = forward_second(place, iterate, initial, second_table)
    gots = [swapped(send) for send in sends]
    keeps = keep_second(place, sums, second_table, steps)
    modes, befores = [], []
    for chunk in range(CHUNKS):
        own_modes, lasts = forward_first(
            place, chunk, keeps[chunk], gots[chunk], first_table, decays, slabs
        )
        modes.append(own_modes)
        ordered, near = half_sum(place, chunk, among_ranks(lasts), closing, slabs)
        far = with_partner(near, ranks(slabs))
        befores.append(among_ranks(close(place, chunk, ordered, near, far, closing, slabs)))
    inverse_table = split_constant(np.swapaxes(first, 2, 3))
    keeps, sends = zip(
        *(
            inverse_first(place, chunk, modes[chunk], befores[chunk], inverse_table, decays, slabs)
            for chunk in range(CHUNKS)
        )
    )
    gots = [swapped(send) for send in sends]
    inverse_table = split_constant(np.swapaxes(second, 1, 2))
    kept = keep_inverse(place, keeps, inverse_table, rows, steps)
    return inverse_second(place, kept, gots, inverse_table, steps)


def solution(mesh):
    return jax.shard_map(
        shards,
        mesh=mesh,
        in_specs=(P(("group", "space"), "tm", None), P(("group", "space"), None)),
        out_specs=P(("group", "space"), "tm", None),
        check_vma=False,
    )
```

```python
import functools
import math

import jax
import jax.numpy as jnp
import numpy as np
from jax import lax
from jax.experimental import pallas as pl
from jax.experimental.pallas import tpu as pltpu
from jax.sharding import PartitionSpec as P

circulant_alpha = 0.01
DIFFUSION = 2.0
REACTION_STEP = 0.5
VMEM_BYTES = 24 * 1024 * 1024
LANES = 128
SUBLANES = 8
TILE = 16
CHUNKS = 2


def sine_table(row_index, column_index, length):
    product = np.outer(row_index + 1, column_index + 1) % (2 * (length + 1))
    return math.sqrt(2.0 / (length + 1)) * np.sin(product * (math.pi / (length + 1)))


def stencil_eigen(mode_index, length):
    return 4.0 * np.sin((mode_index + 1) * (math.pi / (2.0 * (length + 1)))) ** 2


def second_tables(width):
    half = width // 2
    return np.stack([sine_table(np.arange(half), np.arange(s, width, 2), width) for s in (0, 1)])


def first_tables(total):
    rows = total // 2
    return np.stack(
        [
            np.stack(
                [sine_table(s * rows + np.arange(rows), np.arange(c, total, 2), total) for c in (0, 1)]
            )
            for s in (0, 1)
        ]
    )


def decay_tables(total, width):
    first, second = stencil_eigen(np.arange(total), total), stencil_eigen(np.arange(width), width)
    decay = 1.0 / (1.0 + DIFFUSION * (second[:, None] + first[None, :]))
    return np.stack([np.stack([decay[s::2, c::2] for c in (0, 1)]) for s in (0, 1)])


def constant(table):
    return jnp.asarray(np.asarray(table, np.float32))


def split_constant(table):
    table = np.asarray(table, np.float32)
    high = table.astype(jnp.bfloat16)
    low = (table - high.astype(np.float32)).astype(jnp.bfloat16)
    return jnp.asarray(np.concatenate([high, high, low], axis=-2))


def store_split(ref, at, lane, block):
    depth = ref.shape[-1] // 3
    width = block.shape[-1]
    high = block.astype(jnp.bfloat16)
    low = (block - high.astype(jnp.float32)).astype(jnp.bfloat16)
    for part, value in enumerate((high, low, high)):
        ref[(*at, pl.ds(part * depth + lane, width))] = value


def dot(first, second):
    return jnp.dot(first, second, preferred_element_type=jnp.float32)


def lanes_reversed(block):
    index = LANES - 1 - lax.broadcasted_iota(jnp.int32, (block.shape[0], LANES), 1)
    return jnp.take_along_axis(block, index, axis=1, mode="promise_in_bounds")


def store_rows_reversed(ref, start, block):
    rows, width = block.shape
    index = SUBLANES - 1 - lax.broadcasted_iota(jnp.int32, (SUBLANES, width), 0)
    for row in range(0, rows, SUBLANES):
        to = pl.multiple_of(start + rows - SUBLANES - row, SUBLANES)
        ref[pl.ds(to, SUBLANES), :] = jnp.take_along_axis(
            block[row : row + SUBLANES], index, axis=0, mode="promise_in_bounds"
        )


def pitch_of(cells):
    return cells + SUBLANES * (1 - cells // SUBLANES % 2)


def steps_of(ref, cells, steps, pitch):
    lines = [ref[pl.ds(cell, steps, stride=pitch), :] for cell in cells]
    return lines[0] if len(lines) == 1 else jnp.concatenate(lines, axis=0)


IN_VMEM = pl.BlockSpec(memory_space=pltpu.VMEM)
IN_SMEM = pl.BlockSpec(memory_space=pltpu.SMEM)


def in_hbm(array):
    return pltpu.with_memory_space_constraint(array, pltpu.HBM)


def floats(*shape):
    return jax.ShapeDtypeStruct(shape, jnp.float32)


def call(kernel, name, in_specs, out_specs, out_shape, scratch, flops, grid=None):
    if grid is None:
        spec = pl.GridSpec(
            in_specs=[IN_SMEM, *in_specs], out_specs=out_specs, scratch_shapes=scratch
        )
    else:
        spec = pltpu.PrefetchScalarGridSpec(
            num_scalar_prefetch=1,
            grid=(grid,),
            in_specs=in_specs,
            out_specs=out_specs,
            scratch_shapes=scratch,
        )
    return pl.pallas_call(
        kernel,
        grid_spec=spec,
        out_shape=out_shape,
        compiler_params=pltpu.CompilerParams(vmem_limit_bytes=VMEM_BYTES),
        cost_estimate=pl.CostEstimate(flops=flops, bytes_accessed=1 << 23, transcendentals=0),
        name=name,
    )


def forward_second_kernel(place, field, initial, table, sums, *refs):
    sends, scratch = refs[:CHUNKS], refs[CHUNKS:]
    rows, steps, width = field.shape
    half = width // 2
    part = half // CHUNKS
    piece = rows // len(scratch)
    group = max(TILE // steps, 1)
    block, blocks = pl.program_id(0), pl.num_programs(0)
    total = rows * blocks
    pitch = sends[0].shape[0] // (steps + 1)
    body = piece * steps
    is_first = place[0] == 0
    sign = 1.0 - 2.0 * place[1].astype(jnp.float32)

    def put(other, at, sums_at, cells):
        lower = cells[:, :half]
        upper = sign * jnp.concatenate(
            [lanes_reversed(cells[:, lane : lane + LANES]) for lane in range(half, width, LANES)][::-1],
            axis=1,
        )
        sums[pl.ds(sums_at, TILE), :] = lower + upper
        store_split(other, (pl.ds(at, TILE),), 0, lower - upper)

    def prepare(sub):
        kept_at = pl.multiple_of(block * rows + sub * piece, piece)
        kept_base = pl.multiple_of(kept_at * steps, body)
        for row in range(0, piece, group):
            cells = field[pl.ds(sub * piece + row, group)]
            force = cells - cells * cells * cells
            put(scratch[sub], row * steps, kept_base + row * steps, force.reshape(TILE, width))
        for row in range(0, piece, TILE):
            at = pl.ds(sub * piece + row, TILE)
            ends = jnp.where(is_first, initial[at], field[at, steps - 1, :])
            put(scratch[sub], body + row, total * steps + kept_at + row, ends)

    def transform(sub, block):
        sent = dot(scratch[sub][...], table[0])
        sent_at = pl.multiple_of(total - block * rows - (sub + 1) * piece, piece)
        for chunk, send in enumerate(sends):
            lanes = slice(chunk * part, (chunk + 1) * part)
            for row in range(piece):
                line = sent[row * steps : (row + 1) * steps, lanes]
                send[pl.ds(sent_at + piece - 1 - row, steps, stride=pitch), :] = line
            store_rows_reversed(send, pitch * steps + sent_at, sent[body:, lanes])

    last = len(scratch) - 1
    transform(last, jnp.maximum(block - 1, 0))
    for sub in range(last):
        prepare(sub)
        transform(sub, block)
    prepare(last)

    @pl.when(block == blocks - 1)
    def _():
        transform(last, block)


def forward_second(place, field, initial, tables):
    rows, steps, width = field.shape
    half = width // 2
    block, pieces = min(64, rows), 2
    depth = (steps + 1) * block // pieces
    outs = call(
        forward_second_kernel,
        "forward_second",
        [
            pl.BlockSpec((block, steps, width), lambda i, place: (i, 0, 0)),
            pl.BlockSpec((block, width), lambda i, place: (i, 0)),
            pl.BlockSpec((1, 3 * half, half), lambda i, place: (1 - place[1], 0, 0)),
        ],
        [IN_VMEM] * (1 + CHUNKS),
        [floats((steps + 1) * rows, half)]
        + [floats((steps + 1) * pitch_of(rows), half // CHUNKS)] * CHUNKS,
        [pltpu.VMEM((depth, 3 * half), jnp.bfloat16)] * pieces,
        1 << 32,
        rows // block,
    )(place, in_hbm(field), in_hbm(initial), in_hbm(tables))
    return outs[0], outs[1:]


def keep_second_kernel(steps, place, tables, sums, *refs):
    keeps, scratch = refs[:CHUNKS], refs[CHUNKS:]
    depth = scratch[0].shape[0]
    cells = sums.shape[0] // (steps + 1)
    pitch = keeps[0].shape[0] // (steps + 1)
    for at in range(0, sums.shape[0], depth):
        split = scratch[at // depth % 2]
        for row in range(0, depth, TILE):
            store_split(split, (pl.ds(row, TILE),), 0, sums[pl.ds(at + row, TILE)])
        result = dot(split[...], tables[place[1]])
        for chunk, keep in enumerate(keeps):
            part = keep.shape[1]
            lanes = slice(chunk * part, (chunk + 1) * part)
            body = max(0, min(depth, cells * steps - at))
            for row in range(0, body, steps):
                line = result[row : row + steps, lanes]
                keep[pl.ds((at + row) // steps, steps, stride=pitch), :] = line
            if body < depth:
                ends = pl.ds(pitch * steps + at + body - cells * steps, depth - body)
                keep[ends, :] = result[body:, lanes]


def keep_second(place, sums, tables, steps):
    rows, half = sums.shape
    shape = ((steps + 1) * pitch_of(rows // (steps + 1)), half // CHUNKS)
    return call(
        functools.partial(keep_second_kernel, steps),
        "keep_second",
        [IN_VMEM] * 2,
        [IN_VMEM] * CHUNKS,
        [floats(*shape)] * CHUNKS,
        [pltpu.VMEM((rows // 8, 3 * half), jnp.bfloat16)] * 2,
        1 << 31,
    )(place, tables, sums)


def ranks(slabs):
    return slabs // 2


def forward_first_kernel(slabs, chunk, place, keep, got, table, decay, modes, *refs):
    size = ranks(slabs)
    lasts, (state, split, split_end, extra) = refs[:size], refs[size:]
    steps, _, part, rows = modes.shape
    pitch = keep.shape[0] // (steps + 1)
    block = split.shape[1] // part
    strip = place[1]
    near, far = keep[pl.ds(pitch * steps, rows)], got[pl.ds(pitch * steps, rows)]
    for c, cells in enumerate((near + far, near - far)):
        store_split(split_end, (c, slice(None)), 0, cells.T)
        extra[c] = dot(split_end[c], table[strip, c])
    is_first = jnp.where(place[0] == 0, 1.0 / REACTION_STEP, 0.0)
    is_last = jnp.where(place[0] == slabs - 1, 1.0 / REACTION_STEP, 0.0)
    state[...] = jnp.zeros_like(state)
    for step in range(0, steps, block):
        for c in (0, 1):
            for at in range(block):
                cells_at = pl.ds((step + at) * pitch, rows)
                near, far = keep[cells_at], got[cells_at]
                cells = near - far if c else near + far
                store_split(split, (c, pl.ds(at * part, part)), 0, cells.T)
            result = dot(split[c], table[strip, c])
            modes[pl.ds(step, block), c] = result.reshape(block, part, rows)
            if step == 0:
                modes[0, c] = result[:part] + is_first * extra[c]
        for c in (0, 1):
            for row in range(0, part, TILE):
                tile, at_state = pl.ds(row, TILE), pl.ds(c * part + row, TILE)
                value = state[at_state]
                rate = decay[strip, c, pl.ds(chunk * part + row, TILE)]
                for at in range(block):
                    value = rate * (value + modes[step + at, c, tile])
                state[at_state] = value
    for c in (0, 1):
        at_state = pl.ds(c * part, part)
        state[at_state] = state[at_state] - is_last * extra[c]
    rank = lax.rem(place[0], size)
    share = 2 * part // size
    for partner in range(size):
        at = pl.multiple_of((rank ^ partner) * share, share)
        lasts[partner][...] = state[pl.ds(at, share)]


def forward_first(place, chunk, keep, got, tables, decays, slabs):
    rows, part = tables.shape[-1], keep.shape[1]
    steps = keep.shape[0] // pitch_of(rows) - 1
    block = min(8, steps)
    size = ranks(slabs)
    share = 2 * part // size
    outs = call(
        functools.partial(forward_first_kernel, slabs, chunk),
        "forward_first",
        [IN_VMEM] * 4,
        [IN_VMEM] * (1 + size),
        [floats(steps, 2, part, rows)] + [floats(share, rows)] * size,
        [
            pltpu.VMEM((2 * part, rows), jnp.float32),
            pltpu.VMEM((2, block * part, 3 * rows), jnp.bfloat16),
            pltpu.VMEM((2, part, 3 * rows), jnp.bfloat16),
            pltpu.VMEM((2, part, rows), jnp.float32),
        ],
        1 << 31,
    )(place, keep, got, tables, decays)
    return outs[0], outs[1:]


def half_sum_kernel(slabs, chunk, place, closing, *refs):
    size = ranks(slabs)
    lasts, ordered, total = refs[:size], refs[size], refs[size + 1]
    share = total.shape[0]
    rank = lax.rem(place[0], size)
    decay = closing[place[1], chunk, 0, pl.ds(pl.multiple_of(rank * share, share), share)]
    for partner in range(size):
        ordered[rank ^ partner] = lasts[partner][...]
    state = ordered[0]
    for at in range(1, size):
        state = ordered[at] + decay * state
    total[...] = state


def half_sum(place, chunk, lasts, closing, slabs):
    size = ranks(slabs)
    share, rows = lasts[0].shape
    return call(
        functools.partial(half_sum_kernel, slabs, chunk),
        "half_sum",
        [IN_VMEM] * (1 + size),
        [IN_VMEM] * 2,
        [floats(size, share, rows), floats(share, rows)],
        [],
        1 << 20,
    )(place, closing, *lasts)


def close_kernel(slabs, chunk, place, closing, ordered, near, far, *refs):
    size = ranks(slabs)
    befores, states = refs[:size], refs[size]
    share = near.shape[0]
    rank = lax.rem(place[0], size)
    at_share = pl.ds(pl.multiple_of(rank * share, share), share)
    decay, half_decay, gain = (closing[place[1], chunk, at, at_share] for at in range(3))
    entering = jnp.where(place[0] < size, circulant_alpha, 1.0)
    state = gain * (entering * far[...] + circulant_alpha * half_decay * near[...])
    for at in range(size):
        states[at] = state
        if at < size - 1:
            state = ordered[at] + decay * state
    for partner in range(size):
        befores[partner][...] = states[rank ^ partner]


def close(place, chunk, ordered, near, far, closing, slabs):
    size, share, rows = ordered.shape
    return call(
        functools.partial(close_kernel, slabs, chunk),
        "close",
        [IN_VMEM] * 4,
        [IN_VMEM] * size,
        [floats(share, rows)] * size,
        [pltpu.VMEM((size, share, rows), jnp.float32)],
        1 << 20,
    )(place, closing, ordered, near, far)


def inverse_first_kernel(slabs, chunk, place, modes, table, decay, *refs):
    size = ranks(slabs)
    befores, (keep, send, state, split) = refs[:size], refs[size:]
    steps, _, part, rows = modes.shape
    pitch = keep.shape[0] // steps
    block = split.shape[1] // part
    strip = place[1]
    rank = lax.rem(place[0], size)
    share = 2 * part // size
    for partner in range(size):
        at = pl.multiple_of((rank ^ partner) * share, share)
        state[pl.ds(at, share)] = befores[partner][...]
    for step in range(0, steps, block):
        results = []
        for c in (0, 1):
            for row in range(0, part, TILE):
                tile, at_state = pl.ds(row, TILE), pl.ds(c * part + row, TILE)
                value = state[at_state]
                rate = decay[strip, c, pl.ds(chunk * part + row, TILE)]
                for at in range(block):
                    value = rate * (value + modes[step + at, c, tile])
                    store_split(split, (c, pl.ds(at * part + row, TILE)), 0, value)
                state[at_state] = value
            results.append(dot(split[c], table[strip, c]))
        even, odd = results
        for at in range(block):
            piece = slice(at * part, (at + 1) * part)
            cells_at = pl.ds((step + at) * pitch, rows)
            keep[cells_at, :] = (even[piece] + odd[piece]).T
            send[cells_at, :] = (even[piece] - odd[piece]).T


def inverse_first(place, chunk, modes, befores, tables, decays, slabs):
    steps, _, part, rows = modes.shape
    block = min(8, steps)
    return call(
        functools.partial(inverse_first_kernel, slabs, chunk),
        "inverse_first",
        [IN_VMEM] * (3 + len(befores)),
        [IN_VMEM] * 2,
        [floats(steps * pitch_of(rows), part)] * 2,
        [
            pltpu.VMEM((2 * part, rows), jnp.float32),
            pltpu.VMEM((2, block * part, 3 * rows), jnp.bfloat16),
        ],
        1 << 31,
    )(place, modes, tables, decays, *befores)


def keep_inverse_kernel(steps, place, tables, *refs):
    keeps, out, scratch = refs[:CHUNKS], refs[CHUNKS], refs[CHUNKS + 1 :]
    part = keeps[0].shape[1]
    pitch = keeps[0].shape[0] // steps
    depth = scratch[0].shape[0]
    group = max(TILE // steps, 1)
    for at in range(0, out.shape[0], depth):
        split = scratch[at // depth % 2]
        for row in range(0, depth, TILE):
            cell = (at + row) // steps
            for chunk, keep in enumerate(keeps):
                cells = steps_of(keep, range(cell, cell + group), steps, pitch)
                store_split(split, (pl.ds(row, TILE),), chunk * part, cells)
        out[pl.ds(at, depth)] = dot(split[...], tables[place[1]])


def keep_inverse(place, keeps, tables, rows, steps):
    half = keeps[0].shape[1] * CHUNKS
    return call(
        functools.partial(keep_inverse_kernel, steps),
        "keep_inverse",
        [IN_VMEM] * (1 + CHUNKS),
        IN_VMEM,
        floats(rows * steps, half),
        [pltpu.VMEM((rows * steps // 8, 3 * half), jnp.bfloat16)] * 2,
        1 << 31,
    )(place, tables, *keeps)


def inverse_second_kernel(place, tables, kept, *refs):
    gots, out, scratch = refs[:CHUNKS], refs[CHUNKS], refs[CHUNKS + 1 :]
    rows, steps, width = out.shape
    half = width // 2
    part = half // CHUNKS
    pitch = gots[0].shape[0] // steps
    count = len(scratch) // 2
    piece = rows // count
    group = max(TILE // steps, 1)
    strip = place[1]
    sign = 1.0 - 2.0 * strip.astype(jnp.float32)
    total = rows * pl.num_programs(0)
    start = pl.program_id(0) * rows
    for sub in range(count):
        split, result = scratch[2 * sub : 2 * sub + 2]
        base = start + sub * piece
        for row in range(0, piece, group):
            mirrors = [total - 1 - base - row - at for at in range(group)]
            for chunk, got in enumerate(gots):
                cells = steps_of(got, mirrors, steps, pitch)
                store_split(split, (pl.ds(row * steps, TILE),), chunk * part, cells)
        result[...] = dot(split[...], tables[1 - strip])
    for sub in range(count):
        result = scratch[2 * sub + 1]
        kept_base = pl.multiple_of((start + sub * piece) * steps, piece * steps)
        for row in range(0, piece, group):
            first = kept[pl.ds(kept_base + row * steps, TILE)]
            second = result[pl.ds(row * steps, TILE)]
            upper = sign * (first - second)
            parts = [
                lanes_reversed(upper[:, lane : lane + LANES]) for lane in range(0, half, LANES)
            ][::-1]
            whole = jnp.concatenate([first + second, *parts], axis=1)
            out[pl.ds(sub * piece + row, group)] = whole.reshape(group, TILE // group, width)


def inverse_second(place, kept, gots, tables, steps):
    rows, half = kept.shape[0] // steps, kept.shape[1]
    block, pieces = min(64, rows), 2
    depth = steps * block // pieces
    return call(
        inverse_second_kernel,
        "inverse_second",
        [IN_VMEM] * (2 + CHUNKS),
        pl.BlockSpec((block, steps, 2 * half), lambda i, place: (i, 0, 0)),
        floats(rows, steps, 2 * half),
        [pltpu.VMEM((depth, 3 * half), jnp.bfloat16), pltpu.VMEM((depth, half), jnp.float32)]
        * pieces,
        1 << 32,
        rows // block,
    )(place, tables, kept, *gots)


def swapped(block):
    return lax.ppermute(block, "space", [(0, 1), (1, 0)])


def with_partner(block, distance):
    slabs = lax.axis_size("tm")
    return lax.ppermute(block, "tm", [(slab, slab ^ distance) for slab in range(slabs)])


def among_ranks(blocks):
    return [blocks[0]] + [with_partner(block, at) for at, block in enumerate(blocks) if at]


def by_chunk(table):
    strips, _, half, rows = table.shape
    parts = table.reshape(strips, 2, CHUNKS, half // CHUNKS, rows)
    return np.swapaxes(parts, 1, 2).reshape(strips, CHUNKS, 2 * half // CHUNKS, rows)


def shards(iterate, initial):
    rows, steps, width = iterate.shape
    slabs = lax.axis_size("tm")
    total = rows * lax.axis_size("space")
    place = jnp.stack([lax.axis_index("tm"), lax.axis_index("space")]).astype(jnp.int32)
    second = second_tables(width)
    first = first_tables(total)
    decay = decay_tables(total, width)
    slab_decay = decay**steps
    half_decay = slab_decay ** ranks(slabs)
    gain = 1.0 / (1.0 - circulant_alpha * half_decay * half_decay)
    closing = constant(
        np.stack([by_chunk(table) for table in (slab_decay, half_decay, gain)], axis=2)
    )
    first_table, decays = split_constant(first), constant(decay)
    second_table = split_constant(REACTION_STEP * second)
    sums, sends = forward_second(place, iterate, initial, second_table)
    gots = [swapped(send) for send in sends]
    keeps = keep_second(place, sums, second_table, steps)
    modes, befores = [], []
    for chunk in range(CHUNKS):
        own_modes, lasts = forward_first(
            place, chunk, keeps[chunk], gots[chunk], first_table, decays, slabs
        )
        modes.append(own_modes)
        ordered, near = half_sum(place, chunk, among_ranks(lasts), closing, slabs)
        far = with_partner(near, ranks(slabs))
        befores.append(among_ranks(close(place, chunk, ordered, near, far, closing, slabs)))
    inverse_table = split_constant(np.swapaxes(first, 2, 3))
    keeps, sends = zip(
        *(
            inverse_first(place, chunk, modes[chunk], befores[chunk], inverse_table, decays, slabs)
            for chunk in range(CHUNKS)
        )
    )
    gots = [swapped(send) for send in sends]
    inverse_table = split_constant(np.swapaxes(second, 1, 2))
    kept = keep_inverse(place, keeps, inverse_table, rows, steps)
    return inverse_second(place, kept, gots, inverse_table, steps)


def solution(mesh):
    return jax.shard_map(
        shards,
        mesh=mesh,
        in_specs=(P(("group", "space"), "tm", None), P(("group", "space"), None)),
        out_specs=P(("group", "space"), "tm", None),
        check_vma=False,
    )
```

```python
import functools
import math

import jax
import jax.numpy as jnp
import numpy as np
from jax import lax
from jax.experimental import pallas as pl
from jax.experimental.pallas import tpu as pltpu
from jax.sharding import PartitionSpec as P

circulant_alpha = 0.01
DIFFUSION = 2.0
REACTION_STEP = 0.5
VMEM_BYTES = 24 * 1024 * 1024
LANES = 128
SUBLANES = 8
TILE = 16
CHUNKS = 2


def sine_table(row_index, column_index, length):
    product = np.outer(row_index + 1, column_index + 1) % (2 * (length + 1))
    return math.sqrt(2.0 / (length + 1)) * np.sin(product * (math.pi / (length + 1)))


def stencil_eigen(mode_index, length):
    return 4.0 * np.sin((mode_index + 1) * (math.pi / (2.0 * (length + 1)))) ** 2


def second_tables(width):
    half = width // 2
    return np.stack([sine_table(np.arange(half), np.arange(s, width, 2), width) for s in (0, 1)])


def first_tables(total):
    rows = total // 2
    return np.stack(
        [
            np.stack(
                [sine_table(s * rows + np.arange(rows), np.arange(c, total, 2), total) for c in (0, 1)]
            )
            for s in (0, 1)
        ]
    )


def decay_tables(total, width):
    first, second = stencil_eigen(np.arange(total), total), stencil_eigen(np.arange(width), width)
    decay = 1.0 / (1.0 + DIFFUSION * (second[:, None] + first[None, :]))
    return np.stack([np.stack([decay[s::2, c::2] for c in (0, 1)]) for s in (0, 1)])


def constant(table):
    return jnp.asarray(np.asarray(table, np.float32))


def split_constant(table):
    table = np.asarray(table, np.float32)
    high = table.astype(jnp.bfloat16)
    low = (table - high.astype(np.float32)).astype(jnp.bfloat16)
    return jnp.asarray(np.concatenate([high, high, low], axis=-2))


def store_split(ref, at, lane, block):
    depth = ref.shape[-1] // 3
    width = block.shape[-1]
    high = block.astype(jnp.bfloat16)
    low = (block - high.astype(jnp.float32)).astype(jnp.bfloat16)
    for part, value in enumerate((high, low, high)):
        ref[(*at, pl.ds(part * depth + lane, width))] = value


def dot(first, second):
    return jnp.dot(first, second, preferred_element_type=jnp.float32)


def lanes_reversed(block):
    index = LANES - 1 - lax.broadcasted_iota(jnp.int32, (block.shape[0], LANES), 1)
    return jnp.take_along_axis(block, index, axis=1, mode="promise_in_bounds")


def store_rows_reversed(ref, start, block):
    rows, width = block.shape
    index = SUBLANES - 1 - lax.broadcasted_iota(jnp.int32, (SUBLANES, width), 0)
    for row in range(0, rows, SUBLANES):
        to = pl.multiple_of(start + rows - SUBLANES - row, SUBLANES)
        ref[pl.ds(to, SUBLANES), :] = jnp.take_along_axis(
            block[row : row + SUBLANES], index, axis=0, mode="promise_in_bounds"
        )


def pitch_of(cells):
    return cells + SUBLANES * (1 - cells // SUBLANES % 2)


def steps_of(ref, cells, steps, pitch):
    lines = [ref[pl.ds(cell, steps, stride=pitch), :] for cell in cells]
    return lines[0] if len(lines) == 1 else jnp.concatenate(lines, axis=0)


IN_VMEM = pl.BlockSpec(memory_space=pltpu.VMEM)
IN_HBM = pl.BlockSpec(memory_space=pltpu.HBM)
IN_SMEM = pl.BlockSpec(memory_space=pltpu.SMEM)


def in_hbm(array):
    return pltpu.with_memory_space_constraint(array, pltpu.HBM)


def floats(*shape):
    return jax.ShapeDtypeStruct(shape, jnp.float32)


def call(kernel, name, in_specs, out_specs, out_shape, scratch, flops):
    return pl.pallas_call(
        kernel,
        in_specs=[IN_SMEM, *in_specs],
        out_specs=out_specs,
        scratch_shapes=scratch,
        out_shape=out_shape,
        compiler_params=pltpu.CompilerParams(vmem_limit_bytes=VMEM_BYTES),
        cost_estimate=pl.CostEstimate(flops=flops, bytes_accessed=1 << 23, transcendentals=0),
        name=name,
    )


def forward_second_kernel(place, field_in, initial_in, tables, sums, *refs):
    sends, refs = refs[:CHUNKS], refs[CHUNKS:]
    field, initial, table, sems, table_sem, *scratch = refs
    cells, steps, width = field.shape
    half = width // 2
    part = half // CHUNKS
    pieces = sems.shape[0]
    piece = cells // pieces
    rows = piece * len(scratch)
    blocks = cells // rows
    group = max(TILE // steps, 1)
    pitch = sends[0].shape[0] // (steps + 1)
    body = piece * steps
    is_first = place[0] == 0
    sign = 1.0 - 2.0 * place[1].astype(jnp.float32)

    def copies(at):
        here = pl.ds(at * piece, piece)
        return [
            pltpu.make_async_copy(source.at[here], to.at[here], sems.at[at, which])
            for which, (source, to) in enumerate(((field_in, field), (initial_in, initial)))
        ]

    def wait(block):
        for sub in range(len(scratch)):
            for copy in copies(block * len(scratch) + sub):
                copy.wait()

    table_copy = pltpu.make_async_copy(tables.at[1 - place[1]], table, table_sem)
    for at in range(len(scratch)):
        for copy in copies(at):
            copy.start()
    table_copy.start()
    wait(0)
    table_copy.wait()
    for at in range(len(scratch), pieces):
        for copy in copies(at):
            copy.start()

    def put(other, at, sums_at, cells):
        lower = cells[:, :half]
        upper = sign * jnp.concatenate(
            [lanes_reversed(cells[:, lane : lane + LANES]) for lane in range(half, width, LANES)][::-1],
            axis=1,
        )
        sums[pl.ds(sums_at, TILE), :] = lower + upper
        store_split(other, (pl.ds(at, TILE),), 0, lower - upper)

    def prepare(sub, block):
        kept_at = pl.multiple_of(block * rows + sub * piece, piece)
        kept_base = pl.multiple_of(kept_at * steps, body)
        for row in range(0, piece, group):
            values = field[pl.ds(kept_at + row, group)]
            force = values - values * values * values
            put(scratch[sub], row * steps, kept_base + row * steps, force.reshape(TILE, width))
        for row in range(0, piece, TILE):
            at = pl.ds(pl.multiple_of(kept_at + row, TILE), TILE)
            ends = jnp.where(is_first, initial[at], field[at, steps - 1, :])
            put(scratch[sub], body + row, cells * steps + kept_at + row, ends)

    def transform(sub, block):
        sent = dot(scratch[sub][...], table[...])
        sent_at = pl.multiple_of(cells - block * rows - (sub + 1) * piece, piece)
        for chunk, send in enumerate(sends):
            lanes = slice(chunk * part, (chunk + 1) * part)
            for row in range(piece):
                line = sent[row * steps : (row + 1) * steps, lanes]
                send[pl.ds(sent_at + piece - 1 - row, steps, stride=pitch), :] = line
            store_rows_reversed(send, pitch * steps + sent_at, sent[body:, lanes])

    last = len(scratch) - 1

    def prepare_block(block):
        for sub in range(last):
            prepare(sub, block)
            transform(sub, block)
        prepare(last, block)

    prepare_block(0)

    @pl.loop(1, blocks)
    def _(block):
        wait(block)
        transform(last, block - 1)
        prepare_block(block)

    transform(last, blocks - 1)


def forward_second(place, field, initial, tables):
    rows, steps, width = field.shape
    half = width // 2
    piece, pieces = min(32, rows // 2), 2
    outs = call(
        forward_second_kernel,
        "forward_second",
        [IN_HBM] * 3,
        [IN_VMEM] * (1 + CHUNKS),
        [floats((steps + 1) * rows, half)]
        + [floats((steps + 1) * pitch_of(rows), half // CHUNKS)] * CHUNKS,
        [
            pltpu.VMEM(field.shape, jnp.float32),
            pltpu.VMEM(initial.shape, jnp.float32),
            pltpu.VMEM(tables.shape[1:], jnp.bfloat16),
            pltpu.SemaphoreType.DMA((rows // piece, 2)),
            pltpu.SemaphoreType.DMA,
        ]
        + [pltpu.VMEM(((steps + 1) * piece, 3 * half), jnp.bfloat16)] * pieces,
        1 << 32,
    )(place, in_hbm(field), in_hbm(initial), in_hbm(tables))
    return outs[0], outs[1:]


def keep_second_kernel(steps, place, tables, sums, *refs):
    keeps, scratch = refs[:CHUNKS], refs[CHUNKS:]
    depth = scratch[0].shape[0]
    cells = sums.shape[0] // (steps + 1)
    pitch = keeps[0].shape[0] // (steps + 1)
    for at in range(0, sums.shape[0], depth):
        split = scratch[at // depth % 2]
        for row in range(0, depth, TILE):
            store_split(split, (pl.ds(row, TILE),), 0, sums[pl.ds(at + row, TILE)])
        result = dot(split[...], tables[place[1]])
        for chunk, keep in enumerate(keeps):
            part = keep.shape[1]
            lanes = slice(chunk * part, (chunk + 1) * part)
            body = max(0, min(depth, cells * steps - at))
            for row in range(0, body, steps):
                line = result[row : row + steps, lanes]
                keep[pl.ds((at + row) // steps, steps, stride=pitch), :] = line
            if body < depth:
                ends = pl.ds(pitch * steps + at + body - cells * steps, depth - body)
                keep[ends, :] = result[body:, lanes]


def keep_second(place, sums, tables, steps):
    rows, half = sums.shape
    shape = ((steps + 1) * pitch_of(rows // (steps + 1)), half // CHUNKS)
    return call(
        functools.partial(keep_second_kernel, steps),
        "keep_second",
        [IN_VMEM] * 2,
        [IN_VMEM] * CHUNKS,
        [floats(*shape)] * CHUNKS,
        [pltpu.VMEM((rows // 8, 3 * half), jnp.bfloat16)] * 2,
        1 << 31,
    )(place, tables, sums)


def ranks(slabs):
    return slabs // 2


def forward_first_kernel(slabs, chunk, place, keep, got, table, decay, modes, *refs):
    size = ranks(slabs)
    lasts, (state, split, split_end, extra) = refs[:size], refs[size:]
    steps, _, part, rows = modes.shape
    pitch = keep.shape[0] // (steps + 1)
    block = split.shape[1] // part
    strip = place[1]
    near, far = keep[pl.ds(pitch * steps, rows)], got[pl.ds(pitch * steps, rows)]
    for c, cells in enumerate((near + far, near - far)):
        store_split(split_end, (c, slice(None)), 0, cells.T)
        extra[c] = dot(split_end[c], table[strip, c])
    is_first = jnp.where(place[0] == 0, 1.0 / REACTION_STEP, 0.0)
    is_last = jnp.where(place[0] == slabs - 1, 1.0 / REACTION_STEP, 0.0)
    state[...] = jnp.zeros_like(state)
    for step in range(0, steps, block):
        for c in (0, 1):
            for at in range(block):
                cells_at = pl.ds((step + at) * pitch, rows)
                near, far = keep[cells_at], got[cells_at]
                cells = near - far if c else near + far
                store_split(split, (c, pl.ds(at * part, part)), 0, cells.T)
            result = dot(split[c], table[strip, c])
            modes[pl.ds(step, block), c] = result.reshape(block, part, rows)
            if step == 0:
                modes[0, c] = result[:part] + is_first * extra[c]
        for c in (0, 1):
            for row in range(0, part, TILE):
                tile, at_state = pl.ds(row, TILE), pl.ds(c * part + row, TILE)
                value = state[at_state]
                rate = decay[strip, c, pl.ds(chunk * part + row, TILE)]
                for at in range(block):
                    value = rate * (value + modes[step + at, c, tile])
                state[at_state] = value
    for c in (0, 1):
        at_state = pl.ds(c * part, part)
        state[at_state] = state[at_state] - is_last * extra[c]
    rank = lax.rem(place[0], size)
    share = 2 * part // size
    for partner in range(size):
        at = pl.multiple_of((rank ^ partner) * share, share)
        lasts[partner][...] = state[pl.ds(at, share)]


def forward_first(place, chunk, keep, got, tables, decays, slabs):
    rows, part = tables.shape[-1], keep.shape[1]
    steps = keep.shape[0] // pitch_of(rows) - 1
    block = min(8, steps)
    size = ranks(slabs)
    share = 2 * part // size
    outs = call(
        functools.partial(forward_first_kernel, slabs, chunk),
        "forward_first",
        [IN_VMEM] * 4,
        [IN_VMEM] * (1 + size),
        [floats(steps, 2, part, rows)] + [floats(share, rows)] * size,
        [
            pltpu.VMEM((2 * part, rows), jnp.float32),
            pltpu.VMEM((2, block * part, 3 * rows), jnp.bfloat16),
            pltpu.VMEM((2, part, 3 * rows), jnp.bfloat16),
            pltpu.VMEM((2, part, rows), jnp.float32),
        ],
        1 << 31,
    )(place, keep, got, tables, decays)
    return outs[0], outs[1:]


def half_sum_kernel(slabs, chunk, place, closing, *refs):
    size = ranks(slabs)
    lasts, ordered, total = refs[:size], refs[size], refs[size + 1]
    share = total.shape[0]
    rank = lax.rem(place[0], size)
    decay = closing[place[1], chunk, 0, pl.ds(pl.multiple_of(rank * share, share), share)]
    for partner in range(size):
        ordered[rank ^ partner] = lasts[partner][...]
    state = ordered[0]
    for at in range(1, size):
        state = ordered[at] + decay * state
    total[...] = state


def half_sum(place, chunk, lasts, closing, slabs):
    size = ranks(slabs)
    share, rows = lasts[0].shape
    return call(
        functools.partial(half_sum_kernel, slabs, chunk),
        "half_sum",
        [IN_VMEM] * (1 + size),
        [IN_VMEM] * 2,
        [floats(size, share, rows), floats(share, rows)],
        [],
        1 << 20,
    )(place, closing, *lasts)


def close_kernel(slabs, chunk, place, closing, ordered, near, far, *refs):
    size = ranks(slabs)
    befores, states = refs[:size], refs[size]
    share = near.shape[0]
    rank = lax.rem(place[0], size)
    at_share = pl.ds(pl.multiple_of(rank * share, share), share)
    decay, half_decay, gain = (closing[place[1], chunk, at, at_share] for at in range(3))
    entering = jnp.where(place[0] < size, circulant_alpha, 1.0)
    state = gain * (entering * far[...] + circulant_alpha * half_decay * near[...])
    for at in range(size):
        states[at] = state
        if at < size - 1:
            state = ordered[at] + decay * state
    for partner in range(size):
        befores[partner][...] = states[rank ^ partner]


def close(place, chunk, ordered, near, far, closing, slabs):
    size, share, rows = ordered.shape
    return call(
        functools.partial(close_kernel, slabs, chunk),
        "close",
        [IN_VMEM] * 4,
        [IN_VMEM] * size,
        [floats(share, rows)] * size,
        [pltpu.VMEM((size, share, rows), jnp.float32)],
        1 << 20,
    )(place, closing, ordered, near, far)


def inverse_first_kernel(slabs, chunk, place, modes, table, decay, *refs):
    size = ranks(slabs)
    befores, (keep, send, state, split) = refs[:size], refs[size:]
    steps, _, part, rows = modes.shape
    pitch = keep.shape[0] // steps
    block = split.shape[1] // part
    strip = place[1]
    rank = lax.rem(place[0], size)
    share = 2 * part // size
    for partner in range(size):
        at = pl.multiple_of((rank ^ partner) * share, share)
        state[pl.ds(at, share)] = befores[partner][...]
    for step in range(0, steps, block):
        results = []
        for c in (0, 1):
            for row in range(0, part, TILE):
                tile, at_state = pl.ds(row, TILE), pl.ds(c * part + row, TILE)
                value = state[at_state]
                rate = decay[strip, c, pl.ds(chunk * part + row, TILE)]
                for at in range(block):
                    value = rate * (value + modes[step + at, c, tile])
                    store_split(split, (c, pl.ds(at * part + row, TILE)), 0, value)
                state[at_state] = value
            results.append(dot(split[c], table[strip, c]))
        even, odd = results
        for at in range(block):
            piece = slice(at * part, (at + 1) * part)
            cells_at = pl.ds((step + at) * pitch, rows)
            keep[cells_at, :] = (even[piece] + odd[piece]).T
            send[cells_at, :] = (even[piece] - odd[piece]).T


def inverse_first(place, chunk, modes, befores, tables, decays, slabs):
    steps, _, part, rows = modes.shape
    block = min(8, steps)
    return call(
        functools.partial(inverse_first_kernel, slabs, chunk),
        "inverse_first",
        [IN_VMEM] * (3 + len(befores)),
        [IN_VMEM] * 2,
        [floats(steps * pitch_of(rows), part)] * 2,
        [
            pltpu.VMEM((2 * part, rows), jnp.float32),
            pltpu.VMEM((2, block * part, 3 * rows), jnp.bfloat16),
        ],
        1 << 31,
    )(place, modes, tables, decays, *befores)


def keep_inverse_kernel(steps, place, tables, *refs):
    keeps, out, scratch = refs[:CHUNKS], refs[CHUNKS], refs[CHUNKS + 1 :]
    part = keeps[0].shape[1]
    pitch = keeps[0].shape[0] // steps
    depth = scratch[0].shape[0]
    group = max(TILE // steps, 1)
    for at in range(0, out.shape[0], depth):
        split = scratch[at // depth % 2]
        for row in range(0, depth, TILE):
            cell = (at + row) // steps
            for chunk, keep in enumerate(keeps):
                cells = steps_of(keep, range(cell, cell + group), steps, pitch)
                store_split(split, (pl.ds(row, TILE),), chunk * part, cells)
        out[pl.ds(at, depth)] = dot(split[...], tables[place[1]])


def keep_inverse(place, keeps, tables, rows, steps):
    half = keeps[0].shape[1] * CHUNKS
    return call(
        functools.partial(keep_inverse_kernel, steps),
        "keep_inverse",
        [IN_VMEM] * (1 + CHUNKS),
        IN_VMEM,
        floats(rows * steps, half),
        [pltpu.VMEM((rows * steps // 8, 3 * half), jnp.bfloat16)] * 2,
        1 << 31,
    )(place, tables, *keeps)


def inverse_second_kernel(place, tables, kept, *refs):
    gots, target, out, sems, scratch = (
        refs[:CHUNKS], refs[CHUNKS], refs[CHUNKS + 1], refs[CHUNKS + 2], refs[CHUNKS + 3 :]
    )
    cells, steps, width = out.shape
    half = width // 2
    part = half // CHUNKS
    pitch = gots[0].shape[0] // steps
    count = len(scratch) // 2
    pieces = sems.shape[0]
    piece = cells // pieces
    group = max(TILE // steps, 1)
    strip = place[1]
    sign = 1.0 - 2.0 * strip.astype(jnp.float32)

    def copy(at):
        here = pl.ds(at * piece, piece)
        return pltpu.make_async_copy(out.at[here], target.at[here], sems.at[at])

    @pl.loop(0, pieces, step=count)
    def _(first_piece):
        for sub in range(count):
            split, result = scratch[2 * sub : 2 * sub + 2]
            base = (first_piece + sub) * piece
            for row in range(0, piece, group):
                mirrors = [cells - 1 - base - row - at for at in range(group)]
                for chunk, got in enumerate(gots):
                    values = steps_of(got, mirrors, steps, pitch)
                    store_split(split, (pl.ds(row * steps, TILE),), chunk * part, values)
            result[...] = dot(split[...], tables[1 - strip])
        for sub in range(count):
            result = scratch[2 * sub + 1]
            base = pl.multiple_of((first_piece + sub) * piece, piece)
            kept_base = pl.multiple_of(base * steps, piece * steps)
            for row in range(0, piece, group):
                first = kept[pl.ds(kept_base + row * steps, TILE)]
                second = result[pl.ds(row * steps, TILE)]
                upper = sign * (first - second)
                parts = [
                    lanes_reversed(upper[:, lane : lane + LANES]) for lane in range(0, half, LANES)
                ][::-1]
                whole = jnp.concatenate([first + second, *parts], axis=1)
                out[pl.ds(base + row, group)] = whole.reshape(group, TILE // group, width)
            copy(first_piece + sub).start()

    for at in range(pieces):
        copy(at).wait()


def inverse_second(place, kept, gots, tables, steps):
    rows, half = kept.shape[0] // steps, kept.shape[1]
    piece, pieces = min(32, rows // 2), 2
    depth = steps * piece
    return call(
        inverse_second_kernel,
        "inverse_second",
        [IN_VMEM] * (2 + CHUNKS),
        IN_HBM,
        floats(rows, steps, 2 * half),
        [pltpu.VMEM((rows, steps, 2 * half), jnp.float32), pltpu.SemaphoreType.DMA((rows // piece,))]
        + [pltpu.VMEM((depth, 3 * half), jnp.bfloat16), pltpu.VMEM((depth, half), jnp.float32)]
        * pieces,
        1 << 32,
    )(place, tables, kept, *gots)


def swapped(block):
    return lax.ppermute(block, "space", [(0, 1), (1, 0)])


def with_partner(block, distance):
    slabs = lax.axis_size("tm")
    return lax.ppermute(block, "tm", [(slab, slab ^ distance) for slab in range(slabs)])


def among_ranks(blocks):
    return [blocks[0]] + [with_partner(block, at) for at, block in enumerate(blocks) if at]


def by_chunk(table):
    strips, _, half, rows = table.shape
    parts = table.reshape(strips, 2, CHUNKS, half // CHUNKS, rows)
    return np.swapaxes(parts, 1, 2).reshape(strips, CHUNKS, 2 * half // CHUNKS, rows)


def shards(iterate, initial):
    rows, steps, width = iterate.shape
    slabs = lax.axis_size("tm")
    total = rows * lax.axis_size("space")
    place = jnp.stack([lax.axis_index("tm"), lax.axis_index("space")]).astype(jnp.int32)
    second = second_tables(width)
    first = first_tables(total)
    decay = decay_tables(total, width)
    slab_decay = decay**steps
    half_decay = slab_decay ** ranks(slabs)
    gain = 1.0 / (1.0 - circulant_alpha * half_decay * half_decay)
    closing = constant(
        np.stack([by_chunk(table) for table in (slab_decay, half_decay, gain)], axis=2)
    )
    first_table, decays = split_constant(first), constant(decay)
    second_table = split_constant(REACTION_STEP * second)
    sums, sends = forward_second(place, iterate, initial, second_table)
    gots = [swapped(send) for send in sends]
    keeps = keep_second(place, sums, second_table, steps)
    modes, befores = [], []
    for chunk in range(CHUNKS):
        own_modes, lasts = forward_first(
            place, chunk, keeps[chunk], gots[chunk], first_table, decays, slabs
        )
        modes.append(own_modes)
        ordered, near = half_sum(place, chunk, among_ranks(lasts), closing, slabs)
        far = with_partner(near, ranks(slabs))
        befores.append(among_ranks(close(place, chunk, ordered, near, far, closing, slabs)))
    inverse_table = split_constant(np.swapaxes(first, 2, 3))
    keeps, sends = zip(
        *(
            inverse_first(place, chunk, modes[chunk], befores[chunk], inverse_table, decays, slabs)
            for chunk in range(CHUNKS)
        )
    )
    gots = [swapped(send) for send in sends]
    inverse_table = split_constant(np.swapaxes(second, 1, 2))
    kept = keep_inverse(place, keeps, inverse_table, rows, steps)
    return inverse_second(place, kept, gots, inverse_table, steps)


def solution(mesh):
    return jax.shard_map(
        shards,
        mesh=mesh,
        in_specs=(P(("group", "space"), "tm", None), P(("group", "space"), None)),
        out_specs=P(("group", "space"), "tm", None),
        check_vma=False,
    )
```

```python
import functools
import math

import jax
import jax.numpy as jnp
import numpy as np
from jax import lax
from jax.experimental import pallas as pl
from jax.experimental.pallas import tpu as pltpu
from jax.sharding import PartitionSpec as P

circulant_alpha = 0.01
DIFFUSION = 2.0
REACTION_STEP = 0.5
VMEM_BYTES = 24 * 1024 * 1024
LANES = 128
SUBLANES = 8
TILE = 16
CHUNKS = 2


def sine_table(row_index, column_index, length):
    product = np.outer(row_index + 1, column_index + 1) % (2 * (length + 1))
    return math.sqrt(2.0 / (length + 1)) * np.sin(product * (math.pi / (length + 1)))


def stencil_eigen(mode_index, length):
    return 4.0 * np.sin((mode_index + 1) * (math.pi / (2.0 * (length + 1)))) ** 2


def second_tables(width):
    half = width // 2
    return np.stack([sine_table(np.arange(half), np.arange(s, width, 2), width) for s in (0, 1)])


def first_tables(total):
    rows = total // 2
    return np.stack(
        [
            np.stack(
                [sine_table(s * rows + np.arange(rows), np.arange(c, total, 2), total) for c in (0, 1)]
            )
            for s in (0, 1)
        ]
    )


def decay_tables(total, width):
    first, second = stencil_eigen(np.arange(total), total), stencil_eigen(np.arange(width), width)
    decay = 1.0 / (1.0 + DIFFUSION * (second[:, None] + first[None, :]))
    return np.stack([np.stack([decay[s::2, c::2] for c in (0, 1)]) for s in (0, 1)])


def constant(table):
    return jnp.asarray(np.asarray(table, np.float32))


def split_constant(table):
    table = np.asarray(table, np.float32)
    high = table.astype(jnp.bfloat16)
    low = (table - high.astype(np.float32)).astype(jnp.bfloat16)
    return jnp.asarray(np.concatenate([high, high, low], axis=-2))


def store_split(ref, at, lane, block):
    depth = ref.shape[-1] // 2
    width = block.shape[-1]
    high = block.astype(jnp.bfloat16)
    low = (block - high.astype(jnp.float32)).astype(jnp.bfloat16)
    ref[(*at, pl.ds(lane, width))] = high
    ref[(*at, pl.ds(depth + lane, width))] = low


def dot(split, table):
    rows = jnp.concatenate([split, split[:, : split.shape[1] // 2]], axis=1)
    return jnp.dot(rows, table, preferred_element_type=jnp.float32)


def lanes_reversed(block):
    index = LANES - 1 - lax.broadcasted_iota(jnp.int32, (block.shape[0], LANES), 1)
    return jnp.take_along_axis(block, index, axis=1, mode="promise_in_bounds")


def store_rows_reversed(ref, start, block):
    rows, width = block.shape
    index = SUBLANES - 1 - lax.broadcasted_iota(jnp.int32, (SUBLANES, width), 0)
    for row in range(0, rows, SUBLANES):
        to = pl.multiple_of(start + rows - SUBLANES - row, SUBLANES)
        ref[pl.ds(to, SUBLANES), :] = jnp.take_along_axis(
            block[row : row + SUBLANES], index, axis=0, mode="promise_in_bounds"
        )


def pitch_of(cells):
    return cells + SUBLANES * (1 - cells // SUBLANES % 2)


def steps_of(ref, cells, steps, pitch):
    lines = [ref[pl.ds(cell, steps, stride=pitch), :] for cell in cells]
    return lines[0] if len(lines) == 1 else jnp.concatenate(lines, axis=0)


IN_VMEM = pl.BlockSpec(memory_space=pltpu.VMEM)
IN_HBM = pl.BlockSpec(memory_space=pltpu.HBM)
IN_SMEM = pl.BlockSpec(memory_space=pltpu.SMEM)


def in_hbm(array):
    return pltpu.with_memory_space_constraint(array, pltpu.HBM)


def floats(*shape):
    return jax.ShapeDtypeStruct(shape, jnp.float32)


def call(kernel, name, in_specs, out_specs, out_shape, scratch, flops):
    return pl.pallas_call(
        kernel,
        in_specs=[IN_SMEM, *in_specs],
        out_specs=out_specs,
        scratch_shapes=scratch,
        out_shape=out_shape,
        compiler_params=pltpu.CompilerParams(vmem_limit_bytes=VMEM_BYTES),
        cost_estimate=pl.CostEstimate(flops=flops, bytes_accessed=1 << 23, transcendentals=0),
        name=name,
    )


def forward_second_kernel(place, field_in, initial_in, tables, sums, *refs):
    sends, refs = refs[:CHUNKS], refs[CHUNKS:]
    field, initial, table, sems, table_sem, *scratch = refs
    cells, steps, width = field.shape
    half = width // 2
    part = half // CHUNKS
    pieces = sems.shape[0]
    piece = cells // pieces
    rows = piece * len(scratch)
    blocks = cells // rows
    group = max(TILE // steps, 1)
    pitch = sends[0].shape[0] // (steps + 1)
    body = piece * steps
    is_first = place[0] == 0
    sign = 1.0 - 2.0 * place[1].astype(jnp.float32)

    def copies(at):
        here = pl.ds(at * piece, piece)
        return [
            pltpu.make_async_copy(source.at[here], to.at[here], sems.at[at, which])
            for which, (source, to) in enumerate(((field_in, field), (initial_in, initial)))
        ]

    table_copy = pltpu.make_async_copy(tables.at[1 - place[1]], table, table_sem)
    for at in range(pieces):
        for copy in copies(at):
            copy.start()
        if at == 0:
            table_copy.start()

    def put(other, at, sums_at, cells):
        lower = cells[:, :half]
        upper = sign * jnp.concatenate(
            [lanes_reversed(cells[:, lane : lane + LANES]) for lane in range(half, width, LANES)][::-1],
            axis=1,
        )
        sums[pl.ds(sums_at, TILE), :] = lower + upper
        store_split(other, (pl.ds(at, TILE),), 0, lower - upper)

    def prepare(sub, block):
        kept_at = pl.multiple_of(block * rows + sub * piece, piece)
        kept_base = pl.multiple_of(kept_at * steps, body)
        for row in range(0, piece, group):
            values = field[pl.ds(kept_at + row, group)]
            force = values - values * values * values
            put(scratch[sub], row * steps, kept_base + row * steps, force.reshape(TILE, width))
        for row in range(0, piece, TILE):
            at = pl.ds(pl.multiple_of(kept_at + row, TILE), TILE)
            ends = jnp.where(is_first, initial[at], field[at, steps - 1, :])
            put(scratch[sub], body + row, cells * steps + kept_at + row, ends)

    def transform(sub, block):
        sent = dot(scratch[sub][...], table[...])
        sent_at = pl.multiple_of(cells - block * rows - (sub + 1) * piece, piece)
        for chunk, send in enumerate(sends):
            lanes = slice(chunk * part, (chunk + 1) * part)
            for row in range(piece):
                line = sent[row * steps : (row + 1) * steps, lanes]
                send[pl.ds(sent_at + piece - 1 - row, steps, stride=pitch), :] = line
            store_rows_reversed(send, pitch * steps + sent_at, sent[body:, lanes])

    count = len(scratch)

    def piece_of(block, sub):
        for copy in copies(block * count + sub):
            copy.wait()
        if sub:
            transform(sub - 1, block)
        else:
            transform(count - 1, jnp.maximum(block - 1, 0))
        prepare(sub, block)

    table_copy.wait()

    @pl.loop(0, blocks)
    def _(block):
        for sub in range(count):
            piece_of(block, sub)

    transform(count - 1, blocks - 1)


def forward_second(place, field, initial, tables):
    rows, steps, width = field.shape
    half = width // 2
    piece, pieces = min(32, rows // 2), 2
    outs = call(
        forward_second_kernel,
        "forward_second",
        [IN_HBM] * 3,
        [IN_VMEM] * (1 + CHUNKS),
        [floats((steps + 1) * rows, half)]
        + [floats((steps + 1) * pitch_of(rows), half // CHUNKS)] * CHUNKS,
        [
            pltpu.VMEM(field.shape, jnp.float32),
            pltpu.VMEM(initial.shape, jnp.float32),
            pltpu.VMEM(tables.shape[1:], jnp.bfloat16),
            pltpu.SemaphoreType.DMA((rows // piece, 2)),
            pltpu.SemaphoreType.DMA,
        ]
        + [pltpu.VMEM(((steps + 1) * piece, 2 * half), jnp.bfloat16)] * pieces,
        1 << 32,
    )(place, in_hbm(field), in_hbm(initial), in_hbm(tables))
    return outs[0], outs[1:]


def keep_second_kernel(steps, place, tables, sums, *refs):
    keeps, scratch = refs[:CHUNKS], refs[CHUNKS:]
    depth = scratch[0].shape[0]
    cells = sums.shape[0] // (steps + 1)
    pitch = keeps[0].shape[0] // (steps + 1)
    for at in range(0, sums.shape[0], depth):
        split = scratch[at // depth % 2]
        for row in range(0, depth, TILE):
            store_split(split, (pl.ds(row, TILE),), 0, sums[pl.ds(at + row, TILE)])
        result = dot(split[...], tables[place[1]])
        for chunk, keep in enumerate(keeps):
            part = keep.shape[1]
            lanes = slice(chunk * part, (chunk + 1) * part)
            body = max(0, min(depth, cells * steps - at))
            for row in range(0, body, steps):
                line = result[row : row + steps, lanes]
                keep[pl.ds((at + row) // steps, steps, stride=pitch), :] = line
            if body < depth:
                ends = pl.ds(pitch * steps + at + body - cells * steps, depth - body)
                keep[ends, :] = result[body:, lanes]


def keep_second(place, sums, tables, steps):
    rows, half = sums.shape
    shape = ((steps + 1) * pitch_of(rows // (steps + 1)), half // CHUNKS)
    return call(
        functools.partial(keep_second_kernel, steps),
        "keep_second",
        [IN_VMEM] * 2,
        [IN_VMEM] * CHUNKS,
        [floats(*shape)] * CHUNKS,
        [pltpu.VMEM((rows // 8, 2 * half), jnp.bfloat16)] * 2,
        1 << 31,
    )(place, tables, sums)


def ranks(slabs):
    return slabs // 2


def forward_first_kernel(slabs, chunk, place, keep, got, table, decay, modes, *refs):
    size = ranks(slabs)
    lasts, (state, split, split_end, extra) = refs[:size], refs[size:]
    steps, _, part, rows = modes.shape
    pitch = keep.shape[0] // (steps + 1)
    block = split.shape[1] // part
    strip = place[1]
    near, far = keep[pl.ds(pitch * steps, rows)], got[pl.ds(pitch * steps, rows)]
    for c, cells in enumerate((near + far, near - far)):
        store_split(split_end, (c, slice(None)), 0, cells.T)
        extra[c] = dot(split_end[c], table[strip, c])
    is_first = jnp.where(place[0] == 0, 1.0 / REACTION_STEP, 0.0)
    is_last = jnp.where(place[0] == slabs - 1, 1.0 / REACTION_STEP, 0.0)
    state[...] = jnp.zeros_like(state)
    for step in range(0, steps, block):
        for c in (0, 1):
            for at in range(block):
                cells_at = pl.ds((step + at) * pitch, rows)
                near, far = keep[cells_at], got[cells_at]
                cells = near - far if c else near + far
                store_split(split, (c, pl.ds(at * part, part)), 0, cells.T)
            result = dot(split[c], table[strip, c])
            modes[pl.ds(step, block), c] = result.reshape(block, part, rows)
            if step == 0:
                modes[0, c] = result[:part] + is_first * extra[c]
        for c in (0, 1):
            for row in range(0, part, TILE):
                tile, at_state = pl.ds(row, TILE), pl.ds(c * part + row, TILE)
                value = state[at_state]
                rate = decay[strip, c, pl.ds(chunk * part + row, TILE)]
                for at in range(block):
                    value = rate * (value + modes[step + at, c, tile])
                state[at_state] = value
    for c in (0, 1):
        at_state = pl.ds(c * part, part)
        state[at_state] = state[at_state] - is_last * extra[c]
    rank = lax.rem(place[0], size)
    share = 2 * part // size
    for partner in range(size):
        at = pl.multiple_of((rank ^ partner) * share, share)
        lasts[partner][...] = state[pl.ds(at, share)]


def forward_first(place, chunk, keep, got, tables, decays, slabs):
    rows, part = tables.shape[-1], keep.shape[1]
    steps = keep.shape[0] // pitch_of(rows) - 1
    block = min(8, steps)
    size = ranks(slabs)
    share = 2 * part // size
    outs = call(
        functools.partial(forward_first_kernel, slabs, chunk),
        "forward_first",
        [IN_VMEM] * 4,
        [IN_VMEM] * (1 + size),
        [floats(steps, 2, part, rows)] + [floats(share, rows)] * size,
        [
            pltpu.VMEM((2 * part, rows), jnp.float32),
            pltpu.VMEM((2, block * part, 2 * rows), jnp.bfloat16),
            pltpu.VMEM((2, part, 2 * rows), jnp.bfloat16),
            pltpu.VMEM((2, part, rows), jnp.float32),
        ],
        1 << 31,
    )(place, keep, got, tables, decays)
    return outs[0], outs[1:]


def half_sum_kernel(slabs, chunk, place, closing, *refs):
    size = ranks(slabs)
    lasts, ordered, total = refs[:size], refs[size], refs[size + 1]
    share = total.shape[0]
    rank = lax.rem(place[0], size)
    decay = closing[place[1], chunk, 0, pl.ds(pl.multiple_of(rank * share, share), share)]
    for partner in range(size):
        ordered[rank ^ partner] = lasts[partner][...]
    state = ordered[0]
    for at in range(1, size):
        state = ordered[at] + decay * state
    total[...] = state


def half_sum(place, chunk, lasts, closing, slabs):
    size = ranks(slabs)
    share, rows = lasts[0].shape
    return call(
        functools.partial(half_sum_kernel, slabs, chunk),
        "half_sum",
        [IN_VMEM] * (1 + size),
        [IN_VMEM] * 2,
        [floats(size, share, rows), floats(share, rows)],
        [],
        1 << 20,
    )(place, closing, *lasts)


def close_kernel(slabs, chunk, place, closing, ordered, near, far, *refs):
    size = ranks(slabs)
    befores, states = refs[:size], refs[size]
    share = near.shape[0]
    rank = lax.rem(place[0], size)
    at_share = pl.ds(pl.multiple_of(rank * share, share), share)
    decay, half_decay, gain = (closing[place[1], chunk, at, at_share] for at in range(3))
    entering = jnp.where(place[0] < size, circulant_alpha, 1.0)
    state = gain * (entering * far[...] + circulant_alpha * half_decay * near[...])
    for at in range(size):
        states[at] = state
        if at < size - 1:
            state = ordered[at] + decay * state
    for partner in range(size):
        befores[partner][...] = states[rank ^ partner]


def close(place, chunk, ordered, near, far, closing, slabs):
    size, share, rows = ordered.shape
    return call(
        functools.partial(close_kernel, slabs, chunk),
        "close",
        [IN_VMEM] * 4,
        [IN_VMEM] * size,
        [floats(share, rows)] * size,
        [pltpu.VMEM((size, share, rows), jnp.float32)],
        1 << 20,
    )(place, closing, ordered, near, far)


def inverse_first_kernel(slabs, chunk, place, modes, table, decay, *refs):
    size = ranks(slabs)
    befores, (keep, send, state, split) = refs[:size], refs[size:]
    steps, _, part, rows = modes.shape
    pitch = keep.shape[0] // steps
    block = split.shape[1] // part
    strip = place[1]
    rank = lax.rem(place[0], size)
    share = 2 * part // size
    for partner in range(size):
        at = pl.multiple_of((rank ^ partner) * share, share)
        state[pl.ds(at, share)] = befores[partner][...]
    for step in range(0, steps, block):
        results = []
        for c in (0, 1):
            for row in range(0, part, TILE):
                tile, at_state = pl.ds(row, TILE), pl.ds(c * part + row, TILE)
                value = state[at_state]
                rate = decay[strip, c, pl.ds(chunk * part + row, TILE)]
                for at in range(block):
                    value = rate * (value + modes[step + at, c, tile])
                    store_split(split, (c, pl.ds(at * part + row, TILE)), 0, value)
                state[at_state] = value
            results.append(dot(split[c], table[strip, c]))
        even, odd = results
        for at in range(block):
            piece = slice(at * part, (at + 1) * part)
            cells_at = pl.ds((step + at) * pitch, rows)
            keep[cells_at, :] = (even[piece] + odd[piece]).T
            send[cells_at, :] = (even[piece] - odd[piece]).T


def inverse_first(place, chunk, modes, befores, tables, decays, slabs):
    steps, _, part, rows = modes.shape
    block = min(8, steps)
    return call(
        functools.partial(inverse_first_kernel, slabs, chunk),
        "inverse_first",
        [IN_VMEM] * (3 + len(befores)),
        [IN_VMEM] * 2,
        [floats(steps * pitch_of(rows), part)] * 2,
        [
            pltpu.VMEM((2 * part, rows), jnp.float32),
            pltpu.VMEM((2, block * part, 2 * rows), jnp.bfloat16),
        ],
        1 << 31,
    )(place, modes, tables, decays, *befores)


def keep_inverse_kernel(steps, place, tables, *refs):
    keeps, out, scratch = refs[:CHUNKS], refs[CHUNKS], refs[CHUNKS + 1 :]
    part = keeps[0].shape[1]
    pitch = keeps[0].shape[0] // steps
    depth = scratch[0].shape[0]
    group = max(TILE // steps, 1)
    for at in range(0, out.shape[0], depth):
        split = scratch[at // depth % 2]
        for row in range(0, depth, TILE):
            cell = (at + row) // steps
            for chunk, keep in enumerate(keeps):
                cells = steps_of(keep, range(cell, cell + group), steps, pitch)
                store_split(split, (pl.ds(row, TILE),), chunk * part, cells)
        out[pl.ds(at, depth)] = dot(split[...], tables[place[1]])


def keep_inverse(place, keeps, tables, rows, steps):
    half = keeps[0].shape[1] * CHUNKS
    return call(
        functools.partial(keep_inverse_kernel, steps),
        "keep_inverse",
        [IN_VMEM] * (1 + CHUNKS),
        IN_VMEM,
        floats(rows * steps, half),
        [pltpu.VMEM((rows * steps // 8, 2 * half), jnp.bfloat16)] * 2,
        1 << 31,
    )(place, tables, *keeps)


def inverse_second_kernel(place, tables, kept, *refs):
    gots, target, out, sems, scratch = (
        refs[:CHUNKS], refs[CHUNKS], refs[CHUNKS + 1], refs[CHUNKS + 2], refs[CHUNKS + 3 :]
    )
    cells, steps, width = out.shape
    half = width // 2
    part = half // CHUNKS
    pitch = gots[0].shape[0] // steps
    count = len(scratch) // 2
    pieces = sems.shape[0]
    piece = cells // pieces
    group = max(TILE // steps, 1)
    strip = place[1]
    sign = 1.0 - 2.0 * strip.astype(jnp.float32)

    def copy(at):
        here = pl.ds(at * piece, piece)
        return pltpu.make_async_copy(out.at[here], target.at[here], sems.at[at])

    @pl.loop(0, pieces, step=count)
    def _(first_piece):
        for sub in range(count):
            split, result = scratch[2 * sub : 2 * sub + 2]
            base = (first_piece + sub) * piece
            for row in range(0, piece, group):
                mirrors = [cells - 1 - base - row - at for at in range(group)]
                for chunk, got in enumerate(gots):
                    values = steps_of(got, mirrors, steps, pitch)
                    store_split(split, (pl.ds(row * steps, TILE),), chunk * part, values)
            result[...] = dot(split[...], tables[1 - strip])
        for sub in range(count):
            result = scratch[2 * sub + 1]
            base = pl.multiple_of((first_piece + sub) * piece, piece)
            kept_base = pl.multiple_of(base * steps, piece * steps)
            for row in range(0, piece, group):
                first = kept[pl.ds(kept_base + row * steps, TILE)]
                second = result[pl.ds(row * steps, TILE)]
                upper = sign * (first - second)
                parts = [
                    lanes_reversed(upper[:, lane : lane + LANES]) for lane in range(0, half, LANES)
                ][::-1]
                whole = jnp.concatenate([first + second, *parts], axis=1)
                out[pl.ds(base + row, group)] = whole.reshape(group, TILE // group, width)
            copy(first_piece + sub).start()

    for at in range(pieces):
        copy(at).wait()


def inverse_second(place, kept, gots, tables, steps):
    rows, half = kept.shape[0] // steps, kept.shape[1]
    piece, pieces = min(32, rows // 2), 2
    depth = steps * piece
    return call(
        inverse_second_kernel,
        "inverse_second",
        [IN_VMEM] * (2 + CHUNKS),
        IN_HBM,
        floats(rows, steps, 2 * half),
        [pltpu.VMEM((rows, steps, 2 * half), jnp.float32), pltpu.SemaphoreType.DMA((rows // piece,))]
        + [pltpu.VMEM((depth, 2 * half), jnp.bfloat16), pltpu.VMEM((depth, half), jnp.float32)]
        * pieces,
        1 << 32,
    )(place, tables, kept, *gots)


def swapped(block):
    return lax.ppermute(block, "space", [(0, 1), (1, 0)])


def with_partner(block, distance):
    slabs = lax.axis_size("tm")
    return lax.ppermute(block, "tm", [(slab, slab ^ distance) for slab in range(slabs)])


def among_ranks(blocks):
    return [blocks[0]] + [with_partner(block, at) for at, block in enumerate(blocks) if at]


def by_chunk(table):
    strips, _, half, rows = table.shape
    parts = table.reshape(strips, 2, CHUNKS, half // CHUNKS, rows)
    return np.swapaxes(parts, 1, 2).reshape(strips, CHUNKS, 2 * half // CHUNKS, rows)


def shards(iterate, initial):
    rows, steps, width = iterate.shape
    slabs = lax.axis_size("tm")
    total = rows * lax.axis_size("space")
    place = jnp.stack([lax.axis_index("tm"), lax.axis_index("space")]).astype(jnp.int32)
    second = second_tables(width)
    first = first_tables(total)
    decay = decay_tables(total, width)
    slab_decay = decay**steps
    half_decay = slab_decay ** ranks(slabs)
    gain = 1.0 / (1.0 - circulant_alpha * half_decay * half_decay)
    closing = constant(
        np.stack([by_chunk(table) for table in (slab_decay, half_decay, gain)], axis=2)
    )
    first_table, decays = split_constant(first), constant(decay)
    second_table = split_constant(REACTION_STEP * second)
    sums, sends = forward_second(place, iterate, initial, second_table)
    gots = [swapped(send) for send in sends]
    keeps = keep_second(place, sums, second_table, steps)
    modes, befores = [], []
    for chunk in range(CHUNKS):
        own_modes, lasts = forward_first(
            place, chunk, keeps[chunk], gots[chunk], first_table, decays, slabs
        )
        modes.append(own_modes)
        ordered, near = half_sum(place, chunk, among_ranks(lasts), closing, slabs)
        far = with_partner(near, ranks(slabs))
        befores.append(among_ranks(close(place, chunk, ordered, near, far, closing, slabs)))
    inverse_table = split_constant(np.swapaxes(first, 2, 3))
    keeps, sends = zip(
        *(
            inverse_first(place, chunk, modes[chunk], befores[chunk], inverse_table, decays, slabs)
            for chunk in range(CHUNKS)
        )
    )
    gots = [swapped(send) for send in sends]
    inverse_table = split_constant(np.swapaxes(second, 1, 2))
    kept = keep_inverse(place, keeps, inverse_table, rows, steps)
    return inverse_second(place, kept, gots, inverse_table, steps)


def solution(mesh):
    return jax.shard_map(
        shards,
        mesh=mesh,
        in_specs=(P(("group", "space"), "tm", None), P(("group", "space"), None)),
        out_specs=P(("group", "space"), "tm", None),
        check_vma=False,
    )
```

```python
import functools
import math

import jax
import jax.numpy as jnp
import numpy as np
from jax import lax
from jax.experimental import pallas as pl
from jax.experimental.pallas import tpu as pltpu
from jax.sharding import PartitionSpec as P

circulant_alpha = 0.01
DIFFUSION = 2.0
REACTION_STEP = 0.5
VMEM_BYTES = 24 * 1024 * 1024
LANES = 128
SUBLANES = 8
TILE = 16
CHUNKS = 2


def sine_table(row_index, column_index, length):
    product = np.outer(row_index + 1, column_index + 1) % (2 * (length + 1))
    return math.sqrt(2.0 / (length + 1)) * np.sin(product * (math.pi / (length + 1)))


def stencil_eigen(mode_index, length):
    return 4.0 * np.sin((mode_index + 1) * (math.pi / (2.0 * (length + 1)))) ** 2


def second_tables(width):
    half = width // 2
    return np.stack([sine_table(np.arange(half), np.arange(s, width, 2), width) for s in (0, 1)])


def first_tables(total):
    rows = total // 2
    return np.stack(
        [
            np.stack(
                [sine_table(s * rows + np.arange(rows), np.arange(c, total, 2), total) for c in (0, 1)]
            )
            for s in (0, 1)
        ]
    )


def decay_tables(total, width):
    first, second = stencil_eigen(np.arange(total), total), stencil_eigen(np.arange(width), width)
    decay = 1.0 / (1.0 + DIFFUSION * (second[:, None] + first[None, :]))
    return np.stack([np.stack([decay[s::2, c::2] for c in (0, 1)]) for s in (0, 1)])


def constant(table):
    return jnp.asarray(np.asarray(table, np.float32))


def split_constant(table):
    table = np.asarray(table, np.float32)
    high = table.astype(jnp.bfloat16)
    low = (table - high.astype(np.float32)).astype(jnp.bfloat16)
    return jnp.asarray(np.concatenate([high, high, low], axis=-2))


def store_split(ref, at, lane, block):
    depth = ref.shape[-1] // 2
    width = block.shape[-1]
    high = block.astype(jnp.bfloat16)
    low = (block - high.astype(jnp.float32)).astype(jnp.bfloat16)
    ref[(*at, pl.ds(lane, width))] = high
    ref[(*at, pl.ds(depth + lane, width))] = low


def dot(split, table):
    rows = jnp.concatenate([split, split[:, : split.shape[1] // 2]], axis=1)
    return jnp.dot(rows, table, preferred_element_type=jnp.float32)


def lanes_reversed(block):
    index = LANES - 1 - lax.broadcasted_iota(jnp.int32, (block.shape[0], LANES), 1)
    return jnp.take_along_axis(block, index, axis=1, mode="promise_in_bounds")


def store_rows_reversed(ref, start, block):
    rows, width = block.shape
    index = SUBLANES - 1 - lax.broadcasted_iota(jnp.int32, (SUBLANES, width), 0)
    for row in range(0, rows, SUBLANES):
        to = pl.multiple_of(start + rows - SUBLANES - row, SUBLANES)
        ref[pl.ds(to, SUBLANES), :] = jnp.take_along_axis(
            block[row : row + SUBLANES], index, axis=0, mode="promise_in_bounds"
        )


def pitch_of(cells):
    return cells + SUBLANES * (1 - cells // SUBLANES % 2)


def steps_of(ref, cells, steps, pitch):
    lines = [ref[pl.ds(cell, steps, stride=pitch), :] for cell in cells]
    return lines[0] if len(lines) == 1 else jnp.concatenate(lines, axis=0)


IN_VMEM = pl.BlockSpec(memory_space=pltpu.VMEM)
IN_HBM = pl.BlockSpec(memory_space=pltpu.HBM)
IN_SMEM = pl.BlockSpec(memory_space=pltpu.SMEM)


def in_hbm(array):
    return pltpu.with_memory_space_constraint(array, pltpu.HBM)


def floats(*shape):
    return jax.ShapeDtypeStruct(shape, jnp.float32)


def call(kernel, name, in_specs, out_specs, out_shape, scratch, flops):
    return pl.pallas_call(
        kernel,
        in_specs=[IN_SMEM, *in_specs],
        out_specs=out_specs,
        scratch_shapes=scratch,
        out_shape=out_shape,
        compiler_params=pltpu.CompilerParams(vmem_limit_bytes=VMEM_BYTES),
        cost_estimate=pl.CostEstimate(flops=flops, bytes_accessed=1 << 23, transcendentals=0),
        name=name,
    )


def forward_second_kernel(place, field_in, initial_in, tables, sums, *refs):
    sends, refs = refs[:CHUNKS], refs[CHUNKS:]
    field, initial, table, sems, table_sem, *scratch = refs
    cells, steps, width = field.shape
    half = width // 2
    part = half // CHUNKS
    pieces = sems.shape[0]
    piece = cells // pieces
    rows = piece * len(scratch)
    blocks = cells // rows
    group = max(TILE // steps, 1)
    pitch = sends[0].shape[0] // (steps + 1)
    body = piece * steps
    is_first = place[0] == 0
    sign = 1.0 - 2.0 * place[1].astype(jnp.float32)

    def copies(at):
        here = pl.ds(at * piece, piece)
        return [
            pltpu.make_async_copy(source.at[here], to.at[here], sems.at[at, which])
            for which, (source, to) in enumerate(((field_in, field), (initial_in, initial)))
        ]

    table_copy = pltpu.make_async_copy(tables.at[1 - place[1]], table, table_sem)
    for copy in copies(0):
        copy.start()
    table_copy.start()
    for copy in copies(1):
        copy.start()

    def put(other, at, sums_at, cells):
        lower = cells[:, :half]
        upper = sign * jnp.concatenate(
            [lanes_reversed(cells[:, lane : lane + LANES]) for lane in range(half, width, LANES)][::-1],
            axis=1,
        )
        sums[pl.ds(sums_at, TILE), :] = lower + upper
        store_split(other, (pl.ds(at, TILE),), 0, lower - upper)

    def prepare(sub, block):
        kept_at = pl.multiple_of(block * rows + sub * piece, piece)
        kept_base = pl.multiple_of(kept_at * steps, body)
        for row in range(0, piece, group):
            values = field[pl.ds(kept_at + row, group)]
            force = values - values * values * values
            put(scratch[sub], row * steps, kept_base + row * steps, force.reshape(TILE, width))
        for row in range(0, piece, TILE):
            at = pl.ds(pl.multiple_of(kept_at + row, TILE), TILE)
            ends = jnp.where(is_first, initial[at], field[at, steps - 1, :])
            put(scratch[sub], body + row, cells * steps + kept_at + row, ends)

    def transform(sub, block):
        sent = dot(scratch[sub][...], table[...])
        sent_at = pl.multiple_of(cells - block * rows - (sub + 1) * piece, piece)
        for chunk, send in enumerate(sends):
            lanes = slice(chunk * part, (chunk + 1) * part)
            for row in range(piece):
                line = sent[row * steps : (row + 1) * steps, lanes]
                send[pl.ds(sent_at + piece - 1 - row, steps, stride=pitch), :] = line
            store_rows_reversed(send, pitch * steps + sent_at, sent[body:, lanes])

    count = len(scratch)

    def piece_of(block, sub):
        at = block * count + sub
        for copy in copies(at):
            copy.wait()

        @pl.when(at + 2 < pieces)
        def _():
            for copy in copies(at + 2):
                copy.start()

        if sub:
            transform(sub - 1, block)
        else:
            transform(count - 1, jnp.maximum(block - 1, 0))
        prepare(sub, block)

    table_copy.wait()

    @pl.loop(0, blocks)
    def _(block):
        for sub in range(count):
            piece_of(block, sub)

    transform(count - 1, blocks - 1)


def forward_second(place, field, initial, tables):
    rows, steps, width = field.shape
    half = width // 2
    piece, pieces = min(32, rows // 2), 2
    outs = call(
        forward_second_kernel,
        "forward_second",
        [IN_HBM] * 3,
        [IN_VMEM] * (1 + CHUNKS),
        [floats((steps + 1) * rows, half)]
        + [floats((steps + 1) * pitch_of(rows), half // CHUNKS)] * CHUNKS,
        [
            pltpu.VMEM(field.shape, jnp.float32),
            pltpu.VMEM(initial.shape, jnp.float32),
            pltpu.VMEM(tables.shape[1:], jnp.bfloat16),
            pltpu.SemaphoreType.DMA((rows // piece, 2)),
            pltpu.SemaphoreType.DMA,
        ]
        + [pltpu.VMEM(((steps + 1) * piece, 2 * half), jnp.bfloat16)] * pieces,
        1 << 32,
    )(place, in_hbm(field), in_hbm(initial), in_hbm(tables))
    return outs[0], outs[1:]


def keep_second_kernel(steps, place, tables, sums, *refs):
    keeps, scratch = refs[:CHUNKS], refs[CHUNKS:]
    depth = scratch[0].shape[0]
    cells = sums.shape[0] // (steps + 1)
    pitch = keeps[0].shape[0] // (steps + 1)
    for at in range(0, sums.shape[0], depth):
        split = scratch[at // depth % 2]
        for row in range(0, depth, TILE):
            store_split(split, (pl.ds(row, TILE),), 0, sums[pl.ds(at + row, TILE)])
        result = dot(split[...], tables[place[1]])
        for chunk, keep in enumerate(keeps):
            part = keep.shape[1]
            lanes = slice(chunk * part, (chunk + 1) * part)
            body = max(0, min(depth, cells * steps - at))
            for row in range(0, body, steps):
                line = result[row : row + steps, lanes]
                keep[pl.ds((at + row) // steps, steps, stride=pitch), :] = line
            if body < depth:
                ends = pl.ds(pitch * steps + at + body - cells * steps, depth - body)
                keep[ends, :] = result[body:, lanes]


def keep_second(place, sums, tables, steps):
    rows, half = sums.shape
    shape = ((steps + 1) * pitch_of(rows // (steps + 1)), half // CHUNKS)
    return call(
        functools.partial(keep_second_kernel, steps),
        "keep_second",
        [IN_VMEM] * 2,
        [IN_VMEM] * CHUNKS,
        [floats(*shape)] * CHUNKS,
        [pltpu.VMEM((rows // 8, 2 * half), jnp.bfloat16)] * 2,
        1 << 31,
    )(place, tables, sums)


def ranks(slabs):
    return slabs // 2


def forward_first_kernel(slabs, chunk, place, keep, got, table, decay, modes, *refs):
    size = ranks(slabs)
    lasts, (state, split, split_end, extra) = refs[:size], refs[size:]
    steps, _, part, rows = modes.shape
    pitch = keep.shape[0] // (steps + 1)
    block = split.shape[1] // part
    strip = place[1]
    near, far = keep[pl.ds(pitch * steps, rows)], got[pl.ds(pitch * steps, rows)]
    for c, cells in enumerate((near + far, near - far)):
        store_split(split_end, (c, slice(None)), 0, cells.T)
        extra[c] = dot(split_end[c], table[strip, c])
    is_first = jnp.where(place[0] == 0, 1.0 / REACTION_STEP, 0.0)
    is_last = jnp.where(place[0] == slabs - 1, 1.0 / REACTION_STEP, 0.0)
    state[...] = jnp.zeros_like(state)
    for step in range(0, steps, block):
        for c in (0, 1):
            for at in range(block):
                cells_at = pl.ds((step + at) * pitch, rows)
                near, far = keep[cells_at], got[cells_at]
                cells = near - far if c else near + far
                store_split(split, (c, pl.ds(at * part, part)), 0, cells.T)
            result = dot(split[c], table[strip, c])
            modes[pl.ds(step, block), c] = result.reshape(block, part, rows)
            if step == 0:
                modes[0, c] = result[:part] + is_first * extra[c]
        for c in (0, 1):
            for row in range(0, part, TILE):
                tile, at_state = pl.ds(row, TILE), pl.ds(c * part + row, TILE)
                value = state[at_state]
                rate = decay[strip, c, pl.ds(chunk * part + row, TILE)]
                for at in range(block):
                    value = rate * (value + modes[step + at, c, tile])
                state[at_state] = value
    for c in (0, 1):
        at_state = pl.ds(c * part, part)
        state[at_state] = state[at_state] - is_last * extra[c]
    rank = lax.rem(place[0], size)
    share = 2 * part // size
    for partner in range(size):
        at = pl.multiple_of((rank ^ partner) * share, share)
        lasts[partner][...] = state[pl.ds(at, share)]


def forward_first(place, chunk, keep, got, tables, decays, slabs):
    rows, part = tables.shape[-1], keep.shape[1]
    steps = keep.shape[0] // pitch_of(rows) - 1
    block = min(8, steps)
    size = ranks(slabs)
    share = 2 * part // size
    outs = call(
        functools.partial(forward_first_kernel, slabs, chunk),
        "forward_first",
        [IN_VMEM] * 4,
        [IN_VMEM] * (1 + size),
        [floats(steps, 2, part, rows)] + [floats(share, rows)] * size,
        [
            pltpu.VMEM((2 * part, rows), jnp.float32),
            pltpu.VMEM((2, block * part, 2 * rows), jnp.bfloat16),
            pltpu.VMEM((2, part, 2 * rows), jnp.bfloat16),
            pltpu.VMEM((2, part, rows), jnp.float32),
        ],
        1 << 31,
    )(place, keep, got, tables, decays)
    return outs[0], outs[1:]


def half_sum_kernel(slabs, chunk, place, closing, *refs):
    size = ranks(slabs)
    lasts, ordered, total = refs[:size], refs[size], refs[size + 1]
    share = total.shape[0]
    rank = lax.rem(place[0], size)
    decay = closing[place[1], chunk, 0, pl.ds(pl.multiple_of(rank * share, share), share)]
    for partner in range(size):
        ordered[rank ^ partner] = lasts[partner][...]
    state = ordered[0]
    for at in range(1, size):
        state = ordered[at] + decay * state
    total[...] = state


def half_sum(place, chunk, lasts, closing, slabs):
    size = ranks(slabs)
    share, rows = lasts[0].shape
    return call(
        functools.partial(half_sum_kernel, slabs, chunk),
        "half_sum",
        [IN_VMEM] * (1 + size),
        [IN_VMEM] * 2,
        [floats(size, share, rows), floats(share, rows)],
        [],
        1 << 20,
    )(place, closing, *lasts)


def close_kernel(slabs, chunk, place, closing, ordered, near, far, *refs):
    size = ranks(slabs)
    befores, states = refs[:size], refs[size]
    share = near.shape[0]
    rank = lax.rem(place[0], size)
    at_share = pl.ds(pl.multiple_of(rank * share, share), share)
    decay, half_decay, gain = (closing[place[1], chunk, at, at_share] for at in range(3))
    entering = jnp.where(place[0] < size, circulant_alpha, 1.0)
    state = gain * (entering * far[...] + circulant_alpha * half_decay * near[...])
    for at in range(size):
        states[at] = state
        if at < size - 1:
            state = ordered[at] + decay * state
    for partner in range(size):
        befores[partner][...] = states[rank ^ partner]


def close(place, chunk, ordered, near, far, closing, slabs):
    size, share, rows = ordered.shape
    return call(
        functools.partial(close_kernel, slabs, chunk),
        "close",
        [IN_VMEM] * 4,
        [IN_VMEM] * size,
        [floats(share, rows)] * size,
        [pltpu.VMEM((size, share, rows), jnp.float32)],
        1 << 20,
    )(place, closing, ordered, near, far)


def inverse_first_kernel(slabs, chunk, place, modes, table, decay, *refs):
    size = ranks(slabs)
    befores, (keep, send, state, split) = refs[:size], refs[size:]
    steps, _, part, rows = modes.shape
    pitch = keep.shape[0] // steps
    block = split.shape[1] // part
    strip = place[1]
    rank = lax.rem(place[0], size)
    share = 2 * part // size
    for partner in range(size):
        at = pl.multiple_of((rank ^ partner) * share, share)
        state[pl.ds(at, share)] = befores[partner][...]
    for step in range(0, steps, block):
        results = []
        for c in (0, 1):
            for row in range(0, part, TILE):
                tile, at_state = pl.ds(row, TILE), pl.ds(c * part + row, TILE)
                value = state[at_state]
                rate = decay[strip, c, pl.ds(chunk * part + row, TILE)]
                for at in range(block):
                    value = rate * (value + modes[step + at, c, tile])
                    store_split(split, (c, pl.ds(at * part + row, TILE)), 0, value)
                state[at_state] = value
            results.append(dot(split[c], table[strip, c]))
        even, odd = results
        for at in range(block):
            piece = slice(at * part, (at + 1) * part)
            cells_at = pl.ds((step + at) * pitch, rows)
            keep[cells_at, :] = (even[piece] + odd[piece]).T
            send[cells_at, :] = (even[piece] - odd[piece]).T


def inverse_first(place, chunk, modes, befores, tables, decays, slabs):
    steps, _, part, rows = modes.shape
    block = min(8, steps)
    return call(
        functools.partial(inverse_first_kernel, slabs, chunk),
        "inverse_first",
        [IN_VMEM] * (3 + len(befores)),
        [IN_VMEM] * 2,
        [floats(steps * pitch_of(rows), part)] * 2,
        [
            pltpu.VMEM((2 * part, rows), jnp.float32),
            pltpu.VMEM((2, block * part, 2 * rows), jnp.bfloat16),
        ],
        1 << 31,
    )(place, modes, tables, decays, *befores)


def keep_inverse_kernel(steps, place, tables, *refs):
    keeps, out, scratch = refs[:CHUNKS], refs[CHUNKS], refs[CHUNKS + 1 :]
    part = keeps[0].shape[1]
    pitch = keeps[0].shape[0] // steps
    depth = scratch[0].shape[0]
    group = max(TILE // steps, 1)
    for at in range(0, out.shape[0], depth):
        split = scratch[at // depth % 2]
        for row in range(0, depth, TILE):
            cell = (at + row) // steps
            for chunk, keep in enumerate(keeps):
                cells = steps_of(keep, range(cell, cell + group), steps, pitch)
                store_split(split, (pl.ds(row, TILE),), chunk * part, cells)
        out[pl.ds(at, depth)] = dot(split[...], tables[place[1]])


def keep_inverse(place, keeps, tables, rows, steps):
    half = keeps[0].shape[1] * CHUNKS
    return call(
        functools.partial(keep_inverse_kernel, steps),
        "keep_inverse",
        [IN_VMEM] * (1 + CHUNKS),
        IN_VMEM,
        floats(rows * steps, half),
        [pltpu.VMEM((rows * steps // 8, 2 * half), jnp.bfloat16)] * 2,
        1 << 31,
    )(place, tables, *keeps)


def inverse_second_kernel(place, tables, kept, *refs):
    gots, target, out, sems, scratch = (
        refs[:CHUNKS], refs[CHUNKS], refs[CHUNKS + 1], refs[CHUNKS + 2], refs[CHUNKS + 3 :]
    )
    cells, steps, width = out.shape
    half = width // 2
    part = half // CHUNKS
    pitch = gots[0].shape[0] // steps
    count = len(scratch) // 2
    pieces = sems.shape[0]
    piece = cells // pieces
    group = max(TILE // steps, 1)
    strip = place[1]
    sign = 1.0 - 2.0 * strip.astype(jnp.float32)

    def copy(at):
        here = pl.ds(at * piece, piece)
        return pltpu.make_async_copy(out.at[here], target.at[here], sems.at[at])

    @pl.loop(0, pieces, step=count)
    def _(first_piece):
        for sub in range(count):
            split, result = scratch[2 * sub : 2 * sub + 2]
            base = (first_piece + sub) * piece
            for row in range(0, piece, group):
                mirrors = [cells - 1 - base - row - at for at in range(group)]
                for chunk, got in enumerate(gots):
                    values = steps_of(got, mirrors, steps, pitch)
                    store_split(split, (pl.ds(row * steps, TILE),), chunk * part, values)
            result[...] = dot(split[...], tables[1 - strip])
        for sub in range(count):
            result = scratch[2 * sub + 1]
            base = pl.multiple_of((first_piece + sub) * piece, piece)
            kept_base = pl.multiple_of(base * steps, piece * steps)
            for row in range(0, piece, group):
                first = kept[pl.ds(kept_base + row * steps, TILE)]
                second = result[pl.ds(row * steps, TILE)]
                upper = sign * (first - second)
                parts = [
                    lanes_reversed(upper[:, lane : lane + LANES]) for lane in range(0, half, LANES)
                ][::-1]
                whole = jnp.concatenate([first + second, *parts], axis=1)
                out[pl.ds(base + row, group)] = whole.reshape(group, TILE // group, width)
            copy(first_piece + sub).start()

    for at in range(pieces):
        copy(at).wait()


def inverse_second(place, kept, gots, tables, steps):
    rows, half = kept.shape[0] // steps, kept.shape[1]
    piece, pieces = min(32, rows // 2), 2
    depth = steps * piece
    return call(
        inverse_second_kernel,
        "inverse_second",
        [IN_VMEM] * (2 + CHUNKS),
        IN_HBM,
        floats(rows, steps, 2 * half),
        [pltpu.VMEM((rows, steps, 2 * half), jnp.float32), pltpu.SemaphoreType.DMA((rows // piece,))]
        + [pltpu.VMEM((depth, 2 * half), jnp.bfloat16), pltpu.VMEM((depth, half), jnp.float32)]
        * pieces,
        1 << 32,
    )(place, tables, kept, *gots)


def swapped(block):
    return lax.ppermute(block, "space", [(0, 1), (1, 0)])


def with_partner(block, distance):
    slabs = lax.axis_size("tm")
    return lax.ppermute(block, "tm", [(slab, slab ^ distance) for slab in range(slabs)])


def among_ranks(blocks):
    arrived = [with_partner(blocks[at], at) for at in range(len(blocks) - 1, 0, -1)]
    return [blocks[0]] + arrived[::-1]


def by_chunk(table):
    strips, _, half, rows = table.shape
    parts = table.reshape(strips, 2, CHUNKS, half // CHUNKS, rows)
    return np.swapaxes(parts, 1, 2).reshape(strips, CHUNKS, 2 * half // CHUNKS, rows)


def shards(iterate, initial):
    rows, steps, width = iterate.shape
    slabs = lax.axis_size("tm")
    total = rows * lax.axis_size("space")
    place = jnp.stack([lax.axis_index("tm"), lax.axis_index("space")]).astype(jnp.int32)
    second = second_tables(width)
    first = first_tables(total)
    decay = decay_tables(total, width)
    slab_decay = decay**steps
    half_decay = slab_decay ** ranks(slabs)
    gain = 1.0 / (1.0 - circulant_alpha * half_decay * half_decay)
    closing = constant(
        np.stack([by_chunk(table) for table in (slab_decay, half_decay, gain)], axis=2)
    )
    first_table, decays = split_constant(first), constant(decay)
    second_table = split_constant(REACTION_STEP * second)
    sums, sends = forward_second(place, iterate, initial, second_table)
    gots = [swapped(send) for send in sends]
    keeps = keep_second(place, sums, second_table, steps)
    modes, befores = [], []
    for chunk in range(CHUNKS):
        own_modes, lasts = forward_first(
            place, chunk, keeps[chunk], gots[chunk], first_table, decays, slabs
        )
        modes.append(own_modes)
        ordered, near = half_sum(place, chunk, among_ranks(lasts), closing, slabs)
        far = with_partner(near, ranks(slabs))
        befores.append(among_ranks(close(place, chunk, ordered, near, far, closing, slabs)))
    inverse_table = split_constant(np.swapaxes(first, 2, 3))
    keeps, sends = zip(
        *(
            inverse_first(place, chunk, modes[chunk], befores[chunk], inverse_table, decays, slabs)
            for chunk in range(CHUNKS)
        )
    )
    gots = [swapped(send) for send in sends]
    inverse_table = split_constant(np.swapaxes(second, 1, 2))
    kept = keep_inverse(place, keeps, inverse_table, rows, steps)
    return inverse_second(place, kept, gots, inverse_table, steps)


def solution(mesh):
    return jax.shard_map(
        shards,
        mesh=mesh,
        in_specs=(P(("group", "space"), "tm", None), P(("group", "space"), None)),
        out_specs=P(("group", "space"), "tm", None),
        check_vma=False,
    )
```

```python
import functools
import math

import jax
import jax.numpy as jnp
import numpy as np
from jax import lax
from jax.experimental import pallas as pl
from jax.experimental.pallas import tpu as pltpu
from jax.sharding import PartitionSpec as P

circulant_alpha = 0.01
DIFFUSION = 2.0
REACTION_STEP = 0.5
VMEM_BYTES = 24 * 1024 * 1024
SUBLANES = 8
TILE = 16
CHUNKS = 2


def sine_table(row_index, column_index, length):
    product = np.outer(row_index + 1, column_index + 1) % (2 * (length + 1))
    return math.sqrt(2.0 / (length + 1)) * np.sin(product * (math.pi / (length + 1)))


def stencil_eigen(mode_index, length):
    return 4.0 * np.sin((mode_index + 1) * (math.pi / (2.0 * (length + 1)))) ** 2


def second_tables(width):
    cells = np.arange(width)
    return np.stack([sine_table(cells, np.arange(s, width, 2), width) for s in (0, 1)])


def first_tables(total):
    rows = total // 2
    return np.stack(
        [
            np.stack(
                [sine_table(s * rows + np.arange(rows), np.arange(c, total, 2), total) for c in (0, 1)]
            )
            for s in (0, 1)
        ]
    )


def decay_tables(total, width):
    first, second = stencil_eigen(np.arange(total), total), stencil_eigen(np.arange(width), width)
    decay = 1.0 / (1.0 + DIFFUSION * (second[:, None] + first[None, :]))
    return np.stack([np.stack([decay[s::2, c::2] for c in (0, 1)]) for s in (0, 1)])


def constant(table):
    return jnp.asarray(np.asarray(table, np.float32))


def split_constant(table):
    table = np.asarray(table, np.float32)
    high = table.astype(jnp.bfloat16)
    low = (table - high.astype(np.float32)).astype(jnp.bfloat16)
    return jnp.asarray(np.concatenate([high, high, low], axis=-2))


def store_split(ref, at, lane, block):
    depth = ref.shape[-1] // 2
    width = block.shape[-1]
    high = block.astype(jnp.bfloat16)
    low = (block - high.astype(jnp.float32)).astype(jnp.bfloat16)
    ref[(*at, pl.ds(lane, width))] = high
    ref[(*at, pl.ds(depth + lane, width))] = low


def dot(split, table):
    rows = jnp.concatenate([split, split[:, : split.shape[1] // 2]], axis=1)
    return jnp.dot(rows, table, preferred_element_type=jnp.float32)


def store_rows_reversed(ref, start, block):
    rows, width = block.shape
    index = SUBLANES - 1 - lax.broadcasted_iota(jnp.int32, (SUBLANES, width), 0)
    for row in range(0, rows, SUBLANES):
        to = pl.multiple_of(start + rows - SUBLANES - row, SUBLANES)
        ref[pl.ds(to, SUBLANES), :] = jnp.take_along_axis(
            block[row : row + SUBLANES], index, axis=0, mode="promise_in_bounds"
        )


def pitch_of(cells):
    return cells + SUBLANES * (1 - cells // SUBLANES % 2)


def steps_of(ref, cells, steps, pitch):
    lines = [ref[pl.ds(cell, steps, stride=pitch), :] for cell in cells]
    return lines[0] if len(lines) == 1 else jnp.concatenate(lines, axis=0)


IN_VMEM = pl.BlockSpec(memory_space=pltpu.VMEM)
IN_SMEM = pl.BlockSpec(memory_space=pltpu.SMEM)


def in_hbm(array):
    return pltpu.with_memory_space_constraint(array, pltpu.HBM)


def floats(*shape):
    return jax.ShapeDtypeStruct(shape, jnp.float32)


def call(kernel, name, in_specs, out_specs, out_shape, scratch, flops, grid=None):
    if grid is None:
        spec = pl.GridSpec(
            in_specs=[IN_SMEM, *in_specs], out_specs=out_specs, scratch_shapes=scratch
        )
    else:
        spec = pltpu.PrefetchScalarGridSpec(
            num_scalar_prefetch=1,
            grid=(grid,),
            in_specs=in_specs,
            out_specs=out_specs,
            scratch_shapes=scratch,
        )
    return pl.pallas_call(
        kernel,
        grid_spec=spec,
        out_shape=out_shape,
        compiler_params=pltpu.CompilerParams(vmem_limit_bytes=VMEM_BYTES),
        cost_estimate=pl.CostEstimate(flops=flops, bytes_accessed=1 << 23, transcendentals=0),
        name=name,
    )


def forward_second_kernel(place, field, initial, table, split, *sends):
    rows, steps, width = field.shape
    part = width // 2 // CHUNKS
    piece = rows // 2
    group = max(TILE // steps, 1)
    block, blocks = pl.program_id(0), pl.num_programs(0)
    total = rows * blocks
    pitch = sends[0].shape[0] // (steps + 1)
    body = piece * steps
    is_first = place[0] == 0

    def send_ends():
        sent = dot(split[pl.ds(total * steps, total)], table[0])
        for chunk, send in enumerate(sends):
            lanes = slice(chunk * part, (chunk + 1) * part)
            store_rows_reversed(send, pitch * steps, sent[:, lanes])

    for sub in range(2):
        cell = pl.multiple_of(block * rows + sub * piece, piece)
        start = pl.multiple_of(cell * steps, body)
        for row in range(0, piece, group):
            cells = field[pl.ds(sub * piece + row, group)]
            force = cells - cells * cells * cells
            store_split(split, (pl.ds(start + row * steps, TILE),), 0, force.reshape(TILE, width))
        for row in range(0, piece, TILE):
            at = pl.ds(sub * piece + row, TILE)
            ends = jnp.where(is_first, initial[at], field[at, steps - 1, :])
            store_split(split, (pl.ds(total * steps + cell + row, TILE),), 0, ends)
        sent = dot(split[pl.ds(start, body)], table[0])
        for chunk, send in enumerate(sends):
            lanes = slice(chunk * part, (chunk + 1) * part)
            for row in range(piece):
                line = sent[row * steps : (row + 1) * steps, lanes]
                send[pl.ds(total - 1 - cell - row, steps, stride=pitch), :] = line

    pl.when(block == blocks - 1)(send_ends)


def forward_second(place, field, initial, tables):
    rows, steps, width = field.shape
    half = width // 2
    block = min(64, rows)
    outs = call(
        forward_second_kernel,
        "forward_second",
        [
            pl.BlockSpec((block, steps, width), lambda i, place: (i, 0, 0)),
            pl.BlockSpec((block, width), lambda i, place: (i, 0)),
            pl.BlockSpec((1, 3 * width, half), lambda i, place: (1 - place[1], 0, 0)),
        ],
        [IN_VMEM] * (1 + CHUNKS),
        [jax.ShapeDtypeStruct(((steps + 1) * rows, 2 * width), jnp.bfloat16)]
        + [floats((steps + 1) * pitch_of(rows), half // CHUNKS)] * CHUNKS,
        [],
        1 << 32,
        rows // block,
    )(place, in_hbm(field), in_hbm(initial), in_hbm(tables))
    return outs[0], outs[1:]


def keep_second_kernel(steps, place, tables, split, *keeps):
    rows = split.shape[0]
    depth = rows // 8
    cells = rows // (steps + 1)
    pitch = keeps[0].shape[0] // (steps + 1)
    for at in range(0, rows, depth):
        result = dot(split[pl.ds(at, depth)], tables[place[1]])
        for chunk, keep in enumerate(keeps):
            part = keep.shape[1]
            lanes = slice(chunk * part, (chunk + 1) * part)
            body = max(0, min(depth, cells * steps - at))
            for row in range(0, body, steps):
                line = result[row : row + steps, lanes]
                keep[pl.ds((at + row) // steps, steps, stride=pitch), :] = line
            if body < depth:
                ends = pl.ds(pitch * steps + at + body - cells * steps, depth - body)
                keep[ends, :] = result[body:, lanes]


def keep_second(place, split, tables, steps):
    rows = split.shape[0]
    shape = ((steps + 1) * pitch_of(rows // (steps + 1)), tables.shape[2] // CHUNKS)
    return call(
        functools.partial(keep_second_kernel, steps),
        "keep_second",
        [IN_VMEM] * 2,
        [IN_VMEM] * CHUNKS,
        [floats(*shape)] * CHUNKS,
        [],
        1 << 31,
    )(place, tables, split)


def ranks(slabs):
    return slabs // 2


def forward_first_kernel(slabs, chunk, place, keep, got, table, decay, modes, *refs):
    size = ranks(slabs)
    lasts, (state, split, split_end, extra) = refs[:size], refs[size:]
    steps, _, part, rows = modes.shape
    pitch = keep.shape[0] // (steps + 1)
    block = split.shape[1] // part
    strip = place[1]
    near, far = keep[pl.ds(pitch * steps, rows)], got[pl.ds(pitch * steps, rows)]
    for c, cells in enumerate((near + far, near - far)):
        store_split(split_end, (c, slice(None)), 0, cells.T)
        extra[c] = dot(split_end[c], table[strip, c])
    is_first = jnp.where(place[0] == 0, 1.0 / REACTION_STEP, 0.0)
    is_last = jnp.where(place[0] == slabs - 1, 1.0 / REACTION_STEP, 0.0)
    state[...] = jnp.zeros_like(state)
    for step in range(0, steps, block):
        for c in (0, 1):
            for at in range(block):
                cells_at = pl.ds((step + at) * pitch, rows)
                near, far = keep[cells_at], got[cells_at]
                cells = near - far if c else near + far
                store_split(split, (c, pl.ds(at * part, part)), 0, cells.T)
            result = dot(split[c], table[strip, c])
            modes[pl.ds(step, block), c] = result.reshape(block, part, rows)
            if step == 0:
                modes[0, c] = result[:part] + is_first * extra[c]
        for c in (0, 1):
            for row in range(0, part, TILE):
                tile, at_state = pl.ds(row, TILE), pl.ds(c * part + row, TILE)
                value = state[at_state]
                rate = decay[strip, c, pl.ds(chunk * part + row, TILE)]
                for at in range(block):
                    value = rate * (value + modes[step + at, c, tile])
                state[at_state] = value
    for c in (0, 1):
        at_state = pl.ds(c * part, part)
        state[at_state] = state[at_state] - is_last * extra[c]
    rank = lax.rem(place[0], size)
    share = 2 * part // size
    for partner in range(size):
        at = pl.multiple_of((rank ^ partner) * share, share)
        lasts[partner][...] = state[pl.ds(at, share)]


def forward_first(place, chunk, keep, got, tables, decays, slabs):
    rows, part = tables.shape[-1], keep.shape[1]
    steps = keep.shape[0] // pitch_of(rows) - 1
    block = min(8, steps)
    size = ranks(slabs)
    share = 2 * part // size
    outs = call(
        functools.partial(forward_first_kernel, slabs, chunk),
        "forward_first",
        [IN_VMEM] * 4,
        [IN_VMEM] * (1 + size),
        [floats(steps, 2, part, rows)] + [floats(share, rows)] * size,
        [
            pltpu.VMEM((2 * part, rows), jnp.float32),
            pltpu.VMEM((2, block * part, 2 * rows), jnp.bfloat16),
            pltpu.VMEM((2, part, 2 * rows), jnp.bfloat16),
            pltpu.VMEM((2, part, rows), jnp.float32),
        ],
        1 << 31,
    )(place, keep, got, tables, decays)
    return outs[0], outs[1:]


def half_sum_kernel(slabs, chunk, place, closing, *refs):
    size = ranks(slabs)
    lasts, ordered, total = refs[:size], refs[size], refs[size + 1]
    share = total.shape[0]
    rank = lax.rem(place[0], size)
    decay = closing[place[1], chunk, 0, pl.ds(pl.multiple_of(rank * share, share), share)]
    for partner in range(size):
        ordered[rank ^ partner] = lasts[partner][...]
    state = ordered[0]
    for at in range(1, size):
        state = ordered[at] + decay * state
    total[...] = state


def half_sum(place, chunk, lasts, closing, slabs):
    size = ranks(slabs)
    share, rows = lasts[0].shape
    return call(
        functools.partial(half_sum_kernel, slabs, chunk),
        "half_sum",
        [IN_VMEM] * (1 + size),
        [IN_VMEM] * 2,
        [floats(size, share, rows), floats(share, rows)],
        [],
        1 << 20,
    )(place, closing, *lasts)


def close_kernel(slabs, chunk, place, closing, ordered, near, far, *refs):
    size = ranks(slabs)
    befores, states = refs[:size], refs[size]
    share = near.shape[0]
    rank = lax.rem(place[0], size)
    at_share = pl.ds(pl.multiple_of(rank * share, share), share)
    decay, half_decay, gain = (closing[place[1], chunk, at, at_share] for at in range(3))
    entering = jnp.where(place[0] < size, circulant_alpha, 1.0)
    state = gain * (entering * far[...] + circulant_alpha * half_decay * near[...])
    for at in range(size):
        states[at] = state
        if at < size - 1:
            state = ordered[at] + decay * state
    for partner in range(size):
        befores[partner][...] = states[rank ^ partner]


def close(place, chunk, ordered, near, far, closing, slabs):
    size, share, rows = ordered.shape
    return call(
        functools.partial(close_kernel, slabs, chunk),
        "close",
        [IN_VMEM] * 4,
        [IN_VMEM] * size,
        [floats(share, rows)] * size,
        [pltpu.VMEM((size, share, rows), jnp.float32)],
        1 << 20,
    )(place, closing, ordered, near, far)


def inverse_first_kernel(slabs, chunk, place, modes, table, decay, *refs):
    size = ranks(slabs)
    befores, (keep, send, state, split) = refs[:size], refs[size:]
    steps, _, part, rows = modes.shape
    pitch = keep.shape[0] // steps
    block = split.shape[1] // part
    strip = place[1]
    rank = lax.rem(place[0], size)
    share = 2 * part // size
    for partner in range(size):
        at = pl.multiple_of((rank ^ partner) * share, share)
        state[pl.ds(at, share)] = befores[partner][...]
    for step in range(0, steps, block):
        results = []
        for c in (0, 1):
            for row in range(0, part, TILE):
                tile, at_state = pl.ds(row, TILE), pl.ds(c * part + row, TILE)
                value = state[at_state]
                rate = decay[strip, c, pl.ds(chunk * part + row, TILE)]
                for at in range(block):
                    value = rate * (value + modes[step + at, c, tile])
                    store_split(split, (c, pl.ds(at * part + row, TILE)), 0, value)
                state[at_state] = value
            results.append(dot(split[c], table[strip, c]))
        even, odd = results
        for at in range(block):
            piece = slice(at * part, (at + 1) * part)
            cells_at = pl.ds((step + at) * pitch, rows)
            keep[cells_at, :] = (even[piece] + odd[piece]).T
            send[cells_at, :] = (even[piece] - odd[piece]).T


def inverse_first(place, chunk, modes, befores, tables, decays, slabs):
    steps, _, part, rows = modes.shape
    block = min(8, steps)
    return call(
        functools.partial(inverse_first_kernel, slabs, chunk),
        "inverse_first",
        [IN_VMEM] * (3 + len(befores)),
        [IN_VMEM] * 2,
        [floats(steps * pitch_of(rows), part)] * 2,
        [
            pltpu.VMEM((2 * part, rows), jnp.float32),
            pltpu.VMEM((2, block * part, 2 * rows), jnp.bfloat16),
        ],
        1 << 31,
    )(place, modes, tables, decays, *befores)


def keep_inverse_kernel(steps, place, tables, *refs):
    keeps, out, scratch = refs[:CHUNKS], refs[CHUNKS], refs[CHUNKS + 1 :]
    part = keeps[0].shape[1]
    pitch = keeps[0].shape[0] // steps
    depth = scratch[0].shape[0]
    group = max(TILE // steps, 1)
    for at in range(0, out.shape[0], depth):
        split = scratch[at // depth % 2]
        for row in range(0, depth, TILE):
            cell = (at + row) // steps
            for chunk, keep in enumerate(keeps):
                cells = steps_of(keep, range(cell, cell + group), steps, pitch)
                store_split(split, (pl.ds(row, TILE),), chunk * part, cells)
        out[pl.ds(at, depth)] = dot(split[...], tables[place[1]])


def keep_inverse(place, keeps, tables, rows, steps):
    half = keeps[0].shape[1] * CHUNKS
    return call(
        functools.partial(keep_inverse_kernel, steps),
        "keep_inverse",
        [IN_VMEM] * (1 + CHUNKS),
        IN_VMEM,
        floats(rows * steps, 2 * half),
        [pltpu.VMEM((rows * steps // 8, 2 * half), jnp.bfloat16)] * 2,
        1 << 31,
    )(place, tables, *keeps)


def inverse_second_kernel(place, tables, kept, *refs):
    gots, out, scratch = refs[:CHUNKS], refs[CHUNKS], refs[CHUNKS + 1 :]
    rows, steps, width = out.shape
    part = width // 2 // CHUNKS
    pitch = gots[0].shape[0] // steps
    piece = rows // len(scratch)
    group = max(TILE // steps, 1)
    total = rows * pl.num_programs(0)
    start = pl.program_id(0) * rows
    for sub, split in enumerate(scratch):
        base = start + sub * piece
        for row in range(0, piece, group):
            mirrors = [total - 1 - base - row - at for at in range(group)]
            for chunk, got in enumerate(gots):
                cells = steps_of(got, mirrors, steps, pitch)
                store_split(split, (pl.ds(row * steps, TILE),), chunk * part, cells)
        kept_at = pl.ds(pl.multiple_of(base * steps, piece * steps), piece * steps)
        whole = kept[kept_at] + dot(split[...], tables[1 - place[1]])
        out[pl.ds(sub * piece, piece)] = whole.reshape(piece, steps, width)


def inverse_second(place, kept, gots, tables, steps):
    rows, width = kept.shape[0] // steps, kept.shape[1]
    block, pieces = min(64, rows), 2
    return call(
        inverse_second_kernel,
        "inverse_second",
        [IN_VMEM] * (2 + CHUNKS),
        pl.BlockSpec((block, steps, width), lambda i, place: (i, 0, 0)),
        floats(rows, steps, width),
        [pltpu.VMEM((steps * block // pieces, width), jnp.bfloat16)] * pieces,
        1 << 32,
        rows // block,
    )(place, tables, kept, *gots)


def swapped(block):
    return lax.ppermute(block, "space", [(0, 1), (1, 0)])


def with_partner(block, distance):
    slabs = lax.axis_size("tm")
    return lax.ppermute(block, "tm", [(slab, slab ^ distance) for slab in range(slabs)])


def among_ranks(blocks):
    return [blocks[0]] + [with_partner(block, at) for at, block in enumerate(blocks) if at]


def by_chunk(table):
    strips, _, half, rows = table.shape
    parts = table.reshape(strips, 2, CHUNKS, half // CHUNKS, rows)
    return np.swapaxes(parts, 1, 2).reshape(strips, CHUNKS, 2 * half // CHUNKS, rows)


def shards(iterate, initial):
    rows, steps, width = iterate.shape
    slabs = lax.axis_size("tm")
    total = rows * lax.axis_size("space")
    place = jnp.stack([lax.axis_index("tm"), lax.axis_index("space")]).astype(jnp.int32)
    second = second_tables(width)
    first = first_tables(total)
    decay = decay_tables(total, width)
    slab_decay = decay**steps
    half_decay = slab_decay ** ranks(slabs)
    gain = 1.0 / (1.0 - circulant_alpha * half_decay * half_decay)
    closing = constant(
        np.stack([by_chunk(table) for table in (slab_decay, half_decay, gain)], axis=2)
    )
    first_table, decays = split_constant(first), constant(decay)
    second_table = split_constant(REACTION_STEP * second)
    split, sends = forward_second(place, iterate, initial, second_table)
    gots = [swapped(send) for send in sends]
    keeps = keep_second(place, split, second_table, steps)
    modes, befores = [], []
    for chunk in range(CHUNKS):
        own_modes, lasts = forward_first(
            place, chunk, keeps[chunk], gots[chunk], first_table, decays, slabs
        )
        modes.append(own_modes)
        ordered, near = half_sum(place, chunk, among_ranks(lasts), closing, slabs)
        far = with_partner(near, ranks(slabs))
        befores.append(among_ranks(close(place, chunk, ordered, near, far, closing, slabs)))
    inverse_table = split_constant(np.swapaxes(first, 2, 3))
    keeps, sends = zip(
        *(
            inverse_first(place, chunk, modes[chunk], befores[chunk], inverse_table, decays, slabs)
            for chunk in range(CHUNKS)
        )
    )
    gots = [swapped(send) for send in sends]
    inverse_table = split_constant(np.swapaxes(second, 1, 2))
    kept = keep_inverse(place, keeps, inverse_table, rows, steps)
    return inverse_second(place, kept, gots, inverse_table, steps)


def solution(mesh):
    return jax.shard_map(
        shards,
        mesh=mesh,
        in_specs=(P(("group", "space"), "tm", None), P(("group", "space"), None)),
        out_specs=P(("group", "space"), "tm", None),
        check_vma=False,
    )
```

```python
import functools
import math

import jax
import jax.numpy as jnp
import numpy as np
from jax import lax
from jax.experimental import pallas as pl
from jax.experimental.pallas import tpu as pltpu
from jax.sharding import PartitionSpec as P

circulant_alpha = 0.01
DIFFUSION = 2.0
REACTION_STEP = 0.5
VMEM_BYTES = 24 * 1024 * 1024
LANES = 128
SUBLANES = 8
TILE = 16
CHUNKS = 2


def sine_table(row_index, column_index, length):
    product = np.outer(row_index + 1, column_index + 1) % (2 * (length + 1))
    return math.sqrt(2.0 / (length + 1)) * np.sin(product * (math.pi / (length + 1)))


def stencil_eigen(mode_index, length):
    return 4.0 * np.sin((mode_index + 1) * (math.pi / (2.0 * (length + 1)))) ** 2


def second_tables(width):
    half = width // 2
    return np.stack([sine_table(np.arange(half), np.arange(s, width, 2), width) for s in (0, 1)])


def first_tables(total):
    rows = total // 2
    return np.stack(
        [
            np.stack(
                [sine_table(s * rows + np.arange(rows), np.arange(c, total, 2), total) for c in (0, 1)]
            )
            for s in (0, 1)
        ]
    )


def decay_tables(total, width):
    first, second = stencil_eigen(np.arange(total), total), stencil_eigen(np.arange(width), width)
    decay = 1.0 / (1.0 + DIFFUSION * (second[:, None] + first[None, :]))
    return np.stack([np.stack([decay[s::2, c::2] for c in (0, 1)]) for s in (0, 1)])


def constant(table):
    return jnp.asarray(np.asarray(table, np.float32))


def split_constant(table):
    table = np.asarray(table, np.float32)
    high = table.astype(jnp.bfloat16)
    low = (table - high.astype(np.float32)).astype(jnp.bfloat16)
    return jnp.asarray(np.concatenate([high, high, low], axis=-2))


def store_split(ref, at, lane, block):
    depth = ref.shape[-1] // 2
    width = block.shape[-1]
    high = block.astype(jnp.bfloat16)
    low = (block - high.astype(jnp.float32)).astype(jnp.bfloat16)
    ref[(*at, pl.ds(lane, width))] = high
    ref[(*at, pl.ds(depth + lane, width))] = low


def dot(split, table):
    rows = jnp.concatenate([split, split[:, : split.shape[1] // 2]], axis=1)
    return jnp.dot(rows, table, preferred_element_type=jnp.float32)


def lanes_reversed(block):
    index = LANES - 1 - lax.broadcasted_iota(jnp.int32, (block.shape[0], LANES), 1)
    return jnp.take_along_axis(block, index, axis=1, mode="promise_in_bounds")


def store_rows_reversed(ref, start, block):
    rows, width = block.shape
    index = SUBLANES - 1 - lax.broadcasted_iota(jnp.int32, (SUBLANES, width), 0)
    for row in range(0, rows, SUBLANES):
        to = pl.multiple_of(start + rows - SUBLANES - row, SUBLANES)
        ref[pl.ds(to, SUBLANES), :] = jnp.take_along_axis(
            block[row : row + SUBLANES], index, axis=0, mode="promise_in_bounds"
        )


def pitch_of(cells):
    return cells + SUBLANES * (1 - cells // SUBLANES % 2)


def steps_of(ref, cells, steps, pitch):
    lines = [ref[pl.ds(cell, steps, stride=pitch), :] for cell in cells]
    return lines[0] if len(lines) == 1 else jnp.concatenate(lines, axis=0)


IN_VMEM = pl.BlockSpec(memory_space=pltpu.VMEM)
IN_HBM = pl.BlockSpec(memory_space=pltpu.HBM)
IN_SMEM = pl.BlockSpec(memory_space=pltpu.SMEM)


def in_hbm(array):
    return pltpu.with_memory_space_constraint(array, pltpu.HBM)


def floats(*shape):
    return jax.ShapeDtypeStruct(shape, jnp.float32)


def call(kernel, name, in_specs, out_specs, out_shape, scratch, flops):
    return pl.pallas_call(
        kernel,
        in_specs=[IN_SMEM, *in_specs],
        out_specs=out_specs,
        scratch_shapes=scratch,
        out_shape=out_shape,
        compiler_params=pltpu.CompilerParams(vmem_limit_bytes=VMEM_BYTES),
        cost_estimate=pl.CostEstimate(flops=flops, bytes_accessed=1 << 23, transcendentals=0),
        name=name,
    )


def forward_second_kernel(place, field_in, initial_in, tables, sums, *refs):
    sends, refs = refs[:CHUNKS], refs[CHUNKS:]
    field, initial, table, sems, table_sem, *scratch = refs
    cells, steps, width = field.shape
    half = width // 2
    part = half // CHUNKS
    pieces = sems.shape[0]
    piece = cells // pieces
    group = max(TILE // steps, 1)
    pitch = sends[0].shape[0] // (steps + 1)
    body = piece * steps
    is_first = place[0] == 0
    sign = 1.0 - 2.0 * place[1].astype(jnp.float32)

    def copies(at):
        here = pl.ds(at * piece, piece)
        return [
            pltpu.make_async_copy(source.at[here], to.at[here], sems.at[at, which])
            for which, (source, to) in enumerate(((field_in, field), (initial_in, initial)))
        ]

    table_copy = pltpu.make_async_copy(tables.at[1 - place[1]], table, table_sem)

    def start(first, last):
        for at in range(first, min(last, pieces)):
            for copy in copies(at):
                copy.start()

    def put(other, at, sums_at, cells):
        lower = cells[:, :half]
        upper = sign * jnp.concatenate(
            [lanes_reversed(cells[:, lane : lane + LANES]) for lane in range(half, width, LANES)][::-1],
            axis=1,
        )
        sums[pl.ds(sums_at, TILE), :] = lower + upper
        store_split(other, (pl.ds(at, TILE),), 0, lower - upper)

    def prepare(at):
        split = scratch[at % len(scratch)]
        cell = at * piece
        for row in range(0, piece, group):
            values = field[pl.ds(cell + row, group)]
            force = values - values * values * values
            put(split, row * steps, (cell + row) * steps, force.reshape(TILE, width))
        for row in range(0, piece, TILE):
            here = pl.ds(cell + row, TILE)
            ends = jnp.where(is_first, initial[here], field[here, steps - 1, :])
            put(split, body + row, cells * steps + cell + row, ends)

    def transform(at):
        sent = dot(scratch[at % len(scratch)][...], table[...])
        first = cells - (at + 1) * piece
        for chunk, send in enumerate(sends):
            lanes = slice(chunk * part, (chunk + 1) * part)
            for row in range(piece):
                line = sent[row * steps : (row + 1) * steps, lanes]
                send[pl.ds(first + piece - 1 - row, steps, stride=pitch), :] = line
            store_rows_reversed(send, pitch * steps + first, sent[body:, lanes])

    start(0, 1)
    table_copy.start()
    start(1, 2)
    for at in range(pieces):
        for copy in copies(at):
            copy.wait()
        start(2 * at + 2, 2 * at + 4)
        if at == 1:
            table_copy.wait()
        if at:
            transform(at - 1)
        prepare(at)
    transform(pieces - 1)


def forward_second(place, field, initial, tables):
    rows, steps, width = field.shape
    half = width // 2
    piece, pieces = min(32, rows // 2), 2
    outs = call(
        forward_second_kernel,
        "forward_second",
        [IN_HBM] * 3,
        [IN_VMEM] * (1 + CHUNKS),
        [floats((steps + 1) * rows, half)]
        + [floats((steps + 1) * pitch_of(rows), half // CHUNKS)] * CHUNKS,
        [
            pltpu.VMEM(field.shape, jnp.float32),
            pltpu.VMEM(initial.shape, jnp.float32),
            pltpu.VMEM(tables.shape[1:], jnp.bfloat16),
            pltpu.SemaphoreType.DMA((rows // piece, 2)),
            pltpu.SemaphoreType.DMA,
        ]
        + [pltpu.VMEM(((steps + 1) * piece, 2 * half), jnp.bfloat16)] * pieces,
        1 << 32,
    )(place, in_hbm(field), in_hbm(initial), in_hbm(tables))
    return outs[0], outs[1:]


def keep_second_kernel(steps, place, tables, sums, *refs):
    keeps, scratch = refs[:CHUNKS], refs[CHUNKS:]
    depth = scratch[0].shape[0]
    cells = sums.shape[0] // (steps + 1)
    pitch = keeps[0].shape[0] // (steps + 1)
    for at in range(0, sums.shape[0], depth):
        split = scratch[at // depth % 2]
        for row in range(0, depth, TILE):
            store_split(split, (pl.ds(row, TILE),), 0, sums[pl.ds(at + row, TILE)])
        result = dot(split[...], tables[place[1]])
        for chunk, keep in enumerate(keeps):
            part = keep.shape[1]
            lanes = slice(chunk * part, (chunk + 1) * part)
            body = max(0, min(depth, cells * steps - at))
            for row in range(0, body, steps):
                line = result[row : row + steps, lanes]
                keep[pl.ds((at + row) // steps, steps, stride=pitch), :] = line
            if body < depth:
                ends = pl.ds(pitch * steps + at + body - cells * steps, depth - body)
                keep[ends, :] = result[body:, lanes]


def keep_second(place, sums, tables, steps):
    rows, half = sums.shape
    shape = ((steps + 1) * pitch_of(rows // (steps + 1)), half // CHUNKS)
    return call(
        functools.partial(keep_second_kernel, steps),
        "keep_second",
        [IN_VMEM] * 2,
        [IN_VMEM] * CHUNKS,
        [floats(*shape)] * CHUNKS,
        [pltpu.VMEM((rows // 8, 2 * half), jnp.bfloat16)] * 2,
        1 << 31,
    )(place, tables, sums)


def ranks(slabs):
    return slabs // 2


def forward_first_kernel(slabs, chunk, place, keep, got, table, decay, modes, *refs):
    size = ranks(slabs)
    lasts, (state, split, extra) = refs[:size], refs[size:]
    steps, _, part, rows = modes.shape
    pitch = keep.shape[0] // (steps + 1)
    block = split.shape[1] // part - 1
    strip = place[1]
    is_first = jnp.where(place[0] == 0, 1.0 / REACTION_STEP, 0.0)
    is_last = jnp.where(place[0] == slabs - 1, 1.0 / REACTION_STEP, 0.0)
    state[...] = jnp.zeros_like(state)
    for step in range(0, steps, block):
        count = block if step else block + 1
        for c in (0, 1):
            for at in range(count):
                from_step = steps if at == block else step + at
                cells_at = pl.ds(from_step * pitch, rows)
                near, far = keep[cells_at], got[cells_at]
                cells = near - far if c else near + far
                store_split(split, (c, pl.ds(at * part, part)), 0, cells.T)
            result = dot(split[c, pl.ds(0, count * part)], table[strip, c])
            if step == 0:
                extra[c] = result[block * part :]
                modes[0, c] = result[:part] + is_first * result[block * part :]
                modes[pl.ds(1, block - 1), c] = result[part : block * part].reshape(block - 1, part, rows)
            else:
                modes[pl.ds(step, block), c] = result.reshape(block, part, rows)
        for c in (0, 1):
            for row in range(0, part, TILE):
                tile, at_state = pl.ds(row, TILE), pl.ds(c * part + row, TILE)
                value = state[at_state]
                rate = decay[strip, c, pl.ds(chunk * part + row, TILE)]
                for at in range(block):
                    value = rate * (value + modes[step + at, c, tile])
                state[at_state] = value
    for c in (0, 1):
        at_state = pl.ds(c * part, part)
        state[at_state] = state[at_state] - is_last * extra[c]
    rank = lax.rem(place[0], size)
    share = 2 * part // size
    for partner in range(size):
        at = pl.multiple_of((rank ^ partner) * share, share)
        lasts[partner][...] = state[pl.ds(at, share)]


def forward_first(place, chunk, keep, got, tables, decays, slabs):
    rows, part = tables.shape[-1], keep.shape[1]
    steps = keep.shape[0] // pitch_of(rows) - 1
    block = min(8, steps)
    size = ranks(slabs)
    share = 2 * part // size
    outs = call(
        functools.partial(forward_first_kernel, slabs, chunk),
        "forward_first",
        [IN_VMEM] * 4,
        [IN_VMEM] * (1 + size),
        [floats(steps, 2, part, rows)] + [floats(share, rows)] * size,
        [
            pltpu.VMEM((2 * part, rows), jnp.float32),
            pltpu.VMEM((2, (block + 1) * part, 2 * rows), jnp.bfloat16),
            pltpu.VMEM((2, part, rows), jnp.float32),
        ],
        1 << 31,
    )(place, keep, got, tables, decays)
    return outs[0], outs[1:]


def half_sum_kernel(slabs, chunk, place, closing, *refs):
    size = ranks(slabs)
    lasts, ordered, total = refs[:size], refs[size], refs[size + 1]
    share = total.shape[0]
    rank = lax.rem(place[0], size)
    decay = closing[place[1], chunk, 0, pl.ds(pl.multiple_of(rank * share, share), share)]
    for partner in range(size):
        ordered[rank ^ partner] = lasts[partner][...]
    state = ordered[0]
    for at in range(1, size):
        state = ordered[at] + decay * state
    total[...] = state


def half_sum(place, chunk, lasts, closing, slabs):
    size = ranks(slabs)
    share, rows = lasts[0].shape
    return call(
        functools.partial(half_sum_kernel, slabs, chunk),
        "half_sum",
        [IN_VMEM] * (1 + size),
        [IN_VMEM] * 2,
        [floats(size, share, rows), floats(share, rows)],
        [],
        1 << 20,
    )(place, closing, *lasts)


def close_kernel(slabs, chunk, place, closing, ordered, near, far, *refs):
    size = ranks(slabs)
    befores, states = refs[:size], refs[size]
    share = near.shape[0]
    rank = lax.rem(place[0], size)
    at_share = pl.ds(pl.multiple_of(rank * share, share), share)
    decay, half_decay, gain = (closing[place[1], chunk, at, at_share] for at in range(3))
    entering = jnp.where(place[0] < size, circulant_alpha, 1.0)
    state = gain * (entering * far[...] + circulant_alpha * half_decay * near[...])
    for at in range(size):
        states[at] = state
        if at < size - 1:
            state = ordered[at] + decay * state
    for partner in range(size):
        befores[partner][...] = states[rank ^ partner]


def close(place, chunk, ordered, near, far, closing, slabs):
    size, share, rows = ordered.shape
    return call(
        functools.partial(close_kernel, slabs, chunk),
        "close",
        [IN_VMEM] * 4,
        [IN_VMEM] * size,
        [floats(share, rows)] * size,
        [pltpu.VMEM((size, share, rows), jnp.float32)],
        1 << 20,
    )(place, closing, ordered, near, far)


def inverse_first_kernel(slabs, chunk, place, modes, table, decay, *refs):
    size = ranks(slabs)
    befores, (keep, send, state, split) = refs[:size], refs[size:]
    steps, _, part, rows = modes.shape
    pitch = keep.shape[0] // steps
    block = split.shape[1] // part
    strip = place[1]
    rank = lax.rem(place[0], size)
    share = 2 * part // size
    for partner in range(size):
        at = pl.multiple_of((rank ^ partner) * share, share)
        state[pl.ds(at, share)] = befores[partner][...]
    for step in range(0, steps, block):
        results = []
        for c in (0, 1):
            for row in range(0, part, TILE):
                tile, at_state = pl.ds(row, TILE), pl.ds(c * part + row, TILE)
                value = state[at_state]
                rate = decay[strip, c, pl.ds(chunk * part + row, TILE)]
                for at in range(block):
                    value = rate * (value + modes[step + at, c, tile])
                    store_split(split, (c, pl.ds(at * part + row, TILE)), 0, value)
                state[at_state] = value
            results.append(dot(split[c], table[strip, c]))
        even, odd = results
        for at in range(block):
            piece = slice(at * part, (at + 1) * part)
            cells_at = pl.ds((step + at) * pitch, rows)
            keep[cells_at, :] = (even[piece] + odd[piece]).T
            send[cells_at, :] = (even[piece] - odd[piece]).T


def inverse_first(place, chunk, modes, befores, tables, decays, slabs):
    steps, _, part, rows = modes.shape
    block = min(8, steps)
    return call(
        functools.partial(inverse_first_kernel, slabs, chunk),
        "inverse_first",
        [IN_VMEM] * (3 + len(befores)),
        [IN_VMEM] * 2,
        [floats(steps * pitch_of(rows), part)] * 2,
        [
            pltpu.VMEM((2 * part, rows), jnp.float32),
            pltpu.VMEM((2, block * part, 2 * rows), jnp.bfloat16),
        ],
        1 << 31,
    )(place, modes, tables, decays, *befores)


def keep_inverse_kernel(steps, place, tables, *refs):
    keeps, out, scratch = refs[:CHUNKS], refs[CHUNKS], refs[CHUNKS + 1 :]
    part = keeps[0].shape[1]
    pitch = keeps[0].shape[0] // steps
    depth = scratch[0].shape[0]
    group = max(TILE // steps, 1)
    for at in range(0, out.shape[0], depth):
        split = scratch[at // depth % 2]
        for row in range(0, depth, TILE):
            cell = (at + row) // steps
            for chunk, keep in enumerate(keeps):
                cells = steps_of(keep, range(cell, cell + group), steps, pitch)
                store_split(split, (pl.ds(row, TILE),), chunk * part, cells)
        out[pl.ds(at, depth)] = dot(split[...], tables[place[1]])


def keep_inverse(place, keeps, tables, rows, steps):
    half = keeps[0].shape[1] * CHUNKS
    return call(
        functools.partial(keep_inverse_kernel, steps),
        "keep_inverse",
        [IN_VMEM] * (1 + CHUNKS),
        IN_VMEM,
        floats(rows * steps, half),
        [pltpu.VMEM((rows * steps // 8, 2 * half), jnp.bfloat16)] * 2,
        1 << 31,
    )(place, tables, *keeps)


def inverse_second_kernel(place, tables, kept, *refs):
    gots, target, out, sems, scratch = (
        refs[:CHUNKS], refs[CHUNKS], refs[CHUNKS + 1], refs[CHUNKS + 2], refs[CHUNKS + 3 :]
    )
    cells, steps, width = out.shape
    half = width // 2
    part = half // CHUNKS
    pitch = gots[0].shape[0] // steps
    count = len(scratch) // 2
    pieces = sems.shape[0]
    piece = cells // pieces
    group = max(TILE // steps, 1)
    strip = place[1]
    sign = 1.0 - 2.0 * strip.astype(jnp.float32)

    def copy(at):
        here = pl.ds(at * piece, piece)
        return pltpu.make_async_copy(out.at[here], target.at[here], sems.at[at])

    def product(at):
        split, result = scratch[2 * (at % count) : 2 * (at % count) + 2]
        for row in range(0, piece, group):
            mirrors = [cells - 1 - at * piece - row - cell for cell in range(group)]
            for chunk, got in enumerate(gots):
                values = steps_of(got, mirrors, steps, pitch)
                store_split(split, (pl.ds(row * steps, TILE),), chunk * part, values)
        result[...] = dot(split[...], tables[1 - strip])

    def finish(at):
        result = scratch[2 * (at % count) + 1]
        for row in range(0, piece, group):
            first = kept[pl.ds((at * piece + row) * steps, TILE)]
            second = result[pl.ds(row * steps, TILE)]
            upper = sign * (first - second)
            parts = [
                lanes_reversed(upper[:, lane : lane + LANES]) for lane in range(0, half, LANES)
            ][::-1]
            whole = jnp.concatenate([first + second, *parts], axis=1)
            out[pl.ds(at * piece + row, group)] = whole.reshape(group, TILE // group, width)
        copy(at).start()

    for at in range(pieces):
        product(at)
        if at:
            finish(at - 1)
    finish(pieces - 1)
    for at in range(pieces):
        copy(at).wait()


def inverse_second(place, kept, gots, tables, steps):
    rows, half = kept.shape[0] // steps, kept.shape[1]
    piece, pieces = min(32, rows // 2), 2
    depth = steps * piece
    return call(
        inverse_second_kernel,
        "inverse_second",
        [IN_VMEM] * (2 + CHUNKS),
        IN_HBM,
        floats(rows, steps, 2 * half),
        [pltpu.VMEM((rows, steps, 2 * half), jnp.float32), pltpu.SemaphoreType.DMA((rows // piece,))]
        + [pltpu.VMEM((depth, 2 * half), jnp.bfloat16), pltpu.VMEM((depth, half), jnp.float32)]
        * pieces,
        1 << 32,
    )(place, tables, kept, *gots)


def swapped(block):
    return lax.ppermute(block, "space", [(0, 1), (1, 0)])


def with_partner(block, distance):
    slabs = lax.axis_size("tm")
    return lax.ppermute(block, "tm", [(slab, slab ^ distance) for slab in range(slabs)])


def among_ranks(blocks):
    return [blocks[0]] + [with_partner(block, at) for at, block in enumerate(blocks) if at]


def by_chunk(table):
    strips, _, half, rows = table.shape
    parts = table.reshape(strips, 2, CHUNKS, half // CHUNKS, rows)
    return np.swapaxes(parts, 1, 2).reshape(strips, CHUNKS, 2 * half // CHUNKS, rows)


def shards(iterate, initial):
    rows, steps, width = iterate.shape
    slabs = lax.axis_size("tm")
    total = rows * lax.axis_size("space")
    place = jnp.stack([lax.axis_index("tm"), lax.axis_index("space")]).astype(jnp.int32)
    second = second_tables(width)
    first = first_tables(total)
    decay = decay_tables(total, width)
    slab_decay = decay**steps
    half_decay = slab_decay ** ranks(slabs)
    gain = 1.0 / (1.0 - circulant_alpha * half_decay * half_decay)
    closing = constant(
        np.stack([by_chunk(table) for table in (slab_decay, half_decay, gain)], axis=2)
    )
    first_table, decays = split_constant(first), constant(decay)
    second_table = split_constant(REACTION_STEP * second)
    sums, sends = forward_second(place, iterate, initial, second_table)
    gots = [swapped(send) for send in sends]
    keeps = keep_second(place, sums, second_table, steps)
    modes, befores = [], []
    for chunk in range(CHUNKS):
        own_modes, lasts = forward_first(
            place, chunk, keeps[chunk], gots[chunk], first_table, decays, slabs
        )
        modes.append(own_modes)
        ordered, near = half_sum(place, chunk, among_ranks(lasts), closing, slabs)
        far = with_partner(near, ranks(slabs))
        befores.append(among_ranks(close(place, chunk, ordered, near, far, closing, slabs)))
    inverse_table = split_constant(np.swapaxes(first, 2, 3))
    keeps, sends = zip(
        *(
            inverse_first(place, chunk, modes[chunk], befores[chunk], inverse_table, decays, slabs)
            for chunk in range(CHUNKS)
        )
    )
    gots = [swapped(send) for send in sends]
    inverse_table = split_constant(np.swapaxes(second, 1, 2))
    kept = keep_inverse(place, keeps, inverse_table, rows, steps)
    return inverse_second(place, kept, gots, inverse_table, steps)


def solution(mesh):
    return jax.shard_map(
        shards,
        mesh=mesh,
        in_specs=(P(("group", "space"), "tm", None), P(("group", "space"), None)),
        out_specs=P(("group", "space"), "tm", None),
        check_vma=False,
    )
```

```python
import functools
import math

import jax
import jax.numpy as jnp
import numpy as np
from jax import lax
from jax.experimental import pallas as pl
from jax.experimental.pallas import tpu as pltpu
from jax.sharding import PartitionSpec as P

circulant_alpha = 0.01
DIFFUSION = 2.0
REACTION_STEP = 0.5
VMEM_BYTES = 24 * 1024 * 1024
LANES = 128
SUBLANES = 8
TILE = 16
CHUNKS = 2


def sine_table(row_index, column_index, length):
    product = np.outer(row_index + 1, column_index + 1) % (2 * (length + 1))
    return math.sqrt(2.0 / (length + 1)) * np.sin(product * (math.pi / (length + 1)))


def stencil_eigen(mode_index, length):
    return 4.0 * np.sin((mode_index + 1) * (math.pi / (2.0 * (length + 1)))) ** 2


def second_tables(width):
    half = width // 2
    return np.stack([sine_table(np.arange(half), np.arange(s, width, 2), width) for s in (0, 1)])


def first_tables(total):
    rows = total // 2
    return np.stack(
        [
            np.stack(
                [sine_table(s * rows + np.arange(rows), np.arange(c, total, 2), total) for c in (0, 1)]
            )
            for s in (0, 1)
        ]
    )


def decay_tables(total, width):
    first, second = stencil_eigen(np.arange(total), total), stencil_eigen(np.arange(width), width)
    decay = 1.0 / (1.0 + DIFFUSION * (second[:, None] + first[None, :]))
    return np.stack([np.stack([decay[s::2, c::2] for c in (0, 1)]) for s in (0, 1)])


def constant(table):
    return jnp.asarray(np.asarray(table, np.float32))


def split_constant(table):
    table = np.asarray(table, np.float32)
    high = table.astype(jnp.bfloat16)
    low = (table - high.astype(np.float32)).astype(jnp.bfloat16)
    return jnp.asarray(np.concatenate([high, high, low], axis=-2))


def store_split(ref, at, lane, block):
    depth = ref.shape[-1] // 2
    width = block.shape[-1]
    high = block.astype(jnp.bfloat16)
    low = (block - high.astype(jnp.float32)).astype(jnp.bfloat16)
    ref[(*at, pl.ds(lane, width))] = high
    ref[(*at, pl.ds(depth + lane, width))] = low


def dot(split, table):
    rows = jnp.concatenate([split, split[:, : split.shape[1] // 2]], axis=1)
    return jnp.dot(rows, table, preferred_element_type=jnp.float32)


ALONG_LANES = lax.GatherDimensionNumbers(
    offset_dims=(),
    collapsed_slice_dims=(1,),
    start_index_map=(1,),
    operand_batching_dims=(0,),
    start_indices_batching_dims=(0,),
)


def reversal():
    index = LANES - 1 - lax.broadcasted_iota(jnp.int32, (TILE, LANES), 1)
    index = index.reshape(TILE, LANES, 1)
    return lambda block: lax.gather(
        block, index, ALONG_LANES, (1, 1), mode=lax.GatherScatterMode.PROMISE_IN_BOUNDS
    )


def store_rows_reversed(ref, start, block):
    rows, width = block.shape
    index = SUBLANES - 1 - lax.broadcasted_iota(jnp.int32, (SUBLANES, width), 0)
    for row in range(0, rows, SUBLANES):
        to = pl.multiple_of(start + rows - SUBLANES - row, SUBLANES)
        ref[pl.ds(to, SUBLANES), :] = jnp.take_along_axis(
            block[row : row + SUBLANES], index, axis=0, mode="promise_in_bounds"
        )


def pitch_of(cells):
    return cells + SUBLANES * (1 - cells // SUBLANES % 2)


def steps_of(ref, cells, steps, pitch):
    lines = [ref[pl.ds(cell, steps, stride=pitch), :] for cell in cells]
    return lines[0] if len(lines) == 1 else jnp.concatenate(lines, axis=0)


IN_VMEM = pl.BlockSpec(memory_space=pltpu.VMEM)
IN_HBM = pl.BlockSpec(memory_space=pltpu.HBM)
IN_SMEM = pl.BlockSpec(memory_space=pltpu.SMEM)


def in_hbm(array):
    return pltpu.with_memory_space_constraint(array, pltpu.HBM)


def floats(*shape):
    return jax.ShapeDtypeStruct(shape, jnp.float32)


def call(kernel, name, in_specs, out_specs, out_shape, scratch, flops):
    return pl.pallas_call(
        kernel,
        in_specs=[IN_SMEM, *in_specs],
        out_specs=out_specs,
        scratch_shapes=scratch,
        out_shape=out_shape,
        compiler_params=pltpu.CompilerParams(vmem_limit_bytes=VMEM_BYTES),
        cost_estimate=pl.CostEstimate(flops=flops, bytes_accessed=1 << 23, transcendentals=0),
        name=name,
    )


def forward_second_kernel(place, field_in, initial_in, tables, sums, *refs):
    sends, refs = refs[:CHUNKS], refs[CHUNKS:]
    field, initial, table, sems, table_sem, *scratch = refs
    cells, steps, width = field.shape
    half = width // 2
    part = half // CHUNKS
    pieces = sems.shape[0]
    piece = cells // pieces
    group = max(TILE // steps, 1)
    pitch = sends[0].shape[0] // (steps + 1)
    body = piece * steps
    is_first = place[0] == 0
    sign = 1.0 - 2.0 * place[1].astype(jnp.float32)

    def copies(at):
        here = pl.ds(at * piece, piece)
        return [
            pltpu.make_async_copy(source.at[here], to.at[here], sems.at[at, which])
            for which, (source, to) in enumerate(((field_in, field), (initial_in, initial)))
        ]

    table_copy = pltpu.make_async_copy(tables.at[1 - place[1]], table, table_sem)

    def start(first, last):
        for at in range(first, min(last, pieces)):
            for copy in copies(at):
                copy.start()

    lanes_reversed = reversal()

    def put(other, at, sums_at, cells):
        lower = cells[:, :half]
        upper = sign * jnp.concatenate(
            [lanes_reversed(cells[:, lane : lane + LANES]) for lane in range(half, width, LANES)][::-1],
            axis=1,
        )
        sums[pl.ds(sums_at, TILE), :] = lower + upper
        store_split(other, (pl.ds(at, TILE),), 0, lower - upper)

    def prepare(at):
        split = scratch[at % len(scratch)]
        cell = at * piece
        for row in range(0, piece, group):
            values = field[pl.ds(cell + row, group)]
            force = values - values * values * values
            put(split, row * steps, (cell + row) * steps, force.reshape(TILE, width))
        for row in range(0, piece, TILE):
            here = pl.ds(cell + row, TILE)
            ends = jnp.where(is_first, initial[here], field[here, steps - 1, :])
            put(split, body + row, cells * steps + cell + row, ends)

    def transform(at):
        sent = dot(scratch[at % len(scratch)][...], table[...])
        first = cells - (at + 1) * piece
        for chunk, send in enumerate(sends):
            lanes = slice(chunk * part, (chunk + 1) * part)
            for row in range(piece):
                line = sent[row * steps : (row + 1) * steps, lanes]
                send[pl.ds(first + piece - 1 - row, steps, stride=pitch), :] = line
            store_rows_reversed(send, pitch * steps + first, sent[body:, lanes])

    start(0, 1)
    table_copy.start()
    start(1, 2)
    for at in range(pieces):
        for copy in copies(at):
            copy.wait()
        start(2 * at + 2, 2 * at + 4)
        if at == 1:
            table_copy.wait()
        if at:
            transform(at - 1)
        prepare(at)
    transform(pieces - 1)


def forward_second(place, field, initial, tables):
    rows, steps, width = field.shape
    half = width // 2
    piece, pieces = min(32, rows // 2), 2
    outs = call(
        forward_second_kernel,
        "forward_second",
        [IN_HBM] * 3,
        [IN_VMEM] * (1 + CHUNKS),
        [floats((steps + 1) * rows, half)]
        + [floats((steps + 1) * pitch_of(rows), half // CHUNKS)] * CHUNKS,
        [
            pltpu.VMEM(field.shape, jnp.float32),
            pltpu.VMEM(initial.shape, jnp.float32),
            pltpu.VMEM(tables.shape[1:], jnp.bfloat16),
            pltpu.SemaphoreType.DMA((rows // piece, 2)),
            pltpu.SemaphoreType.DMA,
        ]
        + [pltpu.VMEM(((steps + 1) * piece, 2 * half), jnp.bfloat16)] * pieces,
        1 << 32,
    )(place, in_hbm(field), in_hbm(initial), in_hbm(tables))
    return outs[0], outs[1:]


def keep_second_kernel(steps, place, tables, sums, *refs):
    keeps, scratch = refs[:CHUNKS], refs[CHUNKS:]
    depth = scratch[0].shape[0]
    cells = sums.shape[0] // (steps + 1)
    pitch = keeps[0].shape[0] // (steps + 1)
    for at in range(0, sums.shape[0], depth):
        split = scratch[at // depth % 2]
        for row in range(0, depth, TILE):
            store_split(split, (pl.ds(row, TILE),), 0, sums[pl.ds(at + row, TILE)])
        result = dot(split[...], tables[place[1]])
        for chunk, keep in enumerate(keeps):
            part = keep.shape[1]
            lanes = slice(chunk * part, (chunk + 1) * part)
            body = max(0, min(depth, cells * steps - at))
            for row in range(0, body, steps):
                line = result[row : row + steps, lanes]
                keep[pl.ds((at + row) // steps, steps, stride=pitch), :] = line
            if body < depth:
                ends = pl.ds(pitch * steps + at + body - cells * steps, depth - body)
                keep[ends, :] = result[body:, lanes]


def keep_second(place, sums, tables, steps):
    rows, half = sums.shape
    shape = ((steps + 1) * pitch_of(rows // (steps + 1)), half // CHUNKS)
    return call(
        functools.partial(keep_second_kernel, steps),
        "keep_second",
        [IN_VMEM] * 2,
        [IN_VMEM] * CHUNKS,
        [floats(*shape)] * CHUNKS,
        [pltpu.VMEM((rows // 8, 2 * half), jnp.bfloat16)] * 2,
        1 << 31,
    )(place, tables, sums)


def ranks(slabs):
    return slabs // 2


def forward_first_kernel(slabs, chunk, place, keep, got, table, decay, modes, *refs):
    size = ranks(slabs)
    lasts, (state, split, extra) = refs[:size], refs[size:]
    steps, _, part, rows = modes.shape
    pitch = keep.shape[0] // (steps + 1)
    block = split.shape[1] // part - 1
    strip = place[1]
    is_first = jnp.where(place[0] == 0, 1.0 / REACTION_STEP, 0.0)
    is_last = jnp.where(place[0] == slabs - 1, 1.0 / REACTION_STEP, 0.0)
    state[...] = jnp.zeros_like(state)
    for step in range(0, steps, block):
        count = block if step else block + 1
        for c in (0, 1):
            for at in range(count):
                from_step = steps if at == block else step + at
                cells_at = pl.ds(from_step * pitch, rows)
                near, far = keep[cells_at], got[cells_at]
                cells = near - far if c else near + far
                store_split(split, (c, pl.ds(at * part, part)), 0, cells.T)
            result = dot(split[c, pl.ds(0, count * part)], table[strip, c])
            if step == 0:
                extra[c] = result[block * part :]
                modes[0, c] = result[:part] + is_first * result[block * part :]
                modes[pl.ds(1, block - 1), c] = result[part : block * part].reshape(block - 1, part, rows)
            else:
                modes[pl.ds(step, block), c] = result.reshape(block, part, rows)
        for c in (0, 1):
            for row in range(0, part, TILE):
                tile, at_state = pl.ds(row, TILE), pl.ds(c * part + row, TILE)
                value = state[at_state]
                rate = decay[strip, c, pl.ds(chunk * part + row, TILE)]
                for at in range(block):
                    value = rate * (value + modes[step + at, c, tile])
                state[at_state] = value
    for c in (0, 1):
        at_state = pl.ds(c * part, part)
        state[at_state] = state[at_state] - is_last * extra[c]
    rank = lax.rem(place[0], size)
    share = 2 * part // size
    for partner in range(size):
        at = pl.multiple_of((rank ^ partner) * share, share)
        lasts[partner][...] = state[pl.ds(at, share)]


def forward_first(place, chunk, keep, got, tables, decays, slabs):
    rows, part = tables.shape[-1], keep.shape[1]
    steps = keep.shape[0] // pitch_of(rows) - 1
    block = min(8, steps)
    size = ranks(slabs)
    share = 2 * part // size
    outs = call(
        functools.partial(forward_first_kernel, slabs, chunk),
        "forward_first",
        [IN_VMEM] * 4,
        [IN_VMEM] * (1 + size),
        [floats(steps, 2, part, rows)] + [floats(share, rows)] * size,
        [
            pltpu.VMEM((2 * part, rows), jnp.float32),
            pltpu.VMEM((2, (block + 1) * part, 2 * rows), jnp.bfloat16),
            pltpu.VMEM((2, part, rows), jnp.float32),
        ],
        1 << 31,
    )(place, keep, got, tables, decays)
    return outs[0], outs[1:]


def half_sum_kernel(slabs, chunk, place, closing, *refs):
    size = ranks(slabs)
    lasts, ordered, total = refs[:size], refs[size], refs[size + 1]
    share = total.shape[0]
    rank = lax.rem(place[0], size)
    decay = closing[place[1], chunk, 0, pl.ds(pl.multiple_of(rank * share, share), share)]
    for partner in range(size):
        ordered[rank ^ partner] = lasts[partner][...]
    state = ordered[0]
    for at in range(1, size):
        state = ordered[at] + decay * state
    total[...] = state


def half_sum(place, chunk, lasts, closing, slabs):
    size = ranks(slabs)
    share, rows = lasts[0].shape
    return call(
        functools.partial(half_sum_kernel, slabs, chunk),
        "half_sum",
        [IN_VMEM] * (1 + size),
        [IN_VMEM] * 2,
        [floats(size, share, rows), floats(share, rows)],
        [],
        1 << 20,
    )(place, closing, *lasts)


def close_kernel(slabs, chunk, place, closing, ordered, near, far, *refs):
    size = ranks(slabs)
    befores, states = refs[:size], refs[size]
    share = near.shape[0]
    rank = lax.rem(place[0], size)
    at_share = pl.ds(pl.multiple_of(rank * share, share), share)
    decay, half_decay, gain = (closing[place[1], chunk, at, at_share] for at in range(3))
    entering = jnp.where(place[0] < size, circulant_alpha, 1.0)
    state = gain * (entering * far[...] + circulant_alpha * half_decay * near[...])
    for at in range(size):
        states[at] = state
        if at < size - 1:
            state = ordered[at] + decay * state
    for partner in range(size):
        befores[partner][...] = states[rank ^ partner]


def close(place, chunk, ordered, near, far, closing, slabs):
    size, share, rows = ordered.shape
    return call(
        functools.partial(close_kernel, slabs, chunk),
        "close",
        [IN_VMEM] * 4,
        [IN_VMEM] * size,
        [floats(share, rows)] * size,
        [pltpu.VMEM((size, share, rows), jnp.float32)],
        1 << 20,
    )(place, closing, ordered, near, far)


def inverse_first_kernel(slabs, chunk, place, modes, table, decay, *refs):
    size = ranks(slabs)
    befores, (keep, send, state, split) = refs[:size], refs[size:]
    steps, _, part, rows = modes.shape
    pitch = keep.shape[0] // steps
    block = split.shape[1] // part
    strip = place[1]
    rank = lax.rem(place[0], size)
    share = 2 * part // size
    for partner in range(size):
        at = pl.multiple_of((rank ^ partner) * share, share)
        state[pl.ds(at, share)] = befores[partner][...]
    for step in range(0, steps, block):
        results = []
        for c in (0, 1):
            for row in range(0, part, TILE):
                tile, at_state = pl.ds(row, TILE), pl.ds(c * part + row, TILE)
                value = state[at_state]
                rate = decay[strip, c, pl.ds(chunk * part + row, TILE)]
                for at in range(block):
                    value = rate * (value + modes[step + at, c, tile])
                    store_split(split, (c, pl.ds(at * part + row, TILE)), 0, value)
                state[at_state] = value
            results.append(dot(split[c], table[strip, c]))
        even, odd = results
        for at in range(block):
            piece = slice(at * part, (at + 1) * part)
            cells_at = pl.ds((step + at) * pitch, rows)
            keep[cells_at, :] = (even[piece] + odd[piece]).T
            send[cells_at, :] = (even[piece] - odd[piece]).T


def inverse_first(place, chunk, modes, befores, tables, decays, slabs):
    steps, _, part, rows = modes.shape
    block = min(8, steps)
    return call(
        functools.partial(inverse_first_kernel, slabs, chunk),
        "inverse_first",
        [IN_VMEM] * (3 + len(befores)),
        [IN_VMEM] * 2,
        [floats(steps * pitch_of(rows), part)] * 2,
        [
            pltpu.VMEM((2 * part, rows), jnp.float32),
            pltpu.VMEM((2, block * part, 2 * rows), jnp.bfloat16),
        ],
        1 << 31,
    )(place, modes, tables, decays, *befores)


def keep_inverse_kernel(steps, place, tables, *refs):
    keeps, out, scratch = refs[:CHUNKS], refs[CHUNKS], refs[CHUNKS + 1 :]
    part = keeps[0].shape[1]
    pitch = keeps[0].shape[0] // steps
    depth = scratch[0].shape[0]
    group = max(TILE // steps, 1)
    for at in range(0, out.shape[0], depth):
        split = scratch[at // depth % 2]
        for row in range(0, depth, TILE):
            cell = (at + row) // steps
            for chunk, keep in enumerate(keeps):
                cells = steps_of(keep, range(cell, cell + group), steps, pitch)
                store_split(split, (pl.ds(row, TILE),), chunk * part, cells)
        out[pl.ds(at, depth)] = dot(split[...], tables[place[1]])


def keep_inverse(place, keeps, tables, rows, steps):
    half = keeps[0].shape[1] * CHUNKS
    return call(
        functools.partial(keep_inverse_kernel, steps),
        "keep_inverse",
        [IN_VMEM] * (1 + CHUNKS),
        IN_VMEM,
        floats(rows * steps, half),
        [pltpu.VMEM((rows * steps // 8, 2 * half), jnp.bfloat16)] * 2,
        1 << 31,
    )(place, tables, *keeps)


def inverse_second_kernel(place, tables, kept, *refs):
    gots, target, out, sems, scratch = (
        refs[:CHUNKS], refs[CHUNKS], refs[CHUNKS + 1], refs[CHUNKS + 2], refs[CHUNKS + 3 :]
    )
    cells, steps, width = out.shape
    half = width // 2
    part = half // CHUNKS
    pitch = gots[0].shape[0] // steps
    count = len(scratch) // 2
    pieces = sems.shape[0]
    piece = cells // pieces
    group = max(TILE // steps, 1)
    strip = place[1]
    sign = 1.0 - 2.0 * strip.astype(jnp.float32)

    def copy(at):
        here = pl.ds(at * piece, piece)
        return pltpu.make_async_copy(out.at[here], target.at[here], sems.at[at])

    lanes_reversed = reversal()

    def product(at):
        split, result = scratch[2 * (at % count) : 2 * (at % count) + 2]
        for row in range(0, piece, group):
            mirrors = [cells - 1 - at * piece - row - cell for cell in range(group)]
            for chunk, got in enumerate(gots):
                values = steps_of(got, mirrors, steps, pitch)
                store_split(split, (pl.ds(row * steps, TILE),), chunk * part, values)
        result[...] = dot(split[...], tables[1 - strip])

    def finish(at):
        result = scratch[2 * (at % count) + 1]
        for row in range(0, piece, group):
            first = kept[pl.ds((at * piece + row) * steps, TILE)]
            second = result[pl.ds(row * steps, TILE)]
            upper = sign * (first - second)
            parts = [
                lanes_reversed(upper[:, lane : lane + LANES]) for lane in range(0, half, LANES)
            ][::-1]
            whole = jnp.concatenate([first + second, *parts], axis=1)
            out[pl.ds(at * piece + row, group)] = whole.reshape(group, TILE // group, width)
        copy(at).start()

    for at in range(pieces):
        product(at)
        if at:
            finish(at - 1)
    finish(pieces - 1)
    for at in range(pieces):
        copy(at).wait()


def inverse_second(place, kept, gots, tables, steps):
    rows, half = kept.shape[0] // steps, kept.shape[1]
    piece, pieces = min(32, rows // 2), 2
    depth = steps * piece
    return call(
        inverse_second_kernel,
        "inverse_second",
        [IN_VMEM] * (2 + CHUNKS),
        IN_HBM,
        floats(rows, steps, 2 * half),
        [pltpu.VMEM((rows, steps, 2 * half), jnp.float32), pltpu.SemaphoreType.DMA((rows // piece,))]
        + [pltpu.VMEM((depth, 2 * half), jnp.bfloat16), pltpu.VMEM((depth, half), jnp.float32)]
        * pieces,
        1 << 32,
    )(place, tables, kept, *gots)


def swapped(block):
    return lax.ppermute(block, "space", [(0, 1), (1, 0)])


def with_partner(block, distance):
    slabs = lax.axis_size("tm")
    return lax.ppermute(block, "tm", [(slab, slab ^ distance) for slab in range(slabs)])


def among_ranks(blocks):
    return [blocks[0]] + [with_partner(block, at) for at, block in enumerate(blocks) if at]


def by_chunk(table):
    strips, _, half, rows = table.shape
    parts = table.reshape(strips, 2, CHUNKS, half // CHUNKS, rows)
    return np.swapaxes(parts, 1, 2).reshape(strips, CHUNKS, 2 * half // CHUNKS, rows)


def shards(iterate, initial):
    rows, steps, width = iterate.shape
    slabs = lax.axis_size("tm")
    total = rows * lax.axis_size("space")
    place = jnp.stack([lax.axis_index("tm"), lax.axis_index("space")]).astype(jnp.int32)
    second = second_tables(width)
    first = first_tables(total)
    decay = decay_tables(total, width)
    slab_decay = decay**steps
    half_decay = slab_decay ** ranks(slabs)
    gain = 1.0 / (1.0 - circulant_alpha * half_decay * half_decay)
    closing = constant(
        np.stack([by_chunk(table) for table in (slab_decay, half_decay, gain)], axis=2)
    )
    first_table, decays = split_constant(first), constant(decay)
    second_table = split_constant(REACTION_STEP * second)
    sums, sends = forward_second(place, iterate, initial, second_table)
    gots = [swapped(send) for send in sends]
    keeps = keep_second(place, sums, second_table, steps)
    modes, befores = [], []
    for chunk in range(CHUNKS):
        own_modes, lasts = forward_first(
            place, chunk, keeps[chunk], gots[chunk], first_table, decays, slabs
        )
        modes.append(own_modes)
        ordered, near = half_sum(place, chunk, among_ranks(lasts), closing, slabs)
        far = with_partner(near, ranks(slabs))
        befores.append(among_ranks(close(place, chunk, ordered, near, far, closing, slabs)))
    inverse_table = split_constant(np.swapaxes(first, 2, 3))
    keeps, sends = zip(
        *(
            inverse_first(place, chunk, modes[chunk], befores[chunk], inverse_table, decays, slabs)
            for chunk in range(CHUNKS)
        )
    )
    gots = [swapped(send) for send in sends]
    inverse_table = split_constant(np.swapaxes(second, 1, 2))
    kept = keep_inverse(place, keeps, inverse_table, rows, steps)
    return inverse_second(place, kept, gots, inverse_table, steps)


def solution(mesh):
    return jax.shard_map(
        shards,
        mesh=mesh,
        in_specs=(P(("group", "space"), "tm", None), P(("group", "space"), None)),
        out_specs=P(("group", "space"), "tm", None),
        check_vma=False,
    )
```

```python
import functools
import math

import jax
import jax.numpy as jnp
import numpy as np
from jax import lax
from jax.experimental import pallas as pl
from jax.experimental.pallas import tpu as pltpu
from jax.sharding import PartitionSpec as P

circulant_alpha = 0.01
DIFFUSION = 2.0
REACTION_STEP = 0.5
VMEM_BYTES = 24 * 1024 * 1024
LANES = 128
SUBLANES = 8
TILE = 16
CHUNKS = 2


def sine_table(row_index, column_index, length):
    product = np.outer(row_index + 1, column_index + 1) % (2 * (length + 1))
    return math.sqrt(2.0 / (length + 1)) * np.sin(product * (math.pi / (length + 1)))


def stencil_eigen(mode_index, length):
    return 4.0 * np.sin((mode_index + 1) * (math.pi / (2.0 * (length + 1)))) ** 2


def second_tables(width):
    half = width // 2
    return np.stack([sine_table(np.arange(half), np.arange(s, width, 2), width) for s in (0, 1)])


def first_tables(total):
    rows = total // 2
    return np.stack(
        [
            np.stack(
                [sine_table(s * rows + np.arange(rows), np.arange(c, total, 2), total) for c in (0, 1)]
            )
            for s in (0, 1)
        ]
    )


def decay_tables(total, width):
    first, second = stencil_eigen(np.arange(total), total), stencil_eigen(np.arange(width), width)
    decay = 1.0 / (1.0 + DIFFUSION * (second[:, None] + first[None, :]))
    return np.stack([np.stack([decay[s::2, c::2] for c in (0, 1)]) for s in (0, 1)])


def constant(table):
    return jnp.asarray(np.asarray(table, np.float32))


def split_constant(table):
    table = np.asarray(table, np.float32)
    high = table.astype(jnp.bfloat16)
    low = (table - high.astype(np.float32)).astype(jnp.bfloat16)
    return jnp.asarray(np.concatenate([high, high, low], axis=-2))


def store_split(ref, at, lane, block):
    depth = ref.shape[-1] // 2
    width = block.shape[-1]
    high = block.astype(jnp.bfloat16)
    low = (block - high.astype(jnp.float32)).astype(jnp.bfloat16)
    ref[(*at, pl.ds(lane, width))] = high
    ref[(*at, pl.ds(depth + lane, width))] = low


def dot(split, table):
    rows = jnp.concatenate([split, split[:, : split.shape[1] // 2]], axis=1)
    return jnp.dot(rows, table, preferred_element_type=jnp.float32)


ALONG_LANES = lax.GatherDimensionNumbers(
    offset_dims=(),
    collapsed_slice_dims=(1,),
    start_index_map=(1,),
    operand_batching_dims=(0,),
    start_indices_batching_dims=(0,),
)


def reversal():
    index = LANES - 1 - lax.broadcasted_iota(jnp.int32, (TILE, LANES), 1)
    index = index.reshape(TILE, LANES, 1)
    return lambda block: lax.gather(
        block, index, ALONG_LANES, (1, 1), mode=lax.GatherScatterMode.PROMISE_IN_BOUNDS
    )


def store_rows_reversed(ref, start, block):
    rows, width = block.shape
    index = SUBLANES - 1 - lax.broadcasted_iota(jnp.int32, (SUBLANES, width), 0)
    for row in range(0, rows, SUBLANES):
        to = pl.multiple_of(start + rows - SUBLANES - row, SUBLANES)
        ref[pl.ds(to, SUBLANES), :] = jnp.take_along_axis(
            block[row : row + SUBLANES], index, axis=0, mode="promise_in_bounds"
        )


def pitch_of(cells):
    return cells + SUBLANES * (1 - cells // SUBLANES % 2)


def steps_of(ref, cells, steps, pitch):
    lines = [ref[pl.ds(cell, steps, stride=pitch), :] for cell in cells]
    return lines[0] if len(lines) == 1 else jnp.concatenate(lines, axis=0)


IN_VMEM = pl.BlockSpec(memory_space=pltpu.VMEM)
IN_HBM = pl.BlockSpec(memory_space=pltpu.HBM)
IN_SMEM = pl.BlockSpec(memory_space=pltpu.SMEM)


def in_hbm(array):
    return pltpu.with_memory_space_constraint(array, pltpu.HBM)


def floats(*shape):
    return jax.ShapeDtypeStruct(shape, jnp.float32)


def call(kernel, name, in_specs, out_specs, out_shape, scratch, flops):
    return pl.pallas_call(
        kernel,
        in_specs=[IN_SMEM, *in_specs],
        out_specs=out_specs,
        scratch_shapes=scratch,
        out_shape=out_shape,
        compiler_params=pltpu.CompilerParams(vmem_limit_bytes=VMEM_BYTES),
        cost_estimate=pl.CostEstimate(flops=flops, bytes_accessed=1 << 23, transcendentals=0),
        name=name,
    )


def forward_second_kernel(place, field_in, initial_in, tables, sums, *refs):
    sends, refs = refs[:CHUNKS], refs[CHUNKS:]
    field, initial, table, sems, table_sem, *scratch = refs
    cells, steps, width = field.shape
    half = width // 2
    part = half // CHUNKS
    pieces = sems.shape[0]
    piece = cells // pieces
    group = max(TILE // steps, 1)
    pitch = sends[0].shape[0] // (steps + 1)
    body = piece * steps
    is_first = place[0] == 0
    sign = 1.0 - 2.0 * place[1].astype(jnp.float32)

    def copies(at):
        here = pl.ds(at * piece, piece)
        return [
            pltpu.make_async_copy(source.at[here], to.at[here], sems.at[at, which])
            for which, (source, to) in enumerate(((field_in, field), (initial_in, initial)))
        ]

    table_copy = pltpu.make_async_copy(tables.at[1 - place[1]], table, table_sem)

    def start(first, last):
        for at in range(first, min(last, pieces)):
            for copy in copies(at):
                copy.start()

    lanes_reversed = reversal()

    def put(other, at, sums_at, cells):
        lower = cells[:, :half]
        upper = sign * jnp.concatenate(
            [lanes_reversed(cells[:, lane : lane + LANES]) for lane in range(half, width, LANES)][::-1],
            axis=1,
        )
        sums[pl.ds(sums_at, TILE), :] = lower + upper
        store_split(other, (pl.ds(at, TILE),), 0, lower - upper)

    def prepare(at):
        split = scratch[at % len(scratch)]
        cell = at * piece
        for row in range(0, piece, group):
            values = field[pl.ds(cell + row, group)]
            force = values - values * values * values
            put(split, row * steps, (cell + row) * steps, force.reshape(TILE, width))
        for row in range(0, piece, TILE):
            here = pl.ds(cell + row, TILE)
            ends = jnp.where(is_first, initial[here], field[here, steps - 1, :])
            put(split, body + row, cells * steps + cell + row, ends)

    def transform(at):
        sent = dot(scratch[at % len(scratch)][...], table[...])
        first = cells - (at + 1) * piece
        for chunk, send in enumerate(sends):
            lanes = slice(chunk * part, (chunk + 1) * part)
            for row in range(piece):
                line = sent[row * steps : (row + 1) * steps, lanes]
                send[pl.ds(first + piece - 1 - row, steps, stride=pitch), :] = line
            store_rows_reversed(send, pitch * steps + first, sent[body:, lanes])

    start(0, 1)
    table_copy.start()
    start(1, 2)
    for at in range(pieces):
        for copy in copies(at):
            copy.wait()
        start(2 * at + 2, 2 * at + 4)
        if at == 1:
            table_copy.wait()
        if at:
            transform(at - 1)
        prepare(at)
    transform(pieces - 1)


def forward_second(place, field, initial, tables):
    rows, steps, width = field.shape
    half = width // 2
    piece, pieces = min(32, rows // 2), 2
    outs = call(
        forward_second_kernel,
        "forward_second",
        [IN_HBM] * 3,
        [IN_VMEM] * (1 + CHUNKS),
        [floats((steps + 1) * rows, half)]
        + [floats((steps + 1) * pitch_of(rows), half // CHUNKS)] * CHUNKS,
        [
            pltpu.VMEM(field.shape, jnp.float32),
            pltpu.VMEM(initial.shape, jnp.float32),
            pltpu.VMEM(tables.shape[1:], jnp.bfloat16),
            pltpu.SemaphoreType.DMA((rows // piece, 2)),
            pltpu.SemaphoreType.DMA,
        ]
        + [pltpu.VMEM(((steps + 1) * piece, 2 * half), jnp.bfloat16)] * pieces,
        1 << 32,
    )(place, in_hbm(field), in_hbm(initial), in_hbm(tables))
    return outs[0], outs[1:]


def keep_second_kernel(steps, place, tables, sums, *refs):
    keeps, scratch = refs[:CHUNKS], refs[CHUNKS:]
    depth = scratch[0].shape[0]
    cells = sums.shape[0] // (steps + 1)
    pitch = keeps[0].shape[0] // (steps + 1)
    for at in range(0, sums.shape[0], depth):
        split = scratch[at // depth % 2]
        for row in range(0, depth, TILE):
            store_split(split, (pl.ds(row, TILE),), 0, sums[pl.ds(at + row, TILE)])
        result = dot(split[...], tables[place[1]])
        for chunk, keep in enumerate(keeps):
            part = keep.shape[1]
            lanes = slice(chunk * part, (chunk + 1) * part)
            body = max(0, min(depth, cells * steps - at))
            for row in range(0, body, steps):
                line = result[row : row + steps, lanes]
                keep[pl.ds((at + row) // steps, steps, stride=pitch), :] = line
            if body < depth:
                ends = pl.ds(pitch * steps + at + body - cells * steps, depth - body)
                keep[ends, :] = result[body:, lanes]


def keep_second(place, sums, tables, steps):
    rows, half = sums.shape
    shape = ((steps + 1) * pitch_of(rows // (steps + 1)), half // CHUNKS)
    return call(
        functools.partial(keep_second_kernel, steps),
        "keep_second",
        [IN_VMEM] * 2,
        [IN_VMEM] * CHUNKS,
        [floats(*shape)] * CHUNKS,
        [pltpu.VMEM((rows // 8, 2 * half), jnp.bfloat16)] * 2,
        1 << 31,
    )(place, tables, sums)


def ranks(slabs):
    return slabs // 2


def by_distance(blocks):
    return [blocks[0], *blocks[:0:-1]]


def forward_first_kernel(slabs, chunk, place, keep, got, table, decay, modes, *refs):
    size = ranks(slabs)
    lasts, (state, split, extra) = refs[:size], refs[size:]
    steps, _, part, rows = modes.shape
    pitch = keep.shape[0] // (steps + 1)
    block = split.shape[1] // part - 1
    strip = place[1]
    is_first = jnp.where(place[0] == 0, 1.0 / REACTION_STEP, 0.0)
    is_last = jnp.where(place[0] == slabs - 1, 1.0 / REACTION_STEP, 0.0)
    state[...] = jnp.zeros_like(state)
    for step in range(0, steps, block):
        count = block if step else block + 1
        for c in (0, 1):
            for at in range(count):
                from_step = steps if at == block else step + at
                cells_at = pl.ds(from_step * pitch, rows)
                near, far = keep[cells_at], got[cells_at]
                cells = near - far if c else near + far
                store_split(split, (c, pl.ds(at * part, part)), 0, cells.T)
            result = dot(split[c, pl.ds(0, count * part)], table[strip, c])
            if step == 0:
                extra[c] = result[block * part :]
                modes[0, c] = result[:part] + is_first * result[block * part :]
                modes[pl.ds(1, block - 1), c] = result[part : block * part].reshape(block - 1, part, rows)
            else:
                modes[pl.ds(step, block), c] = result.reshape(block, part, rows)
        for c in (0, 1):
            for row in range(0, part, TILE):
                tile, at_state = pl.ds(row, TILE), pl.ds(c * part + row, TILE)
                value = state[at_state]
                rate = decay[strip, c, pl.ds(chunk * part + row, TILE)]
                for at in range(block):
                    value = rate * (value + modes[step + at, c, tile])
                state[at_state] = value
    for c in (0, 1):
        at_state = pl.ds(c * part, part)
        state[at_state] = state[at_state] - is_last * extra[c]
    rank = lax.rem(place[0], size)
    share = 2 * part // size
    for partner in range(size):
        at = pl.multiple_of((rank ^ partner) * share, share)
        lasts[partner][...] = state[pl.ds(at, share)]


def forward_first(place, chunk, keep, got, tables, decays, slabs):
    rows, part = tables.shape[-1], keep.shape[1]
    steps = keep.shape[0] // pitch_of(rows) - 1
    block = min(8, steps)
    size = ranks(slabs)
    share = 2 * part // size
    outs = call(
        functools.partial(forward_first_kernel, slabs, chunk),
        "forward_first",
        [IN_VMEM] * 4,
        [IN_VMEM] * (1 + size),
        [floats(steps, 2, part, rows)] + [floats(share, rows)] * size,
        [
            pltpu.VMEM((2 * part, rows), jnp.float32),
            pltpu.VMEM((2, (block + 1) * part, 2 * rows), jnp.bfloat16),
            pltpu.VMEM((2, part, rows), jnp.float32),
        ],
        1 << 31,
    )(place, keep, got, tables, decays)
    return outs[0], outs[1:]


def half_sum_kernel(slabs, chunk, place, closing, *refs):
    size = ranks(slabs)
    lasts, ordered, total = by_distance(refs[:size]), refs[size], refs[size + 1]
    share = total.shape[0]
    rank = lax.rem(place[0], size)
    decay = closing[place[1], chunk, 0, pl.ds(pl.multiple_of(rank * share, share), share)]
    for partner in range(size):
        ordered[rank ^ partner] = lasts[partner][...]
    state = ordered[0]
    for at in range(1, size):
        state = ordered[at] + decay * state
    total[...] = state


def half_sum(place, chunk, lasts, closing, slabs):
    size = ranks(slabs)
    share, rows = lasts[0].shape
    return call(
        functools.partial(half_sum_kernel, slabs, chunk),
        "half_sum",
        [IN_VMEM] * (1 + size),
        [IN_VMEM] * 2,
        [floats(size, share, rows), floats(share, rows)],
        [],
        1 << 20,
    )(place, closing, *by_distance(lasts))


def close_kernel(slabs, chunk, place, closing, ordered, near, far, *refs):
    size = ranks(slabs)
    befores, states = refs[:size], refs[size]
    share = near.shape[0]
    rank = lax.rem(place[0], size)
    at_share = pl.ds(pl.multiple_of(rank * share, share), share)
    decay, half_decay, gain = (closing[place[1], chunk, at, at_share] for at in range(3))
    entering = jnp.where(place[0] < size, circulant_alpha, 1.0)
    state = gain * (entering * far[...] + circulant_alpha * half_decay * near[...])
    for at in range(size):
        states[at] = state
        if at < size - 1:
            state = ordered[at] + decay * state
    for partner in range(size):
        befores[partner][...] = states[rank ^ partner]


def close(place, chunk, ordered, near, far, closing, slabs):
    size, share, rows = ordered.shape
    return call(
        functools.partial(close_kernel, slabs, chunk),
        "close",
        [IN_VMEM] * 4,
        [IN_VMEM] * size,
        [floats(share, rows)] * size,
        [pltpu.VMEM((size, share, rows), jnp.float32)],
        1 << 20,
    )(place, closing, ordered, near, far)


def inverse_first_kernel(slabs, chunk, place, modes, table, decay, *refs):
    size = ranks(slabs)
    befores, (keep, send, state, split) = by_distance(refs[:size]), refs[size:]
    steps, _, part, rows = modes.shape
    pitch = keep.shape[0] // steps
    block = split.shape[1] // part
    strip = place[1]
    rank = lax.rem(place[0], size)
    share = 2 * part // size
    for partner in range(size):
        at = pl.multiple_of((rank ^ partner) * share, share)
        state[pl.ds(at, share)] = befores[partner][...]
    for step in range(0, steps, block):
        results = []
        for c in (0, 1):
            for row in range(0, part, TILE):
                tile, at_state = pl.ds(row, TILE), pl.ds(c * part + row, TILE)
                value = state[at_state]
                rate = decay[strip, c, pl.ds(chunk * part + row, TILE)]
                for at in range(block):
                    value = rate * (value + modes[step + at, c, tile])
                    store_split(split, (c, pl.ds(at * part + row, TILE)), 0, value)
                state[at_state] = value
            results.append(dot(split[c], table[strip, c]))
        even, odd = results
        for at in range(block):
            piece = slice(at * part, (at + 1) * part)
            cells_at = pl.ds((step + at) * pitch, rows)
            keep[cells_at, :] = (even[piece] + odd[piece]).T
            send[cells_at, :] = (even[piece] - odd[piece]).T


def inverse_first(place, chunk, modes, befores, tables, decays, slabs):
    steps, _, part, rows = modes.shape
    block = min(8, steps)
    return call(
        functools.partial(inverse_first_kernel, slabs, chunk),
        "inverse_first",
        [IN_VMEM] * (3 + len(befores)),
        [IN_VMEM] * 2,
        [floats(steps * pitch_of(rows), part)] * 2,
        [
            pltpu.VMEM((2 * part, rows), jnp.float32),
            pltpu.VMEM((2, block * part, 2 * rows), jnp.bfloat16),
        ],
        1 << 31,
    )(place, modes, tables, decays, *by_distance(befores))


def keep_inverse_kernel(steps, place, tables, *refs):
    keeps, out, scratch = refs[:CHUNKS], refs[CHUNKS], refs[CHUNKS + 1 :]
    part = keeps[0].shape[1]
    pitch = keeps[0].shape[0] // steps
    depth = scratch[0].shape[0]
    group = max(TILE // steps, 1)
    for at in range(0, out.shape[0], depth):
        split = scratch[at // depth % 2]
        for row in range(0, depth, TILE):
            cell = (at + row) // steps
            for chunk, keep in enumerate(keeps):
                cells = steps_of(keep, range(cell, cell + group), steps, pitch)
                store_split(split, (pl.ds(row, TILE),), chunk * part, cells)
        out[pl.ds(at, depth)] = dot(split[...], tables[place[1]])


def keep_inverse(place, keeps, tables, rows, steps):
    half = keeps[0].shape[1] * CHUNKS
    return call(
        functools.partial(keep_inverse_kernel, steps),
        "keep_inverse",
        [IN_VMEM] * (1 + CHUNKS),
        IN_VMEM,
        floats(rows * steps, half),
        [pltpu.VMEM((rows * steps // 8, 2 * half), jnp.bfloat16)] * 2,
        1 << 31,
    )(place, tables, *keeps)


def inverse_second_kernel(place, tables, kept, *refs):
    gots, target, out, sems, scratch = (
        refs[:CHUNKS], refs[CHUNKS], refs[CHUNKS + 1], refs[CHUNKS + 2], refs[CHUNKS + 3 :]
    )
    cells, steps, width = out.shape
    half = width // 2
    part = half // CHUNKS
    pitch = gots[0].shape[0] // steps
    count = len(scratch) // 2
    piece = scratch[0].shape[0] // steps
    pieces = cells // piece
    flight = cells // sems.shape[0]
    group = max(TILE // steps, 1)
    strip = place[1]
    sign = 1.0 - 2.0 * strip.astype(jnp.float32)

    def copy(at):
        here = pl.ds(at * flight, flight)
        return pltpu.make_async_copy(out.at[here], target.at[here], sems.at[at])

    lanes_reversed = reversal()

    def product(at):
        split, result = scratch[2 * (at % count) : 2 * (at % count) + 2]
        for row in range(0, piece, group):
            mirrors = [cells - 1 - at * piece - row - cell for cell in range(group)]
            for chunk, got in enumerate(gots):
                values = steps_of(got, mirrors, steps, pitch)
                store_split(split, (pl.ds(row * steps, TILE),), chunk * part, values)
        result[...] = dot(split[...], tables[1 - strip])

    def finish(at):
        result = scratch[2 * (at % count) + 1]
        for row in range(0, piece, group):
            first = kept[pl.ds((at * piece + row) * steps, TILE)]
            second = result[pl.ds(row * steps, TILE)]
            upper = sign * (first - second)
            parts = [
                lanes_reversed(upper[:, lane : lane + LANES]) for lane in range(0, half, LANES)
            ][::-1]
            whole = jnp.concatenate([first + second, *parts], axis=1)
            out[pl.ds(at * piece + row, group)] = whole.reshape(group, TILE // group, width)
            done = at * piece + row + group
            if done % flight == 0:
                copy(done // flight - 1).start()

    for at in range(pieces):
        product(at)
        if at:
            finish(at - 1)
    finish(pieces - 1)
    for at in range(sems.shape[0]):
        copy(at).wait()


def inverse_second(place, kept, gots, tables, steps):
    rows, half = kept.shape[0] // steps, kept.shape[1]
    piece, pieces = min(32, rows // 2), 2
    depth = steps * piece
    return call(
        inverse_second_kernel,
        "inverse_second",
        [IN_VMEM] * (2 + CHUNKS),
        IN_HBM,
        floats(rows, steps, 2 * half),
        [
            pltpu.VMEM((rows, steps, 2 * half), jnp.float32),
            pltpu.SemaphoreType.DMA((2 * rows // piece,)),
        ]
        + [pltpu.VMEM((depth, 2 * half), jnp.bfloat16), pltpu.VMEM((depth, half), jnp.float32)]
        * pieces,
        1 << 32,
    )(place, tables, kept, *gots)


def swapped(block):
    return lax.ppermute(block, "space", [(0, 1), (1, 0)])


def with_partner(block, distance):
    slabs = lax.axis_size("tm")
    return lax.ppermute(block, "tm", [(slab, slab ^ distance) for slab in range(slabs)])


def among_ranks(blocks):
    return [blocks[0]] + [with_partner(block, at) for at, block in enumerate(blocks) if at]


def by_chunk(table):
    strips, _, half, rows = table.shape
    parts = table.reshape(strips, 2, CHUNKS, half // CHUNKS, rows)
    return np.swapaxes(parts, 1, 2).reshape(strips, CHUNKS, 2 * half // CHUNKS, rows)


def shards(iterate, initial):
    rows, steps, width = iterate.shape
    slabs = lax.axis_size("tm")
    total = rows * lax.axis_size("space")
    place = jnp.stack([lax.axis_index("tm"), lax.axis_index("space")]).astype(jnp.int32)
    second = second_tables(width)
    first = first_tables(total)
    decay = decay_tables(total, width)
    slab_decay = decay**steps
    half_decay = slab_decay ** ranks(slabs)
    gain = 1.0 / (1.0 - circulant_alpha * half_decay * half_decay)
    closing = constant(
        np.stack([by_chunk(table) for table in (slab_decay, half_decay, gain)], axis=2)
    )
    first_table, decays = split_constant(first), constant(decay)
    second_table = split_constant(REACTION_STEP * second)
    sums, sends = forward_second(place, iterate, initial, second_table)
    gots = [swapped(send) for send in sends]
    keeps = keep_second(place, sums, second_table, steps)
    modes, befores = [], []
    for chunk in range(CHUNKS):
        own_modes, lasts = forward_first(
            place, chunk, keeps[chunk], gots[chunk], first_table, decays, slabs
        )
        modes.append(own_modes)
        ordered, near = half_sum(place, chunk, among_ranks(lasts), closing, slabs)
        far = with_partner(near, ranks(slabs))
        befores.append(among_ranks(close(place, chunk, ordered, near, far, closing, slabs)))
    inverse_table = split_constant(np.swapaxes(first, 2, 3))
    keeps, sends = zip(
        *(
            inverse_first(place, chunk, modes[chunk], befores[chunk], inverse_table, decays, slabs)
            for chunk in range(CHUNKS)
        )
    )
    gots = [swapped(send) for send in sends]
    inverse_table = split_constant(np.swapaxes(second, 1, 2))
    kept = keep_inverse(place, keeps, inverse_table, rows, steps)
    return inverse_second(place, kept, gots, inverse_table, steps)


def solution(mesh):
    return jax.shard_map(
        shards,
        mesh=mesh,
        in_specs=(P(("group", "space"), "tm", None), P(("group", "space"), None)),
        out_specs=P(("group", "space"), "tm", None),
        check_vma=False,
    )
```

```python
import functools
import math

import jax
import jax.numpy as jnp
import numpy as np
from jax import lax
from jax.experimental import pallas as pl
from jax.experimental.pallas import tpu as pltpu
from jax.sharding import PartitionSpec as P

circulant_alpha = 0.01
DIFFUSION = 2.0
REACTION_STEP = 0.5
VMEM_BYTES = 24 * 1024 * 1024
LANES = 128
SUBLANES = 8
TILE = 16
CHUNKS = 2


def sine_table(row_index, column_index, length):
    product = np.outer(row_index + 1, column_index + 1) % (2 * (length + 1))
    return math.sqrt(2.0 / (length + 1)) * np.sin(product * (math.pi / (length + 1)))


def stencil_eigen(mode_index, length):
    return 4.0 * np.sin((mode_index + 1) * (math.pi / (2.0 * (length + 1)))) ** 2


def second_tables(width):
    cells = np.arange(width)
    return np.stack([sine_table(cells, np.arange(s, width, 2), width) for s in (0, 1)])


def first_tables(total):
    rows = total // 2
    return np.stack(
        [
            np.stack(
                [sine_table(s * rows + np.arange(rows), np.arange(c, total, 2), total) for c in (0, 1)]
            )
            for s in (0, 1)
        ]
    )


def decay_tables(total, width):
    first, second = stencil_eigen(np.arange(total), total), stencil_eigen(np.arange(width), width)
    decay = 1.0 / (1.0 + DIFFUSION * (second[:, None] + first[None, :]))
    return np.stack([np.stack([decay[s::2, c::2] for c in (0, 1)]) for s in (0, 1)])


def constant(table):
    return jnp.asarray(np.asarray(table, np.float32))


def split_constant(table):
    table = np.asarray(table, np.float32)
    high = table.astype(jnp.bfloat16)
    low = (table - high.astype(np.float32)).astype(jnp.bfloat16)
    return np.concatenate([high, high, low], axis=-2)


def mixed_constant(tables):
    width = 2 * tables.shape[2]
    quarter = width // 4
    outer = tables[:, [*range(quarter), *range(width - quarter, width)]]
    parts = [split_constant(outer), split_constant(tables[:, quarter : 2 * quarter])]
    return np.concatenate(parts, axis=1)


def mixed_dot(outer, inner, table):
    rows = [outer, outer[:, : outer.shape[1] // 2], inner, inner[:, : inner.shape[1] // 2]]
    return jnp.dot(jnp.concatenate(rows, axis=1), table, preferred_element_type=jnp.float32)


def store_split(ref, at, lane, block):
    depth = ref.shape[-1] // 2
    width = block.shape[-1]
    high = block.astype(jnp.bfloat16)
    low = (block - high.astype(jnp.float32)).astype(jnp.bfloat16)
    ref[(*at, pl.ds(lane, width))] = high
    ref[(*at, pl.ds(depth + lane, width))] = low


def dot(split, table):
    rows = jnp.concatenate([split, split[:, : split.shape[1] // 2]], axis=1)
    return jnp.dot(rows, table, preferred_element_type=jnp.float32)


ALONG_LANES = lax.GatherDimensionNumbers(
    offset_dims=(),
    collapsed_slice_dims=(1,),
    start_index_map=(1,),
    operand_batching_dims=(0,),
    start_indices_batching_dims=(0,),
)


def reversal():
    index = LANES - 1 - lax.broadcasted_iota(jnp.int32, (TILE, LANES), 1)
    index = index.reshape(TILE, LANES, 1)
    return lambda block: lax.gather(
        block, index, ALONG_LANES, (1, 1), mode=lax.GatherScatterMode.PROMISE_IN_BOUNDS
    )


def store_rows_reversed(ref, start, block):
    rows, width = block.shape
    index = SUBLANES - 1 - lax.broadcasted_iota(jnp.int32, (SUBLANES, width), 0)
    for row in range(0, rows, SUBLANES):
        to = pl.multiple_of(start + rows - SUBLANES - row, SUBLANES)
        ref[pl.ds(to, SUBLANES), :] = jnp.take_along_axis(
            block[row : row + SUBLANES], index, axis=0, mode="promise_in_bounds"
        )


def pitch_of(cells):
    return cells + SUBLANES * (1 - cells // SUBLANES % 2)


def steps_of(ref, cells, steps, pitch):
    lines = [ref[pl.ds(cell, steps, stride=pitch), :] for cell in cells]
    return lines[0] if len(lines) == 1 else jnp.concatenate(lines, axis=0)


IN_VMEM = pl.BlockSpec(memory_space=pltpu.VMEM)
IN_HBM = pl.BlockSpec(memory_space=pltpu.HBM)
IN_SMEM = pl.BlockSpec(memory_space=pltpu.SMEM)


def in_hbm(array):
    return pltpu.with_memory_space_constraint(array, pltpu.HBM)


def floats(*shape):
    return jax.ShapeDtypeStruct(shape, jnp.float32)


def call(kernel, name, in_specs, out_specs, out_shape, scratch, flops):
    return pl.pallas_call(
        kernel,
        in_specs=[IN_SMEM, *in_specs],
        out_specs=out_specs,
        scratch_shapes=scratch,
        out_shape=out_shape,
        compiler_params=pltpu.CompilerParams(vmem_limit_bytes=VMEM_BYTES),
        cost_estimate=pl.CostEstimate(flops=flops, bytes_accessed=1 << 23, transcendentals=0),
        name=name,
    )


def forward_second_kernel(place, field_in, initial_in, tables, outer, sums, *refs):
    sends, refs = refs[:CHUNKS], refs[CHUNKS:]
    field, initial, table, sems, table_sem, *scratch = refs
    cells, steps, width = field.shape
    half = width // 2
    part = half // CHUNKS
    pieces = sems.shape[0]
    piece = cells // pieces
    group = max(TILE // steps, 1)
    pitch = sends[0].shape[0] // (steps + 1)
    body = piece * steps
    is_first = place[0] == 0
    sign = 1.0 - 2.0 * place[1].astype(jnp.float32)

    def copies(at):
        here = pl.ds(at * piece, piece)
        return [
            pltpu.make_async_copy(source.at[here], to.at[here], sems.at[at, which])
            for which, (source, to) in enumerate(((field_in, field), (initial_in, initial)))
        ]

    table_copy = pltpu.make_async_copy(tables.at[1 - place[1]], table, table_sem)

    def start(first, last):
        for at in range(first, min(last, pieces)):
            for copy in copies(at):
                copy.start()

    lanes_reversed = reversal()

    def put(other, at, to, cells):
        quarter = width // 4
        to = pl.ds(to, TILE)
        store_split(outer, (to,), 0, cells[:, :quarter])
        store_split(outer, (to,), quarter, cells[:, width - quarter :])
        lower = cells[:, quarter:half]
        upper = [
            lanes_reversed(cells[:, lane : lane + LANES])
            for lane in range(half, width - quarter, LANES)
        ]
        upper = sign * jnp.concatenate(upper[::-1], axis=1)
        sums[to, :] = lower + upper
        store_split(other, (pl.ds(at, TILE),), 0, lower - upper)

    def prepare(at):
        split = scratch[at % len(scratch)]
        cell = at * piece
        for row in range(0, piece, group):
            values = field[pl.ds(cell + row, group)]
            force = values - values * values * values
            put(split, row * steps, (cell + row) * steps, force.reshape(TILE, width))
        for row in range(0, piece, TILE):
            here = pl.ds(cell + row, TILE)
            ends = jnp.where(is_first, initial[here], field[here, steps - 1, :])
            put(split, body + row, cells * steps + cell + row, ends)

    def transform(at):
        here = [outer[pl.ds(at * body, body)], outer[pl.ds(cells * steps + at * piece, piece)]]
        sent = mixed_dot(
            jnp.concatenate(here, axis=0), scratch[at % len(scratch)][...], table[...]
        )
        first = cells - (at + 1) * piece
        for chunk, send in enumerate(sends):
            lanes = slice(chunk * part, (chunk + 1) * part)
            for row in range(piece):
                line = sent[row * steps : (row + 1) * steps, lanes]
                send[pl.ds(first + piece - 1 - row, steps, stride=pitch), :] = line
            store_rows_reversed(send, pitch * steps + first, sent[body:, lanes])

    start(0, 1)
    table_copy.start()
    start(1, 2)
    for at in range(pieces):
        for copy in copies(at):
            copy.wait()
        start(2 * at + 2, 2 * at + 4)
        if at == 1:
            table_copy.wait()
        if at:
            transform(at - 1)
        prepare(at)
    transform(pieces - 1)


def forward_second(place, field, initial, tables):
    rows, steps, width = field.shape
    half = width // 2
    piece, pieces = min(32, rows // 2), 2
    outs = call(
        forward_second_kernel,
        "forward_second",
        [IN_HBM] * 3,
        [IN_VMEM] * (2 + CHUNKS),
        [
            jax.ShapeDtypeStruct(((steps + 1) * rows, 2 * half), jnp.bfloat16),
            floats((steps + 1) * rows, half // 2),
        ]
        + [floats((steps + 1) * pitch_of(rows), half // CHUNKS)] * CHUNKS,
        [
            pltpu.VMEM(field.shape, jnp.float32),
            pltpu.VMEM(initial.shape, jnp.float32),
            pltpu.VMEM(tables.shape[1:], jnp.bfloat16),
            pltpu.SemaphoreType.DMA((rows // piece, 2)),
            pltpu.SemaphoreType.DMA,
        ]
        + [pltpu.VMEM(((steps + 1) * piece, half), jnp.bfloat16)] * pieces,
        1 << 32,
    )(place, in_hbm(field), in_hbm(initial), in_hbm(tables))
    return outs[0], outs[1], outs[2:]


def keep_second_kernel(steps, place, tables, outer, sums, *refs):
    keeps, scratch = refs[:CHUNKS], refs[CHUNKS:]
    depth = scratch[0].shape[0]
    cells = sums.shape[0] // (steps + 1)
    pitch = keeps[0].shape[0] // (steps + 1)
    for at in range(0, sums.shape[0], depth):
        split = scratch[at // depth % 2]
        for row in range(0, depth, TILE):
            store_split(split, (pl.ds(row, TILE),), 0, sums[pl.ds(at + row, TILE)])
        result = mixed_dot(outer[pl.ds(at, depth)], split[...], tables[place[1]])
        for chunk, keep in enumerate(keeps):
            part = keep.shape[1]
            lanes = slice(chunk * part, (chunk + 1) * part)
            body = max(0, min(depth, cells * steps - at))
            for row in range(0, body, steps):
                line = result[row : row + steps, lanes]
                keep[pl.ds((at + row) // steps, steps, stride=pitch), :] = line
            if body < depth:
                ends = pl.ds(pitch * steps + at + body - cells * steps, depth - body)
                keep[ends, :] = result[body:, lanes]


def keep_second(place, outer, sums, tables, steps):
    rows, half = outer.shape[0], tables.shape[2]
    shape = ((steps + 1) * pitch_of(rows // (steps + 1)), half // CHUNKS)
    return call(
        functools.partial(keep_second_kernel, steps),
        "keep_second",
        [IN_VMEM] * 3,
        [IN_VMEM] * CHUNKS,
        [floats(*shape)] * CHUNKS,
        [pltpu.VMEM((rows // 8, half), jnp.bfloat16)] * 2,
        1 << 31,
    )(place, tables, outer, sums)


def ranks(slabs):
    return slabs // 2


def by_distance(blocks):
    return [blocks[0], *blocks[:0:-1]]


def forward_first_kernel(slabs, chunk, place, keep, got, table, decay, modes, *refs):
    size = ranks(slabs)
    lasts, (state, split, extra) = refs[:size], refs[size:]
    steps, _, part, rows = modes.shape
    pitch = keep.shape[0] // (steps + 1)
    block = split.shape[1] // part - 1
    strip = place[1]
    is_first = jnp.where(place[0] == 0, 1.0 / REACTION_STEP, 0.0)
    is_last = jnp.where(place[0] == slabs - 1, 1.0 / REACTION_STEP, 0.0)
    state[...] = jnp.zeros_like(state)
    for step in range(0, steps, block):
        count = block if step else block + 1
        for c in (0, 1):
            for at in range(count):
                from_step = steps if at == block else step + at
                cells_at = pl.ds(from_step * pitch, rows)
                near, far = keep[cells_at], got[cells_at]
                cells = near - far if c else near + far
                store_split(split, (c, pl.ds(at * part, part)), 0, cells.T)
            result = dot(split[c, pl.ds(0, count * part)], table[strip, c])
            if step == 0:
                extra[c] = result[block * part :]
                modes[0, c] = result[:part] + is_first * result[block * part :]
                modes[pl.ds(1, block - 1), c] = result[part : block * part].reshape(block - 1, part, rows)
            else:
                modes[pl.ds(step, block), c] = result.reshape(block, part, rows)
        for c in (0, 1):
            for row in range(0, part, TILE):
                tile, at_state = pl.ds(row, TILE), pl.ds(c * part + row, TILE)
                value = state[at_state]
                rate = decay[strip, c, pl.ds(chunk * part + row, TILE)]
                for at in range(block):
                    value = rate * (value + modes[step + at, c, tile])
                state[at_state] = value
    for c in (0, 1):
        at_state = pl.ds(c * part, part)
        state[at_state] = state[at_state] - is_last * extra[c]
    rank = lax.rem(place[0], size)
    share = 2 * part // size
    for partner in range(size):
        at = pl.multiple_of((rank ^ partner) * share, share)
        lasts[partner][...] = state[pl.ds(at, share)]


def forward_first(place, chunk, keep, got, tables, decays, slabs):
    rows, part = tables.shape[-1], keep.shape[1]
    steps = keep.shape[0] // pitch_of(rows) - 1
    block = min(8, steps)
    size = ranks(slabs)
    share = 2 * part // size
    outs = call(
        functools.partial(forward_first_kernel, slabs, chunk),
        "forward_first",
        [IN_VMEM] * 4,
        [IN_VMEM] * (1 + size),
        [floats(steps, 2, part, rows)] + [floats(share, rows)] * size,
        [
            pltpu.VMEM((2 * part, rows), jnp.float32),
            pltpu.VMEM((2, (block + 1) * part, 2 * rows), jnp.bfloat16),
            pltpu.VMEM((2, part, rows), jnp.float32),
        ],
        1 << 31,
    )(place, keep, got, tables, decays)
    return outs[0], outs[1:]


def half_sum_kernel(slabs, chunk, place, closing, *refs):
    size = ranks(slabs)
    lasts, ordered, total = by_distance(refs[:size]), refs[size], refs[size + 1]
    share = total.shape[0]
    rank = lax.rem(place[0], size)
    decay = closing[place[1], chunk, 0, pl.ds(pl.multiple_of(rank * share, share), share)]
    for partner in range(size):
        ordered[rank ^ partner] = lasts[partner][...]
    state = ordered[0]
    for at in range(1, size):
        state = ordered[at] + decay * state
    total[...] = state


def half_sum(place, chunk, lasts, closing, slabs):
    size = ranks(slabs)
    share, rows = lasts[0].shape
    return call(
        functools.partial(half_sum_kernel, slabs, chunk),
        "half_sum",
        [IN_VMEM] * (1 + size),
        [IN_VMEM] * 2,
        [floats(size, share, rows), floats(share, rows)],
        [],
        1 << 20,
    )(place, closing, *by_distance(lasts))


def close_kernel(slabs, chunk, place, closing, ordered, near, far, *refs):
    size = ranks(slabs)
    befores, states = refs[:size], refs[size]
    share = near.shape[0]
    rank = lax.rem(place[0], size)
    at_share = pl.ds(pl.multiple_of(rank * share, share), share)
    decay, half_decay, gain = (closing[place[1], chunk, at, at_share] for at in range(3))
    entering = jnp.where(place[0] < size, circulant_alpha, 1.0)
    state = gain * (entering * far[...] + circulant_alpha * half_decay * near[...])
    for at in range(size):
        states[at] = state
        if at < size - 1:
            state = ordered[at] + decay * state
    for partner in range(size):
        befores[partner][...] = states[rank ^ partner]


def close(place, chunk, ordered, near, far, closing, slabs):
    size, share, rows = ordered.shape
    return call(
        functools.partial(close_kernel, slabs, chunk),
        "close",
        [IN_VMEM] * 4,
        [IN_VMEM] * size,
        [floats(share, rows)] * size,
        [pltpu.VMEM((size, share, rows), jnp.float32)],
        1 << 20,
    )(place, closing, ordered, near, far)


def inverse_first_kernel(slabs, chunk, place, modes, table, decay, *refs):
    size = ranks(slabs)
    befores, (keep, send, state, split) = by_distance(refs[:size]), refs[size:]
    steps, _, part, rows = modes.shape
    pitch = keep.shape[0] // steps
    block = split.shape[1] // part
    strip = place[1]
    rank = lax.rem(place[0], size)
    share = 2 * part // size
    for partner in range(size):
        at = pl.multiple_of((rank ^ partner) * share, share)
        state[pl.ds(at, share)] = befores[partner][...]
    for step in range(0, steps, block):
        results = []
        for c in (0, 1):
            for row in range(0, part, TILE):
                tile, at_state = pl.ds(row, TILE), pl.ds(c * part + row, TILE)
                value = state[at_state]
                rate = decay[strip, c, pl.ds(chunk * part + row, TILE)]
                for at in range(block):
                    value = rate * (value + modes[step + at, c, tile])
                    store_split(split, (c, pl.ds(at * part + row, TILE)), 0, value)
                state[at_state] = value
            results.append(dot(split[c], table[strip, c]))
        even, odd = results
        for at in range(block):
            piece = slice(at * part, (at + 1) * part)
            cells_at = pl.ds((step + at) * pitch, rows)
            keep[cells_at, :] = (even[piece] + odd[piece]).T
            send[cells_at, :] = (even[piece] - odd[piece]).T


def inverse_first(place, chunk, modes, befores, tables, decays, slabs):
    steps, _, part, rows = modes.shape
    block = min(8, steps)
    return call(
        functools.partial(inverse_first_kernel, slabs, chunk),
        "inverse_first",
        [IN_VMEM] * (3 + len(befores)),
        [IN_VMEM] * 2,
        [floats(steps * pitch_of(rows), part)] * 2,
        [
            pltpu.VMEM((2 * part, rows), jnp.float32),
            pltpu.VMEM((2, block * part, 2 * rows), jnp.bfloat16),
        ],
        1 << 31,
    )(place, modes, tables, decays, *by_distance(befores))


def keep_inverse_kernel(steps, place, tables, *refs):
    keeps, out, scratch = refs[:CHUNKS], refs[CHUNKS], refs[CHUNKS + 1 :]
    part = keeps[0].shape[1]
    pitch = keeps[0].shape[0] // steps
    depth = scratch[0].shape[0]
    group = max(TILE // steps, 1)
    for at in range(0, out.shape[0], depth):
        split = scratch[at // depth % 2]
        for row in range(0, depth, TILE):
            cell = (at + row) // steps
            for chunk, keep in enumerate(keeps):
                cells = steps_of(keep, range(cell, cell + group), steps, pitch)
                store_split(split, (pl.ds(row, TILE),), chunk * part, cells)
        out[pl.ds(at, depth)] = dot(split[...], tables[place[1]])


def keep_inverse(place, keeps, tables, rows, steps):
    half = keeps[0].shape[1] * CHUNKS
    return call(
        functools.partial(keep_inverse_kernel, steps),
        "keep_inverse",
        [IN_VMEM] * (1 + CHUNKS),
        IN_VMEM,
        floats(rows * steps, half),
        [pltpu.VMEM((rows * steps // 8, 2 * half), jnp.bfloat16)] * 2,
        1 << 31,
    )(place, tables, *keeps)


def inverse_second_kernel(place, tables, kept, *refs):
    gots, target, out, sems, scratch = (
        refs[:CHUNKS], refs[CHUNKS], refs[CHUNKS + 1], refs[CHUNKS + 2], refs[CHUNKS + 3 :]
    )
    cells, steps, width = out.shape
    half = width // 2
    part = half // CHUNKS
    pitch = gots[0].shape[0] // steps
    count = len(scratch) // 2
    piece = scratch[0].shape[0] // steps
    pieces = cells // piece
    flight = cells // sems.shape[0]
    group = max(TILE // steps, 1)
    strip = place[1]
    sign = 1.0 - 2.0 * strip.astype(jnp.float32)

    def copy(at):
        here = pl.ds(at * flight, flight)
        return pltpu.make_async_copy(out.at[here], target.at[here], sems.at[at])

    lanes_reversed = reversal()

    def product(at):
        split, result = scratch[2 * (at % count) : 2 * (at % count) + 2]
        for row in range(0, piece, group):
            mirrors = [cells - 1 - at * piece - row - cell for cell in range(group)]
            for chunk, got in enumerate(gots):
                values = steps_of(got, mirrors, steps, pitch)
                store_split(split, (pl.ds(row * steps, TILE),), chunk * part, values)
        result[...] = dot(split[...], tables[1 - strip])

    def finish(at):
        result = scratch[2 * (at % count) + 1]
        for row in range(0, piece, group):
            first = kept[pl.ds((at * piece + row) * steps, TILE)]
            second = result[pl.ds(row * steps, TILE)]
            upper = sign * (first - second)
            parts = [
                lanes_reversed(upper[:, lane : lane + LANES]) for lane in range(0, half, LANES)
            ][::-1]
            whole = jnp.concatenate([first + second, *parts], axis=1)
            out[pl.ds(at * piece + row, group)] = whole.reshape(group, TILE // group, width)
            done = at * piece + row + group
            if done % flight == 0:
                copy(done // flight - 1).start()

    for at in range(pieces):
        product(at)
        if at:
            finish(at - 1)
    finish(pieces - 1)
    for at in range(sems.shape[0]):
        copy(at).wait()


def inverse_second(place, kept, gots, tables, steps):
    rows, half = kept.shape[0] // steps, kept.shape[1]
    piece, pieces = min(32, rows // 2), 2
    depth = steps * piece
    return call(
        inverse_second_kernel,
        "inverse_second",
        [IN_VMEM] * (2 + CHUNKS),
        IN_HBM,
        floats(rows, steps, 2 * half),
        [
            pltpu.VMEM((rows, steps, 2 * half), jnp.float32),
            pltpu.SemaphoreType.DMA((2 * rows // piece,)),
        ]
        + [pltpu.VMEM((depth, 2 * half), jnp.bfloat16), pltpu.VMEM((depth, half), jnp.float32)]
        * pieces,
        1 << 32,
    )(place, tables, kept, *gots)


def swapped(block):
    return lax.ppermute(block, "space", [(0, 1), (1, 0)])


def with_partner(block, distance):
    slabs = lax.axis_size("tm")
    return lax.ppermute(block, "tm", [(slab, slab ^ distance) for slab in range(slabs)])


def among_ranks(blocks):
    return [blocks[0]] + [with_partner(block, at) for at, block in enumerate(blocks) if at]


def by_chunk(table):
    strips, _, half, rows = table.shape
    parts = table.reshape(strips, 2, CHUNKS, half // CHUNKS, rows)
    return np.swapaxes(parts, 1, 2).reshape(strips, CHUNKS, 2 * half // CHUNKS, rows)


def shards(iterate, initial):
    rows, steps, width = iterate.shape
    slabs = lax.axis_size("tm")
    total = rows * lax.axis_size("space")
    place = jnp.stack([lax.axis_index("tm"), lax.axis_index("space")]).astype(jnp.int32)
    second = second_tables(width)
    first = first_tables(total)
    decay = decay_tables(total, width)
    slab_decay = decay**steps
    half_decay = slab_decay ** ranks(slabs)
    gain = 1.0 / (1.0 - circulant_alpha * half_decay * half_decay)
    closing = constant(
        np.stack([by_chunk(table) for table in (slab_decay, half_decay, gain)], axis=2)
    )
    first_table, decays = split_constant(first), constant(decay)
    second_table = mixed_constant(REACTION_STEP * second)
    outer, sums, sends = forward_second(place, iterate, initial, second_table)
    gots = [swapped(send) for send in sends]
    keeps = keep_second(place, outer, sums, second_table, steps)
    modes, befores = [], []
    for chunk in range(CHUNKS):
        own_modes, lasts = forward_first(
            place, chunk, keeps[chunk], gots[chunk], first_table, decays, slabs
        )
        modes.append(own_modes)
        ordered, near = half_sum(place, chunk, among_ranks(lasts), closing, slabs)
        far = with_partner(near, ranks(slabs))
        befores.append(among_ranks(close(place, chunk, ordered, near, far, closing, slabs)))
    inverse_table = split_constant(np.swapaxes(first, 2, 3))
    keeps, sends = zip(
        *(
            inverse_first(place, chunk, modes[chunk], befores[chunk], inverse_table, decays, slabs)
            for chunk in range(CHUNKS)
        )
    )
    gots = [swapped(send) for send in sends]
    inverse_table = split_constant(np.swapaxes(second[:, : width // 2], 1, 2))
    kept = keep_inverse(place, keeps, inverse_table, rows, steps)
    return inverse_second(place, kept, gots, inverse_table, steps)


def solution(mesh):
    return jax.shard_map(
        shards,
        mesh=mesh,
        in_specs=(P(("group", "space"), "tm", None), P(("group", "space"), None)),
        out_specs=P(("group", "space"), "tm", None),
        check_vma=False,
    )
```

```python
import functools
import math

import jax
import jax.numpy as jnp
import numpy as np
from jax import lax
from jax.experimental import pallas as pl
from jax.experimental.pallas import tpu as pltpu
from jax.sharding import PartitionSpec as P

circulant_alpha = 0.01
DIFFUSION = 2.0
REACTION_STEP = 0.5
VMEM_BYTES = 24 * 1024 * 1024
LANES = 128
SUBLANES = 8
TILE = 16
CHUNKS = 2


def sine_table(row_index, column_index, length):
    product = np.outer(row_index + 1, column_index + 1) % (2 * (length + 1))
    return math.sqrt(2.0 / (length + 1)) * np.sin(product * (math.pi / (length + 1)))


def stencil_eigen(mode_index, length):
    return 4.0 * np.sin((mode_index + 1) * (math.pi / (2.0 * (length + 1)))) ** 2


def second_tables(width):
    half = width // 2
    return np.stack([sine_table(np.arange(half), np.arange(s, width, 2), width) for s in (0, 1)])


def first_tables(total):
    rows = total // 2
    return np.stack(
        [
            np.stack(
                [sine_table(s * rows + np.arange(rows), np.arange(c, total, 2), total) for c in (0, 1)]
            )
            for s in (0, 1)
        ]
    )


def decay_tables(total, width):
    first, second = stencil_eigen(np.arange(total), total), stencil_eigen(np.arange(width), width)
    decay = 1.0 / (1.0 + DIFFUSION * (second[:, None] + first[None, :]))
    return np.stack([np.stack([decay[s::2, c::2] for c in (0, 1)]) for s in (0, 1)])


def constant(table):
    return jnp.asarray(np.asarray(table, np.float32))


def split_constant(table):
    table = np.asarray(table, np.float32)
    high = table.astype(jnp.bfloat16)
    low = (table - high.astype(np.float32)).astype(jnp.bfloat16)
    return jnp.asarray(np.concatenate([high, high, low], axis=-2))


def store_split(ref, at, lane, block):
    depth = ref.shape[-1] // 2
    width = block.shape[-1]
    high = block.astype(jnp.bfloat16)
    low = (block - high.astype(jnp.float32)).astype(jnp.bfloat16)
    ref[(*at, pl.ds(lane, width))] = high
    ref[(*at, pl.ds(depth + lane, width))] = low


def dot(split, table):
    rows = jnp.concatenate([split, split[:, : split.shape[1] // 2]], axis=1)
    return jnp.dot(rows, table, preferred_element_type=jnp.float32)


ALONG_LANES = lax.GatherDimensionNumbers(
    offset_dims=(),
    collapsed_slice_dims=(1,),
    start_index_map=(1,),
    operand_batching_dims=(0,),
    start_indices_batching_dims=(0,),
)


def reversal():
    index = LANES - 1 - lax.broadcasted_iota(jnp.int32, (TILE, LANES), 1)
    index = index.reshape(TILE, LANES, 1)
    return lambda block: lax.gather(
        block, index, ALONG_LANES, (1, 1), mode=lax.GatherScatterMode.PROMISE_IN_BOUNDS
    )


def store_rows_reversed(ref, start, block):
    rows, width = block.shape
    index = SUBLANES - 1 - lax.broadcasted_iota(jnp.int32, (SUBLANES, width), 0)
    for row in range(0, rows, SUBLANES):
        to = pl.multiple_of(start + rows - SUBLANES - row, SUBLANES)
        ref[pl.ds(to, SUBLANES), :] = jnp.take_along_axis(
            block[row : row + SUBLANES], index, axis=0, mode="promise_in_bounds"
        )


def pitch_of(cells):
    return cells + SUBLANES * (1 - cells // SUBLANES % 2)


def steps_of(ref, cells, steps, pitch):
    lines = [ref[pl.ds(cell, steps, stride=pitch), :] for cell in cells]
    return lines[0] if len(lines) == 1 else jnp.concatenate(lines, axis=0)


IN_VMEM = pl.BlockSpec(memory_space=pltpu.VMEM)
IN_HBM = pl.BlockSpec(memory_space=pltpu.HBM)
IN_SMEM = pl.BlockSpec(memory_space=pltpu.SMEM)


def in_hbm(array):
    return pltpu.with_memory_space_constraint(array, pltpu.HBM)


def floats(*shape):
    return jax.ShapeDtypeStruct(shape, jnp.float32)


def call(kernel, name, in_specs, out_specs, out_shape, scratch, flops):
    return pl.pallas_call(
        kernel,
        in_specs=[IN_SMEM, *in_specs],
        out_specs=out_specs,
        scratch_shapes=scratch,
        out_shape=out_shape,
        compiler_params=pltpu.CompilerParams(vmem_limit_bytes=VMEM_BYTES),
        cost_estimate=pl.CostEstimate(flops=flops, bytes_accessed=1 << 23, transcendentals=0),
        name=name,
    )


def forward_second_kernel(place, field_in, initial_in, tables, sums, *refs):
    sends, refs = refs[:CHUNKS], refs[CHUNKS:]
    field, initial, table, sems, table_sem, result, *scratch = refs
    cells, steps, width = field.shape
    half = width // 2
    part = half // CHUNKS
    pieces = sems.shape[0]
    piece = cells // pieces
    group = max(TILE // steps, 1)
    pitch = sends[0].shape[0] // (steps + 1)
    body = piece * steps
    is_first = place[0] == 0
    sign = 1.0 - 2.0 * place[1].astype(jnp.float32)

    def copies(at):
        here = pl.ds(at * piece, piece)
        return [
            pltpu.make_async_copy(source.at[here], to.at[here], sems.at[at, which])
            for which, (source, to) in enumerate(((field_in, field), (initial_in, initial)))
        ]

    table_copy = pltpu.make_async_copy(tables.at[1 - place[1]], table, table_sem)

    def start(first, last):
        for at in range(first, min(last, pieces)):
            for copy in copies(at):
                copy.start()

    lanes_reversed = reversal()

    def put(other, at, sums_at, cells):
        lower = cells[:, :half]
        upper = sign * jnp.concatenate(
            [lanes_reversed(cells[:, lane : lane + LANES]) for lane in range(half, width, LANES)][::-1],
            axis=1,
        )
        sums[pl.ds(sums_at, TILE), :] = lower + upper
        store_split(other, (pl.ds(at, TILE),), 0, lower - upper)

    def prepare(at):
        split = scratch[at % len(scratch)]
        cell = at * piece
        for row in range(0, piece, group):
            values = field[pl.ds(cell + row, group)]
            force = values - values * values * values
            put(split, row * steps, (cell + row) * steps, force.reshape(TILE, width))
        for row in range(0, piece, TILE):
            here = pl.ds(cell + row, TILE)
            ends = jnp.where(is_first, initial[here], field[here, steps - 1, :])
            put(split, body + row, cells * steps + cell + row, ends)

    def transform(at):
        result[...] = dot(scratch[at % len(scratch)][...], table[...])

    def place_modes(at):
        first = cells - (at + 1) * piece
        for chunk, send in enumerate(sends):
            lanes = pl.ds(chunk * part, part)
            for row in range(piece):
                line = result[pl.ds(row * steps, steps), lanes]
                send[pl.ds(first + piece - 1 - row, steps, stride=pitch), :] = line
            ends = result[pl.ds(body, piece), lanes]
            store_rows_reversed(send, pitch * steps + first, ends)

    start(0, 1)
    table_copy.start()
    start(1, 2)
    for at in range(pieces):
        for copy in copies(at):
            copy.wait()
        start(2 * at + 2, 2 * at + 4)
        if at == 1:
            table_copy.wait()
        if at:
            transform(at - 1)
        prepare(at)
        if at:
            place_modes(at - 1)
    transform(pieces - 1)
    place_modes(pieces - 1)


def forward_second(place, field, initial, tables):
    rows, steps, width = field.shape
    half = width // 2
    piece, pieces = min(32, rows // 2), 2
    outs = call(
        forward_second_kernel,
        "forward_second",
        [IN_HBM] * 3,
        [IN_VMEM] * (1 + CHUNKS),
        [floats((steps + 1) * rows, half)]
        + [floats((steps + 1) * pitch_of(rows), half // CHUNKS)] * CHUNKS,
        [
            pltpu.VMEM(field.shape, jnp.float32),
            pltpu.VMEM(initial.shape, jnp.float32),
            pltpu.VMEM(tables.shape[1:], jnp.bfloat16),
            pltpu.SemaphoreType.DMA((rows // piece, 2)),
            pltpu.SemaphoreType.DMA,
            pltpu.VMEM(((steps + 1) * piece, half), jnp.float32),
        ]
        + [pltpu.VMEM(((steps + 1) * piece, 2 * half), jnp.bfloat16)] * pieces,
        1 << 32,
    )(place, in_hbm(field), in_hbm(initial), in_hbm(tables))
    return outs[0], outs[1:]


def keep_second_kernel(steps, place, tables, sums, *refs):
    keeps, scratch = refs[:CHUNKS], refs[CHUNKS:]
    depth = scratch[0].shape[0]
    cells = sums.shape[0] // (steps + 1)
    pitch = keeps[0].shape[0] // (steps + 1)
    for at in range(0, sums.shape[0], depth):
        split = scratch[at // depth % 2]
        for row in range(0, depth, TILE):
            store_split(split, (pl.ds(row, TILE),), 0, sums[pl.ds(at + row, TILE)])
        result = dot(split[...], tables[place[1]])
        for chunk, keep in enumerate(keeps):
            part = keep.shape[1]
            lanes = slice(chunk * part, (chunk + 1) * part)
            body = max(0, min(depth, cells * steps - at))
            for row in range(0, body, steps):
                line = result[row : row + steps, lanes]
                keep[pl.ds((at + row) // steps, steps, stride=pitch), :] = line
            if body < depth:
                ends = pl.ds(pitch * steps + at + body - cells * steps, depth - body)
                keep[ends, :] = result[body:, lanes]


def keep_second(place, sums, tables, steps):
    rows, half = sums.shape
    shape = ((steps + 1) * pitch_of(rows // (steps + 1)), half // CHUNKS)
    return call(
        functools.partial(keep_second_kernel, steps),
        "keep_second",
        [IN_VMEM] * 2,
        [IN_VMEM] * CHUNKS,
        [floats(*shape)] * CHUNKS,
        [pltpu.VMEM((rows // 8, 2 * half), jnp.bfloat16)] * 2,
        1 << 31,
    )(place, tables, sums)


def ranks(slabs):
    return slabs // 2


def by_distance(blocks):
    return [blocks[0], *blocks[:0:-1]]


def forward_first_kernel(slabs, chunk, place, keep, got, table, decay, modes, *refs):
    size = ranks(slabs)
    lasts, (state, split, extra) = refs[:size], refs[size:]
    steps, _, part, rows = modes.shape
    pitch = keep.shape[0] // (steps + 1)
    block = split.shape[1] // part - 1
    strip = place[1]
    is_first = jnp.where(place[0] == 0, 1.0 / REACTION_STEP, 0.0)
    is_last = jnp.where(place[0] == slabs - 1, 1.0 / REACTION_STEP, 0.0)
    state[...] = jnp.zeros_like(state)
    for step in range(0, steps, block):
        count = block if step else block + 1
        for c in (0, 1):
            for at in range(count):
                from_step = steps if at == block else step + at
                cells_at = pl.ds(from_step * pitch, rows)
                near, far = keep[cells_at], got[cells_at]
                cells = near - far if c else near + far
                store_split(split, (c, pl.ds(at * part, part)), 0, cells.T)
            result = dot(split[c, pl.ds(0, count * part)], table[strip, c])
            if step == 0:
                extra[c] = result[block * part :]
                modes[0, c] = result[:part] + is_first * result[block * part :]
                modes[pl.ds(1, block - 1), c] = result[part : block * part].reshape(block - 1, part, rows)
            else:
                modes[pl.ds(step, block), c] = result.reshape(block, part, rows)
        for c in (0, 1):
            for row in range(0, part, TILE):
                tile, at_state = pl.ds(row, TILE), pl.ds(c * part + row, TILE)
                value = state[at_state]
                rate = decay[strip, c, pl.ds(chunk * part + row, TILE)]
                for at in range(block):
                    value = rate * (value + modes[step + at, c, tile])
                state[at_state] = value
    for c in (0, 1):
        at_state = pl.ds(c * part, part)
        state[at_state] = state[at_state] - is_last * extra[c]
    rank = lax.rem(place[0], size)
    share = 2 * part // size
    for partner in range(size):
        at = pl.multiple_of((rank ^ partner) * share, share)
        lasts[partner][...] = state[pl.ds(at, share)]


def forward_first(place, chunk, keep, got, tables, decays, slabs):
    rows, part = tables.shape[-1], keep.shape[1]
    steps = keep.shape[0] // pitch_of(rows) - 1
    block = min(8, steps)
    size = ranks(slabs)
    share = 2 * part // size
    outs = call(
        functools.partial(forward_first_kernel, slabs, chunk),
        "forward_first",
        [IN_VMEM] * 4,
        [IN_VMEM] * (1 + size),
        [floats(steps, 2, part, rows)] + [floats(share, rows)] * size,
        [
            pltpu.VMEM((2 * part, rows), jnp.float32),
            pltpu.VMEM((2, (block + 1) * part, 2 * rows), jnp.bfloat16),
            pltpu.VMEM((2, part, rows), jnp.float32),
        ],
        1 << 31,
    )(place, keep, got, tables, decays)
    return outs[0], outs[1:]


def half_sum_kernel(slabs, chunk, place, closing, *refs):
    size = ranks(slabs)
    lasts, ordered, total = by_distance(refs[:size]), refs[size], refs[size + 1]
    share = total.shape[0]
    rank = lax.rem(place[0], size)
    decay = closing[place[1], chunk, 0, pl.ds(pl.multiple_of(rank * share, share), share)]
    for partner in range(size):
        ordered[rank ^ partner] = lasts[partner][...]
    state = ordered[0]
    for at in range(1, size):
        state = ordered[at] + decay * state
    total[...] = state


def half_sum(place, chunk, lasts, closing, slabs):
    size = ranks(slabs)
    share, rows = lasts[0].shape
    return call(
        functools.partial(half_sum_kernel, slabs, chunk),
        "half_sum",
        [IN_VMEM] * (1 + size),
        [IN_VMEM] * 2,
        [floats(size, share, rows), floats(share, rows)],
        [],
        1 << 20,
    )(place, closing, *by_distance(lasts))


def close_kernel(slabs, chunk, place, closing, ordered, near, far, *refs):
    size = ranks(slabs)
    befores, states = refs[:size], refs[size]
    share = near.shape[0]
    rank = lax.rem(place[0], size)
    at_share = pl.ds(pl.multiple_of(rank * share, share), share)
    decay, half_decay, gain = (closing[place[1], chunk, at, at_share] for at in range(3))
    entering = jnp.where(place[0] < size, circulant_alpha, 1.0)
    state = gain * (entering * far[...] + circulant_alpha * half_decay * near[...])
    for at in range(size):
        states[at] = state
        if at < size - 1:
            state = ordered[at] + decay * state
    for partner in range(size):
        befores[partner][...] = states[rank ^ partner]


def close(place, chunk, ordered, near, far, closing, slabs):
    size, share, rows = ordered.shape
    return call(
        functools.partial(close_kernel, slabs, chunk),
        "close",
        [IN_VMEM] * 4,
        [IN_VMEM] * size,
        [floats(share, rows)] * size,
        [pltpu.VMEM((size, share, rows), jnp.float32)],
        1 << 20,
    )(place, closing, ordered, near, far)


def inverse_first_kernel(slabs, chunk, place, modes, table, decay, *refs):
    size = ranks(slabs)
    befores, (keep, send, state, split) = by_distance(refs[:size]), refs[size:]
    steps, _, part, rows = modes.shape
    pitch = keep.shape[0] // steps
    block = split.shape[1] // part
    strip = place[1]
    rank = lax.rem(place[0], size)
    share = 2 * part // size
    for partner in range(size):
        at = pl.multiple_of((rank ^ partner) * share, share)
        state[pl.ds(at, share)] = befores[partner][...]
    for step in range(0, steps, block):
        results = []
        for c in (0, 1):
            for row in range(0, part, TILE):
                tile, at_state = pl.ds(row, TILE), pl.ds(c * part + row, TILE)
                value = state[at_state]
                rate = decay[strip, c, pl.ds(chunk * part + row, TILE)]
                for at in range(block):
                    value = rate * (value + modes[step + at, c, tile])
                    store_split(split, (c, pl.ds(at * part + row, TILE)), 0, value)
                state[at_state] = value
            results.append(dot(split[c], table[strip, c]))
        even, odd = results
        for at in range(block):
            piece = slice(at * part, (at + 1) * part)
            cells_at = pl.ds((step + at) * pitch, rows)
            keep[cells_at, :] = (even[piece] + odd[piece]).T
            send[cells_at, :] = (even[piece] - odd[piece]).T


def inverse_first(place, chunk, modes, befores, tables, decays, slabs):
    steps, _, part, rows = modes.shape
    block = min(8, steps)
    return call(
        functools.partial(inverse_first_kernel, slabs, chunk),
        "inverse_first",
        [IN_VMEM] * (3 + len(befores)),
        [IN_VMEM] * 2,
        [floats(steps * pitch_of(rows), part)] * 2,
        [
            pltpu.VMEM((2 * part, rows), jnp.float32),
            pltpu.VMEM((2, block * part, 2 * rows), jnp.bfloat16),
        ],
        1 << 31,
    )(place, modes, tables, decays, *by_distance(befores))


def keep_inverse_kernel(steps, place, tables, *refs):
    keeps, out, scratch = refs[:CHUNKS], refs[CHUNKS], refs[CHUNKS + 1 :]
    part = keeps[0].shape[1]
    pitch = keeps[0].shape[0] // steps
    depth = scratch[0].shape[0]
    group = max(TILE // steps, 1)
    for at in range(0, out.shape[0], depth):
        split = scratch[at // depth % 2]
        for row in range(0, depth, TILE):
            cell = (at + row) // steps
            for chunk, keep in enumerate(keeps):
                cells = steps_of(keep, range(cell, cell + group), steps, pitch)
                store_split(split, (pl.ds(row, TILE),), chunk * part, cells)
        out[pl.ds(at, depth)] = dot(split[...], tables[place[1]])


def keep_inverse(place, keeps, tables, rows, steps):
    half = keeps[0].shape[1] * CHUNKS
    return call(
        functools.partial(keep_inverse_kernel, steps),
        "keep_inverse",
        [IN_VMEM] * (1 + CHUNKS),
        IN_VMEM,
        floats(rows * steps, half),
        [pltpu.VMEM((rows * steps // 8, 2 * half), jnp.bfloat16)] * 2,
        1 << 31,
    )(place, tables, *keeps)


def inverse_second_kernel(place, tables, kept, *refs):
    gots, target, out, sems, scratch = (
        refs[:CHUNKS], refs[CHUNKS], refs[CHUNKS + 1], refs[CHUNKS + 2], refs[CHUNKS + 3 :]
    )
    cells, steps, width = out.shape
    half = width // 2
    part = half // CHUNKS
    pitch = gots[0].shape[0] // steps
    count = len(scratch) // 2
    piece = scratch[0].shape[0] // steps
    pieces = cells // piece
    flight = cells // sems.shape[0]
    group = max(TILE // steps, 1)
    strip = place[1]
    sign = 1.0 - 2.0 * strip.astype(jnp.float32)

    def copy(at):
        here = pl.ds(at * flight, flight)
        return pltpu.make_async_copy(out.at[here], target.at[here], sems.at[at])

    lanes_reversed = reversal()

    def product(at):
        split, result = scratch[2 * (at % count) : 2 * (at % count) + 2]
        for row in range(0, piece, group):
            mirrors = [cells - 1 - at * piece - row - cell for cell in range(group)]
            for chunk, got in enumerate(gots):
                values = steps_of(got, mirrors, steps, pitch)
                store_split(split, (pl.ds(row * steps, TILE),), chunk * part, values)
        result[...] = dot(split[...], tables[1 - strip])

    def finish(at):
        result = scratch[2 * (at % count) + 1]
        for row in range(0, piece, group):
            first = kept[pl.ds((at * piece + row) * steps, TILE)]
            second = result[pl.ds(row * steps, TILE)]
            upper = sign * (first - second)
            parts = [
                lanes_reversed(upper[:, lane : lane + LANES]) for lane in range(0, half, LANES)
            ][::-1]
            whole = jnp.concatenate([first + second, *parts], axis=1)
            out[pl.ds(at * piece + row, group)] = whole.reshape(group, TILE // group, width)
            done = at * piece + row + group
            if done % flight == 0:
                copy(done // flight - 1).start()

    for at in range(pieces):
        product(at)
        if at:
            finish(at - 1)
    finish(pieces - 1)
    for at in range(sems.shape[0]):
        copy(at).wait()


def inverse_second(place, kept, gots, tables, steps):
    rows, half = kept.shape[0] // steps, kept.shape[1]
    piece, pieces = min(32, rows // 2), 2
    depth = steps * piece
    return call(
        inverse_second_kernel,
        "inverse_second",
        [IN_VMEM] * (2 + CHUNKS),
        IN_HBM,
        floats(rows, steps, 2 * half),
        [
            pltpu.VMEM((rows, steps, 2 * half), jnp.float32),
            pltpu.SemaphoreType.DMA((2 * rows // piece,)),
        ]
        + [pltpu.VMEM((depth, 2 * half), jnp.bfloat16), pltpu.VMEM((depth, half), jnp.float32)]
        * pieces,
        1 << 32,
    )(place, tables, kept, *gots)


def swapped(block):
    return lax.ppermute(block, "space", [(0, 1), (1, 0)])


def with_partner(block, distance):
    slabs = lax.axis_size("tm")
    return lax.ppermute(block, "tm", [(slab, slab ^ distance) for slab in range(slabs)])


def among_ranks(blocks):
    return [blocks[0]] + [with_partner(block, at) for at, block in enumerate(blocks) if at]


def by_chunk(table):
    strips, _, half, rows = table.shape
    parts = table.reshape(strips, 2, CHUNKS, half // CHUNKS, rows)
    return np.swapaxes(parts, 1, 2).reshape(strips, CHUNKS, 2 * half // CHUNKS, rows)


def shards(iterate, initial):
    rows, steps, width = iterate.shape
    slabs = lax.axis_size("tm")
    total = rows * lax.axis_size("space")
    place = jnp.stack([lax.axis_index("tm"), lax.axis_index("space")]).astype(jnp.int32)
    second = second_tables(width)
    first = first_tables(total)
    decay = decay_tables(total, width)
    slab_decay = decay**steps
    half_decay = slab_decay ** ranks(slabs)
    gain = 1.0 / (1.0 - circulant_alpha * half_decay * half_decay)
    closing = constant(
        np.stack([by_chunk(table) for table in (slab_decay, half_decay, gain)], axis=2)
    )
    first_table, decays = split_constant(first), constant(decay)
    second_table = split_constant(REACTION_STEP * second)
    sums, sends = forward_second(place, iterate, initial, second_table)
    gots = [swapped(send) for send in sends]
    keeps = keep_second(place, sums, second_table, steps)
    modes, befores = [], []
    for chunk in range(CHUNKS):
        own_modes, lasts = forward_first(
            place, chunk, keeps[chunk], gots[chunk], first_table, decays, slabs
        )
        modes.append(own_modes)
        ordered, near = half_sum(place, chunk, among_ranks(lasts), closing, slabs)
        far = with_partner(near, ranks(slabs))
        befores.append(among_ranks(close(place, chunk, ordered, near, far, closing, slabs)))
    inverse_table = split_constant(np.swapaxes(first, 2, 3))
    keeps, sends = zip(
        *(
            inverse_first(place, chunk, modes[chunk], befores[chunk], inverse_table, decays, slabs)
            for chunk in range(CHUNKS)
        )
    )
    gots = [swapped(send) for send in sends]
    inverse_table = split_constant(np.swapaxes(second, 1, 2))
    kept = keep_inverse(place, keeps, inverse_table, rows, steps)
    return inverse_second(place, kept, gots, inverse_table, steps)


def solution(mesh):
    return jax.shard_map(
        shards,
        mesh=mesh,
        in_specs=(P(("group", "space"), "tm", None), P(("group", "space"), None)),
        out_specs=P(("group", "space"), "tm", None),
        check_vma=False,
    )
```

```python
import functools
import math

import jax
import jax.numpy as jnp
import numpy as np
from jax import lax
from jax.experimental import pallas as pl
from jax.experimental.pallas import tpu as pltpu
from jax.sharding import PartitionSpec as P

circulant_alpha = 0.01
DIFFUSION = 2.0
REACTION_STEP = 0.5
VMEM_BYTES = 24 * 1024 * 1024
LANES = 128
SUBLANES = 8
TILE = 16
CHUNKS = 2


def sine_table(row_index, column_index, length):
    product = np.outer(row_index + 1, column_index + 1) % (2 * (length + 1))
    return math.sqrt(2.0 / (length + 1)) * np.sin(product * (math.pi / (length + 1)))


def stencil_eigen(mode_index, length):
    return 4.0 * np.sin((mode_index + 1) * (math.pi / (2.0 * (length + 1)))) ** 2


def second_tables(width):
    half = width // 2
    return np.stack([sine_table(np.arange(half), np.arange(s, width, 2), width) for s in (0, 1)])


def first_tables(total):
    rows = total // 2
    return np.stack(
        [
            np.stack(
                [sine_table(s * rows + np.arange(rows), np.arange(c, total, 2), total) for c in (0, 1)]
            )
            for s in (0, 1)
        ]
    )


def decay_tables(total, width):
    first, second = stencil_eigen(np.arange(total), total), stencil_eigen(np.arange(width), width)
    decay = 1.0 / (1.0 + DIFFUSION * (second[:, None] + first[None, :]))
    return np.stack([np.stack([decay[s::2, c::2] for c in (0, 1)]) for s in (0, 1)])


def constant(table):
    return jnp.asarray(np.asarray(table, np.float32))


def split_constant(table):
    table = np.asarray(table, np.float32)
    high = table.astype(jnp.bfloat16)
    low = (table - high.astype(np.float32)).astype(jnp.bfloat16)
    return jnp.asarray(np.concatenate([high, high, low], axis=-2))


def store_split(ref, at, lane, block):
    depth = ref.shape[-1] // 2
    width = block.shape[-1]
    high = block.astype(jnp.bfloat16)
    low = (block - high.astype(jnp.float32)).astype(jnp.bfloat16)
    ref[(*at, pl.ds(lane, width))] = high
    ref[(*at, pl.ds(depth + lane, width))] = low


def dot(split, table):
    rows = jnp.concatenate([split, split[:, : split.shape[1] // 2]], axis=1)
    return jnp.dot(rows, table, preferred_element_type=jnp.float32)


ALONG_LANES = lax.GatherDimensionNumbers(
    offset_dims=(),
    collapsed_slice_dims=(1,),
    start_index_map=(1,),
    operand_batching_dims=(0,),
    start_indices_batching_dims=(0,),
)


def reversal():
    index = LANES - 1 - lax.broadcasted_iota(jnp.int32, (TILE, LANES), 1)
    index = index.reshape(TILE, LANES, 1)
    return lambda block: lax.gather(
        block, index, ALONG_LANES, (1, 1), mode=lax.GatherScatterMode.PROMISE_IN_BOUNDS
    )


def store_rows_reversed(ref, start, block):
    rows, width = block.shape
    index = SUBLANES - 1 - lax.broadcasted_iota(jnp.int32, (SUBLANES, width), 0)
    for row in range(0, rows, SUBLANES):
        to = pl.multiple_of(start + rows - SUBLANES - row, SUBLANES)
        ref[pl.ds(to, SUBLANES), :] = jnp.take_along_axis(
            block[row : row + SUBLANES], index, axis=0, mode="promise_in_bounds"
        )


def pitch_of(cells):
    return cells + SUBLANES * (1 - cells // SUBLANES % 2)


def steps_of(ref, cells, steps, pitch):
    lines = [ref[pl.ds(cell, steps, stride=pitch), :] for cell in cells]
    return lines[0] if len(lines) == 1 else jnp.concatenate(lines, axis=0)


IN_VMEM = pl.BlockSpec(memory_space=pltpu.VMEM)
IN_HBM = pl.BlockSpec(memory_space=pltpu.HBM)
IN_SMEM = pl.BlockSpec(memory_space=pltpu.SMEM)


def in_hbm(array):
    return pltpu.with_memory_space_constraint(array, pltpu.HBM)


def floats(*shape):
    return jax.ShapeDtypeStruct(shape, jnp.float32)


def call(kernel, name, in_specs, out_specs, out_shape, scratch, flops):
    return pl.pallas_call(
        kernel,
        in_specs=[IN_SMEM, *in_specs],
        out_specs=out_specs,
        scratch_shapes=scratch,
        out_shape=out_shape,
        compiler_params=pltpu.CompilerParams(vmem_limit_bytes=VMEM_BYTES),
        cost_estimate=pl.CostEstimate(flops=flops, bytes_accessed=1 << 23, transcendentals=0),
        name=name,
    )


def forward_second_kernel(place, field_in, initial_in, tables, sums, *refs):
    sends, refs = refs[:CHUNKS], refs[CHUNKS:]
    field, initial, table, sems, table_sem, result, *scratch = refs
    cells, steps, width = field.shape
    half = width // 2
    part = half // CHUNKS
    pieces = sems.shape[0]
    piece = cells // pieces
    group = max(TILE // steps, 1)
    pitch = sends[0].shape[0] // (steps + 1)
    body = piece * steps
    is_first = place[0] == 0
    sign = 1.0 - 2.0 * place[1].astype(jnp.float32)

    def copies(at):
        here = pl.ds(at * piece, piece)
        return [
            pltpu.make_async_copy(source.at[here], to.at[here], sems.at[at, which])
            for which, (source, to) in enumerate(((field_in, field), (initial_in, initial)))
        ]

    table_copy = pltpu.make_async_copy(tables.at[1 - place[1]], table, table_sem)

    def start(first, last):
        for at in range(first, min(last, pieces)):
            for copy in copies(at):
                copy.start()

    lanes_reversed = reversal()

    def put(other, at, sums_at, cells):
        lower = cells[:, :half]
        upper = sign * jnp.concatenate(
            [lanes_reversed(cells[:, lane : lane + LANES]) for lane in range(half, width, LANES)][::-1],
            axis=1,
        )
        sums[pl.ds(sums_at, TILE), :] = lower + upper
        store_split(other, (pl.ds(at, TILE),), 0, lower - upper)

    def prepare(at, first, last):
        split = scratch[at % len(scratch)]
        cell = at * piece
        for row in range(first, last, group):
            values = field[pl.ds(cell + row, group)]
            force = values - values * values * values
            put(split, row * steps, (cell + row) * steps, force.reshape(TILE, width))
        for row in range(first, last, TILE):
            here = pl.ds(cell + row, TILE)
            ends = jnp.where(is_first, initial[here], field[here, steps - 1, :])
            put(split, body + row, cells * steps + cell + row, ends)

    def transform(at, part_at):
        rows = (piece * steps + piece) // 2
        here = pl.ds(part_at * rows, rows)
        result[here, :] = dot(scratch[at % len(scratch)][here, :], table[...])

    def place_modes(at):
        first = cells - (at + 1) * piece
        for chunk, send in enumerate(sends):
            lanes = pl.ds(chunk * part, part)
            for row in range(piece):
                line = result[pl.ds(row * steps, steps), lanes]
                send[pl.ds(first + piece - 1 - row, steps, stride=pitch), :] = line
            ends = result[pl.ds(body, piece), lanes]
            store_rows_reversed(send, pitch * steps + first, ends)

    start(0, 1)
    table_copy.start()
    start(1, 2)
    for at in range(pieces):
        for copy in copies(at):
            copy.wait()
        start(2 * at + 2, 2 * at + 4)
        if at == 1:
            table_copy.wait()
        for part_at in (0, 1):
            if at:
                transform(at - 1, part_at)
            prepare(at, part_at * piece // 2, (part_at + 1) * piece // 2)
        if at:
            place_modes(at - 1)
    transform(pieces - 1, 0)
    transform(pieces - 1, 1)
    place_modes(pieces - 1)


def forward_second(place, field, initial, tables):
    rows, steps, width = field.shape
    half = width // 2
    piece, pieces = min(32, rows // 2), 2
    outs = call(
        forward_second_kernel,
        "forward_second",
        [IN_HBM] * 3,
        [IN_VMEM] * (1 + CHUNKS),
        [floats((steps + 1) * rows, half)]
        + [floats((steps + 1) * pitch_of(rows), half // CHUNKS)] * CHUNKS,
        [
            pltpu.VMEM(field.shape, jnp.float32),
            pltpu.VMEM(initial.shape, jnp.float32),
            pltpu.VMEM(tables.shape[1:], jnp.bfloat16),
            pltpu.SemaphoreType.DMA((rows // piece, 2)),
            pltpu.SemaphoreType.DMA,
            pltpu.VMEM(((steps + 1) * piece, half), jnp.float32),
        ]
        + [pltpu.VMEM(((steps + 1) * piece, 2 * half), jnp.bfloat16)] * pieces,
        1 << 32,
    )(place, in_hbm(field), in_hbm(initial), in_hbm(tables))
    return outs[0], outs[1:]


def keep_second_kernel(steps, place, tables, sums, *refs):
    keeps, scratch = refs[:CHUNKS], refs[CHUNKS:]
    depth = scratch[0].shape[0]
    cells = sums.shape[0] // (steps + 1)
    pitch = keeps[0].shape[0] // (steps + 1)
    for at in range(0, sums.shape[0], depth):
        split = scratch[at // depth % 2]
        for row in range(0, depth, TILE):
            store_split(split, (pl.ds(row, TILE),), 0, sums[pl.ds(at + row, TILE)])
        result = dot(split[...], tables[place[1]])
        for chunk, keep in enumerate(keeps):
            part = keep.shape[1]
            lanes = slice(chunk * part, (chunk + 1) * part)
            body = max(0, min(depth, cells * steps - at))
            for row in range(0, body, steps):
                line = result[row : row + steps, lanes]
                keep[pl.ds((at + row) // steps, steps, stride=pitch), :] = line
            if body < depth:
                ends = pl.ds(pitch * steps + at + body - cells * steps, depth - body)
                keep[ends, :] = result[body:, lanes]


def keep_second(place, sums, tables, steps):
    rows, half = sums.shape
    shape = ((steps + 1) * pitch_of(rows // (steps + 1)), half // CHUNKS)
    return call(
        functools.partial(keep_second_kernel, steps),
        "keep_second",
        [IN_VMEM] * 2,
        [IN_VMEM] * CHUNKS,
        [floats(*shape)] * CHUNKS,
        [pltpu.VMEM((rows // 8, 2 * half), jnp.bfloat16)] * 2,
        1 << 31,
    )(place, tables, sums)


def ranks(slabs):
    return slabs // 2


def by_distance(blocks):
    return [blocks[0], *blocks[:0:-1]]


def forward_first_kernel(slabs, chunk, place, keep, got, table, decay, modes, *refs):
    size = ranks(slabs)
    lasts, (state, split, extra) = refs[:size], refs[size:]
    steps, _, part, rows = modes.shape
    pitch = keep.shape[0] // (steps + 1)
    block = split.shape[1] // part - 1
    strip = place[1]
    is_first = jnp.where(place[0] == 0, 1.0 / REACTION_STEP, 0.0)
    is_last = jnp.where(place[0] == slabs - 1, 1.0 / REACTION_STEP, 0.0)
    state[...] = jnp.zeros_like(state)
    for step in range(0, steps, block):
        count = block if step else block + 1
        for c in (0, 1):
            for at in range(count):
                from_step = steps if at == block else step + at
                cells_at = pl.ds(from_step * pitch, rows)
                near, far = keep[cells_at], got[cells_at]
                cells = near - far if c else near + far
                store_split(split, (c, pl.ds(at * part, part)), 0, cells.T)
            result = dot(split[c, pl.ds(0, count * part)], table[strip, c])
            if step == 0:
                extra[c] = result[block * part :]
                modes[0, c] = result[:part] + is_first * result[block * part :]
                modes[pl.ds(1, block - 1), c] = result[part : block * part].reshape(block - 1, part, rows)
            else:
                modes[pl.ds(step, block), c] = result.reshape(block, part, rows)
        for c in (0, 1):
            for row in range(0, part, TILE):
                tile, at_state = pl.ds(row, TILE), pl.ds(c * part + row, TILE)
                value = state[at_state]
                rate = decay[strip, c, pl.ds(chunk * part + row, TILE)]
                for at in range(block):
                    value = rate * (value + modes[step + at, c, tile])
                state[at_state] = value
    for c in (0, 1):
        at_state = pl.ds(c * part, part)
        state[at_state] = state[at_state] - is_last * extra[c]
    rank = lax.rem(place[0], size)
    share = 2 * part // size
    for partner in range(size):
        at = pl.multiple_of((rank ^ partner) * share, share)
        lasts[partner][...] = state[pl.ds(at, share)]


def forward_first(place, chunk, keep, got, tables, decays, slabs):
    rows, part = tables.shape[-1], keep.shape[1]
    steps = keep.shape[0] // pitch_of(rows) - 1
    block = min(8, steps)
    size = ranks(slabs)
    share = 2 * part // size
    outs = call(
        functools.partial(forward_first_kernel, slabs, chunk),
        "forward_first",
        [IN_VMEM] * 4,
        [IN_VMEM] * (1 + size),
        [floats(steps, 2, part, rows)] + [floats(share, rows)] * size,
        [
            pltpu.VMEM((2 * part, rows), jnp.float32),
            pltpu.VMEM((2, (block + 1) * part, 2 * rows), jnp.bfloat16),
            pltpu.VMEM((2, part, rows), jnp.float32),
        ],
        1 << 31,
    )(place, keep, got, tables, decays)
    return outs[0], outs[1:]


def half_sum_kernel(slabs, chunk, place, closing, *refs):
    size = ranks(slabs)
    lasts, ordered, total = by_distance(refs[:size]), refs[size], refs[size + 1]
    share = total.shape[0]
    rank = lax.rem(place[0], size)
    decay = closing[place[1], chunk, 0, pl.ds(pl.multiple_of(rank * share, share), share)]
    for partner in range(size):
        ordered[rank ^ partner] = lasts[partner][...]
    state = ordered[0]
    for at in range(1, size):
        state = ordered[at] + decay * state
    total[...] = state


def half_sum(place, chunk, lasts, closing, slabs):
    size = ranks(slabs)
    share, rows = lasts[0].shape
    return call(
        functools.partial(half_sum_kernel, slabs, chunk),
        "half_sum",
        [IN_VMEM] * (1 + size),
        [IN_VMEM] * 2,
        [floats(size, share, rows), floats(share, rows)],
        [],
        1 << 20,
    )(place, closing, *by_distance(lasts))


def close_kernel(slabs, chunk, place, closing, ordered, near, far, *refs):
    size = ranks(slabs)
    befores, states = refs[:size], refs[size]
    share = near.shape[0]
    rank = lax.rem(place[0], size)
    at_share = pl.ds(pl.multiple_of(rank * share, share), share)
    decay, half_decay, gain = (closing[place[1], chunk, at, at_share] for at in range(3))
    entering = jnp.where(place[0] < size, circulant_alpha, 1.0)
    state = gain * (entering * far[...] + circulant_alpha * half_decay * near[...])
    for at in range(size):
        states[at] = state
        if at < size - 1:
            state = ordered[at] + decay * state
    for partner in range(size):
        befores[partner][...] = states[rank ^ partner]


def close(place, chunk, ordered, near, far, closing, slabs):
    size, share, rows = ordered.shape
    return call(
        functools.partial(close_kernel, slabs, chunk),
        "close",
        [IN_VMEM] * 4,
        [IN_VMEM] * size,
        [floats(share, rows)] * size,
        [pltpu.VMEM((size, share, rows), jnp.float32)],
        1 << 20,
    )(place, closing, ordered, near, far)


def inverse_first_kernel(slabs, chunk, place, modes, table, decay, *refs):
    size = ranks(slabs)
    befores, (keep, send, state, split) = by_distance(refs[:size]), refs[size:]
    steps, _, part, rows = modes.shape
    pitch = keep.shape[0] // steps
    block = split.shape[1] // part
    strip = place[1]
    rank = lax.rem(place[0], size)
    share = 2 * part // size
    for partner in range(size):
        at = pl.multiple_of((rank ^ partner) * share, share)
        state[pl.ds(at, share)] = befores[partner][...]
    for step in range(0, steps, block):
        results = []
        for c in (0, 1):
            for row in range(0, part, TILE):
                tile, at_state = pl.ds(row, TILE), pl.ds(c * part + row, TILE)
                value = state[at_state]
                rate = decay[strip, c, pl.ds(chunk * part + row, TILE)]
                for at in range(block):
                    value = rate * (value + modes[step + at, c, tile])
                    store_split(split, (c, pl.ds(at * part + row, TILE)), 0, value)
                state[at_state] = value
            results.append(dot(split[c], table[strip, c]))
        even, odd = results
        for at in range(block):
            piece = slice(at * part, (at + 1) * part)
            cells_at = pl.ds((step + at) * pitch, rows)
            keep[cells_at, :] = (even[piece] + odd[piece]).T
            send[cells_at, :] = (even[piece] - odd[piece]).T


def inverse_first(place, chunk, modes, befores, tables, decays, slabs):
    steps, _, part, rows = modes.shape
    block = min(8, steps)
    return call(
        functools.partial(inverse_first_kernel, slabs, chunk),
        "inverse_first",
        [IN_VMEM] * (3 + len(befores)),
        [IN_VMEM] * 2,
        [floats(steps * pitch_of(rows), part)] * 2,
        [
            pltpu.VMEM((2 * part, rows), jnp.float32),
            pltpu.VMEM((2, block * part, 2 * rows), jnp.bfloat16),
        ],
        1 << 31,
    )(place, modes, tables, decays, *by_distance(befores))


def keep_inverse_kernel(steps, place, tables, *refs):
    keeps, out, scratch = refs[:CHUNKS], refs[CHUNKS], refs[CHUNKS + 1 :]
    part = keeps[0].shape[1]
    pitch = keeps[0].shape[0] // steps
    depth = scratch[0].shape[0]
    group = max(TILE // steps, 1)
    for at in range(0, out.shape[0], depth):
        split = scratch[at // depth % 2]
        for row in range(0, depth, TILE):
            cell = (at + row) // steps
            for chunk, keep in enumerate(keeps):
                cells = steps_of(keep, range(cell, cell + group), steps, pitch)
                store_split(split, (pl.ds(row, TILE),), chunk * part, cells)
        out[pl.ds(at, depth)] = dot(split[...], tables[place[1]])


def keep_inverse(place, keeps, tables, rows, steps):
    half = keeps[0].shape[1] * CHUNKS
    return call(
        functools.partial(keep_inverse_kernel, steps),
        "keep_inverse",
        [IN_VMEM] * (1 + CHUNKS),
        IN_VMEM,
        floats(rows * steps, half),
        [pltpu.VMEM((rows * steps // 8, 2 * half), jnp.bfloat16)] * 2,
        1 << 31,
    )(place, tables, *keeps)


def inverse_second_kernel(place, tables, kept, *refs):
    gots, target, out, sems, scratch = (
        refs[:CHUNKS], refs[CHUNKS], refs[CHUNKS + 1], refs[CHUNKS + 2], refs[CHUNKS + 3 :]
    )
    cells, steps, width = out.shape
    half = width // 2
    part = half // CHUNKS
    pitch = gots[0].shape[0] // steps
    count = len(scratch) // 2
    piece = scratch[0].shape[0] // steps
    pieces = cells // piece
    flight = cells // sems.shape[0]
    group = max(TILE // steps, 1)
    strip = place[1]
    sign = 1.0 - 2.0 * strip.astype(jnp.float32)

    def copy(at):
        here = pl.ds(at * flight, flight)
        return pltpu.make_async_copy(out.at[here], target.at[here], sems.at[at])

    lanes_reversed = reversal()

    def prepare(at):
        split, result = scratch[2 * (at % count) : 2 * (at % count) + 2]
        for row in range(0, piece, group):
            mirrors = [cells - 1 - at * piece - row - cell for cell in range(group)]
            for chunk, got in enumerate(gots):
                values = steps_of(got, mirrors, steps, pitch)
                store_split(split, (pl.ds(row * steps, TILE),), chunk * part, values)

    def product(at, part_at):
        split, result = scratch[2 * (at % count) : 2 * (at % count) + 2]
        rows = piece * steps // 2
        here = pl.ds(part_at * rows, rows)
        result[here, :] = dot(split[here, :], tables[1 - strip])

    def finish(at, part_at):
        result = scratch[2 * (at % count) + 1]
        for row in range(part_at * piece // 2, (part_at + 1) * piece // 2, group):
            first = kept[pl.ds((at * piece + row) * steps, TILE)]
            second = result[pl.ds(row * steps, TILE)]
            upper = sign * (first - second)
            parts = [
                lanes_reversed(upper[:, lane : lane + LANES]) for lane in range(0, half, LANES)
            ][::-1]
            whole = jnp.concatenate([first + second, *parts], axis=1)
            out[pl.ds(at * piece + row, group)] = whole.reshape(group, TILE // group, width)
            done = at * piece + row + group
            if done % flight == 0:
                copy(done // flight - 1).start()

    for at in range(pieces):
        prepare(at)
        for part_at in (0, 1):
            product(at, part_at)
            if at:
                finish(at - 1, part_at)
    finish(pieces - 1, 0)
    finish(pieces - 1, 1)
    for at in range(sems.shape[0]):
        copy(at).wait()


def inverse_second(place, kept, gots, tables, steps):
    rows, half = kept.shape[0] // steps, kept.shape[1]
    piece, pieces = min(32, rows // 2), 2
    depth = steps * piece
    return call(
        inverse_second_kernel,
        "inverse_second",
        [IN_VMEM] * (2 + CHUNKS),
        IN_HBM,
        floats(rows, steps, 2 * half),
        [
            pltpu.VMEM((rows, steps, 2 * half), jnp.float32),
            pltpu.SemaphoreType.DMA((2 * rows // piece,)),
        ]
        + [pltpu.VMEM((depth, 2 * half), jnp.bfloat16), pltpu.VMEM((depth, half), jnp.float32)]
        * pieces,
        1 << 32,
    )(place, tables, kept, *gots)


def swapped(block):
    return lax.ppermute(block, "space", [(0, 1), (1, 0)])


def with_partner(block, distance):
    slabs = lax.axis_size("tm")
    return lax.ppermute(block, "tm", [(slab, slab ^ distance) for slab in range(slabs)])


def among_ranks(blocks):
    return [blocks[0]] + [with_partner(block, at) for at, block in enumerate(blocks) if at]


def by_chunk(table):
    strips, _, half, rows = table.shape
    parts = table.reshape(strips, 2, CHUNKS, half // CHUNKS, rows)
    return np.swapaxes(parts, 1, 2).reshape(strips, CHUNKS, 2 * half // CHUNKS, rows)


def shards(iterate, initial):
    rows, steps, width = iterate.shape
    slabs = lax.axis_size("tm")
    total = rows * lax.axis_size("space")
    place = jnp.stack([lax.axis_index("tm"), lax.axis_index("space")]).astype(jnp.int32)
    second = second_tables(width)
    first = first_tables(total)
    decay = decay_tables(total, width)
    slab_decay = decay**steps
    half_decay = slab_decay ** ranks(slabs)
    gain = 1.0 / (1.0 - circulant_alpha * half_decay * half_decay)
    closing = constant(
        np.stack([by_chunk(table) for table in (slab_decay, half_decay, gain)], axis=2)
    )
    first_table, decays = split_constant(first), constant(decay)
    second_table = split_constant(REACTION_STEP * second)
    sums, sends = forward_second(place, iterate, initial, second_table)
    gots = [swapped(send) for send in sends]
    keeps = keep_second(place, sums, second_table, steps)
    modes, befores = [], []
    for chunk in range(CHUNKS):
        own_modes, lasts = forward_first(
            place, chunk, keeps[chunk], gots[chunk], first_table, decays, slabs
        )
        modes.append(own_modes)
        ordered, near = half_sum(place, chunk, among_ranks(lasts), closing, slabs)
        far = with_partner(near, ranks(slabs))
        befores.append(among_ranks(close(place, chunk, ordered, near, far, closing, slabs)))
    inverse_table = split_constant(np.swapaxes(first, 2, 3))
    keeps, sends = zip(
        *(
            inverse_first(place, chunk, modes[chunk], befores[chunk], inverse_table, decays, slabs)
            for chunk in range(CHUNKS)
        )
    )
    gots = [swapped(send) for send in sends]
    inverse_table = split_constant(np.swapaxes(second, 1, 2))
    kept = keep_inverse(place, keeps, inverse_table, rows, steps)
    return inverse_second(place, kept, gots, inverse_table, steps)


def solution(mesh):
    return jax.shard_map(
        shards,
        mesh=mesh,
        in_specs=(P(("group", "space"), "tm", None), P(("group", "space"), None)),
        out_specs=P(("group", "space"), "tm", None),
        check_vma=False,
    )
```

```python
import functools
import math

import jax
import jax.numpy as jnp
import numpy as np
from jax import lax
from jax.experimental import pallas as pl
from jax.experimental.pallas import tpu as pltpu
from jax.sharding import PartitionSpec as P

circulant_alpha = 0.01
DIFFUSION = 2.0
REACTION_STEP = 0.5
VMEM_BYTES = 24 * 1024 * 1024
LANES = 128
SUBLANES = 8
TILE = 16
CHUNKS = 2
PARTS = 4


def sine_table(row_index, column_index, length):
    product = np.outer(row_index + 1, column_index + 1) % (2 * (length + 1))
    return math.sqrt(2.0 / (length + 1)) * np.sin(product * (math.pi / (length + 1)))


def stencil_eigen(mode_index, length):
    return 4.0 * np.sin((mode_index + 1) * (math.pi / (2.0 * (length + 1)))) ** 2


def second_tables(width):
    half = width // 2
    return np.stack([sine_table(np.arange(half), np.arange(s, width, 2), width) for s in (0, 1)])


def first_tables(total):
    rows = total // 2
    return np.stack(
        [
            np.stack(
                [sine_table(s * rows + np.arange(rows), np.arange(c, total, 2), total) for c in (0, 1)]
            )
            for s in (0, 1)
        ]
    )


def decay_tables(total, width):
    first, second = stencil_eigen(np.arange(total), total), stencil_eigen(np.arange(width), width)
    decay = 1.0 / (1.0 + DIFFUSION * (second[:, None] + first[None, :]))
    return np.stack([np.stack([decay[s::2, c::2] for c in (0, 1)]) for s in (0, 1)])


def constant(table):
    return jnp.asarray(np.asarray(table, np.float32))


def split_constant(table):
    table = np.asarray(table, np.float32)
    high = table.astype(jnp.bfloat16)
    low = (table - high.astype(np.float32)).astype(jnp.bfloat16)
    return jnp.asarray(np.concatenate([high, high, low], axis=-2))


def store_split(ref, at, lane, block):
    depth = ref.shape[-1] // 2
    width = block.shape[-1]
    high = block.astype(jnp.bfloat16)
    low = (block - high.astype(jnp.float32)).astype(jnp.bfloat16)
    ref[(*at, pl.ds(lane, width))] = high
    ref[(*at, pl.ds(depth + lane, width))] = low


def part_of(at, rows):
    tiles = rows // TILE
    first, last = at * tiles // PARTS, (at + 1) * tiles // PARTS
    return pl.ds(first * TILE, (last - first) * TILE)


def dot(split, table):
    rows = jnp.concatenate([split, split[:, : split.shape[1] // 2]], axis=1)
    return jnp.dot(rows, table, preferred_element_type=jnp.float32)


ALONG_LANES = lax.GatherDimensionNumbers(
    offset_dims=(),
    collapsed_slice_dims=(1,),
    start_index_map=(1,),
    operand_batching_dims=(0,),
    start_indices_batching_dims=(0,),
)


def reversal():
    index = LANES - 1 - lax.broadcasted_iota(jnp.int32, (TILE, LANES), 1)
    index = index.reshape(TILE, LANES, 1)
    return lambda block: lax.gather(
        block, index, ALONG_LANES, (1, 1), mode=lax.GatherScatterMode.PROMISE_IN_BOUNDS
    )


def store_rows_reversed(ref, start, block):
    rows, width = block.shape
    index = SUBLANES - 1 - lax.broadcasted_iota(jnp.int32, (SUBLANES, width), 0)
    for row in range(0, rows, SUBLANES):
        to = pl.multiple_of(start + rows - SUBLANES - row, SUBLANES)
        ref[pl.ds(to, SUBLANES), :] = jnp.take_along_axis(
            block[row : row + SUBLANES], index, axis=0, mode="promise_in_bounds"
        )


def pitch_of(cells):
    return cells + SUBLANES * (1 - cells // SUBLANES % 2)


def steps_of(ref, cells, steps, pitch):
    lines = [ref[pl.ds(cell, steps, stride=pitch), :] for cell in cells]
    return lines[0] if len(lines) == 1 else jnp.concatenate(lines, axis=0)


IN_VMEM = pl.BlockSpec(memory_space=pltpu.VMEM)
IN_HBM = pl.BlockSpec(memory_space=pltpu.HBM)
IN_SMEM = pl.BlockSpec(memory_space=pltpu.SMEM)


def in_hbm(array):
    return pltpu.with_memory_space_constraint(array, pltpu.HBM)


def floats(*shape):
    return jax.ShapeDtypeStruct(shape, jnp.float32)


def call(kernel, name, in_specs, out_specs, out_shape, scratch, flops):
    return pl.pallas_call(
        kernel,
        in_specs=[IN_SMEM, *in_specs],
        out_specs=out_specs,
        scratch_shapes=scratch,
        out_shape=out_shape,
        compiler_params=pltpu.CompilerParams(vmem_limit_bytes=VMEM_BYTES),
        cost_estimate=pl.CostEstimate(flops=flops, bytes_accessed=1 << 23, transcendentals=0),
        name=name,
    )


def forward_second_kernel(place, field_in, initial_in, tables, sums, *refs):
    sends, refs = refs[:CHUNKS], refs[CHUNKS:]
    field, initial, table, sems, table_sem, result, *scratch = refs
    cells, steps, width = field.shape
    half = width // 2
    part = half // CHUNKS
    pieces = sems.shape[0]
    piece = cells // pieces
    group = max(TILE // steps, 1)
    pitch = sends[0].shape[0] // (steps + 1)
    body = piece * steps
    is_first = place[0] == 0
    sign = 1.0 - 2.0 * place[1].astype(jnp.float32)

    def copies(at):
        here = pl.ds(at * piece, piece)
        return [
            pltpu.make_async_copy(source.at[here], to.at[here], sems.at[at, which])
            for which, (source, to) in enumerate(((field_in, field), (initial_in, initial)))
        ]

    table_copy = pltpu.make_async_copy(tables.at[1 - place[1]], table, table_sem)

    def start(first, last):
        for at in range(first, min(last, pieces)):
            for copy in copies(at):
                copy.start()

    lanes_reversed = reversal()

    def put(other, at, sums_at, cells):
        lower = cells[:, :half]
        upper = sign * jnp.concatenate(
            [lanes_reversed(cells[:, lane : lane + LANES]) for lane in range(half, width, LANES)][::-1],
            axis=1,
        )
        sums[pl.ds(sums_at, TILE), :] = lower + upper
        store_split(other, (pl.ds(at, TILE),), 0, lower - upper)

    def prepare(at, first, last):
        split = scratch[at % len(scratch)]
        cell = at * piece
        for row in range(first, last, group):
            values = field[pl.ds(cell + row, group)]
            force = values - values * values * values
            put(split, row * steps, (cell + row) * steps, force.reshape(TILE, width))
        for row in range(0, piece if last == piece else 0, TILE):
            here = pl.ds(cell + row, TILE)
            ends = jnp.where(is_first, initial[here], field[here, steps - 1, :])
            put(split, body + row, cells * steps + cell + row, ends)

    def transform(at, part_at):
        here = part_of(part_at, piece * steps + piece)
        result[here, :] = dot(scratch[at % len(scratch)][here, :], table[...])

    def place_modes(at):
        first = cells - (at + 1) * piece
        for chunk, send in enumerate(sends):
            lanes = pl.ds(chunk * part, part)
            for row in range(piece):
                line = result[pl.ds(row * steps, steps), lanes]
                send[pl.ds(first + piece - 1 - row, steps, stride=pitch), :] = line
            ends = result[pl.ds(body, piece), lanes]
            store_rows_reversed(send, pitch * steps + first, ends)

    start(0, 1)
    table_copy.start()
    start(1, 2)
    for at in range(pieces):
        for copy in copies(at):
            copy.wait()
        start(2 * at + 2, 2 * at + 4)
        if at == 1:
            table_copy.wait()
        for part_at in range(PARTS):
            if at:
                transform(at - 1, part_at)
            prepare(at, part_at * piece // PARTS, (part_at + 1) * piece // PARTS)
        if at:
            place_modes(at - 1)
    for part_at in range(PARTS):
        transform(pieces - 1, part_at)
    place_modes(pieces - 1)


def forward_second(place, field, initial, tables):
    rows, steps, width = field.shape
    half = width // 2
    piece, pieces = min(32, rows // 2), 2
    outs = call(
        forward_second_kernel,
        "forward_second",
        [IN_HBM] * 3,
        [IN_VMEM] * (1 + CHUNKS),
        [floats((steps + 1) * rows, half)]
        + [floats((steps + 1) * pitch_of(rows), half // CHUNKS)] * CHUNKS,
        [
            pltpu.VMEM(field.shape, jnp.float32),
            pltpu.VMEM(initial.shape, jnp.float32),
            pltpu.VMEM(tables.shape[1:], jnp.bfloat16),
            pltpu.SemaphoreType.DMA((rows // piece, 2)),
            pltpu.SemaphoreType.DMA,
            pltpu.VMEM(((steps + 1) * piece, half), jnp.float32),
        ]
        + [pltpu.VMEM(((steps + 1) * piece, 2 * half), jnp.bfloat16)] * pieces,
        1 << 32,
    )(place, in_hbm(field), in_hbm(initial), in_hbm(tables))
    return outs[0], outs[1:]


def keep_second_kernel(steps, place, tables, sums, *refs):
    keeps, scratch = refs[:CHUNKS], refs[CHUNKS:]
    depth = scratch[0].shape[0]
    cells = sums.shape[0] // (steps + 1)
    pitch = keeps[0].shape[0] // (steps + 1)
    for at in range(0, sums.shape[0], depth):
        split = scratch[at // depth % 2]
        for row in range(0, depth, TILE):
            store_split(split, (pl.ds(row, TILE),), 0, sums[pl.ds(at + row, TILE)])
        result = dot(split[...], tables[place[1]])
        for chunk, keep in enumerate(keeps):
            part = keep.shape[1]
            lanes = slice(chunk * part, (chunk + 1) * part)
            body = max(0, min(depth, cells * steps - at))
            for row in range(0, body, steps):
                line = result[row : row + steps, lanes]
                keep[pl.ds((at + row) // steps, steps, stride=pitch), :] = line
            if body < depth:
                ends = pl.ds(pitch * steps + at + body - cells * steps, depth - body)
                keep[ends, :] = result[body:, lanes]


def keep_second(place, sums, tables, steps):
    rows, half = sums.shape
    shape = ((steps + 1) * pitch_of(rows // (steps + 1)), half // CHUNKS)
    return call(
        functools.partial(keep_second_kernel, steps),
        "keep_second",
        [IN_VMEM] * 2,
        [IN_VMEM] * CHUNKS,
        [floats(*shape)] * CHUNKS,
        [pltpu.VMEM((rows // 8, 2 * half), jnp.bfloat16)] * 2,
        1 << 31,
    )(place, tables, sums)


def ranks(slabs):
    return slabs // 2


def by_distance(blocks):
    return [blocks[0], *blocks[:0:-1]]


def forward_first_kernel(slabs, chunk, place, keep, got, table, decay, modes, *refs):
    size = ranks(slabs)
    lasts, (state, split, extra) = refs[:size], refs[size:]
    steps, _, part, rows = modes.shape
    pitch = keep.shape[0] // (steps + 1)
    block = split.shape[1] // part - 1
    strip = place[1]
    is_first = jnp.where(place[0] == 0, 1.0 / REACTION_STEP, 0.0)
    is_last = jnp.where(place[0] == slabs - 1, 1.0 / REACTION_STEP, 0.0)
    state[...] = jnp.zeros_like(state)
    for step in range(0, steps, block):
        count = block if step else block + 1
        for c in (0, 1):
            for at in range(count):
                from_step = steps if at == block else step + at
                cells_at = pl.ds(from_step * pitch, rows)
                near, far = keep[cells_at], got[cells_at]
                cells = near - far if c else near + far
                store_split(split, (c, pl.ds(at * part, part)), 0, cells.T)
            result = dot(split[c, pl.ds(0, count * part)], table[strip, c])
            if step == 0:
                extra[c] = result[block * part :]
                modes[0, c] = result[:part] + is_first * result[block * part :]
                modes[pl.ds(1, block - 1), c] = result[part : block * part].reshape(block - 1, part, rows)
            else:
                modes[pl.ds(step, block), c] = result.reshape(block, part, rows)
        for c in (0, 1):
            for row in range(0, part, TILE):
                tile, at_state = pl.ds(row, TILE), pl.ds(c * part + row, TILE)
                value = state[at_state]
                rate = decay[strip, c, pl.ds(chunk * part + row, TILE)]
                for at in range(block):
                    value = rate * (value + modes[step + at, c, tile])
                state[at_state] = value
    for c in (0, 1):
        at_state = pl.ds(c * part, part)
        state[at_state] = state[at_state] - is_last * extra[c]
    rank = lax.rem(place[0], size)
    share = 2 * part // size
    for partner in range(size):
        at = pl.multiple_of((rank ^ partner) * share, share)
        lasts[partner][...] = state[pl.ds(at, share)]


def forward_first(place, chunk, keep, got, tables, decays, slabs):
    rows, part = tables.shape[-1], keep.shape[1]
    steps = keep.shape[0] // pitch_of(rows) - 1
    block = min(8, steps)
    size = ranks(slabs)
    share = 2 * part // size
    outs = call(
        functools.partial(forward_first_kernel, slabs, chunk),
        "forward_first",
        [IN_VMEM] * 4,
        [IN_VMEM] * (1 + size),
        [floats(steps, 2, part, rows)] + [floats(share, rows)] * size,
        [
            pltpu.VMEM((2 * part, rows), jnp.float32),
            pltpu.VMEM((2, (block + 1) * part, 2 * rows), jnp.bfloat16),
            pltpu.VMEM((2, part, rows), jnp.float32),
        ],
        1 << 31,
    )(place, keep, got, tables, decays)
    return outs[0], outs[1:]


def half_sum_kernel(slabs, chunk, place, closing, *refs):
    size = ranks(slabs)
    lasts, ordered, total = by_distance(refs[:size]), refs[size], refs[size + 1]
    share = total.shape[0]
    rank = lax.rem(place[0], size)
    decay = closing[place[1], chunk, 0, pl.ds(pl.multiple_of(rank * share, share), share)]
    for partner in range(size):
        ordered[rank ^ partner] = lasts[partner][...]
    state = ordered[0]
    for at in range(1, size):
        state = ordered[at] + decay * state
    total[...] = state


def half_sum(place, chunk, lasts, closing, slabs):
    size = ranks(slabs)
    share, rows = lasts[0].shape
    return call(
        functools.partial(half_sum_kernel, slabs, chunk),
        "half_sum",
        [IN_VMEM] * (1 + size),
        [IN_VMEM] * 2,
        [floats(size, share, rows), floats(share, rows)],
        [],
        1 << 20,
    )(place, closing, *by_distance(lasts))


def close_kernel(slabs, chunk, place, closing, ordered, near, far, *refs):
    size = ranks(slabs)
    befores, states = refs[:size], refs[size]
    share = near.shape[0]
    rank = lax.rem(place[0], size)
    at_share = pl.ds(pl.multiple_of(rank * share, share), share)
    decay, half_decay, gain = (closing[place[1], chunk, at, at_share] for at in range(3))
    entering = jnp.where(place[0] < size, circulant_alpha, 1.0)
    state = gain * (entering * far[...] + circulant_alpha * half_decay * near[...])
    for at in range(size):
        states[at] = state
        if at < size - 1:
            state = ordered[at] + decay * state
    for partner in range(size):
        befores[partner][...] = states[rank ^ partner]


def close(place, chunk, ordered, near, far, closing, slabs):
    size, share, rows = ordered.shape
    return call(
        functools.partial(close_kernel, slabs, chunk),
        "close",
        [IN_VMEM] * 4,
        [IN_VMEM] * size,
        [floats(share, rows)] * size,
        [pltpu.VMEM((size, share, rows), jnp.float32)],
        1 << 20,
    )(place, closing, ordered, near, far)


def inverse_first_kernel(slabs, chunk, place, modes, table, decay, *refs):
    size = ranks(slabs)
    befores, (keep, send, state, split) = by_distance(refs[:size]), refs[size:]
    steps, _, part, rows = modes.shape
    pitch = keep.shape[0] // steps
    block = split.shape[1] // part
    strip = place[1]
    rank = lax.rem(place[0], size)
    share = 2 * part // size
    for partner in range(size):
        at = pl.multiple_of((rank ^ partner) * share, share)
        state[pl.ds(at, share)] = befores[partner][...]
    for step in range(0, steps, block):
        results = []
        for c in (0, 1):
            for row in range(0, part, TILE):
                tile, at_state = pl.ds(row, TILE), pl.ds(c * part + row, TILE)
                value = state[at_state]
                rate = decay[strip, c, pl.ds(chunk * part + row, TILE)]
                for at in range(block):
                    value = rate * (value + modes[step + at, c, tile])
                    store_split(split, (c, pl.ds(at * part + row, TILE)), 0, value)
                state[at_state] = value
            results.append(dot(split[c], table[strip, c]))
        even, odd = results
        for at in range(block):
            piece = slice(at * part, (at + 1) * part)
            cells_at = pl.ds((step + at) * pitch, rows)
            keep[cells_at, :] = (even[piece] + odd[piece]).T
            send[cells_at, :] = (even[piece] - odd[piece]).T


def inverse_first(place, chunk, modes, befores, tables, decays, slabs):
    steps, _, part, rows = modes.shape
    block = min(8, steps)
    return call(
        functools.partial(inverse_first_kernel, slabs, chunk),
        "inverse_first",
        [IN_VMEM] * (3 + len(befores)),
        [IN_VMEM] * 2,
        [floats(steps * pitch_of(rows), part)] * 2,
        [
            pltpu.VMEM((2 * part, rows), jnp.float32),
            pltpu.VMEM((2, block * part, 2 * rows), jnp.bfloat16),
        ],
        1 << 31,
    )(place, modes, tables, decays, *by_distance(befores))


def keep_inverse_kernel(steps, place, tables, *refs):
    keeps, out, scratch = refs[:CHUNKS], refs[CHUNKS], refs[CHUNKS + 1 :]
    part = keeps[0].shape[1]
    pitch = keeps[0].shape[0] // steps
    depth = scratch[0].shape[0]
    group = max(TILE // steps, 1)
    for at in range(0, out.shape[0], depth):
        split = scratch[at // depth % 2]
        for row in range(0, depth, TILE):
            cell = (at + row) // steps
            for chunk, keep in enumerate(keeps):
                cells = steps_of(keep, range(cell, cell + group), steps, pitch)
                store_split(split, (pl.ds(row, TILE),), chunk * part, cells)
        out[pl.ds(at, depth)] = dot(split[...], tables[place[1]])


def keep_inverse(place, keeps, tables, rows, steps):
    half = keeps[0].shape[1] * CHUNKS
    return call(
        functools.partial(keep_inverse_kernel, steps),
        "keep_inverse",
        [IN_VMEM] * (1 + CHUNKS),
        IN_VMEM,
        floats(rows * steps, half),
        [pltpu.VMEM((rows * steps // 8, 2 * half), jnp.bfloat16)] * 2,
        1 << 31,
    )(place, tables, *keeps)


def inverse_second_kernel(place, tables, kept, *refs):
    gots, target, out, sems, scratch = (
        refs[:CHUNKS], refs[CHUNKS], refs[CHUNKS + 1], refs[CHUNKS + 2], refs[CHUNKS + 3 :]
    )
    cells, steps, width = out.shape
    half = width // 2
    part = half // CHUNKS
    pitch = gots[0].shape[0] // steps
    count = len(scratch) // 2
    piece = scratch[0].shape[0] // steps
    pieces = cells // piece
    flight = cells // sems.shape[0]
    group = max(TILE // steps, 1)
    strip = place[1]
    sign = 1.0 - 2.0 * strip.astype(jnp.float32)

    def copy(at):
        here = pl.ds(at * flight, flight)
        return pltpu.make_async_copy(out.at[here], target.at[here], sems.at[at])

    lanes_reversed = reversal()

    def prepare(at):
        split, result = scratch[2 * (at % count) : 2 * (at % count) + 2]
        for row in range(0, piece, group):
            mirrors = [cells - 1 - at * piece - row - cell for cell in range(group)]
            for chunk, got in enumerate(gots):
                values = steps_of(got, mirrors, steps, pitch)
                store_split(split, (pl.ds(row * steps, TILE),), chunk * part, values)

    def product(at, part_at):
        split, result = scratch[2 * (at % count) : 2 * (at % count) + 2]
        here = part_of(part_at, piece * steps)
        result[here, :] = dot(split[here, :], tables[1 - strip])

    def finish(at, part_at):
        result = scratch[2 * (at % count) + 1]
        for row in range(part_at * piece // PARTS, (part_at + 1) * piece // PARTS, group):
            first = kept[pl.ds((at * piece + row) * steps, TILE)]
            second = result[pl.ds(row * steps, TILE)]
            upper = sign * (first - second)
            parts = [
                lanes_reversed(upper[:, lane : lane + LANES]) for lane in range(0, half, LANES)
            ][::-1]
            whole = jnp.concatenate([first + second, *parts], axis=1)
            out[pl.ds(at * piece + row, group)] = whole.reshape(group, TILE // group, width)
            done = at * piece + row + group
            if done % flight == 0:
                copy(done // flight - 1).start()

    for at in range(pieces):
        prepare(at)
        for part_at in range(PARTS):
            product(at, part_at)
            if at:
                finish(at - 1, part_at)
    for part_at in range(PARTS):
        finish(pieces - 1, part_at)
    for at in range(sems.shape[0]):
        copy(at).wait()


def inverse_second(place, kept, gots, tables, steps):
    rows, half = kept.shape[0] // steps, kept.shape[1]
    piece, pieces = min(32, rows // 2), 2
    depth = steps * piece
    return call(
        inverse_second_kernel,
        "inverse_second",
        [IN_VMEM] * (2 + CHUNKS),
        IN_HBM,
        floats(rows, steps, 2 * half),
        [
            pltpu.VMEM((rows, steps, 2 * half), jnp.float32),
            pltpu.SemaphoreType.DMA((2 * rows // piece,)),
        ]
        + [pltpu.VMEM((depth, 2 * half), jnp.bfloat16), pltpu.VMEM((depth, half), jnp.float32)]
        * pieces,
        1 << 32,
    )(place, tables, kept, *gots)


def swapped(block):
    return lax.ppermute(block, "space", [(0, 1), (1, 0)])


def with_partner(block, distance):
    slabs = lax.axis_size("tm")
    return lax.ppermute(block, "tm", [(slab, slab ^ distance) for slab in range(slabs)])


def among_ranks(blocks):
    return [blocks[0]] + [with_partner(block, at) for at, block in enumerate(blocks) if at]


def by_chunk(table):
    strips, _, half, rows = table.shape
    parts = table.reshape(strips, 2, CHUNKS, half // CHUNKS, rows)
    return np.swapaxes(parts, 1, 2).reshape(strips, CHUNKS, 2 * half // CHUNKS, rows)


def shards(iterate, initial):
    rows, steps, width = iterate.shape
    slabs = lax.axis_size("tm")
    total = rows * lax.axis_size("space")
    place = jnp.stack([lax.axis_index("tm"), lax.axis_index("space")]).astype(jnp.int32)
    second = second_tables(width)
    first = first_tables(total)
    decay = decay_tables(total, width)
    slab_decay = decay**steps
    half_decay = slab_decay ** ranks(slabs)
    gain = 1.0 / (1.0 - circulant_alpha * half_decay * half_decay)
    closing = constant(
        np.stack([by_chunk(table) for table in (slab_decay, half_decay, gain)], axis=2)
    )
    first_table, decays = split_constant(first), constant(decay)
    second_table = split_constant(REACTION_STEP * second)
    sums, sends = forward_second(place, iterate, initial, second_table)
    gots = [swapped(send) for send in sends]
    keeps = keep_second(place, sums, second_table, steps)
    modes, befores = [], []
    for chunk in range(CHUNKS):
        own_modes, lasts = forward_first(
            place, chunk, keeps[chunk], gots[chunk], first_table, decays, slabs
        )
        modes.append(own_modes)
        ordered, near = half_sum(place, chunk, among_ranks(lasts), closing, slabs)
        far = with_partner(near, ranks(slabs))
        befores.append(among_ranks(close(place, chunk, ordered, near, far, closing, slabs)))
    inverse_table = split_constant(np.swapaxes(first, 2, 3))
    keeps, sends = zip(
        *(
            inverse_first(place, chunk, modes[chunk], befores[chunk], inverse_table, decays, slabs)
            for chunk in range(CHUNKS)
        )
    )
    gots = [swapped(send) for send in sends]
    inverse_table = split_constant(np.swapaxes(second, 1, 2))
    kept = keep_inverse(place, keeps, inverse_table, rows, steps)
    return inverse_second(place, kept, gots, inverse_table, steps)


def solution(mesh):
    return jax.shard_map(
        shards,
        mesh=mesh,
        in_specs=(P(("group", "space"), "tm", None), P(("group", "space"), None)),
        out_specs=P(("group", "space"), "tm", None),
        check_vma=False,
    )
```
